32 devices in a mesh: dp: 4 (over z), pipe: 4 (over y, x), tensor: 2 (over core).
Axes of the slice: x: 2, y: 2, z: 4, core: 2. Of those that a mesh axis runs over, the one named last changes fastest.
Arguments:
- tokens: bfloat16 [4096, 8192], P('dp', ('pipe', 'tensor')), may hold values from -6 to 6
- key_value_weight: bfloat16 [8192, 2048], P(('pipe', 'tensor')), may hold values from -0.0625 to 0.0625
- adapter_down: bfloat16 [24, 8192, 128], P(None, ('pipe', 'tensor', 'dp')), may hold values from -0.0625 to 0.0625
- adapter_up: bfloat16 [24, 64, 2048], P(None, 'dp'), may hold values from -0.75 to 0.75
- tenant_of_block: int32 [32], replicated, may hold values from 0 to 23
- slot_of_tenant: int32 [24], replicated, may hold values from 0 to 23, each once
- cotangent: bfloat16 [4096, 2048], P(('dp', 'pipe', 'tensor')), may hold values from -1.5 to 1.5
Outputs:
- key_value: bfloat16 [4096, 2048], P(('dp', 'pipe', 'tensor'))
- input_grad: bfloat16 [4096, 8192], P('dp', ('pipe', 'tensor'))
- grad_a: float32 [24, 8192, 128], P(None, ('pipe', 'tensor', 'dp'))
- grad_b: float32 [24, 64, 2048], P(None, 'dp', ('pipe', 'tensor'))
The draws below stay inside these ranges and needn't reach their ends.
Inputs may be any that keep to these rules, and one draw needn't show every extreme that they name: `slot_of_tenant`: each slot holds exactly one tenant.
All inputs are finite; a program needn't handle non-finite values.
Results may differ from the reference program's by a relative error of at most 0.017.
Values may be sent and summed in bfloat16 or wider, within the bound.
No kernel may reach another device: no remote copies, remote signals or barrier semaphores. Data moves between devices by JAX's collectives and lax.ppermute only.
A program may use at most 64 MiB of HBM per device.

```python
import math
import jax
import jax.numpy as jnp
import numpy as np
from jax import lax

MODEL_WIDTH = 8192
KEY_WIDTH = 1024
ADAPTER_RANK = 64
BLOCK = 128
TENANT_COUNT = 24
TOKENS = 4096
BLOCKS = 32
N_PIPE = 4
N_TENSOR = 2


def with_ends(array, key, low, largest):
    extent = array.shape
    index_at = [jax.random.randint(jax.random.fold_in(key, axis), (), 0, extent[axis]) for axis in range(len(extent))]
    array = array.at[tuple(index_at)].set(low)
    longest = extent.index(max(extent))
    index_at[longest] = (index_at[longest] + 1) % extent[longest]
    return array.at[tuple(index_at)].set(largest)


def with_spikes(values, rng, source, target, shards_of, factor):
    owner, partner = [(jnp.arange(values.shape[axis_at]) // (values.shape[axis_at] // shards_of)).reshape([-1 if axis == axis_at else 1 for axis in range(values.ndim)]) for axis_at in (source, target)]
    chosen = jax.random.permutation(rng, shards_of)[partner]
    strong = (owner == chosen) | (owner == (partner + shards_of // 2) % shards_of)
    return jnp.where(strong, factor * values, values)


def levels(rng, dims, cuts, smallest, high):
    factor_of, own = 1.0, jax.random.fold_in(rng, 6)
    for position, blocks in cuts:
        heights = jnp.exp(jax.random.uniform(jax.random.fold_in(own, position), (blocks,), jnp.float32, smallest / len(cuts), high / len(cuts)))
        factor_of = factor_of * jnp.repeat(heights, dims[position] // blocks).reshape([-1 if axis == position else 1 for axis in range(len(dims))])
    return factor_of


def rank_table(count, lean):
    weights = [(1 << 20) // math.isqrt(standing ** lean) + 1 for standing in range(1, count + 1)]
    spread = 1 + sum(weights) // (1 << 30)
    return np.cumsum(np.array([max(1, weight // spread) for weight in weights]))


def ranked_ids(rng, extent, count, lean):
    listing = rank_table(count, lean)
    pick = jax.random.randint(jax.random.fold_in(rng, 1), extent, 0, int(listing[count - 1]))
    standing = jnp.searchsorted(jnp.asarray(listing, jnp.int32), pick, side="right")
    return jax.random.permutation(jax.random.fold_in(rng, 2), count)[standing].astype(jnp.int32)


def gaussian(own_key, dims, scale, bound, split=(), held_as=jnp.bfloat16):
    values = jax.random.normal(own_key, dims, jnp.float32) * scale
    if len(split) > 0:
        values = levels(own_key, dims, split, -0.22, 0.18) * values
    return jnp.clip(values, min=-bound, max=bound).astype(held_as)


def bell_draw_with(rng, dims, scale, limit, split, heavy, kind=jnp.bfloat16):
    result = scale * jax.random.normal(rng, dims, jnp.float32)
    if split:
        result = result * levels(rng, dims, split, -0.22, 0.18)
    return jnp.clip(with_spikes(result, jax.random.fold_in(rng, 3), *heavy), -limit, limit).astype(kind)


def setup_inputs(seed: int = 0) -> dict:
    keys = jax.random.split(jax.random.key(seed), 8)
    return {
        "tokens": bell_draw_with(keys[0], (TOKENS, MODEL_WIDTH), 1.0, 6.0, ((0, 4), (1, 8)), (1, 0, 8, 2.0)),
        "key_value_weight": gaussian(keys[1], (MODEL_WIDTH, 2 * KEY_WIDTH), MODEL_WIDTH ** -0.5, 0.0625, ((0, 8),)),
        "adapter_down": gaussian(keys[2], (TENANT_COUNT, MODEL_WIDTH, 2 * ADAPTER_RANK), MODEL_WIDTH ** -0.5, 0.0625, ((1, 32),)),
        "adapter_up": gaussian(keys[3], (TENANT_COUNT, ADAPTER_RANK, 2 * KEY_WIDTH), ADAPTER_RANK ** -0.5, 0.75, ((1, 4),)),
        "tenant_of_block": with_ends(ranked_ids(keys[4], (BLOCKS,), TENANT_COUNT, 2), jax.random.fold_in(keys[4], 3), 0, TENANT_COUNT - 1).astype(jnp.int32),
        "slot_of_tenant": jax.random.permutation(keys[5], TENANT_COUNT).astype(jnp.int32),
        "cotangent": gaussian(keys[6], (TOKENS, 2 * KEY_WIDTH), 0.25, 1.5, ((0, 32),)),
    }


def reference(tokens, key_value_weight, adapter_down, adapter_up, tenant_of_block, slot_of_tenant, cotangent):
    group_total = N_PIPE * N_TENSOR
    feature_count = MODEL_WIDTH // group_total
    token_count = tokens.shape[0]
    block_count = token_count // BLOCK
    slot_of_block = slot_of_tenant[tenant_of_block].astype(jnp.int32)
    down_blocks = adapter_down[slot_of_block]
    up_blocks = adapter_up[slot_of_block]

    def one_group(totals, group_index):
        base_sum, low_sum = totals
        first_col = group_index * feature_count
        x_piece = lax.dynamic_slice_in_dim(tokens, first_col, feature_count, 1)
        w_piece = lax.dynamic_slice_in_dim(key_value_weight, first_col, feature_count, 0)
        base_piece = jnp.dot(x_piece, w_piece, preferred_element_type=jnp.float32).astype(jnp.bfloat16)
        base_piece = lax.optimization_barrier(base_piece).astype(jnp.float32)
        a_piece = lax.dynamic_slice_in_dim(down_blocks, first_col, feature_count, 1)
        low_piece = jnp.einsum('bif,bfr->bir', x_piece.reshape(block_count, BLOCK, feature_count).astype(jnp.float32), a_piece.astype(jnp.float32))
        low_piece = lax.optimization_barrier(low_piece.astype(jnp.bfloat16)).astype(jnp.float32)
        return (base_sum + base_piece, low_sum + low_piece), None

    start_totals = (jnp.zeros((token_count, 2 * KEY_WIDTH), jnp.float32), jnp.zeros((block_count, BLOCK, 2 * ADAPTER_RANK), jnp.float32))
    (base_sum, low_sum), _ = lax.scan(one_group, start_totals, jnp.arange(group_total, dtype=jnp.int32))
    low_float = lax.optimization_barrier(low_sum.astype(jnp.bfloat16)).astype(jnp.float32)
    b_float = up_blocks.astype(jnp.float32)
    lowrank = jnp.concatenate([
        jnp.einsum('bir,brc->bic', low_float[..., :ADAPTER_RANK], b_float[..., :KEY_WIDTH]),
        jnp.einsum('bir,brc->bic', low_float[..., ADAPTER_RANK:], b_float[..., KEY_WIDTH:])], axis=2)
    key_value = (base_sum + lowrank.reshape(token_count, 2 * KEY_WIDTH)).astype(jnp.bfloat16)

    cot_blocks = cotangent.reshape(block_count, BLOCK, 2 * KEY_WIDTH).astype(jnp.float32)
    low_grad = jnp.concatenate([
        jnp.einsum('bic,brc->bir', cot_blocks[..., :KEY_WIDTH], b_float[..., :KEY_WIDTH]),
        jnp.einsum('bic,brc->bir', cot_blocks[..., KEY_WIDTH:], b_float[..., KEY_WIDTH:])], axis=2)
    low_grad = lax.optimization_barrier(low_grad.astype(jnp.bfloat16)).astype(jnp.float32)
    input_grad = jnp.dot(cotangent, key_value_weight.T, preferred_element_type=jnp.float32)
    input_grad = input_grad + jnp.einsum('bir,bfr->bif', low_grad, down_blocks.astype(jnp.float32)).reshape(token_count, MODEL_WIDTH)
    input_grad = input_grad.astype(jnp.bfloat16)

    tok_blocks = tokens.reshape(block_count, BLOCK, MODEL_WIDTH).astype(jnp.float32)
    grad_a_blocks = jnp.einsum('bif,bir->bfr', tok_blocks, low_grad)
    grad_a = jax.ops.segment_sum(grad_a_blocks, slot_of_block, num_segments=TENANT_COUNT)
    grad_b_blocks = jnp.concatenate([
        jnp.einsum('bir,bic->brc', low_float[..., :ADAPTER_RANK], cot_blocks[..., :KEY_WIDTH]),
        jnp.einsum('bir,bic->brc', low_float[..., ADAPTER_RANK:], cot_blocks[..., KEY_WIDTH:])], axis=2)
    grad_b = jax.ops.segment_sum(grad_b_blocks, slot_of_block, num_segments=TENANT_COUNT)
    return (key_value, input_grad, grad_a, grad_b)
```

```python
import functools

import jax
import jax.numpy as jnp
from jax import lax
from jax.experimental import pallas as pl
from jax.experimental.pallas import tpu as pltpu
from jax.sharding import PartitionSpec as P

KEY_WIDTH = 1024
ADAPTER_RANK = 64
BLOCK = 128
RANKS = 2 * ADAPTER_RANK
WIDTH = 2 * KEY_WIDTH
VMEM_LIMIT = 48 * 1024 * 1024
LAST_BOTH = (((1,), (1,)), ((), ()))


def params(**more):
    return pltpu.CompilerParams(vmem_limit_bytes=VMEM_LIMIT, **more)


def pick_kernel(tenant_ref, slot_ref, own_ref, down_ref, up_ref, a_ref, b_ref, a_sem, b_sem):
    block_count = a_ref.shape[0]
    data_count = b_ref.shape[0]
    blocks_dev = block_count // data_count

    def a_copy(block):
        slot = slot_ref[tenant_ref[block]]
        return pltpu.make_async_copy(down_ref.at[slot], a_ref.at[block], a_sem.at[block])

    def b_copy(data):
        slot = slot_ref[tenant_ref[data * blocks_dev + own_ref[0]]]
        return pltpu.make_async_copy(up_ref.at[slot], b_ref.at[data], b_sem.at[data])

    @pl.loop(0, data_count)
    def _(data):
        b_copy(data).start()

    @pl.loop(0, block_count)
    def _(block):
        a_copy(block).start()

    @pl.loop(0, data_count)
    def _(data):
        b_copy(data).wait()

    @pl.loop(0, block_count)
    def _(block):
        a_copy(block).wait()


def pick(tenant_of_block, slot_of_tenant, own_block, adapter_down, adapter_up, data_count):
    block_count = tenant_of_block.shape[0]
    smem = pl.BlockSpec(memory_space=pltpu.SMEM)
    hbm = pl.BlockSpec(memory_space=pl.ANY)
    return pl.pallas_call(
        pick_kernel,
        out_shape=(
            jax.ShapeDtypeStruct((block_count,) + adapter_down.shape[1:], adapter_down.dtype),
            jax.ShapeDtypeStruct((data_count,) + adapter_up.shape[1:], adapter_up.dtype),
        ),
        in_specs=[smem, smem, smem, hbm, hbm],
        out_specs=(hbm, hbm),
        scratch_shapes=[
            pltpu.SemaphoreType.DMA((block_count,)),
            pltpu.SemaphoreType.DMA((data_count,)),
        ],
        name="pick_rows",
    )(tenant_of_block, slot_of_tenant, own_block, adapter_down, adapter_up)


def base_kernel(x_ref, w_ref, out_ref):
    pipe_count, _, rows, depth = x_ref.shape
    x = x_ref[...].reshape(pipe_count * rows, depth)
    y = jnp.dot(x, w_ref[...], preferred_element_type=jnp.float32)
    out_ref[0] = y.astype(out_ref.dtype).reshape(out_ref.shape[1:])


def base_product(tokens, weight, pipe_count, tensor_count):
    tok_dev, depth = tokens.shape
    rows = tok_dev // (pipe_count * tensor_count)
    tile = 512
    return pl.pallas_call(
        base_kernel,
        grid=(WIDTH // tile, tensor_count),
        out_shape=jax.ShapeDtypeStruct((tensor_count, pipe_count, rows, WIDTH), jnp.bfloat16),
        in_specs=[
            pl.BlockSpec((pipe_count, 1, rows, depth), lambda n, t: (0, t, 0, 0)),
            pl.BlockSpec((depth, tile), lambda n, t: (0, n)),
        ],
        out_specs=pl.BlockSpec((1, pipe_count, rows, tile), lambda n, t: (t, 0, 0, n)),
        compiler_params=params(),
        cost_estimate=pl.CostEstimate(
            flops=2 * tok_dev * depth * WIDTH, bytes_accessed=16 * 2**20, transcendentals=0
        ),
        name="base_product",
    )(tokens.reshape(pipe_count, tensor_count, rows, depth), weight)


def low_kernel(x_ref, a_ref, out_ref):
    depth = x_ref.shape[1]
    a = a_ref[...].reshape(depth, RANKS)
    out_ref[...] = jnp.dot(x_ref[...], a, preferred_element_type=jnp.float32).astype(out_ref.dtype)


def low_product(tokens, down):
    tok_dev, depth = tokens.shape
    data_count, blocks_dev, down_rows, _ = down.shape
    return pl.pallas_call(
        low_kernel,
        grid=(blocks_dev,),
        out_shape=jax.ShapeDtypeStruct((tok_dev, RANKS), jnp.bfloat16),
        in_specs=[
            pl.BlockSpec((BLOCK, depth), lambda b: (b, 0)),
            pl.BlockSpec((data_count, 1, down_rows, RANKS), lambda b: (0, b, 0, 0)),
        ],
        out_specs=pl.BlockSpec((BLOCK, RANKS), lambda b: (b, 0)),
        compiler_params=params(),
        cost_estimate=pl.CostEstimate(
            flops=2 * tok_dev * depth * RANKS, bytes_accessed=5 * 2**20, transcendentals=0
        ),
        name="low_product",
    )(tokens, down)


def input_grad_kernel(cot_ref, w_ref, grad_ref, a_ref, out_ref):
    tensor_count, pipe_count, rows, width = cot_ref.shape
    cot = cot_ref[...].reshape(tensor_count * pipe_count * rows, width)
    base = lax.dot_general(cot, w_ref[...], LAST_BOTH, preferred_element_type=jnp.float32)
    for t in range(tensor_count):
        for p in range(pipe_count):
            piece = t * pipe_count + p
            first = (p * tensor_count + t) * rows
            a = a_ref[:, first // BLOCK].reshape(out_ref.shape[1], RANKS)
            low = lax.dot_general(
                grad_ref[first : first + rows], a, LAST_BOTH, preferred_element_type=jnp.float32
            )
            out_ref[first : first + rows] = (base[piece * rows : (piece + 1) * rows] + low).astype(
                out_ref.dtype
            )


def input_gradient(cot, weight, grad_low, down):
    data_count, blocks_dev, down_rows, _ = down.shape
    depth = weight.shape[0]
    tok_dev = grad_low.shape[0]
    group = next((n for n in range(1, data_count) if n * down_rows % 256 == 0), data_count)
    tile = group * down_rows
    return pl.pallas_call(
        input_grad_kernel,
        grid=(data_count // group,),
        out_shape=jax.ShapeDtypeStruct((tok_dev, depth), jnp.bfloat16),
        in_specs=[
            pl.BlockSpec(cot.shape, lambda d: (0, 0, 0, 0)),
            pl.BlockSpec((tile, WIDTH), lambda d: (d, 0)),
            pl.BlockSpec((tok_dev, RANKS), lambda d: (0, 0)),
            pl.BlockSpec((group, blocks_dev, down_rows, RANKS), lambda d: (d, 0, 0, 0)),
        ],
        out_specs=pl.BlockSpec((tok_dev, tile), lambda d: (0, d)),
        compiler_params=params(),
        cost_estimate=pl.CostEstimate(
            flops=2 * tok_dev * depth * (WIDTH + RANKS),
            bytes_accessed=12 * 2**20,
            transcendentals=0,
        ),
        name="input_gradient",
    )(cot, weight, grad_low, down)


def grad_a_kernel(tenant_ref, slot_ref, x_ref, grad_ref, out_ref):
    data_count, _, tok_dev = x_ref.shape
    blocks_dev = tok_dev // BLOCK
    out_ref[...] = jnp.zeros(out_ref.shape, out_ref.dtype)

    for data in range(data_count):
        for block in range(blocks_dev):
            slot = slot_ref[tenant_ref[data * blocks_dev + block]]
            x = x_ref[data, :, block * BLOCK : (block + 1) * BLOCK]
            grad = grad_ref[data, block * BLOCK : (block + 1) * BLOCK]
            out_ref[slot] += jnp.dot(x, grad, preferred_element_type=jnp.float32)


def grad_down(tenant_of_block, slot_of_tenant, x_features, grad_low):
    data_count, down_rows, tok_dev = x_features.shape
    slots = slot_of_tenant.shape[0]
    tile = 128 if down_rows % 128 == 0 else down_rows
    smem = pl.BlockSpec(memory_space=pltpu.SMEM)
    return pl.pallas_call(
        grad_a_kernel,
        grid=(down_rows // tile,),
        out_shape=jax.ShapeDtypeStruct((slots, down_rows, RANKS), jnp.float32),
        in_specs=[
            smem,
            smem,
            pl.BlockSpec((data_count, tile, tok_dev), lambda f: (0, f, 0)),
            pl.BlockSpec((data_count, tok_dev, RANKS), lambda f: (0, 0, 0)),
        ],
        out_specs=pl.BlockSpec((slots, tile, RANKS), lambda f: (0, f, 0)),
        compiler_params=params(),
        cost_estimate=pl.CostEstimate(
            flops=2 * data_count * tok_dev * down_rows * RANKS,
            bytes_accessed=6 * 2**20,
            transcendentals=0,
        ),
        name="grad_down",
    )(tenant_of_block, slot_of_tenant, x_features, grad_low)


def halves(product, left, right):
    return jnp.concatenate([product(*pair) for pair in zip(left, right)], axis=1)


def body(
    tokens, key_value_weight, adapter_down, adapter_up, tenant_of_block, slot_of_tenant, cotangent
):
    data_count = lax.axis_size("dp")
    pipe_count = lax.axis_size("pipe")
    tensor_count = lax.axis_size("tensor")
    group_count = pipe_count * tensor_count
    my_group = lax.axis_index(("pipe", "tensor"))
    tok_dev, feature_count = tokens.shape
    blocks_dev = tok_dev // BLOCK
    row_count = tok_dev // group_count
    slots = slot_of_tenant.shape[0]
    all_blocks = tenant_of_block.shape[0]
    down_rows = adapter_down.shape[1]
    up_rows = adapter_up.shape[1]

    cot_chips = lax.all_gather(cotangent, "pipe", axis=0, tiled=False)
    cot_all = lax.all_gather(cot_chips, "tensor", axis=0, tiled=False)

    own_block = (my_group * row_count // BLOCK).reshape(1)
    a_send, b_send = pick(
        tenant_of_block, slot_of_tenant, own_block, adapter_down, adapter_up, data_count
    )
    b_own = lax.all_to_all(b_send, "dp", split_axis=0, concat_axis=0, tiled=True)
    b_own = b_own.reshape(data_count * up_rows, WIDTH)
    a_recv = lax.all_to_all(
        a_send.reshape(data_count, blocks_dev, down_rows, RANKS),
        "dp",
        split_axis=0,
        concat_axis=0,
        tiled=True,
    )

    x_send = tokens.T.reshape(data_count, down_rows, tok_dev)
    x_recv = lax.all_to_all(x_send, "dp", split_axis=0, concat_axis=0, tiled=True)

    base = base_product(tokens, key_value_weight, pipe_count, tensor_count)
    base_chips = lax.psum_scatter(base, "tensor", scatter_dimension=0, tiled=True)
    base_rows = lax.psum_scatter(
        base_chips.reshape(pipe_count, row_count, WIDTH), "pipe", scatter_dimension=0, tiled=True
    ).reshape(row_count, WIDTH)

    low_part = low_product(tokens, a_recv)
    low_all = lax.psum(low_part, ("pipe", "tensor"))
    low_rows = lax.dynamic_slice_in_dim(low_all, my_group * row_count, row_count, 0)

    left = lambda m: (m[:, :ADAPTER_RANK], m[:, ADAPTER_RANK:])
    wide = lambda m: (m[:, :KEY_WIDTH], m[:, KEY_WIDTH:])
    lowrank = halves(
        lambda p, q: jnp.dot(p, q, preferred_element_type=jnp.float32), left(low_rows), wide(b_own)
    )
    key_value = (base_rows.astype(jnp.float32) + lowrank).astype(jnp.bfloat16)

    grad_rows = halves(
        lambda p, q: lax.dot_general(p, q, LAST_BOTH, preferred_element_type=jnp.float32),
        wide(cotangent),
        wide(b_own),
    ).astype(jnp.bfloat16)
    grad_all = lax.all_gather(grad_rows, ("dp", "pipe", "tensor"), axis=0, tiled=True)
    grad_all = grad_all.reshape(data_count, tok_dev, RANKS)
    grad_low = lax.dynamic_index_in_dim(grad_all, lax.axis_index("dp"), 0, False)

    input_grad = input_gradient(cot_all, key_value_weight, grad_low, a_recv)
    grad_a = grad_down(tenant_of_block, slot_of_tenant, x_recv, grad_all)

    col_count = WIDTH // group_count
    col_start = my_group * col_count
    half_index = col_start // KEY_WIDTH
    low_half = lax.dynamic_slice_in_dim(
        low_all, half_index * ADAPTER_RANK, ADAPTER_RANK, 1
    ).reshape(blocks_dev, BLOCK, ADAPTER_RANK)
    cot_cols = lax.dynamic_slice_in_dim(cot_all, col_start, col_count, 3)
    cot_cols = cot_cols.transpose(1, 0, 2, 3).reshape(blocks_dev, BLOCK, col_count)
    grad_b_part = jnp.einsum("bir,bic->brc", low_half, cot_cols, preferred_element_type=jnp.float32)
    grad_b_part = grad_b_part.astype(jnp.bfloat16).reshape(
        blocks_dev, data_count, up_rows, col_count
    )
    grad_b_recv = lax.all_to_all(
        grad_b_part.transpose(1, 0, 2, 3), "dp", split_axis=0, concat_axis=0, tiled=True
    ).astype(jnp.float32)
    tenant_ids = lax.broadcasted_iota(jnp.int32, (all_blocks, slots), 1)
    slot_of_block = jnp.sum(
        jnp.where(tenant_of_block[:, None] == tenant_ids, slot_of_tenant[None, :], 0), axis=1
    )
    slot_weight = (slot_of_block[:, None] == tenant_ids).astype(jnp.float32)
    grad_b = jnp.einsum(
        "bt,bx->tx",
        slot_weight,
        grad_b_recv.reshape(all_blocks, up_rows * col_count),
        precision=lax.Precision.HIGHEST,
    ).reshape(slots, up_rows, col_count)
    return (key_value, input_grad, grad_a, grad_b)


def solution(mesh):
    placed = (
        P("dp", ("pipe", "tensor")),
        P(("pipe", "tensor"), None),
        P(None, ("pipe", "tensor", "dp"), None),
        P(None, "dp", None),
        P(),
        P(),
        P(("dp", "pipe", "tensor"), None),
    )
    return jax.shard_map(
        body,
        mesh=mesh,
        in_specs=placed,
        out_specs=(
            P(("dp", "pipe", "tensor"), None),
            P("dp", ("pipe", "tensor")),
            P(None, ("pipe", "tensor", "dp"), None),
            P(None, "dp", ("pipe", "tensor")),
        ),
        check_vma=False,
    )
```

```python
import jax
import jax.numpy as jnp
from jax import lax
from jax.experimental import pallas as pl
from jax.experimental.pallas import tpu as pltpu
from jax.sharding import PartitionSpec as P

KEY_WIDTH = 1024
ADAPTER_RANK = 64
BLOCK = 128
RANKS = 2 * ADAPTER_RANK
WIDTH = 2 * KEY_WIDTH
VMEM_LIMIT = 48 * 1024 * 1024
LAST_BOTH = (((1,), (1,)), ((), ()))
FIRST_BOTH = (((0,), (0,)), ((), ()))
SMEM = pl.BlockSpec(memory_space=pltpu.SMEM)
VMEM = pl.BlockSpec(memory_space=pltpu.VMEM)
HBM = pl.BlockSpec(memory_space=pl.ANY)


def call(kernel, name, flops, mib, **more):
    return pl.pallas_call(
        kernel,
        compiler_params=pltpu.CompilerParams(vmem_limit_bytes=VMEM_LIMIT),
        cost_estimate=pl.CostEstimate(
            flops=int(flops), bytes_accessed=int(mib * 2**20), transcendentals=0
        ),
        name=name,
        **more,
    )


def shift(piece, axis, step):
    count = lax.axis_size(axis)
    return lax.ppermute(piece, axis, [(i, (i + step) % count) for i in range(count)])


def wrap(index, count):
    return lax.rem(index + 2 * count, count)


def pick(tenant_of_block, slot_of_tenant, place, own_block, adapter_down, adapter_up, data_count):
    block_count = tenant_of_block.shape[0]
    blocks_dev = block_count // data_count

    def kernel(tenant_ref, slot_ref, place_ref, own_ref, down_ref, up_ref, a_ref, *rest):
        b_refs, (a_sem, b_sem) = rest[:data_count], rest[data_count:]

        def a_copy(block):
            slot = slot_ref[tenant_ref[block]]
            return pltpu.make_async_copy(down_ref.at[slot], a_ref.at[block], a_sem.at[block])

        def b_copy(k):
            data = wrap(place_ref[0] + k, data_count)
            slot = slot_ref[tenant_ref[data * blocks_dev + own_ref[0]]]
            return pltpu.make_async_copy(up_ref.at[slot], b_refs[k], b_sem.at[k])

        for k in range(data_count):
            b_copy(k).start()

        @pl.loop(0, block_count)
        def _(block):
            a_copy(block).start()

        for k in range(data_count):
            b_copy(k).wait()

        @pl.loop(0, block_count)
        def _(block):
            a_copy(block).wait()

    up_shape = jax.ShapeDtypeStruct(adapter_up.shape[1:], adapter_up.dtype)
    down_shape = jax.ShapeDtypeStruct((block_count,) + adapter_down.shape[1:], adapter_down.dtype)
    out = call(
        kernel,
        "pick_rows",
        0,
        4,
        out_shape=(down_shape,) + (up_shape,) * data_count,
        in_specs=[SMEM, SMEM, SMEM, SMEM, HBM, HBM],
        out_specs=(VMEM,) * (1 + data_count),
        scratch_shapes=[
            pltpu.SemaphoreType.DMA((block_count,)),
            pltpu.SemaphoreType.DMA((data_count,)),
        ],
    )(tenant_of_block, slot_of_tenant, place, own_block, adapter_down, adapter_up)
    return out[0], out[1:]


def base_product(place, tokens, weight, first, count):
    pipe_count, tensor_count, rows, depth = tokens.shape
    tile = 1024

    def kernel(place_ref, x_ref, w_ref, out_ref):
        x = x_ref[...].reshape(pipe_count * rows, depth)
        y = jnp.dot(x, w_ref[...], preferred_element_type=jnp.float32).astype(out_ref.dtype)
        for chip in range(pipe_count):
            out_ref[0, wrap(chip - place_ref[1], pipe_count)] = y[chip * rows : (chip + 1) * rows]

    return call(
        kernel,
        "base_product",
        2 * pipe_count * count * rows * depth * WIDTH,
        8,
        grid_spec=pltpu.PrefetchScalarGridSpec(
            num_scalar_prefetch=1,
            grid=(WIDTH // tile, count),
            in_specs=[
                pl.BlockSpec(
                    (pipe_count, 1, rows, depth),
                    lambda n, s, at: (0, wrap(at[2] + s + first, tensor_count), 0, 0),
                ),
                pl.BlockSpec((depth, tile), lambda n, s, at: (0, n)),
            ],
            out_specs=pl.BlockSpec((1, pipe_count, rows, tile), lambda n, s, at: (s, 0, 0, n)),
        ),
        out_shape=jax.ShapeDtypeStruct((count, pipe_count, rows, WIDTH), jnp.bfloat16),
    )(place, tokens, weight)


def low_product(place, tokens, down, pipe_count, tensor_count):
    tok_dev, depth = tokens.shape
    rows = tok_dev // (pipe_count * tensor_count)

    def kernel(place_ref, x_ref, a_ref, out_ref):
        for block in range(tok_dev // BLOCK):
            a = a_ref[:, block].reshape(depth, RANKS)
            x = x_ref[block * BLOCK : (block + 1) * BLOCK]
            y = jnp.dot(x, a, preferred_element_type=jnp.float32).astype(out_ref.dtype)
            for part in range(BLOCK // rows):
                chip, core = divmod(block * (BLOCK // rows) + part, tensor_count)
                core = wrap(core - place_ref[2], tensor_count)
                out_ref[core, chip] = y[part * rows : (part + 1) * rows]

    return call(
        kernel,
        "low_product",
        2 * tok_dev * depth * RANKS,
        4.5,
        in_specs=[SMEM, VMEM, VMEM],
        out_specs=VMEM,
        out_shape=jax.ShapeDtypeStruct((tensor_count, pipe_count, rows, RANKS), jnp.bfloat16),
    )(place, tokens, down)


def input_gradient(place, cot_pieces, weight, grad_pieces, down):
    data_count, blocks_dev, down_rows, _ = down.shape
    tensor_count, pipe_count = len(cot_pieces), len(cot_pieces[0])
    rows = cot_pieces[0][0].shape[0]
    depth = weight.shape[0]
    tok_dev = blocks_dev * BLOCK
    planes = next((n for n in range(1, data_count) if n * down_rows % 256 == 0), data_count)
    tile = planes * down_rows
    order = [(s, k) for s in range(tensor_count) for k in range(pipe_count)]

    def kernel(place_ref, w_ref, a_ref, *rest):
        grad_refs, rest = rest[:tensor_count], rest[tensor_count:]
        cot_refs, (out_ref, cot, grad, sems) = rest[: len(order)], rest[len(order) :]

        def first_row(s, k):
            chip = wrap(place_ref[1] - k, pipe_count)
            core = wrap(place_ref[2] - s, tensor_count)
            return pl.multiple_of((chip * tensor_count + core) * rows, rows)

        @pl.when(pl.program_id(0) == 0)
        def _():
            copies = [
                pltpu.make_async_copy(ref, cot.at[pl.ds(first_row(*at), rows)], sems.at[i])
                for i, (at, ref) in enumerate(zip(order, cot_refs))
            ]
            for copy in copies:
                copy.start()
            for s, k in order:
                grad[pl.ds(first_row(s, k), rows)] = grad_refs[s][k, 0]
            for copy in copies:
                copy.wait()

        base = lax.dot_general(cot[...], w_ref[...], LAST_BOTH, preferred_element_type=jnp.float32)
        for block in range(blocks_dev):
            at = slice(block * BLOCK, (block + 1) * BLOCK)
            a = a_ref[:, block].reshape(tile, RANKS)
            low = lax.dot_general(grad[at], a, LAST_BOTH, preferred_element_type=jnp.float32)
            out_ref[at] = (base[at] + low).astype(out_ref.dtype)

    grad_shape = (pipe_count, 1, rows, RANKS)
    return call(
        kernel,
        "input_gradient",
        2 * tok_dev * depth * (WIDTH + RANKS),
        12,
        grid=(data_count // planes,),
        in_specs=[
            SMEM,
            pl.BlockSpec((tile, WIDTH), lambda n: (n, 0)),
            pl.BlockSpec((planes, blocks_dev, down_rows, RANKS), lambda n: (n, 0, 0, 0)),
        ]
        + [pl.BlockSpec(grad_shape, lambda n: (0, 0, 0, 0))] * tensor_count
        + [HBM] * len(order),
        out_specs=pl.BlockSpec((tok_dev, tile), lambda n: (0, n)),
        out_shape=jax.ShapeDtypeStruct((tok_dev, depth), jnp.bfloat16),
        scratch_shapes=[
            pltpu.VMEM((tok_dev, WIDTH), jnp.bfloat16),
            pltpu.VMEM((tok_dev, RANKS), jnp.bfloat16),
            pltpu.SemaphoreType.DMA((len(order),)),
        ],
    )(place, weight, down, *grad_pieces, *[cot_pieces[s][k] for s, k in order])


def grad_down(tenant_of_block, slot_of_tenant, place, x_features, grad_pieces):
    data_count, down_rows, tok_dev = x_features.shape
    tensor_count = len(grad_pieces)
    pipe_count, _, rows, _ = grad_pieces[0].shape
    blocks_dev = tok_dev // BLOCK
    slots = slot_of_tenant.shape[0]

    def kernel(tenant_ref, slot_ref, place_ref, x_ref, *rest):
        grad_refs, (out_ref, grad) = rest[:tensor_count], rest[tensor_count:]
        for s in range(tensor_count):
            core = wrap(place_ref[2] - s, tensor_count)
            for k in range(pipe_count):
                chip = wrap(place_ref[1] - k, pipe_count)
                first = pl.multiple_of((chip * tensor_count + core) * rows, rows)
                for m in range(data_count):
                    data = wrap(place_ref[0] - m, data_count)
                    grad[data, pl.ds(first, rows)] = grad_refs[s][k, m]
        out_ref[...] = jnp.zeros(out_ref.shape, out_ref.dtype)
        for data in range(data_count):
            for block in range(blocks_dev):
                slot = slot_ref[tenant_ref[data * blocks_dev + block]]
                at = slice(block * BLOCK, (block + 1) * BLOCK)
                out_ref[slot] += jnp.dot(
                    x_ref[data, :, at], grad[data, at], preferred_element_type=jnp.float32
                )

    return call(
        kernel,
        "grad_down",
        2 * data_count * tok_dev * down_rows * RANKS,
        6,
        in_specs=[SMEM, SMEM, SMEM, VMEM] + [VMEM] * tensor_count,
        out_specs=VMEM,
        out_shape=jax.ShapeDtypeStruct((slots, down_rows, RANKS), jnp.float32),
        scratch_shapes=[pltpu.VMEM((data_count, tok_dev, RANKS), jnp.bfloat16)],
    )(tenant_of_block, slot_of_tenant, place, x_features, *grad_pieces)


def grad_up_pieces(place, low_pieces, cot_cols, data_count, up_rows):
    tensor_count = len(low_pieces)
    pipe_count, rows, _ = low_pieces[0].shape
    cols = cot_cols.shape[-1]
    tok_dev = tensor_count * pipe_count * rows
    blocks_dev = tok_dev // BLOCK
    group_half = tensor_count * pipe_count // 2

    def kernel(place_ref, cot_ref, *rest):
        low_refs, (out_ref, low, cot) = rest[:tensor_count], rest[tensor_count:]
        for s in range(tensor_count):
            core = wrap(place_ref[2] - s, tensor_count)
            for k in range(pipe_count):
                first = pl.multiple_of((k * tensor_count + core) * rows, rows)
                low[pl.ds(first, rows)] = low_refs[s][k]
                chip = wrap(place_ref[1] - k, pipe_count)
                first = pl.multiple_of((chip * tensor_count + core) * rows, rows)
                cot[pl.ds(first, rows)] = cot_ref[s * pipe_count + k]
        is_key = place_ref[1] * tensor_count + place_ref[2] < group_half
        for block in range(blocks_dev):
            at = slice(block * BLOCK, (block + 1) * BLOCK)
            both = lax.dot_general(low[at], cot[at], FIRST_BOTH, preferred_element_type=jnp.float32)
            half = jnp.where(is_key, both[:ADAPTER_RANK], both[ADAPTER_RANK:])
            half = half.astype(out_ref.dtype)
            for data in range(data_count):
                k = wrap(data - place_ref[0], data_count)
                out_ref[k, block] = half[data * up_rows : (data + 1) * up_rows]

    return call(
        kernel,
        "grad_up_pieces",
        2 * tok_dev * cols * RANKS,
        2,
        in_specs=[SMEM, VMEM] + [VMEM] * tensor_count,
        out_specs=VMEM,
        out_shape=jax.ShapeDtypeStruct((data_count, blocks_dev, up_rows, cols), jnp.bfloat16),
        scratch_shapes=[
            pltpu.VMEM((tok_dev, RANKS), jnp.bfloat16),
            pltpu.VMEM((tok_dev, cols), jnp.bfloat16),
        ],
    )(place, cot_cols, *low_pieces)


def grad_up(tenant_of_block, slot_of_tenant, place, pieces):
    data_count = len(pieces)
    blocks_dev, up_rows, cols = pieces[0].shape
    slots = slot_of_tenant.shape[0]

    def kernel(tenant_ref, slot_ref, place_ref, *rest):
        piece_refs, out_ref = rest[:data_count], rest[data_count]
        out_ref[...] = jnp.zeros(out_ref.shape, out_ref.dtype)
        for k in range(data_count):
            data = wrap(place_ref[0] - k, data_count)
            for block in range(blocks_dev):
                slot = slot_ref[tenant_ref[data * blocks_dev + block]]
                out_ref[slot] += piece_refs[k][block].astype(out_ref.dtype)

    return call(
        kernel,
        "grad_up",
        0,
        1,
        in_specs=[SMEM, SMEM, SMEM] + [VMEM] * data_count,
        out_specs=VMEM,
        out_shape=jax.ShapeDtypeStruct((slots, up_rows, cols), jnp.float32),
    )(tenant_of_block, slot_of_tenant, place, *pieces)


def halves(product, left, right):
    return jnp.concatenate([product(*pair) for pair in zip(left, right)], axis=1)


def body(
    tokens, key_value_weight, adapter_down, adapter_up, tenant_of_block, slot_of_tenant, cotangent
):
    data_count = lax.axis_size("dp")
    pipe_count = lax.axis_size("pipe")
    tensor_count = lax.axis_size("tensor")
    group_count = pipe_count * tensor_count
    at_data, at_pipe, at_tensor = (lax.axis_index(a) for a in ("dp", "pipe", "tensor"))
    place = jnp.stack([at_data, at_pipe, at_tensor]).astype(jnp.int32)
    my_group = at_pipe * tensor_count + at_tensor
    tok_dev, feature_count = tokens.shape
    blocks_dev = tok_dev // BLOCK
    rows = tok_dev // group_count
    down_rows = adapter_down.shape[1]
    up_rows = adapter_up.shape[1]

    own_block = (my_group * rows // BLOCK).reshape(1)
    a_send, b_send = pick(
        tenant_of_block, slot_of_tenant, place, own_block, adapter_down, adapter_up, data_count
    )
    b_came = [b_send[0]] + [shift(b_send[k], "dp", k) for k in range(1, data_count)]
    a_recv = lax.all_to_all(
        a_send.reshape(data_count, blocks_dev, down_rows, RANKS), "dp", 0, 0, tiled=True
    )

    cot_chips = [cotangent] + [shift(cotangent, "pipe", k) for k in range(1, pipe_count)]
    cot_pieces = [cot_chips] + [
        [shift(piece, "tensor", s) for piece in cot_chips] for s in range(1, tensor_count)
    ]

    x_send = tokens.T.reshape(data_count, down_rows, tok_dev)
    x_send, a_recv = lax.optimization_barrier((x_send, a_recv))
    x_recv = lax.all_to_all(x_send, "dp", 0, 0, tiled=True)

    tokens_by_group = tokens.reshape(pipe_count, tensor_count, rows, feature_count)
    base_send = base_product(place, tokens_by_group, key_value_weight, 1, tensor_count - 1)
    base_came = [shift(base_send[s - 1], "tensor", s) for s in range(1, tensor_count)]
    base_keep = base_product(place, tokens_by_group, key_value_weight, 0, 1)[0]
    base_chip = [
        sum([base_keep[k].astype(jnp.float32)] + [b[k].astype(jnp.float32) for b in base_came])
        for k in range(pipe_count)
    ]
    base_chip_came = [
        shift(base_chip[k].astype(jnp.bfloat16), "pipe", k) for k in range(1, pipe_count)
    ]
    base_rows = sum([base_chip[0]] + [b.astype(jnp.float32) for b in base_chip_came])

    b_own = jnp.concatenate(
        [lax.select_n(wrap(at_data - i, data_count), *b_came) for i in range(data_count)]
        if data_count > 1
        else b_came
    )
    left = lambda m: (m[:, :ADAPTER_RANK], m[:, ADAPTER_RANK:])
    wide = lambda m: (m[:, :KEY_WIDTH], m[:, KEY_WIDTH:])
    grad_rows = halves(
        lambda p, q: lax.dot_general(p, q, LAST_BOTH, preferred_element_type=jnp.float32),
        wide(cotangent),
        wide(b_own),
    ).astype(jnp.bfloat16)
    grad_data = jnp.stack([grad_rows] + [shift(grad_rows, "dp", k) for k in range(1, data_count)])
    grad_chips = jnp.stack([grad_data] + [shift(grad_data, "pipe", k) for k in range(1, pipe_count)])
    grad_pieces = [grad_chips] + [shift(grad_chips, "tensor", s) for s in range(1, tensor_count)]

    low_part = low_product(place, tokens, a_recv, pipe_count, tensor_count)
    low_core = sum(
        [low_part[0].astype(jnp.float32)]
        + [shift(low_part[s], "tensor", s).astype(jnp.float32) for s in range(1, tensor_count)]
    ).astype(jnp.bfloat16)
    low_sum = sum(
        [low_core.astype(jnp.float32)]
        + [shift(low_core, "pipe", k).astype(jnp.float32) for k in range(1, pipe_count)]
    ).astype(jnp.bfloat16)
    low_pieces = [low_sum] + [shift(low_sum, "tensor", s) for s in range(1, tensor_count)]
    low_rows = lax.dynamic_index_in_dim(low_sum, at_pipe, 0, False)
    lowrank = halves(
        lambda p, q: jnp.dot(p, q, preferred_element_type=jnp.float32), left(low_rows), wide(b_own)
    )
    key_value = (base_rows + lowrank).astype(jnp.bfloat16)

    col_count = WIDTH // group_count
    cot_cols = jnp.stack(
        [
            lax.dynamic_slice_in_dim(piece, my_group * col_count, col_count, 1)
            for pieces in cot_pieces
            for piece in pieces
        ]
    )
    up_pieces = grad_up_pieces(place, low_pieces, cot_cols, data_count, up_rows)
    up_came = [up_pieces[0]] + [shift(up_pieces[k], "dp", k) for k in range(1, data_count)]
    grad_b = grad_up(tenant_of_block, slot_of_tenant, place, up_came)

    input_grad = input_gradient(place, cot_pieces, key_value_weight, grad_pieces, a_recv)
    grad_a = grad_down(tenant_of_block, slot_of_tenant, place, x_recv, grad_pieces)
    return (key_value, input_grad, grad_a, grad_b)


def solution(mesh):
    placed = (
        P("dp", ("pipe", "tensor")),
        P(("pipe", "tensor"), None),
        P(None, ("pipe", "tensor", "dp"), None),
        P(None, "dp", None),
        P(),
        P(),
        P(("dp", "pipe", "tensor"), None),
    )
    return jax.shard_map(
        body,
        mesh=mesh,
        in_specs=placed,
        out_specs=(
            P(("dp", "pipe", "tensor"), None),
            P("dp", ("pipe", "tensor")),
            P(None, ("pipe", "tensor", "dp"), None),
            P(None, "dp", ("pipe", "tensor")),
        ),
        check_vma=False,
    )
```

```python
import jax
import jax.numpy as jnp
from jax import lax
from jax.experimental import pallas as pl
from jax.experimental.pallas import tpu as pltpu
from jax.sharding import PartitionSpec as P

KEY_WIDTH = 1024
ADAPTER_RANK = 64
BLOCK = 128
RANKS = 2 * ADAPTER_RANK
WIDTH = 2 * KEY_WIDTH
VMEM_LIMIT = 48 * 1024 * 1024
LAST_BOTH = (((1,), (1,)), ((), ()))
FIRST_BOTH = (((0,), (0,)), ((), ()))
SMEM = pl.BlockSpec(memory_space=pltpu.SMEM)
VMEM = pl.BlockSpec(memory_space=pltpu.VMEM)
HBM = pl.BlockSpec(memory_space=pltpu.HBM)
ANY = pl.BlockSpec(memory_space=pl.ANY)


def call(kernel, name, **more):
    return pl.pallas_call(
        kernel,
        compiler_params=pltpu.CompilerParams(vmem_limit_bytes=VMEM_LIMIT),
        cost_estimate=pl.CostEstimate(flops=1024, bytes_accessed=1024, transcendentals=0),
        name=name,
        **more,
    )


def shift(piece, axis, step):
    count = lax.axis_size(axis)
    return lax.ppermute(piece, axis, [(i, (i + step) % count) for i in range(count)])


def wrap(index, count):
    return lax.rem(index + 2 * count, count)


def pick_up(tenant_of_block, slot_of_tenant, place, own_block, adapter_up, data_count):
    blocks_dev = tenant_of_block.shape[0] // data_count

    def kernel(tenant_ref, slot_ref, place_ref, own_ref, up_ref, *rest):
        out_refs, sems = rest[:data_count], rest[data_count]
        copies = []
        for k in range(data_count):
            data = wrap(place_ref[0] + k, data_count)
            slot = slot_ref[tenant_ref[data * blocks_dev + own_ref[0]]]
            copies.append(pltpu.make_async_copy(up_ref.at[slot], out_refs[k], sems.at[k]))
        for copy in copies:
            copy.start()
        for copy in copies:
            copy.wait()

    return call(
        kernel,
        "pick_up",
        out_shape=(jax.ShapeDtypeStruct(adapter_up.shape[1:], adapter_up.dtype),) * data_count,
        in_specs=[SMEM, SMEM, SMEM, SMEM, HBM],
        out_specs=(VMEM,) * data_count,
        scratch_shapes=[pltpu.SemaphoreType.DMA((data_count,))],
    )(tenant_of_block, slot_of_tenant, place, own_block, adapter_up)


def pick_down(tenant_of_block, slot_of_tenant, adapter_down):
    block_count = tenant_of_block.shape[0]

    def kernel(tenant_ref, slot_ref, down_ref, out_ref, sems):
        copies = [
            pltpu.make_async_copy(
                down_ref.at[slot_ref[tenant_ref[block]]], out_ref.at[block], sems.at[block]
            )
            for block in range(block_count)
        ]
        for copy in copies:
            copy.start()
        for copy in copies:
            copy.wait()

    return call(
        kernel,
        "pick_down",
        out_shape=jax.ShapeDtypeStruct((block_count,) + adapter_down.shape[1:], adapter_down.dtype),
        in_specs=[SMEM, SMEM, HBM],
        out_specs=VMEM,
        scratch_shapes=[pltpu.SemaphoreType.DMA((block_count,))],
    )(tenant_of_block, slot_of_tenant, adapter_down)


def base_product(place, tokens, weight, first, count):
    pipe_count, tensor_count, rows, depth = tokens.shape
    tile = 1024

    def kernel(place_ref, x_ref, w_ref, out_ref):
        x = x_ref[...].reshape(pipe_count * rows, depth)
        y = jnp.dot(x, w_ref[...], preferred_element_type=jnp.float32).astype(out_ref.dtype)
        for chip in range(pipe_count):
            out_ref[0, wrap(chip - place_ref[1], pipe_count)] = y[chip * rows : (chip + 1) * rows]

    return call(
        kernel,
        "base_product",
        grid_spec=pltpu.PrefetchScalarGridSpec(
            num_scalar_prefetch=1,
            grid=(WIDTH // tile, count),
            in_specs=[
                pl.BlockSpec(
                    (pipe_count, 1, rows, depth),
                    lambda n, s, at: (0, wrap(at[2] + s + first, tensor_count), 0, 0),
                ),
                pl.BlockSpec((depth, tile), lambda n, s, at: (0, n)),
            ],
            out_specs=pl.BlockSpec((1, pipe_count, rows, tile), lambda n, s, at: (s, 0, 0, n)),
        ),
        out_shape=jax.ShapeDtypeStruct((count, pipe_count, rows, WIDTH), jnp.bfloat16),
    )(place, tokens, weight)


def low_product(place, tokens, down, pipe_count, tensor_count):
    tok_dev, depth = tokens.shape
    rows = tok_dev // (pipe_count * tensor_count)

    def kernel(place_ref, x_ref, a_ref, out_ref):
        for block in range(tok_dev // BLOCK):
            a = a_ref[:, block].reshape(depth, RANKS)
            x = x_ref[block * BLOCK : (block + 1) * BLOCK]
            y = jnp.dot(x, a, preferred_element_type=jnp.float32).astype(out_ref.dtype)
            for part in range(BLOCK // rows):
                chip, core = divmod(block * (BLOCK // rows) + part, tensor_count)
                core = wrap(core - place_ref[2], tensor_count)
                out_ref[core, chip] = y[part * rows : (part + 1) * rows]

    return call(
        kernel,
        "low_product",
        in_specs=[SMEM, VMEM, VMEM],
        out_specs=VMEM,
        out_shape=jax.ShapeDtypeStruct((tensor_count, pipe_count, rows, RANKS), jnp.bfloat16),
    )(place, tokens, down)


def input_gradient(place, cot_pieces, weight, grad_pieces, down):
    data_count, blocks_dev, down_rows, _ = down.shape
    tensor_count, pipe_count = len(cot_pieces), len(cot_pieces[0])
    rows = cot_pieces[0][0].shape[0]
    depth = weight.shape[0]
    tok_dev = blocks_dev * BLOCK
    planes = next((n for n in range(1, data_count) if n * down_rows % 256 == 0), data_count)
    tile = planes * down_rows
    order = [(s, k) for s in range(tensor_count) for k in range(pipe_count)]

    def kernel(place_ref, w_ref, a_ref, *rest):
        grad_refs, rest = rest[:tensor_count], rest[tensor_count:]
        cot_refs, (out_ref, cot, grad, sems) = rest[: len(order)], rest[len(order) :]

        def first_row(s, k):
            chip = wrap(place_ref[1] - k, pipe_count)
            core = wrap(place_ref[2] - s, tensor_count)
            return pl.multiple_of((chip * tensor_count + core) * rows, rows)

        @pl.when(pl.program_id(0) == 0)
        def _():
            copies = [
                pltpu.make_async_copy(ref, cot.at[pl.ds(first_row(*at), rows)], sems.at[i])
                for i, (at, ref) in enumerate(zip(order, cot_refs))
            ]
            for copy in copies:
                copy.start()
            for s, k in order:
                grad[pl.ds(first_row(s, k), rows)] = grad_refs[s][k, 0]
            for copy in copies:
                copy.wait()

        base = lax.dot_general(cot[...], w_ref[...], LAST_BOTH, preferred_element_type=jnp.float32)
        for block in range(blocks_dev):
            at = slice(block * BLOCK, (block + 1) * BLOCK)
            a = a_ref[:, block].reshape(tile, RANKS)
            low = lax.dot_general(grad[at], a, LAST_BOTH, preferred_element_type=jnp.float32)
            out_ref[at] = (base[at] + low).astype(out_ref.dtype)

    grad_shape = (pipe_count, 1, rows, RANKS)
    return call(
        kernel,
        "input_gradient",
        grid=(data_count // planes,),
        in_specs=[
            SMEM,
            pl.BlockSpec((tile, WIDTH), lambda n: (n, 0)),
            pl.BlockSpec((planes, blocks_dev, down_rows, RANKS), lambda n: (n, 0, 0, 0)),
        ]
        + [pl.BlockSpec(grad_shape, lambda n: (0, 0, 0, 0))] * tensor_count
        + [ANY] * len(order),
        out_specs=pl.BlockSpec((tok_dev, tile), lambda n: (0, n)),
        out_shape=jax.ShapeDtypeStruct((tok_dev, depth), jnp.bfloat16),
        scratch_shapes=[
            pltpu.VMEM((tok_dev, WIDTH), jnp.bfloat16),
            pltpu.VMEM((tok_dev, RANKS), jnp.bfloat16),
            pltpu.SemaphoreType.DMA((len(order),)),
        ],
    )(place, weight, down, *grad_pieces, *[cot_pieces[s][k] for s, k in order])


def grad_down(tenant_of_block, slot_of_tenant, place, x_features, grad_pieces):
    data_count, down_rows, tok_dev = x_features.shape
    tensor_count = len(grad_pieces)
    pipe_count, _, rows, _ = grad_pieces[0].shape
    blocks_dev = tok_dev // BLOCK
    slots = slot_of_tenant.shape[0]

    def kernel(tenant_ref, slot_ref, place_ref, x_ref, *rest):
        grad_refs, (out_ref, grad) = rest[:tensor_count], rest[tensor_count:]
        for s in range(tensor_count):
            core = wrap(place_ref[2] - s, tensor_count)
            for k in range(pipe_count):
                chip = wrap(place_ref[1] - k, pipe_count)
                first = pl.multiple_of((chip * tensor_count + core) * rows, rows)
                for m in range(data_count):
                    data = wrap(place_ref[0] - m, data_count)
                    grad[data, pl.ds(first, rows)] = grad_refs[s][k, m]
        out_ref[...] = jnp.zeros(out_ref.shape, out_ref.dtype)
        for data in range(data_count):
            for block in range(blocks_dev):
                slot = slot_ref[tenant_ref[data * blocks_dev + block]]
                at = slice(block * BLOCK, (block + 1) * BLOCK)
                out_ref[slot] += jnp.dot(
                    x_ref[data, :, at], grad[data, at], preferred_element_type=jnp.float32
                )

    return call(
        kernel,
        "grad_down",
        in_specs=[SMEM, SMEM, SMEM, VMEM] + [VMEM] * tensor_count,
        out_specs=VMEM,
        out_shape=jax.ShapeDtypeStruct((slots, down_rows, RANKS), jnp.float32),
        scratch_shapes=[pltpu.VMEM((data_count, tok_dev, RANKS), jnp.bfloat16)],
    )(tenant_of_block, slot_of_tenant, place, x_features, *grad_pieces)


def grad_up_pieces(place, low_pieces, cot_pieces, data_count, up_rows):
    tensor_count, pipe_count = len(cot_pieces), len(cot_pieces[0])
    group_count = tensor_count * pipe_count
    rows = cot_pieces[0][0].shape[0]
    cols = WIDTH // group_count
    tok_dev = group_count * rows
    blocks_dev = tok_dev // BLOCK
    group_half = group_count // 2
    order = [(s, k) for s in range(tensor_count) for k in range(pipe_count)]
    pieces = [cot_pieces[s][k] for s, k in order]
    in_kernel = cols % 128 == 0
    if not in_kernel:
        first_col = (place[1] * tensor_count + place[2]) * cols
        pieces = [lax.dynamic_slice_in_dim(piece, first_col, cols, 1) for piece in pieces]

    def kernel(place_ref, *rest):
        low_refs, rest = rest[:tensor_count], rest[tensor_count:]
        cot_refs, (out_ref, low, cot, sems) = rest[: len(order)], rest[len(order) :]
        my_group = place_ref[1] * tensor_count + place_ref[2]
        copies = []
        for i, (s, k) in enumerate(order):
            core = wrap(place_ref[2] - s, tensor_count)
            chip = wrap(place_ref[1] - k, pipe_count)
            first = pl.multiple_of((chip * tensor_count + core) * rows, rows)
            piece = cot_refs[i]
            if in_kernel:
                piece = piece.at[:, pl.ds(pl.multiple_of(my_group * cols, cols), cols)]
            copies.append(pltpu.make_async_copy(piece, cot.at[pl.ds(first, rows)], sems.at[i]))
        for copy in copies:
            copy.start()
        for s in range(tensor_count):
            core = wrap(place_ref[2] - s, tensor_count)
            for k in range(pipe_count):
                first = pl.multiple_of((k * tensor_count + core) * rows, rows)
                low[pl.ds(first, rows)] = low_refs[s][k]
        for copy in copies:
            copy.wait()
        for block in range(blocks_dev):
            at = slice(block * BLOCK, (block + 1) * BLOCK)
            both = lax.dot_general(low[at], cot[at], FIRST_BOTH, preferred_element_type=jnp.float32)
            half = jnp.where(my_group < group_half, both[:ADAPTER_RANK], both[ADAPTER_RANK:])
            half = half.astype(out_ref.dtype)
            for data in range(data_count):
                k = wrap(data - place_ref[0], data_count)
                out_ref[k, block] = half[data * up_rows : (data + 1) * up_rows]

    return call(
        kernel,
        "grad_up_pieces",
        in_specs=[SMEM] + [VMEM] * tensor_count + [ANY] * len(order),
        out_specs=VMEM,
        out_shape=jax.ShapeDtypeStruct((data_count, blocks_dev, up_rows, cols), jnp.bfloat16),
        scratch_shapes=[
            pltpu.VMEM((tok_dev, RANKS), jnp.bfloat16),
            pltpu.VMEM((tok_dev, cols), jnp.bfloat16),
            pltpu.SemaphoreType.DMA((len(order),)),
        ],
    )(place, *low_pieces, *pieces)


def grad_up(tenant_of_block, slot_of_tenant, place, pieces):
    data_count = len(pieces)
    blocks_dev, up_rows, cols = pieces[0].shape
    slots = slot_of_tenant.shape[0]

    def kernel(tenant_ref, slot_ref, place_ref, *rest):
        piece_refs, out_ref = rest[:data_count], rest[data_count]
        out_ref[...] = jnp.zeros(out_ref.shape, out_ref.dtype)
        for k in range(data_count):
            data = wrap(place_ref[0] - k, data_count)
            for block in range(blocks_dev):
                slot = slot_ref[tenant_ref[data * blocks_dev + block]]
                out_ref[slot] += piece_refs[k][block].astype(out_ref.dtype)

    return call(
        kernel,
        "grad_up",
        in_specs=[SMEM, SMEM, SMEM] + [VMEM] * data_count,
        out_specs=VMEM,
        out_shape=jax.ShapeDtypeStruct((slots, up_rows, cols), jnp.float32),
    )(tenant_of_block, slot_of_tenant, place, *pieces)


def own_rows(place, up, cotangent):
    data_count = len(up)
    rows = cotangent.shape[0]

    def kernel(place_ref, cot_ref, *rest):
        up_refs, (b_ref, grad_ref) = rest[:data_count], rest[data_count:]
        pieces = []
        for data in range(data_count):
            came = wrap(place_ref[0] - data, data_count)
            piece = up_refs[0][...]
            for k in range(1, data_count):
                piece = jnp.where(came == k, up_refs[k][...], piece)
            pieces.append(piece)
        b = jnp.concatenate(pieces, axis=0)
        b_ref[...] = b
        cot = cot_ref[...]
        grad_ref[...] = jnp.concatenate(
            [
                lax.dot_general(cot[:, half], b[:, half], LAST_BOTH, preferred_element_type=jnp.float32)
                for half in (slice(0, KEY_WIDTH), slice(KEY_WIDTH, WIDTH))
            ],
            axis=1,
        ).astype(grad_ref.dtype)

    return call(
        kernel,
        "own_rows",
        in_specs=[SMEM, VMEM] + [VMEM] * data_count,
        out_specs=(VMEM, VMEM),
        out_shape=(
            jax.ShapeDtypeStruct((ADAPTER_RANK, WIDTH), jnp.bfloat16),
            jax.ShapeDtypeStruct((rows, RANKS), jnp.bfloat16),
        ),
    )(place, cotangent, *up)


def keys_and_values(place, base_pieces, low_sum, b_own):
    rows = base_pieces[0].shape[0]
    count = len(base_pieces)

    def kernel(place_ref, low_ref, b_ref, *rest):
        base_refs, out_ref = rest[:count], rest[count]
        low = low_ref[place_ref[1]]
        for first, ranks in ((0, slice(0, ADAPTER_RANK)), (KEY_WIDTH, slice(ADAPTER_RANK, RANKS))):
            at = slice(first, first + KEY_WIDTH)
            y = jnp.dot(low[:, ranks], b_ref[:, at], preferred_element_type=jnp.float32)
            for base_ref in base_refs:
                y += base_ref[:, at].astype(jnp.float32)
            out_ref[:, at] = y.astype(out_ref.dtype)

    return call(
        kernel,
        "keys_and_values",
        in_specs=[SMEM, VMEM, VMEM] + [VMEM] * count,
        out_specs=VMEM,
        out_shape=jax.ShapeDtypeStruct((rows, WIDTH), jnp.bfloat16),
    )(place, low_sum, b_own, *base_pieces)


def body(
    tokens, key_value_weight, adapter_down, adapter_up, tenant_of_block, slot_of_tenant, cotangent
):
    data_count = lax.axis_size("dp")
    pipe_count = lax.axis_size("pipe")
    tensor_count = lax.axis_size("tensor")
    group_count = pipe_count * tensor_count
    at_data, at_pipe, at_tensor = (lax.axis_index(a) for a in ("dp", "pipe", "tensor"))
    place = jnp.stack([at_data, at_pipe, at_tensor]).astype(jnp.int32)
    my_group = at_pipe * tensor_count + at_tensor
    tok_dev, feature_count = tokens.shape
    blocks_dev = tok_dev // BLOCK
    rows = tok_dev // group_count
    down_rows = adapter_down.shape[1]
    up_rows = adapter_up.shape[1]

    own_block = (my_group * rows // BLOCK).reshape(1)
    b_send = pick_up(tenant_of_block, slot_of_tenant, place, own_block, adapter_up, data_count)
    b_came = [b_send[0]] + [shift(b_send[k], "dp", k) for k in range(1, data_count)]
    b_own, grad_rows = own_rows(place, b_came, cotangent)
    grad_data = [grad_rows] + [shift(grad_rows, "dp", k) for k in range(1, data_count)]

    a_send = pick_down(tenant_of_block, slot_of_tenant, adapter_down)
    a_send, grad_data = lax.optimization_barrier((a_send, grad_data))
    a_recv = lax.all_to_all(
        a_send.reshape(data_count, blocks_dev, down_rows, RANKS), "dp", 0, 0, tiled=True
    )

    grad_data = jnp.stack(grad_data)
    grad_chips = jnp.stack([grad_data] + [shift(grad_data, "pipe", k) for k in range(1, pipe_count)])
    grad_pieces = [grad_chips] + [shift(grad_chips, "tensor", s) for s in range(1, tensor_count)]

    cot_send, grad_rows = lax.optimization_barrier((cotangent, grad_rows))
    cot_chips = [cotangent] + [shift(cot_send, "pipe", k) for k in range(1, pipe_count)]
    cot_pieces = [cot_chips] + [
        [shift(piece, "tensor", s) for piece in cot_chips] for s in range(1, tensor_count)
    ]

    base_tokens, a_send = lax.optimization_barrier((tokens, a_send))
    tokens_by_group = base_tokens.reshape(pipe_count, tensor_count, rows, feature_count)
    base_send = base_product(place, tokens_by_group, key_value_weight, 1, tensor_count - 1)
    base_came = [shift(base_send[s - 1], "tensor", s) for s in range(1, tensor_count)]
    base_keep = base_product(place, tokens_by_group, key_value_weight, 0, 1)[0]
    base_chip = [
        sum([base_keep[k].astype(jnp.float32)] + [b[k].astype(jnp.float32) for b in base_came])
        for k in range(pipe_count)
    ]
    base_chip_came = [
        shift(base_chip[k].astype(jnp.bfloat16), "pipe", k) for k in range(1, pipe_count)
    ]
    x_send = tokens.T.reshape(data_count, down_rows, tok_dev)
    a_recv, x_send, base_chip_came, cot_pieces, grad_pieces = lax.optimization_barrier(
        (a_recv, x_send, base_chip_came, cot_pieces, grad_pieces)
    )
    x_recv = lax.all_to_all(x_send, "dp", 0, 0, tiled=True)
    low_part = low_product(place, tokens, a_recv, pipe_count, tensor_count)
    low_core = sum(
        [low_part[0].astype(jnp.float32)]
        + [shift(low_part[s], "tensor", s).astype(jnp.float32) for s in range(1, tensor_count)]
    ).astype(jnp.bfloat16)
    low_sum = sum(
        [low_core.astype(jnp.float32)]
        + [shift(low_core, "pipe", k).astype(jnp.float32) for k in range(1, pipe_count)]
    ).astype(jnp.bfloat16)
    low_pieces = [low_sum] + [shift(low_sum, "tensor", s) for s in range(1, tensor_count)]
    key_value = keys_and_values(place, base_chip[:1] + base_chip_came, low_sum, b_own)

    up_pieces = grad_up_pieces(place, low_pieces, cot_pieces, data_count, up_rows)
    up_came = [up_pieces[0]] + [shift(up_pieces[k], "dp", k) for k in range(1, data_count)]
    grad_b = grad_up(tenant_of_block, slot_of_tenant, place, up_came)

    input_grad = input_gradient(place, cot_pieces, key_value_weight, grad_pieces, a_recv)
    grad_a = grad_down(tenant_of_block, slot_of_tenant, place, x_recv, grad_pieces)
    return (key_value, input_grad, grad_a, grad_b)


def solution(mesh):
    placed = (
        P("dp", ("pipe", "tensor")),
        P(("pipe", "tensor"), None),
        P(None, ("pipe", "tensor", "dp"), None),
        P(None, "dp", None),
        P(),
        P(),
        P(("dp", "pipe", "tensor"), None),
    )
    return jax.shard_map(
        body,
        mesh=mesh,
        in_specs=placed,
        out_specs=(
            P(("dp", "pipe", "tensor"), None),
            P("dp", ("pipe", "tensor")),
            P(None, ("pipe", "tensor", "dp"), None),
            P(None, "dp", ("pipe", "tensor")),
        ),
        check_vma=False,
    )
```

```python
import jax
import jax.numpy as jnp
from jax import lax
from jax.experimental import pallas as pl
from jax.experimental.pallas import tpu as pltpu
from jax.sharding import PartitionSpec as P

KEY_WIDTH = 1024
ADAPTER_RANK = 64
BLOCK = 128
RANKS = 2 * ADAPTER_RANK
WIDTH = 2 * KEY_WIDTH
VMEM_LIMIT = 48 * 1024 * 1024
LAST_BOTH = (((1,), (1,)), ((), ()))
FIRST_BOTH = (((0,), (0,)), ((), ()))
SMEM = pl.BlockSpec(memory_space=pltpu.SMEM)
VMEM = pl.BlockSpec(memory_space=pltpu.VMEM)
HBM = pl.BlockSpec(memory_space=pltpu.HBM)
ANY = pl.BlockSpec(memory_space=pl.ANY)


def call(kernel, name, **more):
    return pl.pallas_call(
        kernel,
        compiler_params=pltpu.CompilerParams(vmem_limit_bytes=VMEM_LIMIT),
        cost_estimate=pl.CostEstimate(flops=1024, bytes_accessed=1024, transcendentals=0),
        name=name,
        **more,
    )


def shift(piece, axis, step):
    count = lax.axis_size(axis)
    return lax.ppermute(piece, axis, [(i, (i + step) % count) for i in range(count)])


def wrap(index, count):
    return lax.rem(index + 2 * count, count)


def pick_up(at, slot_of, adapter_up, data_count):
    def kernel(at_ref, up_ref, *rest):
        out_refs, sems = rest[:data_count], rest[data_count]
        copies = []
        for k in range(data_count):
            data = wrap(at_ref[0] + k, data_count)
            slot = slot_of(at_ref, data, at_ref[3])
            copies.append(pltpu.make_async_copy(up_ref.at[slot], out_refs[k], sems.at[k]))
        for copy in copies:
            copy.start()
        for copy in copies:
            copy.wait()

    return call(
        kernel,
        "pick_up",
        out_shape=(jax.ShapeDtypeStruct(adapter_up.shape[1:], adapter_up.dtype),) * data_count,
        in_specs=[SMEM, HBM],
        out_specs=(VMEM,) * data_count,
        scratch_shapes=[pltpu.SemaphoreType.DMA((data_count,))],
    )(at, adapter_up)


def pick_down(at, slot_of, adapter_down, data_count, blocks_dev):
    def kernel(at_ref, down_ref, out_ref, sems):
        copies = [
            pltpu.make_async_copy(
                down_ref.at[slot_of(at_ref, data, block)], out_ref.at[data, block], sems.at[data, block]
            )
            for data in range(data_count)
            for block in range(blocks_dev)
        ]
        for copy in copies:
            copy.start()
        for copy in copies:
            copy.wait()

    return call(
        kernel,
        "pick_down",
        out_shape=jax.ShapeDtypeStruct(
            (data_count, blocks_dev) + adapter_down.shape[1:], adapter_down.dtype
        ),
        in_specs=[SMEM, HBM],
        out_specs=VMEM,
        scratch_shapes=[pltpu.SemaphoreType.DMA((data_count, blocks_dev))],
    )(at, adapter_down)


def base_product(at, tokens, weight, first, count):
    pipe_count, tensor_count, rows, depth = tokens.shape
    tile = 1024

    def kernel(at_ref, x_ref, w_ref, out_ref):
        x = x_ref[...].reshape(pipe_count * rows, depth)
        y = jnp.dot(x, w_ref[...], preferred_element_type=jnp.float32).astype(out_ref.dtype)
        for chip in range(pipe_count):
            out_ref[0, wrap(chip - at_ref[1], pipe_count)] = y[chip * rows : (chip + 1) * rows]

    return call(
        kernel,
        "base_product",
        grid_spec=pltpu.PrefetchScalarGridSpec(
            num_scalar_prefetch=1,
            grid=(WIDTH // tile, count),
            in_specs=[
                pl.BlockSpec(
                    (pipe_count, 1, rows, depth),
                    lambda n, s, at: (0, wrap(at[2] + s + first, tensor_count), 0, 0),
                ),
                pl.BlockSpec((depth, tile), lambda n, s, at: (0, n)),
            ],
            out_specs=pl.BlockSpec((1, pipe_count, rows, tile), lambda n, s, at: (s, 0, 0, n)),
        ),
        out_shape=jax.ShapeDtypeStruct((count, pipe_count, rows, WIDTH), jnp.bfloat16),
    )(at, tokens, weight)


def low_product(at, tokens, down, pipe_count, tensor_count):
    tok_dev, depth = tokens.shape
    rows = tok_dev // (pipe_count * tensor_count)

    def kernel(at_ref, x_ref, a_ref, out_ref):
        for block in range(tok_dev // BLOCK):
            a = a_ref[:, block].reshape(depth, RANKS)
            x = x_ref[block * BLOCK : (block + 1) * BLOCK]
            y = jnp.dot(x, a, preferred_element_type=jnp.float32).astype(out_ref.dtype)
            for part in range(BLOCK // rows):
                chip, core = divmod(block * (BLOCK // rows) + part, tensor_count)
                core = wrap(core - at_ref[2], tensor_count)
                out_ref[core, chip] = y[part * rows : (part + 1) * rows]

    return call(
        kernel,
        "low_product",
        in_specs=[SMEM, VMEM, VMEM],
        out_specs=VMEM,
        out_shape=jax.ShapeDtypeStruct((tensor_count, pipe_count, rows, RANKS), jnp.bfloat16),
    )(at, tokens, down)


def input_gradient(at, cot_pieces, weight, grad_pieces, down):
    data_count, blocks_dev, down_rows, _ = down.shape
    tensor_count, pipe_count = len(cot_pieces), len(cot_pieces[0])
    rows = cot_pieces[0][0].shape[0]
    depth = weight.shape[0]
    tok_dev = blocks_dev * BLOCK
    planes = next((n for n in range(1, data_count) if n * down_rows % 256 == 0), data_count)
    tile = planes * down_rows
    order = [(s, k) for s in range(tensor_count) for k in range(pipe_count)]

    def kernel(at_ref, w_ref, a_ref, *rest):
        grad_refs, rest = rest[:tensor_count], rest[tensor_count:]
        cot_refs, (out_ref, cot, grad, sems) = rest[: len(order)], rest[len(order) :]

        def first_row(s, k):
            chip = wrap(at_ref[1] - k, pipe_count)
            core = wrap(at_ref[2] - s, tensor_count)
            return pl.multiple_of((chip * tensor_count + core) * rows, rows)

        @pl.when(pl.program_id(0) == 0)
        def _():
            copies = [
                pltpu.make_async_copy(ref, cot.at[pl.ds(first_row(*at), rows)], sems.at[i])
                for i, (at, ref) in enumerate(zip(order, cot_refs))
            ]
            for copy in copies:
                copy.start()
            for s, k in order:
                grad[pl.ds(first_row(s, k), rows)] = grad_refs[s][k, 0]
            for copy in copies:
                copy.wait()

        base = lax.dot_general(cot[...], w_ref[...], LAST_BOTH, preferred_element_type=jnp.float32)
        for block in range(blocks_dev):
            at = slice(block * BLOCK, (block + 1) * BLOCK)
            a = a_ref[:, block].reshape(tile, RANKS)
            low = lax.dot_general(grad[at], a, LAST_BOTH, preferred_element_type=jnp.float32)
            out_ref[at] = (base[at] + low).astype(out_ref.dtype)

    grad_shape = (pipe_count, 1, rows, RANKS)
    return call(
        kernel,
        "input_gradient",
        grid=(data_count // planes,),
        in_specs=[
            SMEM,
            pl.BlockSpec((tile, WIDTH), lambda n: (n, 0)),
            pl.BlockSpec((planes, blocks_dev, down_rows, RANKS), lambda n: (n, 0, 0, 0)),
        ]
        + [pl.BlockSpec(grad_shape, lambda n: (0, 0, 0, 0))] * tensor_count
        + [ANY] * len(order),
        out_specs=pl.BlockSpec((tok_dev, tile), lambda n: (0, n)),
        out_shape=jax.ShapeDtypeStruct((tok_dev, depth), jnp.bfloat16),
        scratch_shapes=[
            pltpu.VMEM((tok_dev, WIDTH), jnp.bfloat16),
            pltpu.VMEM((tok_dev, RANKS), jnp.bfloat16),
            pltpu.SemaphoreType.DMA((len(order),)),
        ],
    )(at, weight, down, *grad_pieces, *[cot_pieces[s][k] for s, k in order])


def grad_down(at, slot_of, slots, x_features, grad_pieces):
    data_count, down_rows, tok_dev = x_features.shape
    tensor_count = len(grad_pieces)
    pipe_count, _, rows, _ = grad_pieces[0].shape
    blocks_dev = tok_dev // BLOCK

    def kernel(at_ref, x_ref, *rest):
        grad_refs, (out_ref, grad) = rest[:tensor_count], rest[tensor_count:]
        for s in range(tensor_count):
            core = wrap(at_ref[2] - s, tensor_count)
            for k in range(pipe_count):
                chip = wrap(at_ref[1] - k, pipe_count)
                first = pl.multiple_of((chip * tensor_count + core) * rows, rows)
                for m in range(data_count):
                    data = wrap(at_ref[0] - m, data_count)
                    grad[data, pl.ds(first, rows)] = grad_refs[s][k, m]
        out_ref[...] = jnp.zeros(out_ref.shape, out_ref.dtype)
        for data in range(data_count):
            for block in range(blocks_dev):
                slot = slot_of(at_ref, data, block)
                at = slice(block * BLOCK, (block + 1) * BLOCK)
                out_ref[slot] += jnp.dot(
                    x_ref[data, :, at], grad[data, at], preferred_element_type=jnp.float32
                )

    return call(
        kernel,
        "grad_down",
        in_specs=[SMEM, VMEM] + [VMEM] * tensor_count,
        out_specs=VMEM,
        out_shape=jax.ShapeDtypeStruct((slots, down_rows, RANKS), jnp.float32),
        scratch_shapes=[pltpu.VMEM((data_count, tok_dev, RANKS), jnp.bfloat16)],
    )(at, x_features, *grad_pieces)


def grad_up_pieces(at, low_pieces, cot_pieces, data_count, up_rows):
    tensor_count, pipe_count = len(cot_pieces), len(cot_pieces[0])
    group_count = tensor_count * pipe_count
    rows = cot_pieces[0][0].shape[0]
    cols = WIDTH // group_count
    tok_dev = group_count * rows
    blocks_dev = tok_dev // BLOCK
    group_half = group_count // 2
    order = [(s, k) for s in range(tensor_count) for k in range(pipe_count)]
    pieces = [cot_pieces[s][k] for s, k in order]
    in_kernel = cols % 128 == 0
    if not in_kernel:
        first_col = (at[1] * tensor_count + at[2]) * cols
        pieces = [lax.dynamic_slice_in_dim(piece, first_col, cols, 1) for piece in pieces]

    def kernel(at_ref, *rest):
        low_refs, rest = rest[:tensor_count], rest[tensor_count:]
        cot_refs, (out_ref, low, cot, sems) = rest[: len(order)], rest[len(order) :]
        my_group = at_ref[1] * tensor_count + at_ref[2]
        copies = []
        for i, (s, k) in enumerate(order):
            core = wrap(at_ref[2] - s, tensor_count)
            chip = wrap(at_ref[1] - k, pipe_count)
            first = pl.multiple_of((chip * tensor_count + core) * rows, rows)
            piece = cot_refs[i]
            if in_kernel:
                piece = piece.at[:, pl.ds(pl.multiple_of(my_group * cols, cols), cols)]
            copies.append(pltpu.make_async_copy(piece, cot.at[pl.ds(first, rows)], sems.at[i]))
        for copy in copies:
            copy.start()
        for s in range(tensor_count):
            core = wrap(at_ref[2] - s, tensor_count)
            for k in range(pipe_count):
                first = pl.multiple_of((k * tensor_count + core) * rows, rows)
                low[pl.ds(first, rows)] = low_refs[s][k]
        for copy in copies:
            copy.wait()
        for block in range(blocks_dev):
            at = slice(block * BLOCK, (block + 1) * BLOCK)
            both = lax.dot_general(low[at], cot[at], FIRST_BOTH, preferred_element_type=jnp.float32)
            half = jnp.where(my_group < group_half, both[:ADAPTER_RANK], both[ADAPTER_RANK:])
            half = half.astype(out_ref.dtype)
            for data in range(data_count):
                k = wrap(data - at_ref[0], data_count)
                out_ref[k, block] = half[data * up_rows : (data + 1) * up_rows]

    return call(
        kernel,
        "grad_up_pieces",
        in_specs=[SMEM] + [VMEM] * tensor_count + [ANY] * len(order),
        out_specs=VMEM,
        out_shape=jax.ShapeDtypeStruct((data_count, blocks_dev, up_rows, cols), jnp.bfloat16),
        scratch_shapes=[
            pltpu.VMEM((tok_dev, RANKS), jnp.bfloat16),
            pltpu.VMEM((tok_dev, cols), jnp.bfloat16),
            pltpu.SemaphoreType.DMA((len(order),)),
        ],
    )(at, *low_pieces, *pieces)


def grad_up(at, slot_of, slots, pieces):
    data_count = len(pieces)
    blocks_dev, up_rows, cols = pieces[0].shape

    def kernel(at_ref, *rest):
        piece_refs, out_ref = rest[:data_count], rest[data_count]
        out_ref[...] = jnp.zeros(out_ref.shape, out_ref.dtype)
        for k in range(data_count):
            data = wrap(at_ref[0] - k, data_count)
            for block in range(blocks_dev):
                slot = slot_of(at_ref, data, block)
                out_ref[slot] += piece_refs[k][block].astype(out_ref.dtype)

    return call(
        kernel,
        "grad_up",
        in_specs=[SMEM] + [VMEM] * data_count,
        out_specs=VMEM,
        out_shape=jax.ShapeDtypeStruct((slots, up_rows, cols), jnp.float32),
    )(at, *pieces)


def own_rows(at, up, cotangent):
    data_count = len(up)
    rows = cotangent.shape[0]

    def kernel(at_ref, cot_ref, *rest):
        up_refs, (b_ref, grad_ref) = rest[:data_count], rest[data_count:]
        pieces = []
        for data in range(data_count):
            came = wrap(at_ref[0] - data, data_count)
            piece = up_refs[0][...]
            for k in range(1, data_count):
                piece = jnp.where(came == k, up_refs[k][...], piece)
            pieces.append(piece)
        b = jnp.concatenate(pieces, axis=0)
        b_ref[...] = b
        cot = cot_ref[...]
        grad_ref[...] = jnp.concatenate(
            [
                lax.dot_general(cot[:, half], b[:, half], LAST_BOTH, preferred_element_type=jnp.float32)
                for half in (slice(0, KEY_WIDTH), slice(KEY_WIDTH, WIDTH))
            ],
            axis=1,
        ).astype(grad_ref.dtype)

    return call(
        kernel,
        "own_rows",
        in_specs=[SMEM, VMEM] + [VMEM] * data_count,
        out_specs=(VMEM, VMEM),
        out_shape=(
            jax.ShapeDtypeStruct((ADAPTER_RANK, WIDTH), jnp.bfloat16),
            jax.ShapeDtypeStruct((rows, RANKS), jnp.bfloat16),
        ),
    )(at, cotangent, *up)


def keys_and_values(at, base_pieces, low_sum, b_own):
    rows = base_pieces[0].shape[0]
    count = len(base_pieces)

    def kernel(at_ref, low_ref, b_ref, *rest):
        base_refs, out_ref = rest[:count], rest[count]
        low = low_ref[at_ref[1]]
        for first, ranks in ((0, slice(0, ADAPTER_RANK)), (KEY_WIDTH, slice(ADAPTER_RANK, RANKS))):
            at = slice(first, first + KEY_WIDTH)
            y = jnp.dot(low[:, ranks], b_ref[:, at], preferred_element_type=jnp.float32)
            for base_ref in base_refs:
                y += base_ref[:, at].astype(jnp.float32)
            out_ref[:, at] = y.astype(out_ref.dtype)

    return call(
        kernel,
        "keys_and_values",
        in_specs=[SMEM, VMEM, VMEM] + [VMEM] * count,
        out_specs=VMEM,
        out_shape=jax.ShapeDtypeStruct((rows, WIDTH), jnp.bfloat16),
    )(at, low_sum, b_own, *base_pieces)


def body(
    tokens, key_value_weight, adapter_down, adapter_up, tenant_of_block, slot_of_tenant, cotangent
):
    data_count = lax.axis_size("dp")
    pipe_count = lax.axis_size("pipe")
    tensor_count = lax.axis_size("tensor")
    group_count = pipe_count * tensor_count
    at_data, at_pipe, at_tensor = (lax.axis_index(a) for a in ("dp", "pipe", "tensor"))
    my_group = at_pipe * tensor_count + at_tensor
    tok_dev, feature_count = tokens.shape
    blocks_dev = tok_dev // BLOCK
    rows = tok_dev // group_count
    down_rows = adapter_down.shape[1]
    up_rows = adapter_up.shape[1]
    slots = adapter_down.shape[0]
    blocks = tenant_of_block.shape[0]

    own_block = my_group * rows // BLOCK
    at = jnp.stack([at_data, at_pipe, at_tensor, own_block]).astype(jnp.int32)
    at = jnp.concatenate([at, tenant_of_block, slot_of_tenant])

    def slot_of(at_ref, data, block):
        return at_ref[4 + blocks + at_ref[4 + data * blocks_dev + block]]

    b_send = pick_up(at, slot_of, adapter_up, data_count)
    b_came = [b_send[0]] + [shift(b_send[k], "dp", k) for k in range(1, data_count)]
    a_send = pick_down(at, slot_of, adapter_down, data_count, blocks_dev)
    a_send, b_came = lax.optimization_barrier((a_send, b_came))
    a_recv = lax.all_to_all(a_send, "dp", 0, 0, tiled=True)
    b_own, grad_rows = own_rows(at, b_came, cotangent)

    cot_send, a_send = lax.optimization_barrier((cotangent, a_send))
    cot_chips = [cotangent] + [shift(cot_send, "pipe", k) for k in range(1, pipe_count)]

    base_tokens, cot_chips[1] = lax.optimization_barrier((tokens, cot_chips[1]))
    tokens_by_group = base_tokens.reshape(pipe_count, tensor_count, rows, feature_count)
    base_send = base_product(at, tokens_by_group, key_value_weight, 1, tensor_count - 1)
    base_came = [shift(base_send[s - 1], "tensor", s) for s in range(1, tensor_count)]
    tokens_by_group, cot_chips = lax.optimization_barrier((tokens_by_group, cot_chips))
    base_keep = base_product(at, tokens_by_group, key_value_weight, 0, 1)[0]
    base_chip = [
        sum([base_keep[k].astype(jnp.float32)] + [b[k].astype(jnp.float32) for b in base_came])
        for k in range(pipe_count)
    ]
    base_chip_came = [
        shift(base_chip[k].astype(jnp.bfloat16), "pipe", k) for k in range(1, pipe_count)
    ]
    grad_rows, cot_chips, base_chip = lax.optimization_barrier((grad_rows, cot_chips, base_chip))
    grad_data = [grad_rows] + [shift(grad_rows, "dp", k) for k in range(1, data_count)]

    x_send = tokens.T.reshape(data_count, down_rows, tok_dev)
    a_recv, x_send, grad_data = lax.optimization_barrier((a_recv, x_send, grad_data))
    x_recv = lax.all_to_all(x_send, "dp", 0, 0, tiled=True)

    cot_pieces = [cot_chips] + [
        [shift(piece, "tensor", s) for piece in cot_chips] for s in range(1, tensor_count)
    ]
    grad_data = jnp.stack(grad_data)
    grad_chips = jnp.stack([grad_data] + [shift(grad_data, "pipe", k) for k in range(1, pipe_count)])
    grad_pieces = [grad_chips] + [shift(grad_chips, "tensor", s) for s in range(1, tensor_count)]

    low_part = low_product(at, tokens, a_recv, pipe_count, tensor_count)
    low_core = sum(
        [low_part[0].astype(jnp.float32)]
        + [shift(low_part[s], "tensor", s).astype(jnp.float32) for s in range(1, tensor_count)]
    ).astype(jnp.bfloat16)
    low_sum = sum(
        [low_core.astype(jnp.float32)]
        + [shift(low_core, "pipe", k).astype(jnp.float32) for k in range(1, pipe_count)]
    ).astype(jnp.bfloat16)
    low_pieces = [low_sum] + [shift(low_sum, "tensor", s) for s in range(1, tensor_count)]
    key_value = keys_and_values(at, base_chip[:1] + base_chip_came, low_sum, b_own)

    up_pieces = grad_up_pieces(at, low_pieces, cot_pieces, data_count, up_rows)
    up_came = [up_pieces[0]] + [shift(up_pieces[k], "dp", k) for k in range(1, data_count)]
    grad_b = grad_up(at, slot_of, slots, up_came)

    input_grad = input_gradient(at, cot_pieces, key_value_weight, grad_pieces, a_recv)
    grad_a = grad_down(at, slot_of, slots, x_recv, grad_pieces)
    return (key_value, input_grad, grad_a, grad_b)


def solution(mesh):
    atd = (
        P("dp", ("pipe", "tensor")),
        P(("pipe", "tensor"), None),
        P(None, ("pipe", "tensor", "dp"), None),
        P(None, "dp", None),
        P(),
        P(),
        P(("dp", "pipe", "tensor"), None),
    )
    return jax.shard_map(
        body,
        mesh=mesh,
        in_specs=atd,
        out_specs=(
            P(("dp", "pipe", "tensor"), None),
            P("dp", ("pipe", "tensor")),
            P(None, ("pipe", "tensor", "dp"), None),
            P(None, "dp", ("pipe", "tensor")),
        ),
        check_vma=False,
    )
```

```python
import jax
import jax.numpy as jnp
from jax import lax
from jax.experimental import pallas as pl
from jax.experimental.pallas import tpu as pltpu
from jax.sharding import PartitionSpec as P

KEY_WIDTH = 1024
ADAPTER_RANK = 64
BLOCK = 128
RANKS = 2 * ADAPTER_RANK
WIDTH = 2 * KEY_WIDTH
VMEM_LIMIT = 24 * 1024 * 1024
VMEM_MOST = 60 * 1024 * 1024
LAST_BOTH = (((1,), (1,)), ((), ()))
FIRST_BOTH = (((0,), (0,)), ((), ()))
SMEM = pl.BlockSpec(memory_space=pltpu.SMEM)
VMEM = pl.BlockSpec(memory_space=pltpu.VMEM)
HBM = pl.BlockSpec(memory_space=pltpu.HBM)
ANY = pl.BlockSpec(memory_space=pl.ANY)


def call(kernel, name, vmem=VMEM_LIMIT, **more):
    return pl.pallas_call(
        kernel,
        compiler_params=pltpu.CompilerParams(vmem_limit_bytes=vmem),
        cost_estimate=pl.CostEstimate(flops=1024, bytes_accessed=1024, transcendentals=0),
        name=name,
        **more,
    )


def shift(piece, axis, step):
    count = lax.axis_size(axis)
    return lax.ppermute(piece, axis, [(i, (i + step) % count) for i in range(count)])


def wrap(index, count):
    return lax.rem(index + 2 * count, count)


def pick_up(at, slot_of, adapter_up, data_count):
    def kernel(at_ref, up_ref, *rest):
        out_refs, sems = rest[:data_count], rest[data_count]
        copies = []
        for k in range(data_count):
            data = wrap(at_ref[0] + k, data_count)
            slot = slot_of(at_ref, data, at_ref[3])
            copies.append(pltpu.make_async_copy(up_ref.at[slot], out_refs[k], sems.at[k]))
        for copy in copies:
            copy.start()
        for copy in copies:
            copy.wait()

    return call(
        kernel,
        "pick_up",
        VMEM_MOST,
        out_shape=(jax.ShapeDtypeStruct(adapter_up.shape[1:], adapter_up.dtype),) * data_count,
        in_specs=[SMEM, HBM],
        out_specs=(VMEM,) * data_count,
        scratch_shapes=[pltpu.SemaphoreType.DMA((data_count,))],
    )(at, adapter_up)


def pick_down(at, slot_of, adapter_down, data_count, blocks_dev):
    rows, ranks = adapter_down.shape[1:]

    def kernel(at_ref, down_ref, out_ref):
        data = pl.program_id(0)
        for block in range(blocks_dev):
            out_ref[0, block] = down_ref[slot_of(at_ref, data, block)]

    return call(
        kernel,
        "pick_down",
        grid=(data_count,),
        out_shape=jax.ShapeDtypeStruct((data_count, blocks_dev, rows, ranks), adapter_down.dtype),
        in_specs=[SMEM, VMEM],
        out_specs=pl.BlockSpec((1, blocks_dev, rows, ranks), lambda d: (d, 0, 0, 0)),
    )(at, adapter_down)


def base_product(at, tokens, weight, first, count):
    pipe_count, tensor_count, rows, depth = tokens.shape
    tile = 1024

    def kernel(at_ref, x_ref, w_ref, out_ref):
        x = x_ref[...].reshape(pipe_count * rows, depth)
        y = jnp.dot(x, w_ref[...], preferred_element_type=jnp.float32).astype(out_ref.dtype)
        for chip in range(pipe_count):
            out_ref[0, wrap(chip - at_ref[1], pipe_count)] = y[chip * rows : (chip + 1) * rows]

    return call(
        kernel,
        "base_product",
        grid_spec=pltpu.PrefetchScalarGridSpec(
            num_scalar_prefetch=1,
            grid=(WIDTH // tile, count),
            in_specs=[
                pl.BlockSpec(
                    (pipe_count, 1, rows, depth),
                    lambda n, s, at: (0, wrap(at[2] + s + first, tensor_count), 0, 0),
                ),
                pl.BlockSpec((depth, tile), lambda n, s, at: (0, n)),
            ],
            out_specs=pl.BlockSpec((1, pipe_count, rows, tile), lambda n, s, at: (s, 0, 0, n)),
        ),
        out_shape=jax.ShapeDtypeStruct((count, pipe_count, rows, WIDTH), jnp.bfloat16),
    )(at, tokens, weight)


def low_product(at, tokens, down, pipe_count, tensor_count):
    tok_dev, depth = tokens.shape
    rows = tok_dev // (pipe_count * tensor_count)

    def kernel(at_ref, x_ref, a_ref, out_ref):
        for block in range(tok_dev // BLOCK):
            a = a_ref[:, block].reshape(depth, RANKS)
            x = x_ref[block * BLOCK : (block + 1) * BLOCK]
            y = jnp.dot(x, a, preferred_element_type=jnp.float32).astype(out_ref.dtype)
            for part in range(BLOCK // rows):
                chip, core = divmod(block * (BLOCK // rows) + part, tensor_count)
                core = wrap(core - at_ref[2], tensor_count)
                out_ref[core, chip] = y[part * rows : (part + 1) * rows]

    return call(
        kernel,
        "low_product",
        in_specs=[SMEM, VMEM, VMEM],
        out_specs=VMEM,
        out_shape=jax.ShapeDtypeStruct((tensor_count, pipe_count, rows, RANKS), jnp.bfloat16),
    )(at, tokens, down)


def input_gradient(at, cot_pieces, weight, grad_pieces, down):
    data_count, blocks_dev, down_rows, _ = down.shape
    tensor_count, pipe_count = len(cot_pieces), len(cot_pieces[0])
    rows = cot_pieces[0][0].shape[0]
    depth = weight.shape[0]
    tok_dev = blocks_dev * BLOCK
    planes = next((n for n in range(1, data_count) if n * down_rows % 256 == 0), data_count)
    tile = planes * down_rows
    order = [(s, k) for s in range(tensor_count) for k in range(pipe_count)]

    def kernel(at_ref, w_ref, a_ref, *rest):
        grad_refs, rest = rest[:tensor_count], rest[tensor_count:]
        cot_refs, (out_ref, cot, grad, sems) = rest[: len(order)], rest[len(order) :]

        def first_row(s, k):
            chip = wrap(at_ref[1] - k, pipe_count)
            core = wrap(at_ref[2] - s, tensor_count)
            return pl.multiple_of((chip * tensor_count + core) * rows, rows)

        @pl.when(pl.program_id(0) == 0)
        def _():
            copies = [
                pltpu.make_async_copy(ref, cot.at[pl.ds(first_row(*at), rows)], sems.at[i])
                for i, (at, ref) in enumerate(zip(order, cot_refs))
            ]
            for copy in copies:
                copy.start()
            for s, k in order:
                grad[pl.ds(first_row(s, k), rows)] = grad_refs[s][k, 0]
            for copy in copies:
                copy.wait()

        base = lax.dot_general(cot[...], w_ref[...], LAST_BOTH, preferred_element_type=jnp.float32)
        for block in range(blocks_dev):
            at = slice(block * BLOCK, (block + 1) * BLOCK)
            a = a_ref[:, block].reshape(tile, RANKS)
            low = lax.dot_general(grad[at], a, LAST_BOTH, preferred_element_type=jnp.float32)
            out_ref[at] = (base[at] + low).astype(out_ref.dtype)

    grad_shape = (pipe_count, 1, rows, RANKS)
    return call(
        kernel,
        "input_gradient",
        grid=(data_count // planes,),
        in_specs=[
            SMEM,
            pl.BlockSpec((tile, WIDTH), lambda n: (n, 0)),
            pl.BlockSpec((planes, blocks_dev, down_rows, RANKS), lambda n: (n, 0, 0, 0)),
        ]
        + [pl.BlockSpec(grad_shape, lambda n: (0, 0, 0, 0))] * tensor_count
        + [ANY] * len(order),
        out_specs=pl.BlockSpec((tok_dev, tile), lambda n: (0, n)),
        out_shape=jax.ShapeDtypeStruct((tok_dev, depth), jnp.bfloat16),
        scratch_shapes=[
            pltpu.VMEM((tok_dev, WIDTH), jnp.bfloat16),
            pltpu.VMEM((tok_dev, RANKS), jnp.bfloat16),
            pltpu.SemaphoreType.DMA((len(order),)),
        ],
    )(at, weight, down, *grad_pieces, *[cot_pieces[s][k] for s, k in order])


def grad_down(at, slot_of, slots, x_features, grad_pieces):
    data_count, down_rows, tok_dev = x_features.shape
    tensor_count = len(grad_pieces)
    pipe_count, _, rows, _ = grad_pieces[0].shape
    blocks_dev = tok_dev // BLOCK

    def kernel(at_ref, x_ref, *rest):
        grad_refs, (out_ref, grad) = rest[:tensor_count], rest[tensor_count:]
        for s in range(tensor_count):
            core = wrap(at_ref[2] - s, tensor_count)
            for k in range(pipe_count):
                chip = wrap(at_ref[1] - k, pipe_count)
                first = pl.multiple_of((chip * tensor_count + core) * rows, rows)
                for m in range(data_count):
                    data = wrap(at_ref[0] - m, data_count)
                    grad[data, pl.ds(first, rows)] = grad_refs[s][k, m]
        out_ref[...] = jnp.zeros(out_ref.shape, out_ref.dtype)
        for data in range(data_count):
            for block in range(blocks_dev):
                slot = slot_of(at_ref, data, block)
                at = slice(block * BLOCK, (block + 1) * BLOCK)
                out_ref[slot] += jnp.dot(
                    x_ref[data, :, at], grad[data, at], preferred_element_type=jnp.float32
                )

    return call(
        kernel,
        "grad_down",
        in_specs=[SMEM, VMEM] + [VMEM] * tensor_count,
        out_specs=VMEM,
        out_shape=jax.ShapeDtypeStruct((slots, down_rows, RANKS), jnp.float32),
        scratch_shapes=[pltpu.VMEM((data_count, tok_dev, RANKS), jnp.bfloat16)],
    )(at, x_features, *grad_pieces)


def grad_up_pieces(at, low_pieces, cot_pieces, data_count, up_rows):
    tensor_count, pipe_count = len(cot_pieces), len(cot_pieces[0])
    group_count = tensor_count * pipe_count
    rows = cot_pieces[0][0].shape[0]
    cols = WIDTH // group_count
    tok_dev = group_count * rows
    blocks_dev = tok_dev // BLOCK
    group_half = group_count // 2
    order = [(s, k) for s in range(tensor_count) for k in range(pipe_count)]
    pieces = [cot_pieces[s][k] for s, k in order]
    in_kernel = cols % 128 == 0
    if not in_kernel:
        first_col = (at[1] * tensor_count + at[2]) * cols
        pieces = [lax.dynamic_slice_in_dim(piece, first_col, cols, 1) for piece in pieces]

    def kernel(at_ref, *rest):
        low_refs, rest = rest[:tensor_count], rest[tensor_count:]
        cot_refs, (out_ref, low, cot, sems) = rest[: len(order)], rest[len(order) :]
        my_group = at_ref[1] * tensor_count + at_ref[2]
        copies = []
        for i, (s, k) in enumerate(order):
            core = wrap(at_ref[2] - s, tensor_count)
            chip = wrap(at_ref[1] - k, pipe_count)
            first = pl.multiple_of((chip * tensor_count + core) * rows, rows)
            piece = cot_refs[i]
            if in_kernel:
                piece = piece.at[:, pl.ds(pl.multiple_of(my_group * cols, cols), cols)]
            copies.append(pltpu.make_async_copy(piece, cot.at[pl.ds(first, rows)], sems.at[i]))
        for copy in copies:
            copy.start()
        for s in range(tensor_count):
            core = wrap(at_ref[2] - s, tensor_count)
            for k in range(pipe_count):
                first = pl.multiple_of((k * tensor_count + core) * rows, rows)
                low[pl.ds(first, rows)] = low_refs[s][k]
        for copy in copies:
            copy.wait()
        for block in range(blocks_dev):
            at = slice(block * BLOCK, (block + 1) * BLOCK)
            both = lax.dot_general(low[at], cot[at], FIRST_BOTH, preferred_element_type=jnp.float32)
            half = jnp.where(my_group < group_half, both[:ADAPTER_RANK], both[ADAPTER_RANK:])
            half = half.astype(out_ref.dtype)
            for data in range(data_count):
                k = wrap(data - at_ref[0], data_count)
                out_ref[k, block] = half[data * up_rows : (data + 1) * up_rows]

    return call(
        kernel,
        "grad_up_pieces",
        in_specs=[SMEM] + [VMEM] * tensor_count + [ANY] * len(order),
        out_specs=VMEM,
        out_shape=jax.ShapeDtypeStruct((data_count, blocks_dev, up_rows, cols), jnp.bfloat16),
        scratch_shapes=[
            pltpu.VMEM((tok_dev, RANKS), jnp.bfloat16),
            pltpu.VMEM((tok_dev, cols), jnp.bfloat16),
            pltpu.SemaphoreType.DMA((len(order),)),
        ],
    )(at, *low_pieces, *pieces)


def grad_up(at, slot_of, slots, pieces):
    data_count = len(pieces)
    blocks_dev, up_rows, cols = pieces[0].shape

    def kernel(at_ref, *rest):
        piece_refs, out_ref = rest[:data_count], rest[data_count]
        out_ref[...] = jnp.zeros(out_ref.shape, out_ref.dtype)
        for k in range(data_count):
            data = wrap(at_ref[0] - k, data_count)
            for block in range(blocks_dev):
                slot = slot_of(at_ref, data, block)
                out_ref[slot] += piece_refs[k][block].astype(out_ref.dtype)

    return call(
        kernel,
        "grad_up",
        in_specs=[SMEM] + [VMEM] * data_count,
        out_specs=VMEM,
        out_shape=jax.ShapeDtypeStruct((slots, up_rows, cols), jnp.float32),
    )(at, *pieces)


def own_rows(at, up, cotangent):
    data_count = len(up)
    rows = cotangent.shape[0]

    def kernel(at_ref, cot_ref, *rest):
        up_refs, (b_ref, grad_ref) = rest[:data_count], rest[data_count:]
        pieces = []
        for data in range(data_count):
            came = wrap(at_ref[0] - data, data_count)
            piece = up_refs[0][...]
            for k in range(1, data_count):
                piece = jnp.where(came == k, up_refs[k][...], piece)
            pieces.append(piece)
        b = jnp.concatenate(pieces, axis=0)
        b_ref[...] = b
        cot = cot_ref[...]
        grad_ref[...] = jnp.concatenate(
            [
                lax.dot_general(cot[:, half], b[:, half], LAST_BOTH, preferred_element_type=jnp.float32)
                for half in (slice(0, KEY_WIDTH), slice(KEY_WIDTH, WIDTH))
            ],
            axis=1,
        ).astype(grad_ref.dtype)

    return call(
        kernel,
        "own_rows",
        in_specs=[SMEM, VMEM] + [VMEM] * data_count,
        out_specs=(VMEM, VMEM),
        out_shape=(
            jax.ShapeDtypeStruct((ADAPTER_RANK, WIDTH), jnp.bfloat16),
            jax.ShapeDtypeStruct((rows, RANKS), jnp.bfloat16),
        ),
    )(at, cotangent, *up)


def keys_and_values(at, base_pieces, low_sum, b_own):
    rows = base_pieces[0].shape[0]
    count = len(base_pieces)

    def kernel(at_ref, low_ref, b_ref, *rest):
        base_refs, out_ref = rest[:count], rest[count]
        low = low_ref[at_ref[1]]
        for first, ranks in ((0, slice(0, ADAPTER_RANK)), (KEY_WIDTH, slice(ADAPTER_RANK, RANKS))):
            at = slice(first, first + KEY_WIDTH)
            y = jnp.dot(low[:, ranks], b_ref[:, at], preferred_element_type=jnp.float32)
            for base_ref in base_refs:
                y += base_ref[:, at].astype(jnp.float32)
            out_ref[:, at] = y.astype(out_ref.dtype)

    return call(
        kernel,
        "keys_and_values",
        in_specs=[SMEM, VMEM, VMEM] + [VMEM] * count,
        out_specs=VMEM,
        out_shape=jax.ShapeDtypeStruct((rows, WIDTH), jnp.bfloat16),
    )(at, low_sum, b_own, *base_pieces)


def body(
    tokens, key_value_weight, adapter_down, adapter_up, tenant_of_block, slot_of_tenant, cotangent
):
    data_count = lax.axis_size("dp")
    pipe_count = lax.axis_size("pipe")
    tensor_count = lax.axis_size("tensor")
    group_count = pipe_count * tensor_count
    at_data, at_pipe, at_tensor = (lax.axis_index(a) for a in ("dp", "pipe", "tensor"))
    my_group = at_pipe * tensor_count + at_tensor
    tok_dev, feature_count = tokens.shape
    blocks_dev = tok_dev // BLOCK
    rows = tok_dev // group_count
    down_rows = adapter_down.shape[1]
    up_rows = adapter_up.shape[1]
    slots = adapter_down.shape[0]
    blocks = tenant_of_block.shape[0]

    own_block = my_group * rows // BLOCK
    at = jnp.stack([at_data, at_pipe, at_tensor, own_block]).astype(jnp.int32)
    at = jnp.concatenate([at, tenant_of_block, slot_of_tenant])

    def slot_of(at_ref, data, block):
        return at_ref[4 + blocks + at_ref[4 + data * blocks_dev + block]]

    b_send = pick_up(at, slot_of, adapter_up, data_count)
    b_came = [b_send[0]] + [shift(b_send[k], "dp", k) for k in range(1, data_count)]
    a_send = pick_down(at, slot_of, adapter_down, data_count, blocks_dev)
    a_send, b_came = lax.optimization_barrier((a_send, b_came))
    a_recv = lax.all_to_all(a_send, "dp", 0, 0, tiled=True)
    b_own, grad_rows = own_rows(at, b_came, cotangent)

    cot_send, a_send = lax.optimization_barrier((cotangent, a_send))
    cot_cores = [shift(cot_send, "tensor", s) for s in range(1, tensor_count)]

    base_tokens, cot_cores = lax.optimization_barrier((tokens, cot_cores))
    tokens_by_group = base_tokens.reshape(pipe_count, tensor_count, rows, feature_count)
    base_send = base_product(at, tokens_by_group, key_value_weight, 1, tensor_count - 1)
    base_came = [shift(base_send[s - 1], "tensor", s) for s in range(1, tensor_count)]
    base_keep = base_product(at, tokens_by_group, key_value_weight, 0, 1)[0]
    base_chip = [
        sum([base_keep[k].astype(jnp.float32)] + [b[k].astype(jnp.float32) for b in base_came])
        for k in range(pipe_count)
    ]
    base_chip[1:] = [piece.astype(jnp.bfloat16) for piece in base_chip[1:]]
    base_chip_came = [shift(base_chip[k], "pipe", k) for k in range(1, pipe_count)]

    cot_send, base_chip = lax.optimization_barrier((cot_send, base_chip))
    cot_chips = [cotangent] + [shift(cot_send, "pipe", k) for k in range(1, pipe_count)]
    grad_rows, base_chip_came = lax.optimization_barrier((grad_rows, base_chip_came))
    grad_data = [grad_rows] + [shift(grad_rows, "dp", k) for k in range(1, data_count)]

    x_send = tokens.T.reshape(data_count, down_rows, tok_dev)
    a_recv, x_send, grad_data = lax.optimization_barrier((a_recv, x_send, grad_data))
    x_recv = lax.all_to_all(x_send, "dp", 0, 0, tiled=True)

    cot_pieces = [cot_chips] + [
        [cot_cores[s - 1]] + [shift(piece, "tensor", s) for piece in cot_chips[1:]]
        for s in range(1, tensor_count)
    ]
    grad_data = jnp.stack(grad_data)
    grad_chips = jnp.stack([grad_data] + [shift(grad_data, "pipe", k) for k in range(1, pipe_count)])
    grad_pieces = [grad_chips] + [shift(grad_chips, "tensor", s) for s in range(1, tensor_count)]
    input_grad = input_gradient(at, cot_pieces, key_value_weight, grad_pieces, a_recv)

    low_part = low_product(at, tokens, a_recv, pipe_count, tensor_count)
    low_core = sum(
        [low_part[0].astype(jnp.float32)]
        + [shift(low_part[s], "tensor", s).astype(jnp.float32) for s in range(1, tensor_count)]
    ).astype(jnp.bfloat16)
    low_came = [shift(low_core, "pipe", k) for k in range(1, pipe_count)]
    low_came, input_grad = lax.optimization_barrier((low_came, input_grad))
    low_sum = sum([piece.astype(jnp.float32) for piece in [low_core] + low_came])
    low_sum = low_sum.astype(jnp.bfloat16)
    low_pieces = [low_sum] + [shift(low_sum, "tensor", s) for s in range(1, tensor_count)]
    key_value = keys_and_values(at, base_chip[:1] + base_chip_came, low_sum, b_own)

    up_pieces = grad_up_pieces(at, low_pieces, cot_pieces, data_count, up_rows)
    up_came = [up_pieces[0]] + [shift(up_pieces[k], "dp", k) for k in range(1, data_count)]
    grad_b = grad_up(at, slot_of, slots, up_came)

    grad_a = grad_down(at, slot_of, slots, x_recv, grad_pieces)
    return (key_value, input_grad, grad_a, grad_b)


def solution(mesh):
    atd = (
        P("dp", ("pipe", "tensor")),
        P(("pipe", "tensor"), None),
        P(None, ("pipe", "tensor", "dp"), None),
        P(None, "dp", None),
        P(),
        P(),
        P(("dp", "pipe", "tensor"), None),
    )
    return jax.shard_map(
        body,
        mesh=mesh,
        in_specs=atd,
        out_specs=(
            P(("dp", "pipe", "tensor"), None),
            P("dp", ("pipe", "tensor")),
            P(None, ("pipe", "tensor", "dp"), None),
            P(None, "dp", ("pipe", "tensor")),
        ),
        check_vma=False,
    )
```

```python
import jax
import jax.numpy as jnp
from jax import lax
from jax.experimental import pallas as pl
from jax.experimental.pallas import tpu as pltpu
from jax.sharding import PartitionSpec as P

KEY_WIDTH = 1024
ADAPTER_RANK = 64
BLOCK = 128
RANKS = 2 * ADAPTER_RANK
WIDTH = 2 * KEY_WIDTH
VMEM_LIMIT = 24 * 1024 * 1024
LAST_BOTH = (((1,), (1,)), ((), ()))
FIRST_BOTH = (((0,), (0,)), ((), ()))
SMEM = pl.BlockSpec(memory_space=pltpu.SMEM)
VMEM = pl.BlockSpec(memory_space=pltpu.VMEM)
HBM = pl.BlockSpec(memory_space=pltpu.HBM)
ANY = pl.BlockSpec(memory_space=pl.ANY)


def call(kernel, name, **more):
    return pl.pallas_call(
        kernel,
        compiler_params=pltpu.CompilerParams(vmem_limit_bytes=VMEM_LIMIT),
        cost_estimate=pl.CostEstimate(flops=1024, bytes_accessed=1024, transcendentals=0),
        name=name,
        **more,
    )


def shift(piece, axis, step):
    count = lax.axis_size(axis)
    return lax.ppermute(piece, axis, [(i, (i + step) % count) for i in range(count)])


def wrap(index, count):
    return lax.rem(index + 2 * count, count)


def pick_up(at, slot_of, adapter_up, data_count):
    def kernel(at_ref, up_ref, *rest):
        out_refs, sems = rest[:data_count], rest[data_count]
        copies = []
        for k in range(data_count):
            data = wrap(at_ref[0] + k, data_count)
            slot = slot_of(at_ref, data, at_ref[3])
            copies.append(pltpu.make_async_copy(up_ref.at[slot], out_refs[k], sems.at[k]))
        for copy in copies:
            copy.start()
        for copy in copies:
            copy.wait()

    return call(
        kernel,
        "pick_up",
        out_shape=(jax.ShapeDtypeStruct(adapter_up.shape[1:], adapter_up.dtype),) * data_count,
        in_specs=[SMEM, HBM],
        out_specs=(VMEM,) * data_count,
        scratch_shapes=[pltpu.SemaphoreType.DMA((data_count,))],
    )(at, adapter_up)


def pick_down(at, slot_of, adapter_down, grad_rows, data_count, blocks_dev):
    down_rows, ranks = adapter_down.shape[1:]
    rows = grad_rows.shape[0]
    first_grad = blocks_dev * down_rows

    def kernel(at_ref, down_ref, grad_ref, out_ref):
        data = pl.program_id(0)
        for block in range(blocks_dev):
            here = slice(block * down_rows, (block + 1) * down_rows)
            out_ref[0, here] = down_ref[slot_of(at_ref, data, block)]
        out_ref[0, first_grad:] = grad_ref[...]

    return call(
        kernel,
        "pick_down",
        grid=(data_count,),
        out_shape=pltpu.HBM((data_count, first_grad + rows, ranks), adapter_down.dtype),
        in_specs=[SMEM, VMEM, VMEM],
        out_specs=pl.BlockSpec((1, first_grad + rows, ranks), lambda d: (d, 0, 0)),
    )(at, adapter_down, grad_rows)


def base_product(at, tokens, weight, first, count):
    pipe_count, tensor_count, rows, depth = tokens.shape
    tile = 1024

    def kernel(at_ref, x_ref, w_ref, out_ref):
        x = x_ref[...].reshape(pipe_count * rows, depth)
        y = jnp.dot(x, w_ref[...], preferred_element_type=jnp.float32).astype(out_ref.dtype)
        for chip in range(pipe_count):
            out_ref[0, wrap(chip - at_ref[1], pipe_count)] = y[chip * rows : (chip + 1) * rows]

    return call(
        kernel,
        "base_product",
        grid_spec=pltpu.PrefetchScalarGridSpec(
            num_scalar_prefetch=1,
            grid=(WIDTH // tile, count),
            in_specs=[
                pl.BlockSpec(
                    (pipe_count, 1, rows, depth),
                    lambda n, s, at: (0, wrap(at[2] + s + first, tensor_count), 0, 0),
                ),
                pl.BlockSpec((depth, tile), lambda n, s, at: (0, n)),
            ],
            out_specs=pl.BlockSpec((1, pipe_count, rows, tile), lambda n, s, at: (s, 0, 0, n)),
        ),
        out_shape=jax.ShapeDtypeStruct((count, pipe_count, rows, WIDTH), jnp.bfloat16),
    )(at, tokens, weight)


def low_product(at, tokens, down, pipe_count, tensor_count):
    tok_dev, depth = tokens.shape
    down_rows = depth // down.shape[0]
    rows = tok_dev // (pipe_count * tensor_count)

    def kernel(at_ref, x_ref, a_ref, out_ref):
        for block in range(tok_dev // BLOCK):
            a = a_ref[:, block * down_rows : (block + 1) * down_rows].reshape(depth, RANKS)
            x = x_ref[block * BLOCK : (block + 1) * BLOCK]
            y = jnp.dot(x, a, preferred_element_type=jnp.float32).astype(out_ref.dtype)
            for part in range(BLOCK // rows):
                chip, core = divmod(block * (BLOCK // rows) + part, tensor_count)
                core = wrap(core - at_ref[2], tensor_count)
                out_ref[core, chip] = y[part * rows : (part + 1) * rows]

    return call(
        kernel,
        "low_product",
        in_specs=[SMEM, VMEM, VMEM],
        out_specs=VMEM,
        out_shape=jax.ShapeDtypeStruct((tensor_count, pipe_count, rows, RANKS), jnp.bfloat16),
    )(at, tokens, down)


def input_gradient(at, cot_pieces, weight, grad_pieces, down):
    data_count, all_rows, _ = down.shape
    tensor_count, pipe_count = len(cot_pieces), len(cot_pieces[0])
    rows = cot_pieces[0][0].shape[0]
    depth = weight.shape[0]
    down_rows = depth // data_count
    tok_dev = tensor_count * pipe_count * rows
    blocks_dev = tok_dev // BLOCK
    planes = next((n for n in range(1, data_count) if n * down_rows % 256 == 0), data_count)
    tile = planes * down_rows
    order = [(s, k) for s in range(tensor_count) for k in range(pipe_count)]

    def kernel(at_ref, w_ref, a_ref, *rest):
        grad_refs, rest = rest[:tensor_count], rest[tensor_count:]
        cot_refs, (out_ref, cot, grad, sems) = rest[: len(order)], rest[len(order) :]

        def first_row(s, k):
            chip = wrap(at_ref[1] - k, pipe_count)
            core = wrap(at_ref[2] - s, tensor_count)
            return pl.multiple_of((chip * tensor_count + core) * rows, rows)

        @pl.when(pl.program_id(0) == 0)
        def _():
            copies = [
                pltpu.make_async_copy(ref, cot.at[pl.ds(first_row(*at), rows)], sems.at[i])
                for i, (at, ref) in enumerate(zip(order, cot_refs))
            ]
            for copy in copies:
                copy.start()
            for s, k in order:
                grad[pl.ds(first_row(s, k), rows)] = grad_refs[s][k, at_ref[0]]
            for copy in copies:
                copy.wait()

        base = lax.dot_general(cot[...], w_ref[...], LAST_BOTH, preferred_element_type=jnp.float32)
        for block in range(blocks_dev):
            at = slice(block * BLOCK, (block + 1) * BLOCK)
            a = a_ref[:, block * down_rows : (block + 1) * down_rows].reshape(tile, RANKS)
            low = lax.dot_general(grad[at], a, LAST_BOTH, preferred_element_type=jnp.float32)
            out_ref[at] = (base[at] + low).astype(out_ref.dtype)

    grad_shape = (pipe_count, data_count, rows, RANKS)
    return call(
        kernel,
        "input_gradient",
        grid=(data_count // planes,),
        in_specs=[
            SMEM,
            pl.BlockSpec((tile, WIDTH), lambda n: (n, 0)),
            pl.BlockSpec((planes, all_rows, RANKS), lambda n: (n, 0, 0)),
        ]
        + [pl.BlockSpec(grad_shape, lambda n: (0, 0, 0, 0))] * tensor_count
        + [ANY] * len(order),
        out_specs=pl.BlockSpec((tok_dev, tile), lambda n: (0, n)),
        out_shape=jax.ShapeDtypeStruct((tok_dev, depth), jnp.bfloat16),
        scratch_shapes=[
            pltpu.VMEM((tok_dev, WIDTH), jnp.bfloat16),
            pltpu.VMEM((tok_dev, RANKS), jnp.bfloat16),
            pltpu.SemaphoreType.DMA((len(order),)),
        ],
    )(at, weight, down, *grad_pieces, *[cot_pieces[s][k] for s, k in order])


def grad_down(at, slot_of, slots, x_features, grad_pieces):
    data_count, down_rows, tok_dev = x_features.shape
    tensor_count = len(grad_pieces)
    pipe_count, _, rows, _ = grad_pieces[0].shape
    blocks_dev = tok_dev // BLOCK

    def kernel(at_ref, x_ref, *rest):
        grad_refs, (out_ref, grad) = rest[:tensor_count], rest[tensor_count:]
        for s in range(tensor_count):
            core = wrap(at_ref[2] - s, tensor_count)
            for k in range(pipe_count):
                chip = wrap(at_ref[1] - k, pipe_count)
                first = pl.multiple_of((chip * tensor_count + core) * rows, rows)
                for data in range(data_count):
                    grad[data, pl.ds(first, rows)] = grad_refs[s][k, data]
        out_ref[...] = jnp.zeros(out_ref.shape, out_ref.dtype)
        for data in range(data_count):
            for block in range(blocks_dev):
                slot = slot_of(at_ref, data, block)
                at = slice(block * BLOCK, (block + 1) * BLOCK)
                out_ref[slot] += jnp.dot(
                    x_ref[data, :, at], grad[data, at], preferred_element_type=jnp.float32
                )

    return call(
        kernel,
        "grad_down",
        in_specs=[SMEM, VMEM] + [VMEM] * tensor_count,
        out_specs=VMEM,
        out_shape=jax.ShapeDtypeStruct((slots, down_rows, RANKS), jnp.float32),
        scratch_shapes=[pltpu.VMEM((data_count, tok_dev, RANKS), jnp.bfloat16)],
    )(at, x_features, *grad_pieces)


def grad_up_pieces(at, low_pieces, cot_pieces, data_count, up_rows):
    tensor_count, pipe_count = len(cot_pieces), len(cot_pieces[0])
    group_count = tensor_count * pipe_count
    rows = cot_pieces[0][0].shape[0]
    cols = WIDTH // group_count
    tok_dev = group_count * rows
    blocks_dev = tok_dev // BLOCK
    group_half = group_count // 2
    order = [(s, k) for s in range(tensor_count) for k in range(pipe_count)]
    pieces = [cot_pieces[s][k] for s, k in order]
    in_kernel = cols % 128 == 0
    if not in_kernel:
        first_col = (at[1] * tensor_count + at[2]) * cols
        pieces = [lax.dynamic_slice_in_dim(piece, first_col, cols, 1) for piece in pieces]

    def kernel(at_ref, *rest):
        low_refs, rest = rest[:tensor_count], rest[tensor_count:]
        cot_refs, (out_ref, low, cot, sems) = rest[: len(order)], rest[len(order) :]
        my_group = at_ref[1] * tensor_count + at_ref[2]
        copies = []
        for i, (s, k) in enumerate(order):
            core = wrap(at_ref[2] - s, tensor_count)
            chip = wrap(at_ref[1] - k, pipe_count)
            first = pl.multiple_of((chip * tensor_count + core) * rows, rows)
            piece = cot_refs[i]
            if in_kernel:
                piece = piece.at[:, pl.ds(pl.multiple_of(my_group * cols, cols), cols)]
            copies.append(pltpu.make_async_copy(piece, cot.at[pl.ds(first, rows)], sems.at[i]))
        for copy in copies:
            copy.start()
        for s in range(tensor_count):
            core = wrap(at_ref[2] - s, tensor_count)
            for k in range(pipe_count):
                first = pl.multiple_of((k * tensor_count + core) * rows, rows)
                low[pl.ds(first, rows)] = low_refs[s][k]
        for copy in copies:
            copy.wait()
        for block in range(blocks_dev):
            at = slice(block * BLOCK, (block + 1) * BLOCK)
            both = lax.dot_general(low[at], cot[at], FIRST_BOTH, preferred_element_type=jnp.float32)
            half = jnp.where(my_group < group_half, both[:ADAPTER_RANK], both[ADAPTER_RANK:])
            half = half.astype(out_ref.dtype)
            for data in range(data_count):
                k = wrap(data - at_ref[0], data_count)
                out_ref[k, block] = half[data * up_rows : (data + 1) * up_rows]

    return call(
        kernel,
        "grad_up_pieces",
        in_specs=[SMEM] + [VMEM] * tensor_count + [ANY] * len(order),
        out_specs=VMEM,
        out_shape=jax.ShapeDtypeStruct((data_count, blocks_dev, up_rows, cols), jnp.bfloat16),
        scratch_shapes=[
            pltpu.VMEM((tok_dev, RANKS), jnp.bfloat16),
            pltpu.VMEM((tok_dev, cols), jnp.bfloat16),
            pltpu.SemaphoreType.DMA((len(order),)),
        ],
    )(at, *low_pieces, *pieces)


def grad_up(at, slot_of, slots, pieces):
    data_count = len(pieces)
    blocks_dev, up_rows, cols = pieces[0].shape

    def kernel(at_ref, *rest):
        piece_refs, out_ref = rest[:data_count], rest[data_count]
        out_ref[...] = jnp.zeros(out_ref.shape, out_ref.dtype)
        for k in range(data_count):
            data = wrap(at_ref[0] - k, data_count)
            for block in range(blocks_dev):
                slot = slot_of(at_ref, data, block)
                out_ref[slot] += piece_refs[k][block].astype(out_ref.dtype)

    return call(
        kernel,
        "grad_up",
        in_specs=[SMEM] + [VMEM] * data_count,
        out_specs=VMEM,
        out_shape=jax.ShapeDtypeStruct((slots, up_rows, cols), jnp.float32),
    )(at, *pieces)


def own_rows(at, up, cotangent):
    data_count = len(up)
    rows = cotangent.shape[0]

    def kernel(at_ref, cot_ref, *rest):
        up_refs, (b_ref, grad_ref) = rest[:data_count], rest[data_count:]
        pieces = []
        for data in range(data_count):
            came = wrap(at_ref[0] - data, data_count)
            piece = up_refs[0][...]
            for k in range(1, data_count):
                piece = jnp.where(came == k, up_refs[k][...], piece)
            pieces.append(piece)
        b = jnp.concatenate(pieces, axis=0)
        b_ref[...] = b
        cot = cot_ref[...]
        grad_ref[...] = jnp.concatenate(
            [
                lax.dot_general(cot[:, half], b[:, half], LAST_BOTH, preferred_element_type=jnp.float32)
                for half in (slice(0, KEY_WIDTH), slice(KEY_WIDTH, WIDTH))
            ],
            axis=1,
        ).astype(grad_ref.dtype)

    return call(
        kernel,
        "own_rows",
        in_specs=[SMEM, VMEM] + [VMEM] * data_count,
        out_specs=(VMEM, VMEM),
        out_shape=(
            jax.ShapeDtypeStruct((ADAPTER_RANK, WIDTH), jnp.bfloat16),
            jax.ShapeDtypeStruct((rows, RANKS), jnp.bfloat16),
        ),
    )(at, cotangent, *up)


def keys_and_values(at, base_pieces, low_sum, b_own):
    rows = base_pieces[0].shape[0]
    count = len(base_pieces)

    def kernel(at_ref, low_ref, b_ref, *rest):
        base_refs, out_ref = rest[:count], rest[count]
        low = low_ref[at_ref[1]]
        for first, ranks in ((0, slice(0, ADAPTER_RANK)), (KEY_WIDTH, slice(ADAPTER_RANK, RANKS))):
            at = slice(first, first + KEY_WIDTH)
            y = jnp.dot(low[:, ranks], b_ref[:, at], preferred_element_type=jnp.float32)
            for base_ref in base_refs:
                y += base_ref[:, at].astype(jnp.float32)
            out_ref[:, at] = y.astype(out_ref.dtype)

    return call(
        kernel,
        "keys_and_values",
        in_specs=[SMEM, VMEM, VMEM] + [VMEM] * count,
        out_specs=VMEM,
        out_shape=jax.ShapeDtypeStruct((rows, WIDTH), jnp.bfloat16),
    )(at, low_sum, b_own, *base_pieces)


def body(
    tokens, key_value_weight, adapter_down, adapter_up, tenant_of_block, slot_of_tenant, cotangent
):
    data_count = lax.axis_size("dp")
    pipe_count = lax.axis_size("pipe")
    tensor_count = lax.axis_size("tensor")
    group_count = pipe_count * tensor_count
    at_data, at_pipe, at_tensor = (lax.axis_index(a) for a in ("dp", "pipe", "tensor"))
    my_group = at_pipe * tensor_count + at_tensor
    tok_dev, feature_count = tokens.shape
    blocks_dev = tok_dev // BLOCK
    rows = tok_dev // group_count
    down_rows = adapter_down.shape[1]
    up_rows = adapter_up.shape[1]
    slots = adapter_down.shape[0]
    blocks = tenant_of_block.shape[0]

    own_block = my_group * rows // BLOCK
    at = jnp.stack([at_data, at_pipe, at_tensor, own_block]).astype(jnp.int32)
    at = jnp.concatenate([at, tenant_of_block, slot_of_tenant])

    def slot_of(at_ref, data, block):
        return at_ref[4 + blocks + at_ref[4 + data * blocks_dev + block]]

    b_send = pick_up(at, slot_of, adapter_up, data_count)
    b_came = [b_send[0]] + [shift(b_send[k], "dp", k) for k in range(1, data_count)]
    b_own, grad_rows = own_rows(at, b_came, cotangent)

    a_send = pick_down(at, slot_of, adapter_down, grad_rows, data_count, blocks_dev)
    a_recv = lax.all_to_all(a_send, "dp", 0, 0, tiled=True)

    cot_send, a_send = lax.optimization_barrier((cotangent, a_send))
    cot_chips = [cotangent] + [shift(cot_send, "pipe", k) for k in range(1, pipe_count)]

    base_tokens, cot_chips[1] = lax.optimization_barrier((tokens, cot_chips[1]))
    tokens_by_group = base_tokens.reshape(pipe_count, tensor_count, rows, feature_count)
    base_send = base_product(at, tokens_by_group, key_value_weight, 1, tensor_count - 1)
    base_came = [shift(base_send[s - 1], "tensor", s) for s in range(1, tensor_count)]
    base_keep = base_product(at, tokens_by_group, key_value_weight, 0, 1)[0]
    base_chip = [
        sum([base_keep[k].astype(jnp.float32)] + [b[k].astype(jnp.float32) for b in base_came])
        for k in range(pipe_count)
    ]
    base_chip[1:] = [piece.astype(jnp.bfloat16) for piece in base_chip[1:]]
    base_chip_came = [shift(base_chip[k], "pipe", k) for k in range(1, pipe_count)]

    x_tokens, base_chip = lax.optimization_barrier((tokens, base_chip))
    x_send = x_tokens.T.reshape(data_count, down_rows, tok_dev)
    a_recv, x_send, cot_chips, base_chip_came = lax.optimization_barrier(
        (a_recv, x_send, cot_chips, base_chip_came)
    )
    x_recv = lax.all_to_all(x_send, "dp", 0, 0, tiled=True)

    cot_pieces = [cot_chips] + [
        [shift(piece, "tensor", s) for piece in cot_chips] for s in range(1, tensor_count)
    ]
    grad_data = a_recv[:, blocks_dev * down_rows :]
    grad_chips = jnp.stack([grad_data] + [shift(grad_data, "pipe", k) for k in range(1, pipe_count)])
    grad_pieces = [grad_chips] + [shift(grad_chips, "tensor", s) for s in range(1, tensor_count)]
    input_grad = input_gradient(at, cot_pieces, key_value_weight, grad_pieces, a_recv)

    low_part = low_product(at, tokens, a_recv, pipe_count, tensor_count)
    low_core = sum(
        [low_part[0].astype(jnp.float32)]
        + [shift(low_part[s], "tensor", s).astype(jnp.float32) for s in range(1, tensor_count)]
    ).astype(jnp.bfloat16)
    low_came = [shift(low_core, "pipe", k) for k in range(1, pipe_count)]
    low_came, input_grad = lax.optimization_barrier((low_came, input_grad))
    low_sum = sum([piece.astype(jnp.float32) for piece in [low_core] + low_came])
    low_sum = low_sum.astype(jnp.bfloat16)
    low_pieces = [low_sum] + [shift(low_sum, "tensor", s) for s in range(1, tensor_count)]
    key_value = keys_and_values(at, base_chip[:1] + base_chip_came, low_sum, b_own)

    up_pieces = grad_up_pieces(at, low_pieces, cot_pieces, data_count, up_rows)
    up_came = [up_pieces[0]] + [shift(up_pieces[k], "dp", k) for k in range(1, data_count)]
    grad_b = grad_up(at, slot_of, slots, up_came)

    grad_a = grad_down(at, slot_of, slots, x_recv, grad_pieces)
    return (key_value, input_grad, grad_a, grad_b)


def solution(mesh):
    atd = (
        P("dp", ("pipe", "tensor")),
        P(("pipe", "tensor"), None),
        P(None, ("pipe", "tensor", "dp"), None),
        P(None, "dp", None),
        P(),
        P(),
        P(("dp", "pipe", "tensor"), None),
    )
    return jax.shard_map(
        body,
        mesh=mesh,
        in_specs=atd,
        out_specs=(
            P(("dp", "pipe", "tensor"), None),
            P("dp", ("pipe", "tensor")),
            P(None, ("pipe", "tensor", "dp"), None),
            P(None, "dp", ("pipe", "tensor")),
        ),
        check_vma=False,
    )
```

```python
import jax
import jax.numpy as jnp
from jax import lax
from jax.experimental import pallas as pl
from jax.experimental.pallas import tpu as pltpu
from jax.sharding import PartitionSpec as P

KEY_WIDTH = 1024
ADAPTER_RANK = 64
BLOCK = 128
RANKS = 2 * ADAPTER_RANK
WIDTH = 2 * KEY_WIDTH
VMEM_LIMIT = 24 * 1024 * 1024
LAST_BOTH = (((1,), (1,)), ((), ()))
FIRST_BOTH = (((0,), (0,)), ((), ()))
SMEM = pl.BlockSpec(memory_space=pltpu.SMEM)
VMEM = pl.BlockSpec(memory_space=pltpu.VMEM)
HBM = pl.BlockSpec(memory_space=pltpu.HBM)
ANY = pl.BlockSpec(memory_space=pl.ANY)


def call(kernel, name, **more):
    return pl.pallas_call(
        kernel,
        compiler_params=pltpu.CompilerParams(vmem_limit_bytes=VMEM_LIMIT),
        cost_estimate=pl.CostEstimate(flops=1024, bytes_accessed=1024, transcendentals=0),
        name=name,
        **more,
    )


def wrap(index, count):
    return lax.rem(index + 2 * count, count)


def shift(piece, axis, k):
    count = lax.axis_size(axis)
    return lax.ppermute(piece, axis, [(i, (i + k) % count) for i in range(count)])


def paired(count):
    return count & (count - 1) == 0


def partner(index, k, count):
    return index ^ k if paired(count) else (index + k) % count


def came_from(index, k, count):
    return index ^ k if paired(count) else wrap(index - k, count)


def which_partner(other, index, count):
    return other ^ index if paired(count) else wrap(other - index, count)


def swap(piece, axis, k):
    count = lax.axis_size(axis)
    return lax.ppermute(piece, axis, [(i, partner(i, k, count)) for i in range(count)])


def pick_up(at, slot_of, adapter_up, data_count):
    def kernel(at_ref, up_ref, *rest):
        out_refs, sems = rest[:data_count], rest[data_count]
        copies = []
        for k in range(data_count):
            data = wrap(at_ref[0] + k, data_count)
            slot = slot_of(at_ref, data, at_ref[3])
            copies.append(pltpu.make_async_copy(up_ref.at[slot], out_refs[k], sems.at[k]))
        for copy in copies:
            copy.start()
        for copy in copies:
            copy.wait()

    return call(
        kernel,
        "pick_up",
        out_shape=(jax.ShapeDtypeStruct(adapter_up.shape[1:], adapter_up.dtype),) * data_count,
        in_specs=[SMEM, HBM],
        out_specs=(VMEM,) * data_count,
        scratch_shapes=[pltpu.SemaphoreType.DMA((data_count,))],
    )(at, adapter_up)


def pick_down(at, slot_of, adapter_down, grad_rows, data_count, blocks_dev):
    down_rows, ranks = adapter_down.shape[1:]
    rows = grad_rows.shape[0]
    first_grad = blocks_dev * down_rows

    def kernel(at_ref, down_ref, grad_ref, out_ref):
        data = pl.program_id(0)
        for block in range(blocks_dev):
            here = slice(block * down_rows, (block + 1) * down_rows)
            out_ref[0, here] = down_ref[slot_of(at_ref, data, block)]
        out_ref[0, first_grad:] = grad_ref[...]

    return call(
        kernel,
        "pick_down",
        grid=(data_count,),
        out_shape=pltpu.HBM((data_count, first_grad + rows, ranks), adapter_down.dtype),
        in_specs=[SMEM, VMEM, VMEM],
        out_specs=pl.BlockSpec((1, first_grad + rows, ranks), lambda d: (d, 0, 0)),
    )(at, adapter_down, grad_rows)


def features(at, tokens, k, data_count):
    tok_dev, depth = tokens.shape
    count = depth // data_count
    if count % 128:
        return lax.dynamic_slice_in_dim(tokens, wrap(at[0] + k, data_count) * count, count, 1).T

    def kernel(at_ref, x_ref, out_ref):
        out_ref[...] = x_ref[...].T

    tile = 256 if tok_dev % 256 == 0 else tok_dev
    return call(
        kernel,
        "features",
        grid_spec=pltpu.PrefetchScalarGridSpec(
            num_scalar_prefetch=1,
            grid=(tok_dev // tile,),
            in_specs=[pl.BlockSpec((tile, count), lambda n, at: (n, wrap(at[0] + k, data_count)))],
            out_specs=pl.BlockSpec((count, tile), lambda n, at: (0, n)),
        ),
        out_shape=jax.ShapeDtypeStruct((count, tok_dev), tokens.dtype),
    )(at, tokens)


def base_product(at, tokens, weight, first, count):
    pipe_count, tensor_count, rows, depth = tokens.shape
    tile = 1024

    def kernel(at_ref, x_ref, w_ref, out_ref):
        x = x_ref[...].reshape(pipe_count * rows, depth)
        y = jnp.dot(x, w_ref[...], preferred_element_type=jnp.float32).astype(out_ref.dtype)
        for chip in range(pipe_count):
            out_ref[0, which_partner(chip, at_ref[1], pipe_count)] = y[chip * rows : (chip + 1) * rows]

    return call(
        kernel,
        "base_product",
        grid_spec=pltpu.PrefetchScalarGridSpec(
            num_scalar_prefetch=1,
            grid=(WIDTH // tile, count),
            in_specs=[
                pl.BlockSpec(
                    (pipe_count, 1, rows, depth),
                    lambda n, s, at: (0, partner(at[2], s + first, tensor_count), 0, 0),
                ),
                pl.BlockSpec((depth, tile), lambda n, s, at: (0, n)),
            ],
            out_specs=pl.BlockSpec((1, pipe_count, rows, tile), lambda n, s, at: (s, 0, 0, n)),
        ),
        out_shape=jax.ShapeDtypeStruct((count, pipe_count, rows, WIDTH), jnp.bfloat16),
    )(at, tokens, weight)


def low_product(at, tokens, down, pipe_count, tensor_count):
    tok_dev, depth = tokens.shape
    down_rows = depth // down.shape[0]
    rows = tok_dev // (pipe_count * tensor_count)

    def kernel(at_ref, x_ref, a_ref, out_ref):
        for block in range(tok_dev // BLOCK):
            a = a_ref[:, block * down_rows : (block + 1) * down_rows].reshape(depth, RANKS)
            x = x_ref[block * BLOCK : (block + 1) * BLOCK]
            y = jnp.dot(x, a, preferred_element_type=jnp.float32).astype(out_ref.dtype)
            for part in range(BLOCK // rows):
                chip, core = divmod(block * (BLOCK // rows) + part, tensor_count)
                core = which_partner(core, at_ref[2], tensor_count)
                out_ref[core, chip] = y[part * rows : (part + 1) * rows]

    return call(
        kernel,
        "low_product",
        in_specs=[SMEM, VMEM, VMEM],
        out_specs=VMEM,
        out_shape=jax.ShapeDtypeStruct((tensor_count, pipe_count, rows, RANKS), jnp.bfloat16),
    )(at, tokens, down)


def cotangent_product(at, cot_pieces, weight):
    tensor_count, pipe_count = len(cot_pieces), len(cot_pieces[0])
    rows = cot_pieces[0][0].shape[0]
    depth = weight.shape[0]
    tok_dev = tensor_count * pipe_count * rows
    tile = 256 if depth % 256 == 0 else depth
    order = [(s, k) for s in range(tensor_count) for k in range(pipe_count)]

    def kernel(at_ref, w_ref, *rest):
        cot_refs, (out_ref, cot, sems) = rest[: len(order)], rest[len(order) :]

        @pl.when(pl.program_id(0) == 0)
        def _():
            copies = []
            for i, (s, k) in enumerate(order):
                chip = came_from(at_ref[1], k, pipe_count)
                core = came_from(at_ref[2], s, tensor_count)
                first = pl.multiple_of((chip * tensor_count + core) * rows, rows)
                copies.append(
                    pltpu.make_async_copy(cot_refs[i], cot.at[pl.ds(first, rows)], sems.at[i])
                )
            for copy in copies:
                copy.start()
            for copy in copies:
                copy.wait()

        out_ref[...] = lax.dot_general(
            cot[...], w_ref[...], LAST_BOTH, preferred_element_type=jnp.float32
        )

    return call(
        kernel,
        "cotangent_product",
        grid=(depth // tile,),
        in_specs=[SMEM, pl.BlockSpec((tile, WIDTH), lambda n: (n, 0))] + [ANY] * len(order),
        out_specs=pl.BlockSpec((tok_dev, tile), lambda n: (0, n)),
        out_shape=jax.ShapeDtypeStruct((tok_dev, depth), jnp.float32),
        scratch_shapes=[
            pltpu.VMEM((tok_dev, WIDTH), jnp.bfloat16),
            pltpu.SemaphoreType.DMA((len(order),)),
        ],
    )(at, weight, *[cot_pieces[s][k] for s, k in order])


def input_gradient(at, base, grad_pieces, down):
    data_count, all_rows, _ = down.shape
    tensor_count = len(grad_pieces)
    pipe_count, _, rows, _ = grad_pieces[0].shape
    tok_dev, depth = base.shape
    down_rows = depth // data_count
    planes = next((n for n in range(1, data_count) if n * down_rows % 256 == 0), data_count)
    tile = planes * down_rows

    def kernel(at_ref, base_ref, a_ref, *rest):
        grad_refs, (out_ref, grad) = rest[:tensor_count], rest[tensor_count:]

        @pl.when(pl.program_id(0) == 0)
        def _():
            for s in range(tensor_count):
                core = came_from(at_ref[2], s, tensor_count)
                for k in range(pipe_count):
                    chip = came_from(at_ref[1], k, pipe_count)
                    first = pl.multiple_of((chip * tensor_count + core) * rows, rows)
                    grad[pl.ds(first, rows)] = grad_refs[s][k, at_ref[0]]

        for block in range(tok_dev // BLOCK):
            here = slice(block * BLOCK, (block + 1) * BLOCK)
            a = a_ref[:, block * down_rows : (block + 1) * down_rows].reshape(tile, RANKS)
            low = lax.dot_general(grad[here], a, LAST_BOTH, preferred_element_type=jnp.float32)
            out_ref[here] = (base_ref[here] + low).astype(out_ref.dtype)

    grad_shape = (pipe_count, data_count, rows, RANKS)
    return call(
        kernel,
        "input_gradient",
        grid=(data_count // planes,),
        in_specs=[
            SMEM,
            pl.BlockSpec((tok_dev, tile), lambda n: (0, n)),
            pl.BlockSpec((planes, all_rows, RANKS), lambda n: (n, 0, 0)),
        ]
        + [pl.BlockSpec(grad_shape, lambda n: (0, 0, 0, 0))] * tensor_count,
        out_specs=pl.BlockSpec((tok_dev, tile), lambda n: (0, n)),
        out_shape=jax.ShapeDtypeStruct((tok_dev, depth), jnp.bfloat16),
        scratch_shapes=[pltpu.VMEM((tok_dev, RANKS), jnp.bfloat16)],
    )(at, base, down, *grad_pieces)


def grad_down(at, slot_of, slots, x_features, grad_pieces):
    data_count = len(x_features)
    down_rows = sum(part.shape[0] for part in x_features[0])
    tok_dev = x_features[0][0].shape[1]
    parts = [(k, part) for k in range(data_count) for part in x_features[k]]
    tensor_count = len(grad_pieces)
    pipe_count, _, rows, _ = grad_pieces[0].shape
    blocks_dev = tok_dev // BLOCK

    def kernel(at_ref, *rest):
        x_refs, rest = rest[: len(parts)], rest[len(parts) :]
        grad_refs, (out_ref, grad) = rest[:tensor_count], rest[tensor_count:]
        for s in range(tensor_count):
            core = came_from(at_ref[2], s, tensor_count)
            for k in range(pipe_count):
                chip = came_from(at_ref[1], k, pipe_count)
                first = pl.multiple_of((chip * tensor_count + core) * rows, rows)
                for data in range(data_count):
                    grad[data, pl.ds(first, rows)] = grad_refs[s][k, data]
        out_ref[...] = jnp.zeros(out_ref.shape, out_ref.dtype)
        first = 0
        for (k, part), x_ref in zip(parts, x_refs):
            data = wrap(at_ref[0] - k, data_count)
            features_at = slice(first, first + part.shape[0])
            first = features_at.stop % down_rows
            for block in range(blocks_dev):
                slot = slot_of(at_ref, data, block)
                here = slice(block * BLOCK, (block + 1) * BLOCK)
                out_ref[slot, features_at] += jnp.dot(
                    x_ref[:, here], grad[data, here], preferred_element_type=jnp.float32
                )

    return call(
        kernel,
        "grad_down",
        in_specs=[SMEM] + [VMEM] * (len(parts) + tensor_count),
        out_specs=VMEM,
        out_shape=jax.ShapeDtypeStruct((slots, down_rows, RANKS), jnp.float32),
        scratch_shapes=[pltpu.VMEM((data_count, tok_dev, RANKS), jnp.bfloat16)],
    )(at, *[part for _, part in parts], *grad_pieces)


def grad_up_pieces(at, low_pieces, cot_pieces, data_count, up_rows):
    tensor_count, pipe_count = len(cot_pieces), len(cot_pieces[0])
    group_count = tensor_count * pipe_count
    rows = cot_pieces[0][0].shape[0]
    cols = WIDTH // group_count
    tok_dev = group_count * rows
    blocks_dev = tok_dev // BLOCK
    group_half = group_count // 2
    order = [(s, k) for s in range(tensor_count) for k in range(pipe_count)]
    pieces = [cot_pieces[s][k] for s, k in order]
    in_kernel = cols % 128 == 0
    if not in_kernel:
        first_col = (at[1] * tensor_count + at[2]) * cols
        pieces = [lax.dynamic_slice_in_dim(piece, first_col, cols, 1) for piece in pieces]

    def kernel(at_ref, *rest):
        low_refs, rest = rest[:tensor_count], rest[tensor_count:]
        cot_refs, (out_ref, low, cot, sems) = rest[: len(order)], rest[len(order) :]
        my_group = at_ref[1] * tensor_count + at_ref[2]
        copies = []
        for i, (s, k) in enumerate(order):
            core = came_from(at_ref[2], s, tensor_count)
            chip = came_from(at_ref[1], k, pipe_count)
            first = pl.multiple_of((chip * tensor_count + core) * rows, rows)
            piece = cot_refs[i]
            if in_kernel:
                piece = piece.at[:, pl.ds(pl.multiple_of(my_group * cols, cols), cols)]
            copies.append(pltpu.make_async_copy(piece, cot.at[pl.ds(first, rows)], sems.at[i]))
        for copy in copies:
            copy.start()
        for s in range(tensor_count):
            core = came_from(at_ref[2], s, tensor_count)
            for k in range(pipe_count):
                first = pl.multiple_of((k * tensor_count + core) * rows, rows)
                low[pl.ds(first, rows)] = low_refs[s][k]
        for copy in copies:
            copy.wait()
        for block in range(blocks_dev):
            at = slice(block * BLOCK, (block + 1) * BLOCK)
            both = lax.dot_general(low[at], cot[at], FIRST_BOTH, preferred_element_type=jnp.float32)
            half = jnp.where(my_group < group_half, both[:ADAPTER_RANK], both[ADAPTER_RANK:])
            half = half.astype(out_ref.dtype)
            for data in range(data_count):
                k = wrap(data - at_ref[0], data_count)
                out_ref[k, block] = half[data * up_rows : (data + 1) * up_rows]

    return call(
        kernel,
        "grad_up_pieces",
        in_specs=[SMEM] + [VMEM] * tensor_count + [ANY] * len(order),
        out_specs=VMEM,
        out_shape=jax.ShapeDtypeStruct((data_count, blocks_dev, up_rows, cols), jnp.bfloat16),
        scratch_shapes=[
            pltpu.VMEM((tok_dev, RANKS), jnp.bfloat16),
            pltpu.VMEM((tok_dev, cols), jnp.bfloat16),
            pltpu.SemaphoreType.DMA((len(order),)),
        ],
    )(at, *low_pieces, *pieces)


def grad_up(at, slot_of, slots, pieces):
    data_count = len(pieces)
    blocks_dev, up_rows, cols = pieces[0].shape

    def kernel(at_ref, *rest):
        piece_refs, out_ref = rest[:data_count], rest[data_count]
        out_ref[...] = jnp.zeros(out_ref.shape, out_ref.dtype)
        for k in range(data_count):
            data = wrap(at_ref[0] - k, data_count)
            for block in range(blocks_dev):
                slot = slot_of(at_ref, data, block)
                out_ref[slot] += piece_refs[k][block].astype(out_ref.dtype)

    return call(
        kernel,
        "grad_up",
        in_specs=[SMEM] + [VMEM] * data_count,
        out_specs=VMEM,
        out_shape=jax.ShapeDtypeStruct((slots, up_rows, cols), jnp.float32),
    )(at, *pieces)


def own_rows(at, up, cotangent):
    data_count = len(up)
    rows = cotangent.shape[0]

    def kernel(at_ref, cot_ref, *rest):
        up_refs, (b_ref, grad_ref) = rest[:data_count], rest[data_count:]
        pieces = []
        for data in range(data_count):
            came = wrap(at_ref[0] - data, data_count)
            piece = up_refs[0][...]
            for k in range(1, data_count):
                piece = jnp.where(came == k, up_refs[k][...], piece)
            pieces.append(piece)
        b = jnp.concatenate(pieces, axis=0)
        b_ref[...] = b
        cot = cot_ref[...]
        grad_ref[...] = jnp.concatenate(
            [
                lax.dot_general(cot[:, half], b[:, half], LAST_BOTH, preferred_element_type=jnp.float32)
                for half in (slice(0, KEY_WIDTH), slice(KEY_WIDTH, WIDTH))
            ],
            axis=1,
        ).astype(grad_ref.dtype)

    return call(
        kernel,
        "own_rows",
        in_specs=[SMEM, VMEM] + [VMEM] * data_count,
        out_specs=(VMEM, VMEM),
        out_shape=(
            jax.ShapeDtypeStruct((ADAPTER_RANK, WIDTH), jnp.bfloat16),
            jax.ShapeDtypeStruct((rows, RANKS), jnp.bfloat16),
        ),
    )(at, cotangent, *up)


def keys_and_values(at, base_pieces, low_sum, b_own):
    rows = base_pieces[0].shape[0]
    count = len(base_pieces)

    def kernel(at_ref, low_ref, b_ref, *rest):
        base_refs, out_ref = rest[:count], rest[count]
        low = low_ref[at_ref[1]]
        for first, ranks in ((0, slice(0, ADAPTER_RANK)), (KEY_WIDTH, slice(ADAPTER_RANK, RANKS))):
            at = slice(first, first + KEY_WIDTH)
            y = jnp.dot(low[:, ranks], b_ref[:, at], preferred_element_type=jnp.float32)
            for base_ref in base_refs:
                y += base_ref[:, at].astype(jnp.float32)
            out_ref[:, at] = y.astype(out_ref.dtype)

    return call(
        kernel,
        "keys_and_values",
        in_specs=[SMEM, VMEM, VMEM] + [VMEM] * count,
        out_specs=VMEM,
        out_shape=jax.ShapeDtypeStruct((rows, WIDTH), jnp.bfloat16),
    )(at, low_sum, b_own, *base_pieces)


def body(
    tokens, key_value_weight, adapter_down, adapter_up, tenant_of_block, slot_of_tenant, cotangent
):
    data_count = lax.axis_size("dp")
    pipe_count = lax.axis_size("pipe")
    tensor_count = lax.axis_size("tensor")
    group_count = pipe_count * tensor_count
    at_data, at_pipe, at_tensor = (lax.axis_index(a) for a in ("dp", "pipe", "tensor"))
    my_group = at_pipe * tensor_count + at_tensor
    tok_dev, feature_count = tokens.shape
    blocks_dev = tok_dev // BLOCK
    rows = tok_dev // group_count
    down_rows = adapter_down.shape[1]
    up_rows = adapter_up.shape[1]
    slots = adapter_down.shape[0]
    blocks = tenant_of_block.shape[0]

    own_block = my_group * rows // BLOCK
    at = jnp.stack([at_data, at_pipe, at_tensor, own_block]).astype(jnp.int32)
    at = jnp.concatenate([at, tenant_of_block, slot_of_tenant])

    def slot_of(at_ref, data, block):
        return at_ref[4 + blocks + at_ref[4 + data * blocks_dev + block]]

    x_came = [[features(at, tokens, 0, data_count)]]
    x_came += [[shift(features(at, tokens, 1, data_count), "dp", 1)]] if data_count > 1 else []

    b_send = pick_up(at, slot_of, adapter_up, data_count)
    b_came = [b_send[0]] + [shift(b_send[k], "dp", k) for k in range(1, data_count)]
    b_came, x_came[1:] = lax.optimization_barrier((b_came, x_came[1:]))
    b_own, grad_rows = own_rows(at, b_came, cotangent)

    a_send = pick_down(at, slot_of, adapter_down, grad_rows, data_count, blocks_dev)
    a_recv = lax.all_to_all(a_send, "dp", 0, 0, tiled=True)

    cot_send, b_send = lax.optimization_barrier((cotangent, b_send))
    cot_chips = [cotangent] + [swap(cot_send, "pipe", k) for k in range(1, pipe_count - 1)]
    cot_send, a_send = lax.optimization_barrier((cotangent, a_send))
    cot_chips += [swap(cot_send, "pipe", pipe_count - 1)]

    base_tokens, cot_chips[-1] = lax.optimization_barrier((tokens, cot_chips[-1]))
    tokens_by_group = base_tokens.reshape(pipe_count, tensor_count, rows, feature_count)
    base_send = base_product(at, tokens_by_group, key_value_weight, 1, tensor_count - 1)
    base_came = [swap(base_send[s - 1], "tensor", s) for s in range(1, tensor_count)]
    base_keep = base_product(at, tokens_by_group, key_value_weight, 0, 1)[0]
    base_chip = [
        sum([base_keep[k].astype(jnp.float32)] + [b[k].astype(jnp.float32) for b in base_came])
        for k in range(pipe_count)
    ]
    base_chip[1:] = [piece.astype(jnp.bfloat16) for piece in base_chip[1:]]
    base_chip_came = [swap(base_chip[k], "pipe", k) for k in range(1, pipe_count)]

    cot_pieces = [cot_chips] + [
        [swap(piece, "tensor", s) for piece in cot_chips] for s in range(1, tensor_count)
    ]
    input_base = cotangent_product(at, cot_pieces, key_value_weight)

    x_tokens, base_chip = lax.optimization_barrier((tokens, base_chip))
    x_send = [[features(at, x_tokens, k, data_count)] for k in range(2, data_count)]
    if down_rows % 256 == 0:
        x_send[:-1] = [jnp.split(whole, 2) for (whole,) in x_send[:-1]]
    a_recv, x_send, input_base, base_chip_came[:1] = lax.optimization_barrier(
        (a_recv, x_send, input_base, base_chip_came[:1])
    )
    x_came += [[shift(part, "dp", k + 2) for part in parts] for k, parts in enumerate(x_send)]

    grad_data = a_recv[:, blocks_dev * down_rows :]
    grad_chips = jnp.stack([grad_data] + [swap(grad_data, "pipe", k) for k in range(1, pipe_count)])
    grad_pieces = [grad_chips] + [swap(grad_chips, "tensor", s) for s in range(1, tensor_count)]
    input_grad = input_gradient(at, input_base, grad_pieces, a_recv)

    x_first = [parts[0] for parts in x_came[2:-1]]
    low_down, base_chip_came, x_first = lax.optimization_barrier((a_recv, base_chip_came, x_first))
    low_part = low_product(at, tokens, low_down, pipe_count, tensor_count)
    low_core = sum(
        [low_part[0].astype(jnp.float32)]
        + [swap(low_part[s], "tensor", s).astype(jnp.float32) for s in range(1, tensor_count)]
    ).astype(jnp.bfloat16)
    low_came = [swap(low_core, "pipe", k) for k in range(1, pipe_count)]
    x_rest = [parts[1:] for parts in x_came[2:-1]]
    low_came, x_rest = lax.optimization_barrier((low_came, x_rest))
    low_sum = sum([piece.astype(jnp.float32) for piece in [low_core] + low_came])
    low_sum = low_sum.astype(jnp.bfloat16)
    low_pieces = [low_sum] + [swap(low_sum, "tensor", s) for s in range(1, tensor_count)]
    key_value = keys_and_values(at, base_chip[:1] + base_chip_came, low_sum, b_own)

    up_pieces = grad_up_pieces(at, low_pieces, cot_pieces, data_count, up_rows)
    up_came = [up_pieces[0]] + [shift(up_pieces[k], "dp", k) for k in range(1, data_count)]
    grad_b = grad_up(at, slot_of, slots, up_came)

    x_came[2:-1] = [[part] + rest for part, rest in zip(x_first, x_rest)]
    grad_a = grad_down(at, slot_of, slots, x_came, grad_pieces)
    return (key_value, input_grad, grad_a, grad_b)


def solution(mesh):
    atd = (
        P("dp", ("pipe", "tensor")),
        P(("pipe", "tensor"), None),
        P(None, ("pipe", "tensor", "dp"), None),
        P(None, "dp", None),
        P(),
        P(),
        P(("dp", "pipe", "tensor"), None),
    )
    return jax.shard_map(
        body,
        mesh=mesh,
        in_specs=atd,
        out_specs=(
            P(("dp", "pipe", "tensor"), None),
            P("dp", ("pipe", "tensor")),
            P(None, ("pipe", "tensor", "dp"), None),
            P(None, "dp", ("pipe", "tensor")),
        ),
        check_vma=False,
    )
```

```python
import jax
import jax.numpy as jnp
from jax import lax
from jax.experimental import pallas as pl
from jax.experimental.pallas import tpu as pltpu
from jax.sharding import PartitionSpec as P

KEY_WIDTH = 1024
ADAPTER_RANK = 64
BLOCK = 128
RANKS = 2 * ADAPTER_RANK
WIDTH = 2 * KEY_WIDTH
VMEM_LIMIT = 24 * 1024 * 1024
LAST_BOTH = (((1,), (1,)), ((), ()))
FIRST_BOTH = (((0,), (0,)), ((), ()))
SMEM = pl.BlockSpec(memory_space=pltpu.SMEM)
VMEM = pl.BlockSpec(memory_space=pltpu.VMEM)
HBM = pl.BlockSpec(memory_space=pltpu.HBM)
ANY = pl.BlockSpec(memory_space=pl.ANY)


def call(kernel, name, **more):
    return pl.pallas_call(
        kernel,
        compiler_params=pltpu.CompilerParams(vmem_limit_bytes=VMEM_LIMIT),
        cost_estimate=pl.CostEstimate(flops=1024, bytes_accessed=1024, transcendentals=0),
        name=name,
        **more,
    )


def wrap(index, count):
    return lax.rem(index + 2 * count, count)


def shift(piece, axis, k):
    count = lax.axis_size(axis)
    return lax.ppermute(piece, axis, [(i, (i + k) % count) for i in range(count)])


def paired(count):
    return count & (count - 1) == 0


def partner(index, k, count):
    return index ^ k if paired(count) else (index + k) % count


def came_from(index, k, count):
    return index ^ k if paired(count) else wrap(index - k, count)


def which_partner(other, index, count):
    return other ^ index if paired(count) else wrap(other - index, count)


def swap(piece, axis, k):
    count = lax.axis_size(axis)
    return lax.ppermute(piece, axis, [(i, partner(i, k, count)) for i in range(count)])


def up_rides(adapter_up):
    return adapter_up.shape[1] % 16 == 0


def pick(at, slot_of, adapter_down, adapter_up, data_count, blocks_dev):
    down_rows, ranks = adapter_down.shape[1:]
    up_rows, width = adapter_up.shape[1:]
    first_up = blocks_dev * down_rows
    rides = up_rides(adapter_up)
    total = first_up + (up_rows * width // ranks if rides else 0)

    def kernel(at_ref, down_ref, up_ref, out_ref):
        data = pl.program_id(0)
        for block in range(blocks_dev):
            here = slice(block * down_rows, (block + 1) * down_rows)
            out_ref[0, here] = down_ref[slot_of(at_ref, data, block)]
        if rides:
            slot = slot_of(at_ref, data, at_ref[3])
            for n in range(width // ranks):
                first = first_up + n * up_rows
                out_ref[0, first : first + up_rows] = up_ref[slot, :, n * ranks : (n + 1) * ranks]

    return call(
        kernel,
        "pick_rows",
        grid=(data_count,),
        out_shape=pltpu.HBM((data_count, total, ranks), adapter_down.dtype),
        in_specs=[SMEM, VMEM, VMEM],
        out_specs=pl.BlockSpec((1, total, ranks), lambda d: (d, 0, 0)),
    )(at, adapter_down, adapter_up)


def pick_up(at, slot_of, adapter_up, data_count):
    slots = jnp.stack([slot_of(at, data, at[3]) for data in range(data_count)])
    return jnp.take(adapter_up, slots, axis=0)


def base_product(at, tokens, weight, first, count):
    pipe_count, tensor_count, rows, depth = tokens.shape
    tile = 1024

    def kernel(at_ref, x_ref, w_ref, out_ref):
        x = x_ref[...].reshape(pipe_count * rows, depth)
        y = jnp.dot(x, w_ref[...], preferred_element_type=jnp.float32).astype(out_ref.dtype)
        for chip in range(pipe_count):
            out_ref[0, which_partner(chip, at_ref[1], pipe_count)] = y[chip * rows : (chip + 1) * rows]

    return call(
        kernel,
        "base_product",
        grid_spec=pltpu.PrefetchScalarGridSpec(
            num_scalar_prefetch=1,
            grid=(WIDTH // tile, count),
            in_specs=[
                pl.BlockSpec(
                    (pipe_count, 1, rows, depth),
                    lambda n, s, at: (0, partner(at[2], s + first, tensor_count), 0, 0),
                ),
                pl.BlockSpec((depth, tile), lambda n, s, at: (0, n)),
            ],
            out_specs=pl.BlockSpec((1, pipe_count, rows, tile), lambda n, s, at: (s, 0, 0, n)),
        ),
        out_shape=jax.ShapeDtypeStruct((count, pipe_count, rows, WIDTH), jnp.bfloat16),
    )(at, tokens, weight)


def low_product(at, tokens, down, pipe_count, tensor_count):
    tok_dev, depth = tokens.shape
    down_rows = depth // down.shape[0]
    rows = tok_dev // (pipe_count * tensor_count)

    def kernel(at_ref, x_ref, a_ref, out_ref):
        for block in range(tok_dev // BLOCK):
            a = a_ref[:, block * down_rows : (block + 1) * down_rows].reshape(depth, RANKS)
            x = x_ref[block * BLOCK : (block + 1) * BLOCK]
            y = jnp.dot(x, a, preferred_element_type=jnp.float32).astype(out_ref.dtype)
            for part in range(BLOCK // rows):
                chip, core = divmod(block * (BLOCK // rows) + part, tensor_count)
                core = which_partner(core, at_ref[2], tensor_count)
                out_ref[core, chip] = y[part * rows : (part + 1) * rows]

    return call(
        kernel,
        "low_product",
        in_specs=[SMEM, VMEM, VMEM],
        out_specs=VMEM,
        out_shape=jax.ShapeDtypeStruct((tensor_count, pipe_count, rows, RANKS), jnp.bfloat16),
    )(at, tokens, down)


def cotangent_product(at, cot_pieces, weight):
    tensor_count, pipe_count = len(cot_pieces), len(cot_pieces[0])
    rows = cot_pieces[0][0].shape[0]
    depth = weight.shape[0]
    tok_dev = tensor_count * pipe_count * rows
    tile = 256 if depth % 256 == 0 else depth
    order = [(s, k) for s in range(tensor_count) for k in range(pipe_count)]

    def kernel(at_ref, w_ref, *rest):
        cot_refs, (out_ref, cot, sems) = rest[: len(order)], rest[len(order) :]

        @pl.when(pl.program_id(0) == 0)
        def _():
            copies = []
            for i, (s, k) in enumerate(order):
                chip = came_from(at_ref[1], k, pipe_count)
                core = came_from(at_ref[2], s, tensor_count)
                first = pl.multiple_of((chip * tensor_count + core) * rows, rows)
                copies.append(
                    pltpu.make_async_copy(cot_refs[i], cot.at[pl.ds(first, rows)], sems.at[i])
                )
            for copy in copies:
                copy.start()
            for copy in copies:
                copy.wait()

        out_ref[...] = lax.dot_general(
            cot[...], w_ref[...], LAST_BOTH, preferred_element_type=jnp.float32
        )

    return call(
        kernel,
        "cotangent_product",
        grid=(depth // tile,),
        in_specs=[SMEM, pl.BlockSpec((tile, WIDTH), lambda n: (n, 0))] + [ANY] * len(order),
        out_specs=pl.BlockSpec((tok_dev, tile), lambda n: (0, n)),
        out_shape=jax.ShapeDtypeStruct((tok_dev, depth), jnp.float32),
        scratch_shapes=[
            pltpu.VMEM((tok_dev, WIDTH), jnp.bfloat16),
            pltpu.SemaphoreType.DMA((len(order),)),
        ],
    )(at, weight, *[cot_pieces[s][k] for s, k in order])


def input_gradient(at, base, grad_pieces, down):
    data_count, all_rows, _ = down.shape
    tensor_count = len(grad_pieces)
    pipe_count, _, rows, _ = grad_pieces[0].shape
    tok_dev, depth = base.shape
    down_rows = depth // data_count
    planes = next((n for n in range(1, data_count) if n * down_rows % 256 == 0), data_count)
    tile = planes * down_rows

    def kernel(at_ref, base_ref, a_ref, *rest):
        grad_refs, (out_ref, grad) = rest[:tensor_count], rest[tensor_count:]

        @pl.when(pl.program_id(0) == 0)
        def _():
            for s in range(tensor_count):
                core = came_from(at_ref[2], s, tensor_count)
                for k in range(pipe_count):
                    chip = came_from(at_ref[1], k, pipe_count)
                    first = pl.multiple_of((chip * tensor_count + core) * rows, rows)
                    grad[pl.ds(first, rows)] = grad_refs[s][k, 0]

        for block in range(tok_dev // BLOCK):
            here = slice(block * BLOCK, (block + 1) * BLOCK)
            a = a_ref[:, block * down_rows : (block + 1) * down_rows].reshape(tile, RANKS)
            low = lax.dot_general(grad[here], a, LAST_BOTH, preferred_element_type=jnp.float32)
            out_ref[here] = (base_ref[here] + low).astype(out_ref.dtype)

    grad_shape = (pipe_count, data_count, rows, RANKS)
    return call(
        kernel,
        "input_gradient",
        grid=(data_count // planes,),
        in_specs=[
            SMEM,
            pl.BlockSpec((tok_dev, tile), lambda n: (0, n)),
            pl.BlockSpec((planes, all_rows, RANKS), lambda n: (n, 0, 0)),
        ]
        + [pl.BlockSpec(grad_shape, lambda n: (0, 0, 0, 0))] * tensor_count,
        out_specs=pl.BlockSpec((tok_dev, tile), lambda n: (0, n)),
        out_shape=jax.ShapeDtypeStruct((tok_dev, depth), jnp.bfloat16),
        scratch_shapes=[pltpu.VMEM((tok_dev, RANKS), jnp.bfloat16)],
    )(at, base, down, *grad_pieces)


def grad_down(at, slot_of, slots, x_features, grad_pieces):
    data_count, down_rows, tok_dev = x_features.shape
    tensor_count = len(grad_pieces)
    pipe_count, _, rows, _ = grad_pieces[0].shape
    blocks_dev = tok_dev // BLOCK

    def kernel(at_ref, x_ref, *rest):
        grad_refs, (out_ref, grad) = rest[:tensor_count], rest[tensor_count:]
        for s in range(tensor_count):
            core = came_from(at_ref[2], s, tensor_count)
            for k in range(pipe_count):
                chip = came_from(at_ref[1], k, pipe_count)
                first = pl.multiple_of((chip * tensor_count + core) * rows, rows)
                for m in range(data_count):
                    data = wrap(at_ref[0] - m, data_count)
                    grad[data, pl.ds(first, rows)] = grad_refs[s][k, m]
        out_ref[...] = jnp.zeros(out_ref.shape, out_ref.dtype)
        for data in range(data_count):
            for block in range(blocks_dev):
                slot = slot_of(at_ref, data, block)
                here = slice(block * BLOCK, (block + 1) * BLOCK)
                out_ref[slot] += jnp.dot(
                    x_ref[data, :, here], grad[data, here], preferred_element_type=jnp.float32
                )

    return call(
        kernel,
        "grad_down",
        in_specs=[SMEM, VMEM] + [VMEM] * tensor_count,
        out_specs=VMEM,
        out_shape=jax.ShapeDtypeStruct((slots, down_rows, RANKS), jnp.float32),
        scratch_shapes=[pltpu.VMEM((data_count, tok_dev, RANKS), jnp.bfloat16)],
    )(at, x_features, *grad_pieces)


def grad_up_pieces(at, low_pieces, cot_pieces, data_count, up_rows):
    tensor_count, pipe_count = len(cot_pieces), len(cot_pieces[0])
    group_count = tensor_count * pipe_count
    rows = cot_pieces[0][0].shape[0]
    cols = WIDTH // group_count
    tok_dev = group_count * rows
    blocks_dev = tok_dev // BLOCK
    group_half = group_count // 2
    order = [(s, k) for s in range(tensor_count) for k in range(pipe_count)]
    pieces = [cot_pieces[s][k] for s, k in order]
    in_kernel = cols % 128 == 0
    if not in_kernel:
        first_col = (at[1] * tensor_count + at[2]) * cols
        pieces = [lax.dynamic_slice_in_dim(piece, first_col, cols, 1) for piece in pieces]

    def kernel(at_ref, *rest):
        low_refs, rest = rest[:tensor_count], rest[tensor_count:]
        cot_refs, (out_ref, low, cot, sems) = rest[: len(order)], rest[len(order) :]
        my_group = at_ref[1] * tensor_count + at_ref[2]
        copies = []
        for i, (s, k) in enumerate(order):
            core = came_from(at_ref[2], s, tensor_count)
            chip = came_from(at_ref[1], k, pipe_count)
            first = pl.multiple_of((chip * tensor_count + core) * rows, rows)
            piece = cot_refs[i]
            if in_kernel:
                piece = piece.at[:, pl.ds(pl.multiple_of(my_group * cols, cols), cols)]
            copies.append(pltpu.make_async_copy(piece, cot.at[pl.ds(first, rows)], sems.at[i]))
        for copy in copies:
            copy.start()
        for s in range(tensor_count):
            core = came_from(at_ref[2], s, tensor_count)
            for k in range(pipe_count):
                first = pl.multiple_of((k * tensor_count + core) * rows, rows)
                low[pl.ds(first, rows)] = low_refs[s][k]
        for copy in copies:
            copy.wait()
        for block in range(blocks_dev):
            at = slice(block * BLOCK, (block + 1) * BLOCK)
            both = lax.dot_general(low[at], cot[at], FIRST_BOTH, preferred_element_type=jnp.float32)
            half = jnp.where(my_group < group_half, both[:ADAPTER_RANK], both[ADAPTER_RANK:])
            half = half.astype(out_ref.dtype)
            for data in range(data_count):
                k = wrap(data - at_ref[0], data_count)
                out_ref[k, block] = half[data * up_rows : (data + 1) * up_rows]

    return call(
        kernel,
        "grad_up_pieces",
        in_specs=[SMEM] + [VMEM] * tensor_count + [ANY] * len(order),
        out_specs=VMEM,
        out_shape=jax.ShapeDtypeStruct((data_count, blocks_dev, up_rows, cols), jnp.bfloat16),
        scratch_shapes=[
            pltpu.VMEM((tok_dev, RANKS), jnp.bfloat16),
            pltpu.VMEM((tok_dev, cols), jnp.bfloat16),
            pltpu.SemaphoreType.DMA((len(order),)),
        ],
    )(at, *low_pieces, *pieces)


def grad_up(at, slot_of, slots, pieces):
    data_count = len(pieces)
    blocks_dev, up_rows, cols = pieces[0].shape

    def kernel(at_ref, *rest):
        piece_refs, out_ref = rest[:data_count], rest[data_count]
        out_ref[...] = jnp.zeros(out_ref.shape, out_ref.dtype)
        for k in range(data_count):
            data = wrap(at_ref[0] - k, data_count)
            for block in range(blocks_dev):
                slot = slot_of(at_ref, data, block)
                out_ref[slot] += piece_refs[k][block].astype(out_ref.dtype)

    return call(
        kernel,
        "grad_up",
        in_specs=[SMEM] + [VMEM] * data_count,
        out_specs=VMEM,
        out_shape=jax.ShapeDtypeStruct((slots, up_rows, cols), jnp.float32),
    )(at, *pieces)


def own_rows(came, up, cotangent, first_up):
    rows = cotangent.shape[0]
    data_count = came.shape[0]
    up_rows = ADAPTER_RANK // data_count

    def kernel(cot_ref, came_ref, b_ref, grad_ref, tiles, sem):
        if up is None:
            copy = pltpu.make_async_copy(came_ref.at[:, pl.ds(first_up, tiles.shape[1])], tiles, sem)
            copy.start()
            copy.wait()
            for data in range(data_count):
                for n in range(WIDTH // RANKS):
                    b_ref[
                        data * up_rows : (data + 1) * up_rows, n * RANKS : (n + 1) * RANKS
                    ] = tiles[data, n * up_rows : (n + 1) * up_rows]
        else:
            b_ref[...] = came_ref[...]
        cot, b = cot_ref[...], b_ref[...]
        grad_ref[...] = jnp.concatenate(
            [
                lax.dot_general(cot[:, half], b[:, half], LAST_BOTH, preferred_element_type=jnp.float32)
                for half in (slice(0, KEY_WIDTH), slice(KEY_WIDTH, WIDTH))
            ],
            axis=1,
        ).astype(grad_ref.dtype)

    tile_rows = up_rows * WIDTH // RANKS
    return call(
        kernel,
        "own_rows",
        in_specs=[VMEM, ANY if up is None else VMEM],
        out_specs=(VMEM, VMEM),
        out_shape=(
            jax.ShapeDtypeStruct((ADAPTER_RANK, WIDTH), jnp.bfloat16),
            jax.ShapeDtypeStruct((rows, RANKS), jnp.bfloat16),
        ),
        scratch_shapes=[
            pltpu.VMEM((data_count, tile_rows, RANKS), jnp.bfloat16),
            pltpu.SemaphoreType.DMA,
        ],
    )(cotangent, came if up is None else up)


def keys_and_values(at, base_pieces, low_sum, b_own):
    rows = base_pieces[0].shape[0]
    count = len(base_pieces)

    def kernel(at_ref, low_ref, b_ref, *rest):
        base_refs, out_ref = rest[:count], rest[count]
        low = low_ref[at_ref[1]]
        for first, ranks in ((0, slice(0, ADAPTER_RANK)), (KEY_WIDTH, slice(ADAPTER_RANK, RANKS))):
            at = slice(first, first + KEY_WIDTH)
            y = jnp.dot(low[:, ranks], b_ref[:, at], preferred_element_type=jnp.float32)
            for base_ref in base_refs:
                y += base_ref[:, at].astype(jnp.float32)
            out_ref[:, at] = y.astype(out_ref.dtype)

    return call(
        kernel,
        "keys_and_values",
        in_specs=[SMEM, VMEM, VMEM] + [VMEM] * count,
        out_specs=VMEM,
        out_shape=jax.ShapeDtypeStruct((rows, WIDTH), jnp.bfloat16),
    )(at, low_sum, b_own, *base_pieces)


def body(
    tokens, key_value_weight, adapter_down, adapter_up, tenant_of_block, slot_of_tenant, cotangent
):
    data_count = lax.axis_size("dp")
    pipe_count = lax.axis_size("pipe")
    tensor_count = lax.axis_size("tensor")
    group_count = pipe_count * tensor_count
    at_data, at_pipe, at_tensor = (lax.axis_index(a) for a in ("dp", "pipe", "tensor"))
    my_group = at_pipe * tensor_count + at_tensor
    tok_dev, feature_count = tokens.shape
    blocks_dev = tok_dev // BLOCK
    rows = tok_dev // group_count
    down_rows = adapter_down.shape[1]
    up_rows = adapter_up.shape[1]
    slots = adapter_down.shape[0]
    blocks = tenant_of_block.shape[0]

    own_block = my_group * rows // BLOCK
    at = jnp.stack([at_data, at_pipe, at_tensor, own_block]).astype(jnp.int32)
    at = jnp.concatenate([at, tenant_of_block, slot_of_tenant])

    def slot_of(at_ref, data, block):
        return at_ref[4 + blocks + at_ref[4 + data * blocks_dev + block]]

    a_send = pick(at, slot_of, adapter_down, adapter_up, data_count, blocks_dev)
    a_recv = lax.all_to_all(a_send, "dp", 0, 0, tiled=True)
    up = None
    if not up_rides(adapter_up):
        up = lax.all_to_all(pick_up(at, slot_of, adapter_up, data_count), "dp", 0, 0, tiled=True)
        up = up.reshape(ADAPTER_RANK, WIDTH)

    cot_send, a_send = lax.optimization_barrier((cotangent, a_send))
    cot_chips = [cotangent] + [swap(cot_send, "pipe", k) for k in range(1, pipe_count)]

    base_tokens, cot_chips = lax.optimization_barrier((tokens, cot_chips))
    tokens_by_group = base_tokens.reshape(pipe_count, tensor_count, rows, feature_count)
    base_send = base_product(at, tokens_by_group, key_value_weight, 1, tensor_count - 1)
    base_came = [swap(base_send[s - 1], "tensor", s) for s in range(1, tensor_count)]
    base_keep = base_product(at, tokens_by_group, key_value_weight, 0, 1)[0]
    base_chip = [
        sum([base_keep[k].astype(jnp.float32)] + [b[k].astype(jnp.float32) for b in base_came])
        for k in range(pipe_count)
    ]
    base_chip[1:] = [piece.astype(jnp.bfloat16) for piece in base_chip[1:]]
    base_chip_came = [swap(base_chip[k], "pipe", k) for k in range(1, pipe_count)]

    cot_pieces = [cot_chips] + [
        [swap(piece, "tensor", s) for piece in cot_chips] for s in range(1, tensor_count)
    ]
    input_base = cotangent_product(at, cot_pieces, key_value_weight)

    x_tokens, base_chip = lax.optimization_barrier((tokens, base_chip))
    x_send = x_tokens.T.reshape(data_count, down_rows, tok_dev)

    a_recv, x_send, input_base = lax.optimization_barrier((a_recv, x_send, input_base))
    b_own, grad_rows = own_rows(a_recv, up, cotangent, blocks_dev * down_rows)
    grad_data = [grad_rows] + [shift(grad_rows, "dp", k) for k in range(1, data_count)]
    x_send, grad_data = lax.optimization_barrier((x_send, grad_data))
    x_recv = lax.all_to_all(x_send, "dp", 0, 0, tiled=True)

    grad_all = jnp.stack(grad_data)
    grad_chips = jnp.stack([grad_all] + [swap(grad_all, "pipe", k) for k in range(1, pipe_count)])
    grad_pieces = [grad_chips] + [swap(grad_chips, "tensor", s) for s in range(1, tensor_count)]
    input_grad = input_gradient(at, input_base, grad_pieces, a_recv)

    low_down, base_chip_came, grad_data = lax.optimization_barrier(
        (a_recv, base_chip_came, grad_data)
    )
    low_part = low_product(at, tokens, low_down, pipe_count, tensor_count)
    low_core = sum(
        [low_part[0].astype(jnp.float32)]
        + [swap(low_part[s], "tensor", s).astype(jnp.float32) for s in range(1, tensor_count)]
    ).astype(jnp.bfloat16)
    low_came = [swap(low_core, "pipe", k) for k in range(1, pipe_count)]
    low_sum = sum([piece.astype(jnp.float32) for piece in [low_core] + low_came])
    low_sum = low_sum.astype(jnp.bfloat16)
    low_pieces = [low_sum] + [swap(low_sum, "tensor", s) for s in range(1, tensor_count)]
    key_value = keys_and_values(at, base_chip[:1] + base_chip_came, low_sum, b_own)

    up_pieces = grad_up_pieces(at, low_pieces, cot_pieces, data_count, up_rows)
    up_came = [up_pieces[0]] + [shift(up_pieces[k], "dp", k) for k in range(1, data_count)]
    grad_a = grad_down(at, slot_of, slots, x_recv, grad_pieces)
    up_came, grad_a = lax.optimization_barrier((up_came, grad_a))
    grad_b = grad_up(at, slot_of, slots, up_came)
    return (key_value, input_grad, grad_a, grad_b)


def solution(mesh):
    atd = (
        P("dp", ("pipe", "tensor")),
        P(("pipe", "tensor"), None),
        P(None, ("pipe", "tensor", "dp"), None),
        P(None, "dp", None),
        P(),
        P(),
        P(("dp", "pipe", "tensor"), None),
    )
    return jax.shard_map(
        body,
        mesh=mesh,
        in_specs=atd,
        out_specs=(
            P(("dp", "pipe", "tensor"), None),
            P("dp", ("pipe", "tensor")),
            P(None, ("pipe", "tensor", "dp"), None),
            P(None, "dp", ("pipe", "tensor")),
        ),
        check_vma=False,
    )
```

```python
import jax
import jax.numpy as jnp
from jax import lax
from jax.experimental import pallas as pl
from jax.experimental.pallas import tpu as pltpu
from jax.sharding import PartitionSpec as P

KEY_WIDTH = 1024
ADAPTER_RANK = 64
BLOCK = 128
RANKS = 2 * ADAPTER_RANK
WIDTH = 2 * KEY_WIDTH
VMEM_LIMIT = 24 * 1024 * 1024
LAST_BOTH = (((1,), (1,)), ((), ()))
FIRST_BOTH = (((0,), (0,)), ((), ()))
SMEM = pl.BlockSpec(memory_space=pltpu.SMEM)
VMEM = pl.BlockSpec(memory_space=pltpu.VMEM)
HBM = pl.BlockSpec(memory_space=pltpu.HBM)
ANY = pl.BlockSpec(memory_space=pl.ANY)


def call(kernel, name, **more):
    return pl.pallas_call(
        kernel,
        compiler_params=pltpu.CompilerParams(vmem_limit_bytes=VMEM_LIMIT),
        cost_estimate=pl.CostEstimate(flops=1024, bytes_accessed=1024, transcendentals=0),
        name=name,
        **more,
    )


def wrap(index, count):
    return lax.rem(index + 2 * count, count)


def shift(piece, axis, k):
    count = lax.axis_size(axis)
    return lax.ppermute(piece, axis, [(i, (i + k) % count) for i in range(count)])


def paired(count):
    return count & (count - 1) == 0


def partner(index, k, count):
    return index ^ k if paired(count) else (index + k) % count


def came_from(index, k, count):
    return index ^ k if paired(count) else wrap(index - k, count)


def which_partner(other, index, count):
    return other ^ index if paired(count) else wrap(other - index, count)


def swap(piece, axis, k):
    count = lax.axis_size(axis)
    return lax.ppermute(piece, axis, [(i, partner(i, k, count)) for i in range(count)])


def gather_chips(piece, behind):
    count = lax.axis_size("pipe")
    in_halves = count == 4 and piece.shape[0] % 32 == 0
    came = [swap(piece, "pipe", k) for k in range(1, 3 if in_halves else count)]
    came, one, two = lax.optimization_barrier((came, behind, behind))
    if in_halves:
        half = piece.shape[0] // 2
        third = [swap(came[1][:half], "pipe", 1), swap(came[0][half:], "pipe", 2)]
        came = came + [jnp.concatenate(third)]
    return came, one, two


def up_rides(adapter_up):
    return adapter_up.shape[1] % 16 == 0


def pick(at, slot_of, adapter_down, adapter_up, data_count, blocks_dev):
    down_rows, ranks = adapter_down.shape[1:]
    up_rows, width = adapter_up.shape[1:]
    first_up = blocks_dev * down_rows
    rides = up_rides(adapter_up)
    total = first_up + (up_rows * width // ranks if rides else 0)

    def kernel(at_ref, down_ref, up_ref, out_ref):
        data = pl.program_id(0)
        for block in range(blocks_dev):
            here = slice(block * down_rows, (block + 1) * down_rows)
            out_ref[0, here] = down_ref[slot_of(at_ref, data, block)]
        if rides:
            slot = slot_of(at_ref, data, at_ref[3])
            for n in range(width // ranks):
                first = first_up + n * up_rows
                out_ref[0, first : first + up_rows] = up_ref[slot, :, n * ranks : (n + 1) * ranks]

    return call(
        kernel,
        "pick_rows",
        grid=(data_count,),
        out_shape=pltpu.HBM((data_count, total, ranks), adapter_down.dtype),
        in_specs=[SMEM, VMEM, VMEM],
        out_specs=pl.BlockSpec((1, total, ranks), lambda d: (d, 0, 0)),
    )(at, adapter_down, adapter_up)


def pick_up(at, slot_of, adapter_up, data_count):
    slots = jnp.stack([slot_of(at, data, at[3]) for data in range(data_count)])
    return jnp.take(adapter_up, slots, axis=0)


def base_product(at, tokens, weight, first, count):
    pipe_count, tensor_count, rows, depth = tokens.shape
    tile = 1024

    def kernel(at_ref, x_ref, w_ref, out_ref):
        x = x_ref[...].reshape(pipe_count * rows, depth)
        y = jnp.dot(x, w_ref[...], preferred_element_type=jnp.float32).astype(out_ref.dtype)
        for chip in range(pipe_count):
            out_ref[0, which_partner(chip, at_ref[1], pipe_count)] = y[chip * rows : (chip + 1) * rows]

    return call(
        kernel,
        "base_product",
        grid_spec=pltpu.PrefetchScalarGridSpec(
            num_scalar_prefetch=1,
            grid=(WIDTH // tile, count),
            in_specs=[
                pl.BlockSpec(
                    (pipe_count, 1, rows, depth),
                    lambda n, s, at: (0, partner(at[2], s + first, tensor_count), 0, 0),
                ),
                pl.BlockSpec((depth, tile), lambda n, s, at: (0, n)),
            ],
            out_specs=pl.BlockSpec((1, pipe_count, rows, tile), lambda n, s, at: (s, 0, 0, n)),
        ),
        out_shape=jax.ShapeDtypeStruct((count, pipe_count, rows, WIDTH), jnp.bfloat16),
    )(at, tokens, weight)


def low_product(at, tokens, down, pipe_count, tensor_count):
    tok_dev, depth = tokens.shape
    down_rows = depth // down.shape[0]
    rows = tok_dev // (pipe_count * tensor_count)

    def kernel(at_ref, x_ref, a_ref, out_ref):
        for block in range(tok_dev // BLOCK):
            a = a_ref[:, block * down_rows : (block + 1) * down_rows].reshape(depth, RANKS)
            x = x_ref[block * BLOCK : (block + 1) * BLOCK]
            y = jnp.dot(x, a, preferred_element_type=jnp.float32).astype(out_ref.dtype)
            for part in range(BLOCK // rows):
                chip, core = divmod(block * (BLOCK // rows) + part, tensor_count)
                core = which_partner(core, at_ref[2], tensor_count)
                out_ref[core, chip] = y[part * rows : (part + 1) * rows]

    return call(
        kernel,
        "low_product",
        in_specs=[SMEM, VMEM, VMEM],
        out_specs=VMEM,
        out_shape=jax.ShapeDtypeStruct((tensor_count, pipe_count, rows, RANKS), jnp.bfloat16),
    )(at, tokens, down)


def cotangent_product(at, cot_pieces, weight):
    tensor_count, pipe_count = len(cot_pieces), len(cot_pieces[0])
    rows = cot_pieces[0][0].shape[0]
    depth = weight.shape[0]
    tok_dev = tensor_count * pipe_count * rows
    tile = 256 if depth % 256 == 0 else depth
    order = [(s, k) for s in range(tensor_count) for k in range(pipe_count)]

    def kernel(at_ref, w_ref, *rest):
        cot_refs, (out_ref, cot, sems) = rest[: len(order)], rest[len(order) :]

        @pl.when(pl.program_id(0) == 0)
        def _():
            copies = []
            for i, (s, k) in enumerate(order):
                chip = came_from(at_ref[1], k, pipe_count)
                core = came_from(at_ref[2], s, tensor_count)
                first = pl.multiple_of((chip * tensor_count + core) * rows, rows)
                copies.append(
                    pltpu.make_async_copy(cot_refs[i], cot.at[pl.ds(first, rows)], sems.at[i])
                )
            for copy in copies:
                copy.start()
            for copy in copies:
                copy.wait()

        out_ref[...] = lax.dot_general(
            cot[...], w_ref[...], LAST_BOTH, preferred_element_type=jnp.float32
        )

    return call(
        kernel,
        "cotangent_product",
        grid=(depth // tile,),
        in_specs=[SMEM, pl.BlockSpec((tile, WIDTH), lambda n: (n, 0))] + [ANY] * len(order),
        out_specs=pl.BlockSpec((tok_dev, tile), lambda n: (0, n)),
        out_shape=jax.ShapeDtypeStruct((tok_dev, depth), jnp.float32),
        scratch_shapes=[
            pltpu.VMEM((tok_dev, WIDTH), jnp.bfloat16),
            pltpu.SemaphoreType.DMA((len(order),)),
        ],
    )(at, weight, *[cot_pieces[s][k] for s, k in order])


def input_gradient(at, base, grad_pieces, down):
    data_count, all_rows, _ = down.shape
    tensor_count = len(grad_pieces)
    pipe_count, _, rows, _ = grad_pieces[0].shape
    tok_dev, depth = base.shape
    down_rows = depth // data_count
    planes = next((n for n in range(1, data_count) if n * down_rows % 256 == 0), data_count)
    tile = planes * down_rows

    def kernel(at_ref, base_ref, a_ref, *rest):
        grad_refs, (out_ref, grad) = rest[:tensor_count], rest[tensor_count:]

        @pl.when(pl.program_id(0) == 0)
        def _():
            for s in range(tensor_count):
                core = came_from(at_ref[2], s, tensor_count)
                for k in range(pipe_count):
                    chip = came_from(at_ref[1], k, pipe_count)
                    first = pl.multiple_of((chip * tensor_count + core) * rows, rows)
                    grad[pl.ds(first, rows)] = grad_refs[s][k, 0]

        for block in range(tok_dev // BLOCK):
            here = slice(block * BLOCK, (block + 1) * BLOCK)
            a = a_ref[:, block * down_rows : (block + 1) * down_rows].reshape(tile, RANKS)
            low = lax.dot_general(grad[here], a, LAST_BOTH, preferred_element_type=jnp.float32)
            out_ref[here] = (base_ref[here] + low).astype(out_ref.dtype)

    grad_shape = (pipe_count, data_count, rows, RANKS)
    return call(
        kernel,
        "input_gradient",
        grid=(data_count // planes,),
        in_specs=[
            SMEM,
            pl.BlockSpec((tok_dev, tile), lambda n: (0, n)),
            pl.BlockSpec((planes, all_rows, RANKS), lambda n: (n, 0, 0)),
        ]
        + [pl.BlockSpec(grad_shape, lambda n: (0, 0, 0, 0))] * tensor_count,
        out_specs=pl.BlockSpec((tok_dev, tile), lambda n: (0, n)),
        out_shape=jax.ShapeDtypeStruct((tok_dev, depth), jnp.bfloat16),
        scratch_shapes=[pltpu.VMEM((tok_dev, RANKS), jnp.bfloat16)],
    )(at, base, down, *grad_pieces)


def grad_down(at, slot_of, slots, x_features, grad_pieces):
    data_count, down_rows, tok_dev = x_features.shape
    tensor_count = len(grad_pieces)
    pipe_count, _, rows, _ = grad_pieces[0].shape
    blocks_dev = tok_dev // BLOCK

    def kernel(at_ref, x_ref, *rest):
        grad_refs, (out_ref, grad) = rest[:tensor_count], rest[tensor_count:]
        for s in range(tensor_count):
            core = came_from(at_ref[2], s, tensor_count)
            for k in range(pipe_count):
                chip = came_from(at_ref[1], k, pipe_count)
                first = pl.multiple_of((chip * tensor_count + core) * rows, rows)
                for m in range(data_count):
                    data = wrap(at_ref[0] - m, data_count)
                    grad[data, pl.ds(first, rows)] = grad_refs[s][k, m]
        out_ref[...] = jnp.zeros(out_ref.shape, out_ref.dtype)
        for data in range(data_count):
            for block in range(blocks_dev):
                slot = slot_of(at_ref, data, block)
                here = slice(block * BLOCK, (block + 1) * BLOCK)
                out_ref[slot] += jnp.dot(
                    x_ref[data, :, here], grad[data, here], preferred_element_type=jnp.float32
                )

    return call(
        kernel,
        "grad_down",
        in_specs=[SMEM, VMEM] + [VMEM] * tensor_count,
        out_specs=VMEM,
        out_shape=jax.ShapeDtypeStruct((slots, down_rows, RANKS), jnp.float32),
        scratch_shapes=[pltpu.VMEM((data_count, tok_dev, RANKS), jnp.bfloat16)],
    )(at, x_features, *grad_pieces)


def grad_up_pieces(at, low_pieces, cot_pieces, data_count, up_rows):
    tensor_count, pipe_count = len(cot_pieces), len(cot_pieces[0])
    group_count = tensor_count * pipe_count
    rows = cot_pieces[0][0].shape[0]
    cols = WIDTH // group_count
    tok_dev = group_count * rows
    blocks_dev = tok_dev // BLOCK
    group_half = group_count // 2
    order = [(s, k) for s in range(tensor_count) for k in range(pipe_count)]
    pieces = [cot_pieces[s][k] for s, k in order]
    in_kernel = cols % 128 == 0
    if not in_kernel:
        first_col = (at[1] * tensor_count + at[2]) * cols
        pieces = [lax.dynamic_slice_in_dim(piece, first_col, cols, 1) for piece in pieces]

    def kernel(at_ref, *rest):
        low_refs, rest = rest[:tensor_count], rest[tensor_count:]
        cot_refs, (out_ref, low, cot, sems) = rest[: len(order)], rest[len(order) :]
        my_group = at_ref[1] * tensor_count + at_ref[2]
        copies = []
        for i, (s, k) in enumerate(order):
            core = came_from(at_ref[2], s, tensor_count)
            chip = came_from(at_ref[1], k, pipe_count)
            first = pl.multiple_of((chip * tensor_count + core) * rows, rows)
            piece = cot_refs[i]
            if in_kernel:
                piece = piece.at[:, pl.ds(pl.multiple_of(my_group * cols, cols), cols)]
            copies.append(pltpu.make_async_copy(piece, cot.at[pl.ds(first, rows)], sems.at[i]))
        for copy in copies:
            copy.start()
        for s in range(tensor_count):
            core = came_from(at_ref[2], s, tensor_count)
            for k in range(pipe_count):
                first = pl.multiple_of((k * tensor_count + core) * rows, rows)
                low[pl.ds(first, rows)] = low_refs[s][k]
        for copy in copies:
            copy.wait()
        for block in range(blocks_dev):
            at = slice(block * BLOCK, (block + 1) * BLOCK)
            both = lax.dot_general(low[at], cot[at], FIRST_BOTH, preferred_element_type=jnp.float32)
            half = jnp.where(my_group < group_half, both[:ADAPTER_RANK], both[ADAPTER_RANK:])
            half = half.astype(out_ref.dtype)
            for data in range(data_count):
                k = wrap(data - at_ref[0], data_count)
                out_ref[k, block] = half[data * up_rows : (data + 1) * up_rows]

    return call(
        kernel,
        "grad_up_pieces",
        in_specs=[SMEM] + [VMEM] * tensor_count + [ANY] * len(order),
        out_specs=VMEM,
        out_shape=jax.ShapeDtypeStruct((data_count, blocks_dev, up_rows, cols), jnp.bfloat16),
        scratch_shapes=[
            pltpu.VMEM((tok_dev, RANKS), jnp.bfloat16),
            pltpu.VMEM((tok_dev, cols), jnp.bfloat16),
            pltpu.SemaphoreType.DMA((len(order),)),
        ],
    )(at, *low_pieces, *pieces)


def grad_up(at, slot_of, slots, pieces):
    data_count = len(pieces)
    blocks_dev, up_rows, cols = pieces[0].shape

    def kernel(at_ref, *rest):
        piece_refs, out_ref = rest[:data_count], rest[data_count]
        out_ref[...] = jnp.zeros(out_ref.shape, out_ref.dtype)
        for k in range(data_count):
            data = wrap(at_ref[0] - k, data_count)
            for block in range(blocks_dev):
                slot = slot_of(at_ref, data, block)
                out_ref[slot] += piece_refs[k][block].astype(out_ref.dtype)

    return call(
        kernel,
        "grad_up",
        in_specs=[SMEM] + [VMEM] * data_count,
        out_specs=VMEM,
        out_shape=jax.ShapeDtypeStruct((slots, up_rows, cols), jnp.float32),
    )(at, *pieces)


def own_rows(came, up, cotangent, first_up):
    rows = cotangent.shape[0]
    data_count = came.shape[0]
    up_rows = ADAPTER_RANK // data_count

    def kernel(cot_ref, came_ref, b_ref, grad_ref, tiles, sem):
        if up is None:
            copy = pltpu.make_async_copy(came_ref.at[:, pl.ds(first_up, tiles.shape[1])], tiles, sem)
            copy.start()
            copy.wait()
            for data in range(data_count):
                for n in range(WIDTH // RANKS):
                    b_ref[
                        data * up_rows : (data + 1) * up_rows, n * RANKS : (n + 1) * RANKS
                    ] = tiles[data, n * up_rows : (n + 1) * up_rows]
        else:
            b_ref[...] = came_ref[...]
        cot, b = cot_ref[...], b_ref[...]
        grad_ref[...] = jnp.concatenate(
            [
                lax.dot_general(cot[:, half], b[:, half], LAST_BOTH, preferred_element_type=jnp.float32)
                for half in (slice(0, KEY_WIDTH), slice(KEY_WIDTH, WIDTH))
            ],
            axis=1,
        ).astype(grad_ref.dtype)

    tile_rows = up_rows * WIDTH // RANKS
    return call(
        kernel,
        "own_rows",
        in_specs=[VMEM, ANY if up is None else VMEM],
        out_specs=(VMEM, VMEM),
        out_shape=(
            jax.ShapeDtypeStruct((ADAPTER_RANK, WIDTH), jnp.bfloat16),
            jax.ShapeDtypeStruct((rows, RANKS), jnp.bfloat16),
        ),
        scratch_shapes=[
            pltpu.VMEM((data_count, tile_rows, RANKS), jnp.bfloat16),
            pltpu.SemaphoreType.DMA,
        ],
    )(cotangent, came if up is None else up)


def keys_and_values(at, base_pieces, low_sum, b_own):
    rows = base_pieces[0].shape[0]
    count = len(base_pieces)

    def kernel(at_ref, low_ref, b_ref, *rest):
        base_refs, out_ref = rest[:count], rest[count]
        low = low_ref[at_ref[1]]
        for first, ranks in ((0, slice(0, ADAPTER_RANK)), (KEY_WIDTH, slice(ADAPTER_RANK, RANKS))):
            at = slice(first, first + KEY_WIDTH)
            y = jnp.dot(low[:, ranks], b_ref[:, at], preferred_element_type=jnp.float32)
            for base_ref in base_refs:
                y += base_ref[:, at].astype(jnp.float32)
            out_ref[:, at] = y.astype(out_ref.dtype)

    return call(
        kernel,
        "keys_and_values",
        in_specs=[SMEM, VMEM, VMEM] + [VMEM] * count,
        out_specs=VMEM,
        out_shape=jax.ShapeDtypeStruct((rows, WIDTH), jnp.bfloat16),
    )(at, low_sum, b_own, *base_pieces)


def body(
    tokens, key_value_weight, adapter_down, adapter_up, tenant_of_block, slot_of_tenant, cotangent
):
    data_count = lax.axis_size("dp")
    pipe_count = lax.axis_size("pipe")
    tensor_count = lax.axis_size("tensor")
    group_count = pipe_count * tensor_count
    at_data, at_pipe, at_tensor = (lax.axis_index(a) for a in ("dp", "pipe", "tensor"))
    my_group = at_pipe * tensor_count + at_tensor
    tok_dev, feature_count = tokens.shape
    blocks_dev = tok_dev // BLOCK
    rows = tok_dev // group_count
    down_rows = adapter_down.shape[1]
    up_rows = adapter_up.shape[1]
    slots = adapter_down.shape[0]
    blocks = tenant_of_block.shape[0]

    own_block = my_group * rows // BLOCK
    at = jnp.stack([at_data, at_pipe, at_tensor, own_block]).astype(jnp.int32)
    at = jnp.concatenate([at, tenant_of_block, slot_of_tenant])

    def slot_of(at_ref, data, block):
        return at_ref[4 + blocks + at_ref[4 + data * blocks_dev + block]]

    a_send = pick(at, slot_of, adapter_down, adapter_up, data_count, blocks_dev)
    a_recv = lax.all_to_all(a_send, "dp", 0, 0, tiled=True)
    up = None
    if not up_rides(adapter_up):
        up = lax.all_to_all(pick_up(at, slot_of, adapter_up, data_count), "dp", 0, 0, tiled=True)
        up = up.reshape(ADAPTER_RANK, WIDTH)

    cot_send, a_send = lax.optimization_barrier((cotangent, a_send))
    cot_chips, base_tokens, x_tokens = gather_chips(cot_send, tokens)
    cot_chips = [cotangent] + cot_chips

    tokens_by_group = base_tokens.reshape(pipe_count, tensor_count, rows, feature_count)
    base_send = base_product(at, tokens_by_group, key_value_weight, 1, tensor_count - 1)
    base_came = [swap(base_send[s - 1], "tensor", s) for s in range(1, tensor_count)]
    base_keep = base_product(at, tokens_by_group, key_value_weight, 0, 1)[0]
    base_chip = [
        sum([base_keep[k].astype(jnp.float32)] + [b[k].astype(jnp.float32) for b in base_came])
        for k in range(pipe_count)
    ]
    base_chip[1:] = [piece.astype(jnp.bfloat16) for piece in base_chip[1:]]
    base_chip_came = [swap(base_chip[k], "pipe", k) for k in range(1, pipe_count)]

    cot_pieces = [cot_chips] + [
        [swap(piece, "tensor", s) for piece in cot_chips] for s in range(1, tensor_count)
    ]
    input_base = cotangent_product(at, cot_pieces, key_value_weight)

    x_send = x_tokens.T.reshape(data_count, down_rows, tok_dev)

    a_recv, x_send, input_base, base_chip_came[:2] = lax.optimization_barrier(
        (a_recv, x_send, input_base, base_chip_came[:2])
    )
    b_own, grad_rows = own_rows(a_recv, up, cotangent, blocks_dev * down_rows)
    grad_data = [grad_rows] + [shift(grad_rows, "dp", k) for k in range(1, data_count)]
    x_send, grad_data = lax.optimization_barrier((x_send, grad_data))
    x_recv = lax.all_to_all(x_send, "dp", 0, 0, tiled=True)

    grad_all = jnp.stack(grad_data)
    grad_chips = jnp.stack([grad_all] + [swap(grad_all, "pipe", k) for k in range(1, pipe_count)])
    grad_pieces = [grad_chips] + [swap(grad_chips, "tensor", s) for s in range(1, tensor_count)]
    input_grad = input_gradient(at, input_base, grad_pieces, a_recv)

    low_down, base_chip_came, grad_data = lax.optimization_barrier(
        (a_recv, base_chip_came, grad_data)
    )
    low_part = low_product(at, tokens, low_down, pipe_count, tensor_count)
    low_core = sum(
        [low_part[0].astype(jnp.float32)]
        + [swap(low_part[s], "tensor", s).astype(jnp.float32) for s in range(1, tensor_count)]
    ).astype(jnp.bfloat16)
    low_came = [swap(low_core, "pipe", k) for k in range(1, pipe_count)]
    low_sum = sum([piece.astype(jnp.float32) for piece in [low_core] + low_came])
    low_sum = low_sum.astype(jnp.bfloat16)
    low_pieces = [low_sum] + [swap(low_sum, "tensor", s) for s in range(1, tensor_count)]
    key_value = keys_and_values(at, base_chip[:1] + base_chip_came, low_sum, b_own)

    up_pieces = grad_up_pieces(at, low_pieces, cot_pieces, data_count, up_rows)
    up_came = [up_pieces[0]] + [shift(up_pieces[k], "dp", k) for k in range(1, data_count)]
    grad_a = grad_down(at, slot_of, slots, x_recv, grad_pieces)
    up_came, grad_a = lax.optimization_barrier((up_came, grad_a))
    grad_b = grad_up(at, slot_of, slots, up_came)
    return (key_value, input_grad, grad_a, grad_b)


def solution(mesh):
    atd = (
        P("dp", ("pipe", "tensor")),
        P(("pipe", "tensor"), None),
        P(None, ("pipe", "tensor", "dp"), None),
        P(None, "dp", None),
        P(),
        P(),
        P(("dp", "pipe", "tensor"), None),
    )
    return jax.shard_map(
        body,
        mesh=mesh,
        in_specs=atd,
        out_specs=(
            P(("dp", "pipe", "tensor"), None),
            P("dp", ("pipe", "tensor")),
            P(None, ("pipe", "tensor", "dp"), None),
            P(None, "dp", ("pipe", "tensor")),
        ),
        check_vma=False,
    )
```

```python
import jax
import jax.numpy as jnp
from jax import lax
from jax.experimental import pallas as pl
from jax.experimental.pallas import tpu as pltpu
from jax.sharding import PartitionSpec as P

KEY_WIDTH = 1024
ADAPTER_RANK = 64
BLOCK = 128
RANKS = 2 * ADAPTER_RANK
WIDTH = 2 * KEY_WIDTH
VMEM_LIMIT = 24 * 1024 * 1024
VMEM_MOST = 60 * 1024 * 1024
LAST_BOTH = (((1,), (1,)), ((), ()))
FIRST_BOTH = (((0,), (0,)), ((), ()))
SMEM = pl.BlockSpec(memory_space=pltpu.SMEM)
VMEM = pl.BlockSpec(memory_space=pltpu.VMEM)
HBM = pl.BlockSpec(memory_space=pltpu.HBM)
ANY = pl.BlockSpec(memory_space=pl.ANY)


def call(kernel, name, vmem=VMEM_LIMIT, **more):
    return pl.pallas_call(
        kernel,
        compiler_params=pltpu.CompilerParams(vmem_limit_bytes=vmem),
        cost_estimate=pl.CostEstimate(flops=1024, bytes_accessed=1024, transcendentals=0),
        name=name,
        **more,
    )


def wrap(index, count):
    return lax.rem(index + 2 * count, count)


def shift(piece, axis, k):
    count = lax.axis_size(axis)
    return lax.ppermute(piece, axis, [(i, (i + k) % count) for i in range(count)])


def paired(count):
    return count & (count - 1) == 0


def partner(index, k, count):
    return index ^ k if paired(count) else (index + k) % count


def came_from(index, k, count):
    return index ^ k if paired(count) else wrap(index - k, count)


def which_partner(other, index, count):
    return other ^ index if paired(count) else wrap(other - index, count)


def swap(piece, axis, k):
    count = lax.axis_size(axis)
    return lax.ppermute(piece, axis, [(i, partner(i, k, count)) for i in range(count)])


def gather_chips(piece, behind):
    count = lax.axis_size("pipe")
    in_halves = count == 4 and piece.shape[0] % 32 == 0
    came = [swap(piece, "pipe", k) for k in range(1, 3 if in_halves else count)]
    came, one, two = lax.optimization_barrier((came, behind, behind))
    if in_halves:
        half = piece.shape[0] // 2
        third = [swap(came[1][:half], "pipe", 1), swap(came[0][half:], "pipe", 2)]
        came = came + [jnp.concatenate(third)]
    return came, one, two


def up_rides(adapter_up):
    return adapter_up.shape[1] % 16 == 0


def pick(at, slot_of, adapter_down, adapter_up, data_count, blocks_dev):
    down_rows, ranks = adapter_down.shape[1:]
    up_rows, width = adapter_up.shape[1:]
    first_up = blocks_dev * down_rows
    rides = up_rides(adapter_up)
    total = first_up + (up_rows * width // ranks if rides else 0)

    def kernel(at_ref, down_ref, up_ref, out_ref, rows, tiles, down_sem, up_sem, out_sem):
        downs, ups, outs = [], [], []
        for data in range(data_count):
            downs.append([])
            for block in range(blocks_dev):
                here = rows.at[data, pl.ds(block * down_rows, down_rows)]
                slot = slot_of(at_ref, data, block)
                downs[data].append(
                    pltpu.make_async_copy(down_ref.at[slot], here, down_sem.at[data, block])
                )
            if rides:
                slot = slot_of(at_ref, data, at_ref[3])
                ups.append(pltpu.make_async_copy(up_ref.at[slot], tiles.at[data], up_sem.at[data]))
            outs.append(pltpu.make_async_copy(rows.at[data], out_ref.at[data], out_sem.at[data]))
            for copy in downs[data] + ups[data:]:
                copy.start()
        for data in range(data_count):
            for copy in downs[data] + ups[data : data + 1]:
                copy.wait()
            for n in range(width // ranks if rides else 0):
                first = first_up + n * up_rows
                rows[data, first : first + up_rows] = tiles[data, :, n * ranks : (n + 1) * ranks]
            outs[data].start()
        for copy in outs:
            copy.wait()

    return call(
        kernel,
        "pick_rows",
        VMEM_MOST,
        out_shape=pltpu.HBM((data_count, total, ranks), adapter_down.dtype),
        in_specs=[SMEM, HBM, HBM],
        out_specs=HBM,
        scratch_shapes=[
            pltpu.VMEM((data_count, total, ranks), adapter_down.dtype),
            pltpu.VMEM((data_count, up_rows, width), adapter_up.dtype),
            pltpu.SemaphoreType.DMA((data_count, blocks_dev)),
            pltpu.SemaphoreType.DMA((data_count,)),
            pltpu.SemaphoreType.DMA((data_count,)),
        ],
    )(at, adapter_down, adapter_up)


def pick_up(at, slot_of, adapter_up, data_count):
    slots = jnp.stack([slot_of(at, data, at[3]) for data in range(data_count)])
    return jnp.take(adapter_up, slots, axis=0)


def base_product(at, tokens, weight, first, count):
    pipe_count, tensor_count, rows, depth = tokens.shape
    tile = 1024

    def kernel(at_ref, x_ref, w_ref, out_ref):
        x = x_ref[...].reshape(pipe_count * rows, depth)
        y = jnp.dot(x, w_ref[...], preferred_element_type=jnp.float32).astype(out_ref.dtype)
        for chip in range(pipe_count):
            out_ref[0, which_partner(chip, at_ref[1], pipe_count)] = y[chip * rows : (chip + 1) * rows]

    return call(
        kernel,
        "base_product",
        grid_spec=pltpu.PrefetchScalarGridSpec(
            num_scalar_prefetch=1,
            grid=(WIDTH // tile, count),
            in_specs=[
                pl.BlockSpec(
                    (pipe_count, 1, rows, depth),
                    lambda n, s, at: (0, partner(at[2], s + first, tensor_count), 0, 0),
                ),
                pl.BlockSpec((depth, tile), lambda n, s, at: (0, n)),
            ],
            out_specs=pl.BlockSpec((1, pipe_count, rows, tile), lambda n, s, at: (s, 0, 0, n)),
        ),
        out_shape=jax.ShapeDtypeStruct((count, pipe_count, rows, WIDTH), jnp.bfloat16),
    )(at, tokens, weight)


def low_product(at, tokens, down, pipe_count, tensor_count):
    tok_dev, depth = tokens.shape
    down_rows = depth // down.shape[0]
    rows = tok_dev // (pipe_count * tensor_count)

    def kernel(at_ref, x_ref, a_ref, out_ref):
        for block in range(tok_dev // BLOCK):
            a = a_ref[:, block * down_rows : (block + 1) * down_rows].reshape(depth, RANKS)
            x = x_ref[block * BLOCK : (block + 1) * BLOCK]
            y = jnp.dot(x, a, preferred_element_type=jnp.float32).astype(out_ref.dtype)
            for part in range(BLOCK // rows):
                chip, core = divmod(block * (BLOCK // rows) + part, tensor_count)
                core = which_partner(core, at_ref[2], tensor_count)
                out_ref[core, chip] = y[part * rows : (part + 1) * rows]

    return call(
        kernel,
        "low_product",
        in_specs=[SMEM, VMEM, VMEM],
        out_specs=VMEM,
        out_shape=jax.ShapeDtypeStruct((tensor_count, pipe_count, rows, RANKS), jnp.bfloat16),
    )(at, tokens, down)


def cotangent_product(at, cot_pieces, weight):
    tensor_count, pipe_count = len(cot_pieces), len(cot_pieces[0])
    rows = cot_pieces[0][0].shape[0]
    depth = weight.shape[0]
    tok_dev = tensor_count * pipe_count * rows
    tile = 256 if depth % 256 == 0 else depth
    order = [(s, k) for s in range(tensor_count) for k in range(pipe_count)]

    def kernel(at_ref, w_ref, *rest):
        cot_refs, (out_ref, cot, sems) = rest[: len(order)], rest[len(order) :]

        @pl.when(pl.program_id(0) == 0)
        def _():
            copies = []
            for i, (s, k) in enumerate(order):
                chip = came_from(at_ref[1], k, pipe_count)
                core = came_from(at_ref[2], s, tensor_count)
                first = pl.multiple_of((chip * tensor_count + core) * rows, rows)
                copies.append(
                    pltpu.make_async_copy(cot_refs[i], cot.at[pl.ds(first, rows)], sems.at[i])
                )
            for copy in copies:
                copy.start()
            for copy in copies:
                copy.wait()

        out_ref[...] = lax.dot_general(
            cot[...], w_ref[...], LAST_BOTH, preferred_element_type=jnp.float32
        )

    return call(
        kernel,
        "cotangent_product",
        grid=(depth // tile,),
        in_specs=[SMEM, pl.BlockSpec((tile, WIDTH), lambda n: (n, 0))] + [ANY] * len(order),
        out_specs=pl.BlockSpec((tok_dev, tile), lambda n: (0, n)),
        out_shape=jax.ShapeDtypeStruct((tok_dev, depth), jnp.float32),
        scratch_shapes=[
            pltpu.VMEM((tok_dev, WIDTH), jnp.bfloat16),
            pltpu.SemaphoreType.DMA((len(order),)),
        ],
    )(at, weight, *[cot_pieces[s][k] for s, k in order])


def input_gradient(at, base, grad_pieces, down):
    data_count, all_rows, _ = down.shape
    tensor_count = len(grad_pieces)
    pipe_count, _, rows, _ = grad_pieces[0].shape
    tok_dev, depth = base.shape
    down_rows = depth // data_count
    planes = next((n for n in range(1, data_count) if n * down_rows % 256 == 0), data_count)
    tile = planes * down_rows

    def kernel(at_ref, base_ref, a_ref, *rest):
        grad_refs, (out_ref, grad) = rest[:tensor_count], rest[tensor_count:]

        @pl.when(pl.program_id(0) == 0)
        def _():
            for s in range(tensor_count):
                core = came_from(at_ref[2], s, tensor_count)
                for k in range(pipe_count):
                    chip = came_from(at_ref[1], k, pipe_count)
                    first = pl.multiple_of((chip * tensor_count + core) * rows, rows)
                    grad[pl.ds(first, rows)] = grad_refs[s][k, 0]

        for block in range(tok_dev // BLOCK):
            here = slice(block * BLOCK, (block + 1) * BLOCK)
            a = a_ref[:, block * down_rows : (block + 1) * down_rows].reshape(tile, RANKS)
            low = lax.dot_general(grad[here], a, LAST_BOTH, preferred_element_type=jnp.float32)
            out_ref[here] = (base_ref[here] + low).astype(out_ref.dtype)

    grad_shape = (pipe_count, data_count, rows, RANKS)
    return call(
        kernel,
        "input_gradient",
        grid=(data_count // planes,),
        in_specs=[
            SMEM,
            pl.BlockSpec((tok_dev, tile), lambda n: (0, n)),
            pl.BlockSpec((planes, all_rows, RANKS), lambda n: (n, 0, 0)),
        ]
        + [pl.BlockSpec(grad_shape, lambda n: (0, 0, 0, 0))] * tensor_count,
        out_specs=pl.BlockSpec((tok_dev, tile), lambda n: (0, n)),
        out_shape=jax.ShapeDtypeStruct((tok_dev, depth), jnp.bfloat16),
        scratch_shapes=[pltpu.VMEM((tok_dev, RANKS), jnp.bfloat16)],
    )(at, base, down, *grad_pieces)


def grad_down(at, slot_of, slots, x_features, grad_pieces):
    data_count, down_rows, tok_dev = x_features.shape
    tensor_count = len(grad_pieces)
    pipe_count, _, rows, _ = grad_pieces[0].shape
    blocks_dev = tok_dev // BLOCK

    def kernel(at_ref, x_ref, *rest):
        grad_refs, (out_ref, grad, x, sems) = rest[:tensor_count], rest[tensor_count:]
        copies = [
            pltpu.make_async_copy(x_ref.at[data], x.at[data], sems.at[data])
            for data in range(data_count)
        ]
        for copy in copies:
            copy.start()
        for s in range(tensor_count):
            core = came_from(at_ref[2], s, tensor_count)
            for k in range(pipe_count):
                chip = came_from(at_ref[1], k, pipe_count)
                first = pl.multiple_of((chip * tensor_count + core) * rows, rows)
                for m in range(data_count):
                    data = wrap(at_ref[0] - m, data_count)
                    grad[data, pl.ds(first, rows)] = grad_refs[s][k, m]
        out_ref[...] = jnp.zeros(out_ref.shape, out_ref.dtype)
        for data in range(data_count):
            copies[data].wait()
            for block in range(blocks_dev):
                slot = slot_of(at_ref, data, block)
                here = slice(block * BLOCK, (block + 1) * BLOCK)
                out_ref[slot] += jnp.dot(
                    x[data, :, here], grad[data, here], preferred_element_type=jnp.float32
                )

    return call(
        kernel,
        "grad_down",
        VMEM_MOST,
        in_specs=[SMEM, HBM] + [VMEM] * tensor_count,
        out_specs=VMEM,
        out_shape=jax.ShapeDtypeStruct((slots, down_rows, RANKS), jnp.float32),
        scratch_shapes=[
            pltpu.VMEM((data_count, tok_dev, RANKS), jnp.bfloat16),
            pltpu.VMEM(x_features.shape, jnp.bfloat16),
            pltpu.SemaphoreType.DMA((data_count,)),
        ],
    )(at, x_features, *grad_pieces)


def grad_up_pieces(at, low_pieces, cot_pieces, data_count, up_rows):
    tensor_count, pipe_count = len(cot_pieces), len(cot_pieces[0])
    group_count = tensor_count * pipe_count
    rows = cot_pieces[0][0].shape[0]
    cols = WIDTH // group_count
    tok_dev = group_count * rows
    blocks_dev = tok_dev // BLOCK
    group_half = group_count // 2
    order = [(s, k) for s in range(tensor_count) for k in range(pipe_count)]
    pieces = [cot_pieces[s][k] for s, k in order]
    in_kernel = cols % 128 == 0
    if not in_kernel:
        first_col = (at[1] * tensor_count + at[2]) * cols
        pieces = [lax.dynamic_slice_in_dim(piece, first_col, cols, 1) for piece in pieces]

    def kernel(at_ref, *rest):
        low_refs, rest = rest[:tensor_count], rest[tensor_count:]
        cot_refs, (out_ref, low, cot, sems) = rest[: len(order)], rest[len(order) :]
        my_group = at_ref[1] * tensor_count + at_ref[2]
        copies = []
        for i, (s, k) in enumerate(order):
            core = came_from(at_ref[2], s, tensor_count)
            chip = came_from(at_ref[1], k, pipe_count)
            first = pl.multiple_of((chip * tensor_count + core) * rows, rows)
            piece = cot_refs[i]
            if in_kernel:
                piece = piece.at[:, pl.ds(pl.multiple_of(my_group * cols, cols), cols)]
            copies.append(pltpu.make_async_copy(piece, cot.at[pl.ds(first, rows)], sems.at[i]))
        for copy in copies:
            copy.start()
        for s in range(tensor_count):
            core = came_from(at_ref[2], s, tensor_count)
            for k in range(pipe_count):
                first = pl.multiple_of((k * tensor_count + core) * rows, rows)
                low[pl.ds(first, rows)] = low_refs[s][k]
        for copy in copies:
            copy.wait()
        for block in range(blocks_dev):
            at = slice(block * BLOCK, (block + 1) * BLOCK)
            both = lax.dot_general(low[at], cot[at], FIRST_BOTH, preferred_element_type=jnp.float32)
            half = jnp.where(my_group < group_half, both[:ADAPTER_RANK], both[ADAPTER_RANK:])
            half = half.astype(out_ref.dtype)
            for data in range(data_count):
                k = wrap(data - at_ref[0], data_count)
                out_ref[k, block] = half[data * up_rows : (data + 1) * up_rows]

    return call(
        kernel,
        "grad_up_pieces",
        in_specs=[SMEM] + [VMEM] * tensor_count + [ANY] * len(order),
        out_specs=VMEM,
        out_shape=jax.ShapeDtypeStruct((data_count, blocks_dev, up_rows, cols), jnp.bfloat16),
        scratch_shapes=[
            pltpu.VMEM((tok_dev, RANKS), jnp.bfloat16),
            pltpu.VMEM((tok_dev, cols), jnp.bfloat16),
            pltpu.SemaphoreType.DMA((len(order),)),
        ],
    )(at, *low_pieces, *pieces)


def grad_up(at, slot_of, slots, pieces):
    data_count = len(pieces)
    blocks_dev, up_rows, cols = pieces[0].shape

    def kernel(at_ref, *rest):
        piece_refs, out_ref = rest[:data_count], rest[data_count]
        out_ref[...] = jnp.zeros(out_ref.shape, out_ref.dtype)
        for k in range(data_count):
            data = wrap(at_ref[0] - k, data_count)
            for block in range(blocks_dev):
                slot = slot_of(at_ref, data, block)
                out_ref[slot] += piece_refs[k][block].astype(out_ref.dtype)

    return call(
        kernel,
        "grad_up",
        in_specs=[SMEM] + [VMEM] * data_count,
        out_specs=VMEM,
        out_shape=jax.ShapeDtypeStruct((slots, up_rows, cols), jnp.float32),
    )(at, *pieces)


def own_rows(came, up, cotangent, first_up):
    rows = cotangent.shape[0]
    data_count = came.shape[0]
    up_rows = ADAPTER_RANK // data_count

    def kernel(cot_ref, came_ref, b_ref, grad_ref, tiles, sem):
        if up is None:
            copy = pltpu.make_async_copy(came_ref.at[:, pl.ds(first_up, tiles.shape[1])], tiles, sem)
            copy.start()
            copy.wait()
            for data in range(data_count):
                for n in range(WIDTH // RANKS):
                    b_ref[
                        data * up_rows : (data + 1) * up_rows, n * RANKS : (n + 1) * RANKS
                    ] = tiles[data, n * up_rows : (n + 1) * up_rows]
        else:
            b_ref[...] = came_ref[...]
        cot, b = cot_ref[...], b_ref[...]
        grad_ref[...] = jnp.concatenate(
            [
                lax.dot_general(cot[:, half], b[:, half], LAST_BOTH, preferred_element_type=jnp.float32)
                for half in (slice(0, KEY_WIDTH), slice(KEY_WIDTH, WIDTH))
            ],
            axis=1,
        ).astype(grad_ref.dtype)

    tile_rows = up_rows * WIDTH // RANKS
    return call(
        kernel,
        "own_rows",
        in_specs=[VMEM, ANY if up is None else VMEM],
        out_specs=(VMEM, VMEM),
        out_shape=(
            jax.ShapeDtypeStruct((ADAPTER_RANK, WIDTH), jnp.bfloat16),
            jax.ShapeDtypeStruct((rows, RANKS), jnp.bfloat16),
        ),
        scratch_shapes=[
            pltpu.VMEM((data_count, tile_rows, RANKS), jnp.bfloat16),
            pltpu.SemaphoreType.DMA,
        ],
    )(cotangent, came if up is None else up)


def keys_and_values(at, base_pieces, low_sum, b_own):
    rows = base_pieces[0].shape[0]
    count = len(base_pieces)

    def kernel(at_ref, low_ref, b_ref, *rest):
        base_refs, out_ref = rest[:count], rest[count]
        low = low_ref[at_ref[1]]
        for first, ranks in ((0, slice(0, ADAPTER_RANK)), (KEY_WIDTH, slice(ADAPTER_RANK, RANKS))):
            at = slice(first, first + KEY_WIDTH)
            y = jnp.dot(low[:, ranks], b_ref[:, at], preferred_element_type=jnp.float32)
            for base_ref in base_refs:
                y += base_ref[:, at].astype(jnp.float32)
            out_ref[:, at] = y.astype(out_ref.dtype)

    return call(
        kernel,
        "keys_and_values",
        in_specs=[SMEM, VMEM, VMEM] + [VMEM] * count,
        out_specs=VMEM,
        out_shape=jax.ShapeDtypeStruct((rows, WIDTH), jnp.bfloat16),
    )(at, low_sum, b_own, *base_pieces)


def body(
    tokens, key_value_weight, adapter_down, adapter_up, tenant_of_block, slot_of_tenant, cotangent
):
    data_count = lax.axis_size("dp")
    pipe_count = lax.axis_size("pipe")
    tensor_count = lax.axis_size("tensor")
    group_count = pipe_count * tensor_count
    at_data, at_pipe, at_tensor = (lax.axis_index(a) for a in ("dp", "pipe", "tensor"))
    my_group = at_pipe * tensor_count + at_tensor
    tok_dev, feature_count = tokens.shape
    blocks_dev = tok_dev // BLOCK
    rows = tok_dev // group_count
    down_rows = adapter_down.shape[1]
    up_rows = adapter_up.shape[1]
    slots = adapter_down.shape[0]
    blocks = tenant_of_block.shape[0]

    own_block = my_group * rows // BLOCK
    at = jnp.stack([at_data, at_pipe, at_tensor, own_block]).astype(jnp.int32)
    at = jnp.concatenate([at, tenant_of_block, slot_of_tenant])

    def slot_of(at_ref, data, block):
        return at_ref[4 + blocks + at_ref[4 + data * blocks_dev + block]]

    a_send = pick(at, slot_of, adapter_down, adapter_up, data_count, blocks_dev)
    a_recv = lax.all_to_all(a_send, "dp", 0, 0, tiled=True)
    up = None
    if not up_rides(adapter_up):
        up = lax.all_to_all(pick_up(at, slot_of, adapter_up, data_count), "dp", 0, 0, tiled=True)
        up = up.reshape(ADAPTER_RANK, WIDTH)

    behind, a_send = lax.optimization_barrier((tokens, a_send))
    cot_chips, base_tokens, x_tokens = gather_chips(cotangent, behind)
    cot_chips = [cotangent] + cot_chips

    tokens_by_group = base_tokens.reshape(pipe_count, tensor_count, rows, feature_count)
    base_send = base_product(at, tokens_by_group, key_value_weight, 1, tensor_count - 1)
    base_came = [swap(base_send[s - 1], "tensor", s) for s in range(1, tensor_count)]
    base_keep = base_product(at, tokens_by_group, key_value_weight, 0, 1)[0]
    base_chip = [
        sum([base_keep[k].astype(jnp.float32)] + [b[k].astype(jnp.float32) for b in base_came])
        for k in range(pipe_count)
    ]
    base_chip[1:] = [piece.astype(jnp.bfloat16) for piece in base_chip[1:]]
    base_chip_came = [swap(base_chip[k], "pipe", k) for k in range(1, pipe_count)]

    cot_pieces = [cot_chips] + [
        [swap(piece, "tensor", s) for piece in cot_chips] for s in range(1, tensor_count)
    ]
    input_base = cotangent_product(at, cot_pieces, key_value_weight)

    x_send = x_tokens.T.reshape(data_count, down_rows, tok_dev)

    a_recv, x_send, input_base, base_chip_came[:2] = lax.optimization_barrier(
        (a_recv, x_send, input_base, base_chip_came[:2])
    )
    b_own, grad_rows = own_rows(a_recv, up, cotangent, blocks_dev * down_rows)
    grad_data = [grad_rows] + [shift(grad_rows, "dp", k) for k in range(1, data_count)]
    x_send, grad_data = lax.optimization_barrier((x_send, grad_data))
    x_recv = lax.all_to_all(x_send, "dp", 0, 0, tiled=True)

    grad_all = jnp.stack(grad_data)
    grad_chips = jnp.stack([grad_all] + [swap(grad_all, "pipe", k) for k in range(1, pipe_count)])
    grad_pieces = [grad_chips] + [swap(grad_chips, "tensor", s) for s in range(1, tensor_count)]
    input_grad = input_gradient(at, input_base, grad_pieces, a_recv)

    low_down, base_chip_came, grad_data = lax.optimization_barrier(
        (a_recv, base_chip_came, grad_data)
    )
    low_part = low_product(at, tokens, low_down, pipe_count, tensor_count)
    low_core = sum(
        [low_part[0].astype(jnp.float32)]
        + [swap(low_part[s], "tensor", s).astype(jnp.float32) for s in range(1, tensor_count)]
    ).astype(jnp.bfloat16)
    low_came = [swap(low_core, "pipe", k) for k in range(1, pipe_count)]
    low_sum = sum([piece.astype(jnp.float32) for piece in [low_core] + low_came])
    low_sum = low_sum.astype(jnp.bfloat16)
    low_pieces = [low_sum] + [swap(low_sum, "tensor", s) for s in range(1, tensor_count)]
    key_value = keys_and_values(at, base_chip[:1] + base_chip_came, low_sum, b_own)

    up_pieces = grad_up_pieces(at, low_pieces, cot_pieces, data_count, up_rows)
    up_came = [up_pieces[0]] + [shift(up_pieces[k], "dp", k) for k in range(1, data_count)]
    grad_a = grad_down(at, slot_of, slots, x_recv, grad_pieces)
    up_came, grad_a = lax.optimization_barrier((up_came, grad_a))
    grad_b = grad_up(at, slot_of, slots, up_came)
    return (key_value, input_grad, grad_a, grad_b)


def solution(mesh):
    atd = (
        P("dp", ("pipe", "tensor")),
        P(("pipe", "tensor"), None),
        P(None, ("pipe", "tensor", "dp"), None),
        P(None, "dp", None),
        P(),
        P(),
        P(("dp", "pipe", "tensor"), None),
    )
    return jax.shard_map(
        body,
        mesh=mesh,
        in_specs=atd,
        out_specs=(
            P(("dp", "pipe", "tensor"), None),
            P("dp", ("pipe", "tensor")),
            P(None, ("pipe", "tensor", "dp"), None),
            P(None, "dp", ("pipe", "tensor")),
        ),
        check_vma=False,
    )
```

```python
import jax
import jax.numpy as jnp
from jax import lax
from jax.experimental import pallas as pl
from jax.experimental.pallas import tpu as pltpu
from jax.sharding import PartitionSpec as P

KEY_WIDTH = 1024
ADAPTER_RANK = 64
BLOCK = 128
RANKS = 2 * ADAPTER_RANK
WIDTH = 2 * KEY_WIDTH
VMEM_LIMIT = 24 * 1024 * 1024
VMEM_MOST = 60 * 1024 * 1024
LAST_BOTH = (((1,), (1,)), ((), ()))
FIRST_BOTH = (((0,), (0,)), ((), ()))
SMEM = pl.BlockSpec(memory_space=pltpu.SMEM)
VMEM = pl.BlockSpec(memory_space=pltpu.VMEM)
HBM = pl.BlockSpec(memory_space=pltpu.HBM)
ANY = pl.BlockSpec(memory_space=pl.ANY)


def call(kernel, name, vmem=VMEM_LIMIT, **more):
    return pl.pallas_call(
        kernel,
        compiler_params=pltpu.CompilerParams(vmem_limit_bytes=vmem),
        cost_estimate=pl.CostEstimate(flops=1024, bytes_accessed=1024, transcendentals=0),
        name=name,
        **more,
    )


def wrap(index, count):
    return lax.rem(index + 2 * count, count)


def shift(piece, axis, k):
    count = lax.axis_size(axis)
    return lax.ppermute(piece, axis, [(i, (i + k) % count) for i in range(count)])


def paired(count):
    return count & (count - 1) == 0


def partner(index, k, count):
    return index ^ k if paired(count) else (index + k) % count


def came_from(index, k, count):
    return index ^ k if paired(count) else wrap(index - k, count)


def which_partner(other, index, count):
    return other ^ index if paired(count) else wrap(other - index, count)


def swap(piece, axis, k):
    count = lax.axis_size(axis)
    return lax.ppermute(piece, axis, [(i, partner(i, k, count)) for i in range(count)])


def gather_chips(piece, behind):
    count = lax.axis_size("pipe")
    in_halves = count == 4 and piece.shape[0] % 32 == 0
    came = [swap(piece, "pipe", k) for k in range(1, 3 if in_halves else count)]
    came, one, two = lax.optimization_barrier((came, behind, behind))
    if in_halves:
        half = piece.shape[0] // 2
        third = [swap(came[1][:half], "pipe", 1), swap(came[0][half:], "pipe", 2)]
        came = came + [jnp.concatenate(third)]
    return came, one, two


def pick_up(at, slot_of, adapter_up, data_count):
    def kernel(at_ref, up_ref, *rest):
        out_refs, sems = rest[:data_count], rest[data_count]
        copies = []
        for k in range(data_count):
            data = wrap(at_ref[0] + k, data_count)
            slot = slot_of(at_ref, data, at_ref[3])
            copies.append(pltpu.make_async_copy(up_ref.at[slot], out_refs[k], sems.at[k]))
        for copy in copies:
            copy.start()
        for copy in copies:
            copy.wait()

    return call(
        kernel,
        "pick_up",
        out_shape=(jax.ShapeDtypeStruct(adapter_up.shape[1:], adapter_up.dtype),) * data_count,
        in_specs=[SMEM, HBM],
        out_specs=(VMEM,) * data_count,
        scratch_shapes=[pltpu.SemaphoreType.DMA((data_count,))],
    )(at, adapter_up)


def pick_down(at, slot_of, adapter_down, data_count, blocks_dev, spare):
    down_rows, ranks = adapter_down.shape[1:]
    used = blocks_dev * down_rows

    def kernel(at_ref, down_ref, out_ref, rows, down_sem, out_sem):
        downs, outs = [], []
        for data in range(data_count):
            downs.append([])
            for block in range(blocks_dev):
                here = rows.at[data, pl.ds(block * down_rows, down_rows)]
                slot = slot_of(at_ref, data, block)
                downs[data].append(
                    pltpu.make_async_copy(down_ref.at[slot], here, down_sem.at[data, block])
                )
            there = out_ref.at[data, pl.ds(0, used)]
            outs.append(pltpu.make_async_copy(rows.at[data], there, out_sem.at[data]))
            for copy in downs[data]:
                copy.start()
        for data in range(data_count):
            for copy in downs[data]:
                copy.wait()
            outs[data].start()
        for copy in outs:
            copy.wait()

    return call(
        kernel,
        "pick_down",
        VMEM_MOST,
        out_shape=pltpu.HBM((data_count, used + spare, ranks), adapter_down.dtype),
        in_specs=[SMEM, HBM],
        out_specs=HBM,
        scratch_shapes=[
            pltpu.VMEM((data_count, used, ranks), adapter_down.dtype),
            pltpu.SemaphoreType.DMA((data_count, blocks_dev)),
            pltpu.SemaphoreType.DMA((data_count,)),
        ],
    )(at, adapter_down)


def base_product(at, tokens, weight, first, count):
    pipe_count, tensor_count, rows, depth = tokens.shape
    tile = 1024

    def kernel(at_ref, x_ref, w_ref, out_ref):
        x = x_ref[...].reshape(pipe_count * rows, depth)
        y = jnp.dot(x, w_ref[...], preferred_element_type=jnp.float32).astype(out_ref.dtype)
        for chip in range(pipe_count):
            out_ref[0, which_partner(chip, at_ref[1], pipe_count)] = y[chip * rows : (chip + 1) * rows]

    return call(
        kernel,
        "base_product",
        grid_spec=pltpu.PrefetchScalarGridSpec(
            num_scalar_prefetch=1,
            grid=(WIDTH // tile, count),
            in_specs=[
                pl.BlockSpec(
                    (pipe_count, 1, rows, depth),
                    lambda n, s, at: (0, partner(at[2], s + first, tensor_count), 0, 0),
                ),
                pl.BlockSpec((depth, tile), lambda n, s, at: (0, n)),
            ],
            out_specs=pl.BlockSpec((1, pipe_count, rows, tile), lambda n, s, at: (s, 0, 0, n)),
        ),
        out_shape=jax.ShapeDtypeStruct((count, pipe_count, rows, WIDTH), jnp.bfloat16),
    )(at, tokens, weight)


def low_product(at, tokens, down, pipe_count, tensor_count):
    tok_dev, depth = tokens.shape
    down_rows = depth // down.shape[0]
    rows = tok_dev // (pipe_count * tensor_count)

    def kernel(at_ref, x_ref, a_ref, out_ref):
        for block in range(tok_dev // BLOCK):
            a = a_ref[:, block * down_rows : (block + 1) * down_rows].reshape(depth, RANKS)
            x = x_ref[block * BLOCK : (block + 1) * BLOCK]
            y = jnp.dot(x, a, preferred_element_type=jnp.float32).astype(out_ref.dtype)
            for part in range(BLOCK // rows):
                chip, core = divmod(block * (BLOCK // rows) + part, tensor_count)
                core = which_partner(core, at_ref[2], tensor_count)
                out_ref[core, chip] = y[part * rows : (part + 1) * rows]

    return call(
        kernel,
        "low_product",
        in_specs=[SMEM, VMEM, VMEM],
        out_specs=VMEM,
        out_shape=jax.ShapeDtypeStruct((tensor_count, pipe_count, rows, RANKS), jnp.bfloat16),
    )(at, tokens, down)


def cotangent_product(at, cot_pieces, weight):
    tensor_count, pipe_count = len(cot_pieces), len(cot_pieces[0])
    rows = cot_pieces[0][0].shape[0]
    depth = weight.shape[0]
    tok_dev = tensor_count * pipe_count * rows
    tile = 256 if depth % 256 == 0 else depth
    order = [(s, k) for s in range(tensor_count) for k in range(pipe_count)]

    def kernel(at_ref, w_ref, *rest):
        cot_refs, (out_ref, cot, sems) = rest[: len(order)], rest[len(order) :]

        @pl.when(pl.program_id(0) == 0)
        def _():
            copies = []
            for i, (s, k) in enumerate(order):
                chip = came_from(at_ref[1], k, pipe_count)
                core = came_from(at_ref[2], s, tensor_count)
                first = pl.multiple_of((chip * tensor_count + core) * rows, rows)
                copies.append(
                    pltpu.make_async_copy(cot_refs[i], cot.at[pl.ds(first, rows)], sems.at[i])
                )
            for copy in copies:
                copy.start()
            for copy in copies:
                copy.wait()

        out_ref[...] = lax.dot_general(
            cot[...], w_ref[...], LAST_BOTH, preferred_element_type=jnp.float32
        )

    return call(
        kernel,
        "cotangent_product",
        grid=(depth // tile,),
        in_specs=[SMEM, pl.BlockSpec((tile, WIDTH), lambda n: (n, 0))] + [ANY] * len(order),
        out_specs=pl.BlockSpec((tok_dev, tile), lambda n: (0, n)),
        out_shape=jax.ShapeDtypeStruct((tok_dev, depth), jnp.float32),
        scratch_shapes=[
            pltpu.VMEM((tok_dev, WIDTH), jnp.bfloat16),
            pltpu.SemaphoreType.DMA((len(order),)),
        ],
    )(at, weight, *[cot_pieces[s][k] for s, k in order])


def input_gradient(at, base, grad_pieces, down):
    data_count, all_rows, _ = down.shape
    tensor_count = len(grad_pieces)
    pipe_count, _, rows, _ = grad_pieces[0].shape
    tok_dev, depth = base.shape
    down_rows = depth // data_count
    planes = next((n for n in range(1, data_count) if n * down_rows % 256 == 0), data_count)
    tile = planes * down_rows

    def kernel(at_ref, base_ref, a_ref, *rest):
        grad_refs, (out_ref, grad) = rest[:tensor_count], rest[tensor_count:]

        @pl.when(pl.program_id(0) == 0)
        def _():
            for s in range(tensor_count):
                core = came_from(at_ref[2], s, tensor_count)
                for k in range(pipe_count):
                    chip = came_from(at_ref[1], k, pipe_count)
                    first = pl.multiple_of((chip * tensor_count + core) * rows, rows)
                    grad[pl.ds(first, rows)] = grad_refs[s][k, at_ref[0]]

        for block in range(tok_dev // BLOCK):
            here = slice(block * BLOCK, (block + 1) * BLOCK)
            a = a_ref[:, block * down_rows : (block + 1) * down_rows].reshape(tile, RANKS)
            low = lax.dot_general(grad[here], a, LAST_BOTH, preferred_element_type=jnp.float32)
            out_ref[here] = (base_ref[here] + low).astype(out_ref.dtype)

    grad_shape = (pipe_count, data_count, rows, RANKS)
    return call(
        kernel,
        "input_gradient",
        grid=(data_count // planes,),
        in_specs=[
            SMEM,
            pl.BlockSpec((tok_dev, tile), lambda n: (0, n)),
            pl.BlockSpec((planes, all_rows, RANKS), lambda n: (n, 0, 0)),
        ]
        + [pl.BlockSpec(grad_shape, lambda n: (0, 0, 0, 0))] * tensor_count,
        out_specs=pl.BlockSpec((tok_dev, tile), lambda n: (0, n)),
        out_shape=jax.ShapeDtypeStruct((tok_dev, depth), jnp.bfloat16),
        scratch_shapes=[pltpu.VMEM((tok_dev, RANKS), jnp.bfloat16)],
    )(at, base, down, *grad_pieces)


def grad_down(at, slot_of, slots, x_features, grad_pieces):
    data_count, down_rows, tok_dev = x_features.shape
    tensor_count = len(grad_pieces)
    pipe_count, _, rows, _ = grad_pieces[0].shape
    blocks_dev = tok_dev // BLOCK

    def kernel(at_ref, x_ref, *rest):
        grad_refs, (out_ref, grad, x, products, sems) = rest[:tensor_count], rest[tensor_count:]
        copies = [
            pltpu.make_async_copy(x_ref.at[data], x.at[data], sems.at[data])
            for data in range(data_count)
        ]
        for copy in copies:
            copy.start()
        for s in range(tensor_count):
            core = came_from(at_ref[2], s, tensor_count)
            for k in range(pipe_count):
                chip = came_from(at_ref[1], k, pipe_count)
                first = pl.multiple_of((chip * tensor_count + core) * rows, rows)
                for data in range(data_count):
                    grad[data, pl.ds(first, rows)] = grad_refs[s][k, data]
        out_ref[...] = jnp.zeros(out_ref.shape, out_ref.dtype)
        for data in range(data_count):
            copies[data].wait()
            for block in range(blocks_dev):
                here = slice(block * BLOCK, (block + 1) * BLOCK)
                products[data % 2, block] = jnp.dot(
                    x[data, :, here], grad[data, here], preferred_element_type=jnp.float32
                )
            for block in range(blocks_dev):
                slot = slot_of(at_ref, data, block)
                out_ref[slot] += products[data % 2, block]

    return call(
        kernel,
        "grad_down",
        VMEM_MOST,
        in_specs=[SMEM, HBM] + [VMEM] * tensor_count,
        out_specs=VMEM,
        out_shape=jax.ShapeDtypeStruct((slots, down_rows, RANKS), jnp.float32),
        scratch_shapes=[
            pltpu.VMEM((data_count, tok_dev, RANKS), jnp.bfloat16),
            pltpu.VMEM(x_features.shape, jnp.bfloat16),
            pltpu.VMEM((2, blocks_dev, down_rows, RANKS), jnp.float32),
            pltpu.SemaphoreType.DMA((data_count,)),
        ],
    )(at, x_features, *grad_pieces)


def grad_up_pieces(at, low_pieces, cot_pieces, data_count, up_rows):
    tensor_count, pipe_count = len(cot_pieces), len(cot_pieces[0])
    group_count = tensor_count * pipe_count
    rows = cot_pieces[0][0].shape[0]
    cols = WIDTH // group_count
    tok_dev = group_count * rows
    blocks_dev = tok_dev // BLOCK
    group_half = group_count // 2
    order = [(s, k) for s in range(tensor_count) for k in range(pipe_count)]
    pieces = [cot_pieces[s][k] for s, k in order]
    in_kernel = cols % 128 == 0
    if not in_kernel:
        first_col = (at[1] * tensor_count + at[2]) * cols
        pieces = [lax.dynamic_slice_in_dim(piece, first_col, cols, 1) for piece in pieces]

    def kernel(at_ref, *rest):
        low_refs, rest = rest[:tensor_count], rest[tensor_count:]
        cot_refs, (out_ref, low, cot, sems) = rest[: len(order)], rest[len(order) :]
        my_group = at_ref[1] * tensor_count + at_ref[2]
        copies = []
        for i, (s, k) in enumerate(order):
            core = came_from(at_ref[2], s, tensor_count)
            chip = came_from(at_ref[1], k, pipe_count)
            first = pl.multiple_of((chip * tensor_count + core) * rows, rows)
            piece = cot_refs[i]
            if in_kernel:
                piece = piece.at[:, pl.ds(pl.multiple_of(my_group * cols, cols), cols)]
            copies.append(pltpu.make_async_copy(piece, cot.at[pl.ds(first, rows)], sems.at[i]))
        for copy in copies:
            copy.start()
        for s in range(tensor_count):
            core = came_from(at_ref[2], s, tensor_count)
            for k in range(pipe_count):
                first = pl.multiple_of((k * tensor_count + core) * rows, rows)
                low[pl.ds(first, rows)] = low_refs[s][k]
        for copy in copies:
            copy.wait()
        for block in range(blocks_dev):
            at = slice(block * BLOCK, (block + 1) * BLOCK)
            both = lax.dot_general(low[at], cot[at], FIRST_BOTH, preferred_element_type=jnp.float32)
            half = jnp.where(my_group < group_half, both[:ADAPTER_RANK], both[ADAPTER_RANK:])
            half = half.astype(out_ref.dtype)
            for data in range(data_count):
                k = wrap(data - at_ref[0], data_count)
                out_ref[k, block] = half[data * up_rows : (data + 1) * up_rows]

    return call(
        kernel,
        "grad_up_pieces",
        in_specs=[SMEM] + [VMEM] * tensor_count + [ANY] * len(order),
        out_specs=VMEM,
        out_shape=jax.ShapeDtypeStruct((data_count, blocks_dev, up_rows, cols), jnp.bfloat16),
        scratch_shapes=[
            pltpu.VMEM((tok_dev, RANKS), jnp.bfloat16),
            pltpu.VMEM((tok_dev, cols), jnp.bfloat16),
            pltpu.SemaphoreType.DMA((len(order),)),
        ],
    )(at, *low_pieces, *pieces)


def grad_up(at, slot_of, slots, pieces):
    data_count = len(pieces)
    blocks_dev, up_rows, cols = pieces[0].shape

    def kernel(at_ref, *rest):
        piece_refs, out_ref = rest[:data_count], rest[data_count]
        out_ref[...] = jnp.zeros(out_ref.shape, out_ref.dtype)
        for k in range(data_count):
            data = wrap(at_ref[0] - k, data_count)
            for block in range(blocks_dev):
                slot = slot_of(at_ref, data, block)
                out_ref[slot] += piece_refs[k][block].astype(out_ref.dtype)

    return call(
        kernel,
        "grad_up",
        in_specs=[SMEM] + [VMEM] * data_count,
        out_specs=VMEM,
        out_shape=jax.ShapeDtypeStruct((slots, up_rows, cols), jnp.float32),
    )(at, *pieces)


def own_rows(at, up, cotangent, a_send):
    data_count = len(up)
    rows = cotangent.shape[0]
    used = a_send.shape[1] - rows

    def kernel(at_ref, cot_ref, send_in_ref, *rest):
        del send_in_ref
        up_refs, (b_ref, send_ref, grad, sems) = rest[:data_count], rest[data_count:]
        pieces = []
        for data in range(data_count):
            came = wrap(at_ref[0] - data, data_count)
            piece = up_refs[0][...]
            for k in range(1, data_count):
                piece = jnp.where(came == k, up_refs[k][...], piece)
            pieces.append(piece)
        b = jnp.concatenate(pieces, axis=0)
        cot = cot_ref[...]
        grad[...] = jnp.concatenate(
            [
                lax.dot_general(cot[:, half], b[:, half], LAST_BOTH, preferred_element_type=jnp.float32)
                for half in (slice(0, KEY_WIDTH), slice(KEY_WIDTH, WIDTH))
            ],
            axis=1,
        ).astype(grad.dtype)
        copies = [
            pltpu.make_async_copy(grad, send_ref.at[data, pl.ds(used, rows)], sems.at[data])
            for data in range(data_count)
        ]
        for copy in copies:
            copy.start()
        b_ref[...] = b
        for copy in copies:
            copy.wait()

    return call(
        kernel,
        "own_rows",
        in_specs=[SMEM, VMEM, HBM] + [VMEM] * data_count,
        out_specs=(VMEM, HBM),
        out_shape=(
            jax.ShapeDtypeStruct((ADAPTER_RANK, WIDTH), jnp.bfloat16),
            pltpu.HBM(a_send.shape, a_send.dtype),
        ),
        input_output_aliases={2: 1},
        scratch_shapes=[
            pltpu.VMEM((rows, RANKS), jnp.bfloat16),
            pltpu.SemaphoreType.DMA((data_count,)),
        ],
    )(at, cotangent, a_send, *up)


def keys_and_values(at, base_pieces, low_sum, b_own):
    rows = base_pieces[0].shape[0]
    count = len(base_pieces)

    def kernel(at_ref, low_ref, b_ref, *rest):
        base_refs, out_ref = rest[:count], rest[count]
        low = low_ref[at_ref[1]]
        for first, ranks in ((0, slice(0, ADAPTER_RANK)), (KEY_WIDTH, slice(ADAPTER_RANK, RANKS))):
            at = slice(first, first + KEY_WIDTH)
            y = jnp.dot(low[:, ranks], b_ref[:, at], preferred_element_type=jnp.float32)
            for base_ref in base_refs:
                y += base_ref[:, at].astype(jnp.float32)
            out_ref[:, at] = y.astype(out_ref.dtype)

    return call(
        kernel,
        "keys_and_values",
        in_specs=[SMEM, VMEM, VMEM] + [VMEM] * count,
        out_specs=VMEM,
        out_shape=jax.ShapeDtypeStruct((rows, WIDTH), jnp.bfloat16),
    )(at, low_sum, b_own, *base_pieces)


def body(
    tokens, key_value_weight, adapter_down, adapter_up, tenant_of_block, slot_of_tenant, cotangent
):
    data_count = lax.axis_size("dp")
    pipe_count = lax.axis_size("pipe")
    tensor_count = lax.axis_size("tensor")
    group_count = pipe_count * tensor_count
    at_data, at_pipe, at_tensor = (lax.axis_index(a) for a in ("dp", "pipe", "tensor"))
    my_group = at_pipe * tensor_count + at_tensor
    tok_dev, feature_count = tokens.shape
    blocks_dev = tok_dev // BLOCK
    rows = tok_dev // group_count
    down_rows = adapter_down.shape[1]
    up_rows = adapter_up.shape[1]
    slots = adapter_down.shape[0]
    blocks = tenant_of_block.shape[0]

    own_block = my_group * rows // BLOCK
    at = jnp.stack([at_data, at_pipe, at_tensor, own_block]).astype(jnp.int32)
    at = jnp.concatenate([at, tenant_of_block, slot_of_tenant])

    def slot_of(at_ref, data, block):
        return at_ref[4 + blocks + at_ref[4 + data * blocks_dev + block]]

    b_send = pick_up(at, slot_of, adapter_up, data_count)
    b_came = [b_send[0]] + [shift(b_send[k], "dp", k) for k in range(1, data_count)]

    adapter_down, b_send = lax.optimization_barrier((adapter_down, b_send))
    a_send = pick_down(at, slot_of, adapter_down, data_count, blocks_dev, rows)
    a_send, cot_send = lax.optimization_barrier((a_send, cotangent))
    b_own, a_send = own_rows(at, b_came, cotangent, a_send)
    a_recv = lax.all_to_all(a_send, "dp", 0, 0, tiled=True)

    behind, a_send = lax.optimization_barrier((tokens, a_send))
    cot_chips, base_tokens, x_tokens = gather_chips(cot_send, behind)
    cot_chips = [cotangent] + cot_chips

    tokens_by_group = base_tokens.reshape(pipe_count, tensor_count, rows, feature_count)
    base_send = base_product(at, tokens_by_group, key_value_weight, 1, tensor_count - 1)
    base_came = [swap(base_send[s - 1], "tensor", s) for s in range(1, tensor_count)]
    base_keep = base_product(at, tokens_by_group, key_value_weight, 0, 1)[0]
    base_chip = [
        sum([base_keep[k].astype(jnp.float32)] + [b[k].astype(jnp.float32) for b in base_came])
        for k in range(pipe_count)
    ]
    base_chip[1:] = [piece.astype(jnp.bfloat16) for piece in base_chip[1:]]
    base_chip_came = [swap(base_chip[k], "pipe", k) for k in range(1, pipe_count)]

    cot_pieces = [cot_chips] + [
        [swap(piece, "tensor", s) for piece in cot_chips] for s in range(1, tensor_count)
    ]
    input_base = cotangent_product(at, cot_pieces, key_value_weight)

    x_send = x_tokens.T.reshape(data_count, down_rows, tok_dev)

    a_recv, x_send, input_base, base_chip_came[:2] = lax.optimization_barrier(
        (a_recv, x_send, input_base, base_chip_came[:2])
    )
    x_recv = lax.all_to_all(x_send, "dp", 0, 0, tiled=True)

    grad_data = a_recv[:, blocks_dev * down_rows :]
    grad_chips = jnp.stack([grad_data] + [swap(grad_data, "pipe", k) for k in range(1, pipe_count)])
    grad_pieces = [grad_chips] + [swap(grad_chips, "tensor", s) for s in range(1, tensor_count)]
    input_grad = input_gradient(at, input_base, grad_pieces, a_recv)

    low_down, base_chip_came = lax.optimization_barrier((a_recv, base_chip_came))
    low_part = low_product(at, tokens, low_down, pipe_count, tensor_count)
    low_core = sum(
        [low_part[0].astype(jnp.float32)]
        + [swap(low_part[s], "tensor", s).astype(jnp.float32) for s in range(1, tensor_count)]
    ).astype(jnp.bfloat16)
    low_came = [swap(low_core, "pipe", k) for k in range(1, pipe_count)]
    low_sum = sum([piece.astype(jnp.float32) for piece in [low_core] + low_came])
    low_sum = low_sum.astype(jnp.bfloat16)
    low_pieces = [low_sum] + [swap(low_sum, "tensor", s) for s in range(1, tensor_count)]
    key_value = keys_and_values(at, base_chip[:1] + base_chip_came, low_sum, b_own)

    up_pieces = grad_up_pieces(at, low_pieces, cot_pieces, data_count, up_rows)
    up_came = [up_pieces[0]] + [shift(up_pieces[k], "dp", k) for k in range(1, data_count)]
    grad_a = grad_down(at, slot_of, slots, x_recv, grad_pieces)
    up_came, grad_a = lax.optimization_barrier((up_came, grad_a))
    grad_b = grad_up(at, slot_of, slots, up_came)
    return (key_value, input_grad, grad_a, grad_b)


def solution(mesh):
    atd = (
        P("dp", ("pipe", "tensor")),
        P(("pipe", "tensor"), None),
        P(None, ("pipe", "tensor", "dp"), None),
        P(None, "dp", None),
        P(),
        P(),
        P(("dp", "pipe", "tensor"), None),
    )
    return jax.shard_map(
        body,
        mesh=mesh,
        in_specs=atd,
        out_specs=(
            P(("dp", "pipe", "tensor"), None),
            P("dp", ("pipe", "tensor")),
            P(None, ("pipe", "tensor", "dp"), None),
            P(None, "dp", ("pipe", "tensor")),
        ),
        check_vma=False,
    )
```

```python
import jax
import jax.numpy as jnp
from jax import lax
from jax.experimental import pallas as pl
from jax.experimental.pallas import tpu as pltpu
from jax.sharding import PartitionSpec as P

KEY_WIDTH = 1024
ADAPTER_RANK = 64
BLOCK = 128
RANKS = 2 * ADAPTER_RANK
WIDTH = 2 * KEY_WIDTH
VMEM_LIMIT = 24 * 1024 * 1024
VMEM_MOST = 60 * 1024 * 1024
LAST_BOTH = (((1,), (1,)), ((), ()))
FIRST_BOTH = (((0,), (0,)), ((), ()))
SMEM = pl.BlockSpec(memory_space=pltpu.SMEM)
VMEM = pl.BlockSpec(memory_space=pltpu.VMEM)
HBM = pl.BlockSpec(memory_space=pltpu.HBM)
ANY = pl.BlockSpec(memory_space=pl.ANY)


def call(kernel, name, vmem=VMEM_LIMIT, **more):
    return pl.pallas_call(
        kernel,
        compiler_params=pltpu.CompilerParams(vmem_limit_bytes=vmem),
        cost_estimate=pl.CostEstimate(flops=1024, bytes_accessed=1024, transcendentals=0),
        name=name,
        **more,
    )


def wrap(index, count):
    return lax.rem(index + 2 * count, count)


def shift(piece, axis, k):
    count = lax.axis_size(axis)
    return lax.ppermute(piece, axis, [(i, (i + k) % count) for i in range(count)])


def paired(count):
    return count & (count - 1) == 0


def partner(index, k, count):
    return index ^ k if paired(count) else (index + k) % count


def came_from(index, k, count):
    return index ^ k if paired(count) else wrap(index - k, count)


def which_partner(other, index, count):
    return other ^ index if paired(count) else wrap(other - index, count)


def swap(piece, axis, k):
    count = lax.axis_size(axis)
    return lax.ppermute(piece, axis, [(i, partner(i, k, count)) for i in range(count)])


def gather_chips(piece, behind):
    count = lax.axis_size("pipe")
    in_halves = count == 4 and piece.shape[0] % 32 == 0
    came = [swap(piece, "pipe", k) for k in range(1, 3 if in_halves else count)]
    came, one, two = lax.optimization_barrier((came, behind, behind))
    if in_halves:
        half = piece.shape[0] // 2
        third = [swap(came[1][:half], "pipe", 1), swap(came[0][half:], "pipe", 2)]
        came = came + [jnp.concatenate(third)]
    return came, one, two


def pick(tenant_of_block, slot_of_tenant, adapter_down, adapter_up, group_rows, spare):
    data_count = lax.axis_size("dp")
    blocks_dev = tenant_of_block.shape[0] // data_count
    down_rows, ranks = adapter_down.shape[1:]
    used = blocks_dev * down_rows

    def kernel(tenant_ref, slot_ref, down_ref, up_ref, *rest):
        up_refs, (out_ref, rows, up_sem, down_sem, out_sem) = rest[:data_count], rest[data_count:]
        own_block = lax.axis_index(("pipe", "tensor")) * group_rows // BLOCK
        ups, downs, outs = [], [], []
        for k in range(data_count):
            data = wrap(lax.axis_index("dp") + k, data_count)
            slot = slot_ref[tenant_ref[data * blocks_dev + own_block]]
            ups.append(pltpu.make_async_copy(up_ref.at[slot], up_refs[k], up_sem.at[k]))
            ups[-1].start()
        for data in range(data_count):
            downs.append([])
            for block in range(blocks_dev):
                here = rows.at[data, pl.ds(block * down_rows, down_rows)]
                slot = slot_ref[tenant_ref[data * blocks_dev + block]]
                downs[data].append(
                    pltpu.make_async_copy(down_ref.at[slot], here, down_sem.at[data, block])
                )
                downs[data][-1].start()
            there = out_ref.at[data, pl.ds(0, used)]
            outs.append(pltpu.make_async_copy(rows.at[data], there, out_sem.at[data]))
        for data in range(data_count):
            for copy in downs[data]:
                copy.wait()
            outs[data].start()
        for copy in ups + outs:
            copy.wait()

    up_shape = jax.ShapeDtypeStruct(adapter_up.shape[1:], adapter_up.dtype)
    out = call(
        kernel,
        "pick_rows",
        VMEM_MOST,
        out_shape=(up_shape,) * data_count
        + (pltpu.HBM((data_count, used + spare, ranks), adapter_down.dtype),),
        in_specs=[SMEM, SMEM, HBM, HBM],
        out_specs=(VMEM,) * data_count + (HBM,),
        scratch_shapes=[
            pltpu.VMEM((data_count, used, ranks), adapter_down.dtype),
            pltpu.SemaphoreType.DMA((data_count,)),
            pltpu.SemaphoreType.DMA((data_count, blocks_dev)),
            pltpu.SemaphoreType.DMA((data_count,)),
        ],
    )(tenant_of_block, slot_of_tenant, adapter_down, adapter_up)
    return out[:data_count], out[data_count]


def base_product(at, tokens, weight, first, count):
    pipe_count, tensor_count, rows, depth = tokens.shape
    tile = 1024

    def kernel(at_ref, x_ref, w_ref, out_ref):
        x = x_ref[...].reshape(pipe_count * rows, depth)
        y = jnp.dot(x, w_ref[...], preferred_element_type=jnp.float32).astype(out_ref.dtype)
        for chip in range(pipe_count):
            out_ref[0, which_partner(chip, at_ref[1], pipe_count)] = y[chip * rows : (chip + 1) * rows]

    return call(
        kernel,
        "base_product",
        grid_spec=pltpu.PrefetchScalarGridSpec(
            num_scalar_prefetch=1,
            grid=(WIDTH // tile, count),
            in_specs=[
                pl.BlockSpec(
                    (pipe_count, 1, rows, depth),
                    lambda n, s, at: (0, partner(at[2], s + first, tensor_count), 0, 0),
                ),
                pl.BlockSpec((depth, tile), lambda n, s, at: (0, n)),
            ],
            out_specs=pl.BlockSpec((1, pipe_count, rows, tile), lambda n, s, at: (s, 0, 0, n)),
        ),
        out_shape=jax.ShapeDtypeStruct((count, pipe_count, rows, WIDTH), jnp.bfloat16),
    )(at, tokens, weight)


def low_product(at, tokens, down, pipe_count, tensor_count):
    tok_dev, depth = tokens.shape
    down_rows = depth // down.shape[0]
    rows = tok_dev // (pipe_count * tensor_count)

    def kernel(at_ref, x_ref, a_ref, out_ref):
        for block in range(tok_dev // BLOCK):
            a = a_ref[:, block * down_rows : (block + 1) * down_rows].reshape(depth, RANKS)
            x = x_ref[block * BLOCK : (block + 1) * BLOCK]
            y = jnp.dot(x, a, preferred_element_type=jnp.float32).astype(out_ref.dtype)
            for part in range(BLOCK // rows):
                chip, core = divmod(block * (BLOCK // rows) + part, tensor_count)
                core = which_partner(core, at_ref[2], tensor_count)
                out_ref[core, chip] = y[part * rows : (part + 1) * rows]

    return call(
        kernel,
        "low_product",
        in_specs=[SMEM, VMEM, VMEM],
        out_specs=VMEM,
        out_shape=jax.ShapeDtypeStruct((tensor_count, pipe_count, rows, RANKS), jnp.bfloat16),
    )(at, tokens, down)


def cotangent_product(at, cot_pieces, weight):
    tensor_count, pipe_count = len(cot_pieces), len(cot_pieces[0])
    rows = cot_pieces[0][0].shape[0]
    depth = weight.shape[0]
    tok_dev = tensor_count * pipe_count * rows
    tile = 256 if depth % 256 == 0 else depth
    order = [(s, k) for s in range(tensor_count) for k in range(pipe_count)]

    def kernel(at_ref, w_ref, *rest):
        cot_refs, (out_ref, cot, sems) = rest[: len(order)], rest[len(order) :]

        @pl.when(pl.program_id(0) == 0)
        def _():
            copies = []
            for i, (s, k) in enumerate(order):
                chip = came_from(at_ref[1], k, pipe_count)
                core = came_from(at_ref[2], s, tensor_count)
                first = pl.multiple_of((chip * tensor_count + core) * rows, rows)
                copies.append(
                    pltpu.make_async_copy(cot_refs[i], cot.at[pl.ds(first, rows)], sems.at[i])
                )
            for copy in copies:
                copy.start()
            for copy in copies:
                copy.wait()

        out_ref[...] = lax.dot_general(
            cot[...], w_ref[...], LAST_BOTH, preferred_element_type=jnp.float32
        )

    return call(
        kernel,
        "cotangent_product",
        grid=(depth // tile,),
        in_specs=[SMEM, pl.BlockSpec((tile, WIDTH), lambda n: (n, 0))] + [ANY] * len(order),
        out_specs=pl.BlockSpec((tok_dev, tile), lambda n: (0, n)),
        out_shape=jax.ShapeDtypeStruct((tok_dev, depth), jnp.float32),
        scratch_shapes=[
            pltpu.VMEM((tok_dev, WIDTH), jnp.bfloat16),
            pltpu.SemaphoreType.DMA((len(order),)),
        ],
    )(at, weight, *[cot_pieces[s][k] for s, k in order])


def input_gradient(at, base, grad_pieces, down):
    data_count, all_rows, _ = down.shape
    tensor_count = len(grad_pieces)
    pipe_count, _, rows, _ = grad_pieces[0].shape
    tok_dev, depth = base.shape
    down_rows = depth // data_count
    planes = next((n for n in range(1, data_count) if n * down_rows % 256 == 0), data_count)
    tile = planes * down_rows

    def kernel(at_ref, base_ref, a_ref, *rest):
        grad_refs, (out_ref, grad) = rest[:tensor_count], rest[tensor_count:]

        @pl.when(pl.program_id(0) == 0)
        def _():
            for s in range(tensor_count):
                core = came_from(at_ref[2], s, tensor_count)
                for k in range(pipe_count):
                    chip = came_from(at_ref[1], k, pipe_count)
                    first = pl.multiple_of((chip * tensor_count + core) * rows, rows)
                    grad[pl.ds(first, rows)] = grad_refs[s][k, at_ref[0]]

        for block in range(tok_dev // BLOCK):
            here = slice(block * BLOCK, (block + 1) * BLOCK)
            a = a_ref[:, block * down_rows : (block + 1) * down_rows].reshape(tile, RANKS)
            low = lax.dot_general(grad[here], a, LAST_BOTH, preferred_element_type=jnp.float32)
            out_ref[here] = (base_ref[here] + low).astype(out_ref.dtype)

    grad_shape = (pipe_count, data_count, rows, RANKS)
    return call(
        kernel,
        "input_gradient",
        grid=(data_count // planes,),
        in_specs=[
            SMEM,
            pl.BlockSpec((tok_dev, tile), lambda n: (0, n)),
            pl.BlockSpec((planes, all_rows, RANKS), lambda n: (n, 0, 0)),
        ]
        + [pl.BlockSpec(grad_shape, lambda n: (0, 0, 0, 0))] * tensor_count,
        out_specs=pl.BlockSpec((tok_dev, tile), lambda n: (0, n)),
        out_shape=jax.ShapeDtypeStruct((tok_dev, depth), jnp.bfloat16),
        scratch_shapes=[pltpu.VMEM((tok_dev, RANKS), jnp.bfloat16)],
    )(at, base, down, *grad_pieces)


def grad_down(at, slot_of, slots, x_features, grad_pieces):
    data_count, down_rows, tok_dev = x_features.shape
    tensor_count = len(grad_pieces)
    pipe_count, _, rows, _ = grad_pieces[0].shape
    blocks_dev = tok_dev // BLOCK

    parts = 2 if down_rows % 256 == 0 else 1
    part_rows = down_rows // parts

    def kernel(at_ref, x_ref, *rest):
        grad_refs, rest = rest[:tensor_count], rest[tensor_count:]
        out_ref, grad, x, total, products, x_sem, grad_sem, out_sem = rest
        copies = []
        for s in range(tensor_count):
            core = came_from(at_ref[2], s, tensor_count)
            for k in range(pipe_count):
                chip = came_from(at_ref[1], k, pipe_count)
                first = pl.multiple_of((chip * tensor_count + core) * rows, rows)
                there = grad.at[:, pl.ds(first, rows)]
                copies.append(pltpu.make_async_copy(grad_refs[s].at[k], there, grad_sem.at[s, k]))
        x_copies = [
            pltpu.make_async_copy(x_ref.at[data], x.at[data], x_sem.at[data])
            for data in range(data_count)
        ]
        for copy in copies + x_copies:
            copy.start()
        total[...] = jnp.zeros(total.shape, total.dtype)
        for copy in copies:
            copy.wait()
        outs = []
        for part in range(parts):
            at = slice(part * part_rows, (part + 1) * part_rows)
            for data in range(data_count):
                if part == 0:
                    x_copies[data].wait()
                for block in range(blocks_dev):
                    here = slice(block * BLOCK, (block + 1) * BLOCK)
                    products[data % 2, block] = jnp.dot(
                        x[data, at, here], grad[data, here], preferred_element_type=jnp.float32
                    )
                for block in range(blocks_dev):
                    slot = slot_of(at_ref, data, block)
                    total[part, slot] += products[data % 2, block]
            there = out_ref.at[:, pl.ds(part * part_rows, part_rows)]
            outs.append(pltpu.make_async_copy(total.at[part], there, out_sem.at[part]))
            outs[-1].start()
        for copy in outs:
            copy.wait()

    return call(
        kernel,
        "grad_down",
        VMEM_MOST,
        in_specs=[SMEM, HBM] + [HBM] * tensor_count,
        out_specs=HBM,
        out_shape=pltpu.HBM((slots, down_rows, RANKS), jnp.float32),
        scratch_shapes=[
            pltpu.VMEM((data_count, tok_dev, RANKS), jnp.bfloat16),
            pltpu.VMEM(x_features.shape, jnp.bfloat16),
            pltpu.VMEM((parts, slots, part_rows, RANKS), jnp.float32),
            pltpu.VMEM((2, blocks_dev, part_rows, RANKS), jnp.float32),
            pltpu.SemaphoreType.DMA((data_count,)),
            pltpu.SemaphoreType.DMA((tensor_count, pipe_count)),
            pltpu.SemaphoreType.DMA((parts,)),
        ],
    )(at, x_features, *grad_pieces)


def grad_up_pieces(at, low_pieces, cot_pieces, data_count, up_rows):
    tensor_count, pipe_count = len(cot_pieces), len(cot_pieces[0])
    group_count = tensor_count * pipe_count
    rows = cot_pieces[0][0].shape[0]
    cols = WIDTH // group_count
    tok_dev = group_count * rows
    blocks_dev = tok_dev // BLOCK
    group_half = group_count // 2
    order = [(s, k) for s in range(tensor_count) for k in range(pipe_count)]
    pieces = [cot_pieces[s][k] for s, k in order]
    in_kernel = cols % 128 == 0
    if not in_kernel:
        first_col = (at[1] * tensor_count + at[2]) * cols
        pieces = [lax.dynamic_slice_in_dim(piece, first_col, cols, 1) for piece in pieces]

    def kernel(at_ref, *rest):
        low_refs, rest = rest[:tensor_count], rest[tensor_count:]
        cot_refs, (out_ref, low, cot, sems) = rest[: len(order)], rest[len(order) :]
        my_group = at_ref[1] * tensor_count + at_ref[2]
        copies = []
        for i, (s, k) in enumerate(order):
            core = came_from(at_ref[2], s, tensor_count)
            chip = came_from(at_ref[1], k, pipe_count)
            first = pl.multiple_of((chip * tensor_count + core) * rows, rows)
            piece = cot_refs[i]
            if in_kernel:
                piece = piece.at[:, pl.ds(pl.multiple_of(my_group * cols, cols), cols)]
            copies.append(pltpu.make_async_copy(piece, cot.at[pl.ds(first, rows)], sems.at[i]))
        for copy in copies:
            copy.start()
        for s in range(tensor_count):
            core = came_from(at_ref[2], s, tensor_count)
            for k in range(pipe_count):
                first = pl.multiple_of((k * tensor_count + core) * rows, rows)
                low[pl.ds(first, rows)] = low_refs[s][k]
        for copy in copies:
            copy.wait()
        for block in range(blocks_dev):
            at = slice(block * BLOCK, (block + 1) * BLOCK)
            both = lax.dot_general(low[at], cot[at], FIRST_BOTH, preferred_element_type=jnp.float32)
            half = jnp.where(my_group < group_half, both[:ADAPTER_RANK], both[ADAPTER_RANK:])
            half = half.astype(out_ref.dtype)
            for data in range(data_count):
                k = wrap(data - at_ref[0], data_count)
                out_ref[k, block] = half[data * up_rows : (data + 1) * up_rows]

    return call(
        kernel,
        "grad_up_pieces",
        in_specs=[SMEM] + [VMEM] * tensor_count + [ANY] * len(order),
        out_specs=VMEM,
        out_shape=jax.ShapeDtypeStruct((data_count, blocks_dev, up_rows, cols), jnp.bfloat16),
        scratch_shapes=[
            pltpu.VMEM((tok_dev, RANKS), jnp.bfloat16),
            pltpu.VMEM((tok_dev, cols), jnp.bfloat16),
            pltpu.SemaphoreType.DMA((len(order),)),
        ],
    )(at, *low_pieces, *pieces)


def grad_up(at, slot_of, slots, pieces):
    data_count = len(pieces)
    blocks_dev, up_rows, cols = pieces[0].shape

    def kernel(at_ref, *rest):
        piece_refs, out_ref = rest[:data_count], rest[data_count]
        out_ref[...] = jnp.zeros(out_ref.shape, out_ref.dtype)
        for k in range(data_count):
            data = wrap(at_ref[0] - k, data_count)
            for block in range(blocks_dev):
                slot = slot_of(at_ref, data, block)
                out_ref[slot] += piece_refs[k][block].astype(out_ref.dtype)

    return call(
        kernel,
        "grad_up",
        in_specs=[SMEM] + [VMEM] * data_count,
        out_specs=VMEM,
        out_shape=jax.ShapeDtypeStruct((slots, up_rows, cols), jnp.float32),
    )(at, *pieces)


def own_rows(at, up, cotangent, a_send):
    data_count = len(up)
    rows = cotangent.shape[0]
    used = a_send.shape[1] - rows

    def kernel(at_ref, cot_ref, send_in_ref, *rest):
        del send_in_ref
        up_refs, (b_ref, send_ref, grad, sems) = rest[:data_count], rest[data_count:]
        pieces = []
        for data in range(data_count):
            came = wrap(at_ref[0] - data, data_count)
            piece = up_refs[0][...]
            for k in range(1, data_count):
                piece = jnp.where(came == k, up_refs[k][...], piece)
            pieces.append(piece)
        b = jnp.concatenate(pieces, axis=0)
        cot = cot_ref[...]
        grad[...] = jnp.concatenate(
            [
                lax.dot_general(cot[:, half], b[:, half], LAST_BOTH, preferred_element_type=jnp.float32)
                for half in (slice(0, KEY_WIDTH), slice(KEY_WIDTH, WIDTH))
            ],
            axis=1,
        ).astype(grad.dtype)
        copies = [
            pltpu.make_async_copy(grad, send_ref.at[data, pl.ds(used, rows)], sems.at[data])
            for data in range(data_count)
        ]
        for copy in copies:
            copy.start()
        b_ref[...] = b
        for copy in copies:
            copy.wait()

    return call(
        kernel,
        "own_rows",
        in_specs=[SMEM, VMEM, HBM] + [VMEM] * data_count,
        out_specs=(VMEM, HBM),
        out_shape=(
            jax.ShapeDtypeStruct((ADAPTER_RANK, WIDTH), jnp.bfloat16),
            pltpu.HBM(a_send.shape, a_send.dtype),
        ),
        input_output_aliases={2: 1},
        scratch_shapes=[
            pltpu.VMEM((rows, RANKS), jnp.bfloat16),
            pltpu.SemaphoreType.DMA((data_count,)),
        ],
    )(at, cotangent, a_send, *up)


def keys_and_values(at, base_pieces, low_sum, b_own):
    rows = base_pieces[0].shape[0]
    count = len(base_pieces)

    def kernel(at_ref, low_ref, b_ref, *rest):
        base_refs, out_ref = rest[:count], rest[count]
        low = low_ref[at_ref[1]]
        for first, ranks in ((0, slice(0, ADAPTER_RANK)), (KEY_WIDTH, slice(ADAPTER_RANK, RANKS))):
            at = slice(first, first + KEY_WIDTH)
            y = jnp.dot(low[:, ranks], b_ref[:, at], preferred_element_type=jnp.float32)
            for base_ref in base_refs:
                y += base_ref[:, at].astype(jnp.float32)
            out_ref[:, at] = y.astype(out_ref.dtype)

    return call(
        kernel,
        "keys_and_values",
        in_specs=[SMEM, VMEM, VMEM] + [VMEM] * count,
        out_specs=VMEM,
        out_shape=jax.ShapeDtypeStruct((rows, WIDTH), jnp.bfloat16),
    )(at, low_sum, b_own, *base_pieces)


def body(
    tokens, key_value_weight, adapter_down, adapter_up, tenant_of_block, slot_of_tenant, cotangent
):
    data_count = lax.axis_size("dp")
    pipe_count = lax.axis_size("pipe")
    tensor_count = lax.axis_size("tensor")
    group_count = pipe_count * tensor_count
    at_data, at_pipe, at_tensor = (lax.axis_index(a) for a in ("dp", "pipe", "tensor"))
    my_group = at_pipe * tensor_count + at_tensor
    tok_dev, feature_count = tokens.shape
    blocks_dev = tok_dev // BLOCK
    rows = tok_dev // group_count
    down_rows = adapter_down.shape[1]
    up_rows = adapter_up.shape[1]
    slots = adapter_down.shape[0]
    blocks = tenant_of_block.shape[0]

    at = jnp.stack([at_data, at_pipe, at_tensor]).astype(jnp.int32)
    at = jnp.concatenate([at, tenant_of_block, slot_of_tenant])

    def slot_of(at_ref, data, block):
        return at_ref[3 + blocks + at_ref[3 + data * blocks_dev + block]]

    b_send, a_send = pick(
        tenant_of_block, slot_of_tenant, adapter_down, adapter_up, rows, rows
    )
    b_came = [b_send[0]] + [shift(b_send[k], "dp", k) for k in range(1, data_count)]

    b_own, a_send = own_rows(at, b_came, cotangent, a_send)
    a_recv = lax.all_to_all(a_send, "dp", 0, 0, tiled=True)

    behind, a_send = lax.optimization_barrier((tokens, a_send))
    cot_chips, base_tokens, x_tokens = gather_chips(cotangent, behind)
    cot_chips = [cotangent] + cot_chips

    tokens_by_group = base_tokens.reshape(pipe_count, tensor_count, rows, feature_count)
    base_send = base_product(at, tokens_by_group, key_value_weight, 1, tensor_count - 1)
    base_came = [swap(base_send[s - 1], "tensor", s) for s in range(1, tensor_count)]
    base_keep = base_product(at, tokens_by_group, key_value_weight, 0, 1)[0]
    base_chip = [
        sum([base_keep[k].astype(jnp.float32)] + [b[k].astype(jnp.float32) for b in base_came])
        for k in range(pipe_count)
    ]
    base_chip[1:] = [piece.astype(jnp.bfloat16) for piece in base_chip[1:]]
    base_chip_came = [swap(base_chip[k], "pipe", k) for k in range(1, pipe_count)]

    cot_pieces = [cot_chips] + [
        [swap(piece, "tensor", s) for piece in cot_chips] for s in range(1, tensor_count)
    ]
    input_base = cotangent_product(at, cot_pieces, key_value_weight)

    x_send = x_tokens.T.reshape(data_count, down_rows, tok_dev)

    a_recv, x_send, input_base, base_chip_came[:2] = lax.optimization_barrier(
        (a_recv, x_send, input_base, base_chip_came[:2])
    )
    x_recv = lax.all_to_all(x_send, "dp", 0, 0, tiled=True)

    grad_data = a_recv[:, blocks_dev * down_rows :]
    grad_chips = jnp.stack([grad_data] + [swap(grad_data, "pipe", k) for k in range(1, pipe_count)])
    grad_pieces = [grad_chips] + [swap(grad_chips, "tensor", s) for s in range(1, tensor_count)]
    input_grad = input_gradient(at, input_base, grad_pieces, a_recv)

    low_down, base_chip_came = lax.optimization_barrier((a_recv, base_chip_came))
    low_part = low_product(at, tokens, low_down, pipe_count, tensor_count)
    low_core = sum(
        [low_part[0].astype(jnp.float32)]
        + [swap(low_part[s], "tensor", s).astype(jnp.float32) for s in range(1, tensor_count)]
    ).astype(jnp.bfloat16)
    low_came = [swap(low_core, "pipe", k) for k in range(1, pipe_count)]
    low_sum = sum([piece.astype(jnp.float32) for piece in [low_core] + low_came])
    low_sum = low_sum.astype(jnp.bfloat16)
    low_pieces = [low_sum] + [swap(low_sum, "tensor", s) for s in range(1, tensor_count)]
    key_value = keys_and_values(at, base_chip[:1] + base_chip_came, low_sum, b_own)

    up_pieces = grad_up_pieces(at, low_pieces, cot_pieces, data_count, up_rows)
    up_came = [up_pieces[0]] + [shift(up_pieces[k], "dp", k) for k in range(1, data_count)]
    grad_a = grad_down(at, slot_of, slots, x_recv, grad_pieces)
    up_came, grad_a = lax.optimization_barrier((up_came, grad_a))
    grad_b = grad_up(at, slot_of, slots, up_came)
    return (key_value, input_grad, grad_a, grad_b)


def solution(mesh):
    atd = (
        P("dp", ("pipe", "tensor")),
        P(("pipe", "tensor"), None),
        P(None, ("pipe", "tensor", "dp"), None),
        P(None, "dp", None),
        P(),
        P(),
        P(("dp", "pipe", "tensor"), None),
    )
    return jax.shard_map(
        body,
        mesh=mesh,
        in_specs=atd,
        out_specs=(
            P(("dp", "pipe", "tensor"), None),
            P("dp", ("pipe", "tensor")),
            P(None, ("pipe", "tensor", "dp"), None),
            P(None, "dp", ("pipe", "tensor")),
        ),
        check_vma=False,
    )
```

```python
import jax
import jax.numpy as jnp
from jax import lax
from jax.experimental import pallas as pl
from jax.experimental.pallas import tpu as pltpu
from jax.sharding import PartitionSpec as P

KEY_WIDTH = 1024
ADAPTER_RANK = 64
BLOCK = 128
RANKS = 2 * ADAPTER_RANK
WIDTH = 2 * KEY_WIDTH
VMEM_LIMIT = 24 * 1024 * 1024
VMEM_MOST = 60 * 1024 * 1024
LAST_BOTH = (((1,), (1,)), ((), ()))
FIRST_BOTH = (((0,), (0,)), ((), ()))
SMEM = pl.BlockSpec(memory_space=pltpu.SMEM)
VMEM = pl.BlockSpec(memory_space=pltpu.VMEM)
HBM = pl.BlockSpec(memory_space=pltpu.HBM)
ANY = pl.BlockSpec(memory_space=pl.ANY)


def call(kernel, name, vmem=VMEM_LIMIT, **more):
    return pl.pallas_call(
        kernel,
        compiler_params=pltpu.CompilerParams(vmem_limit_bytes=vmem),
        cost_estimate=pl.CostEstimate(flops=1024, bytes_accessed=1024, transcendentals=0),
        name=name,
        **more,
    )


def wrap(index, count):
    return lax.rem(index + 2 * count, count)


def shift(piece, axis, k):
    count = lax.axis_size(axis)
    return lax.ppermute(piece, axis, [(i, (i + k) % count) for i in range(count)])


def paired(count):
    return count & (count - 1) == 0


def partner(index, k, count):
    return index ^ k if paired(count) else (index + k) % count


def came_from(index, k, count):
    return index ^ k if paired(count) else wrap(index - k, count)


def which_partner(other, index, count):
    return other ^ index if paired(count) else wrap(other - index, count)


def swap(piece, axis, k):
    count = lax.axis_size(axis)
    return lax.ppermute(piece, axis, [(i, partner(i, k, count)) for i in range(count)])


def gather_chips(piece, behind):
    count = lax.axis_size("pipe")
    in_halves = count == 4 and piece.shape[0] % 32 == 0
    came = [swap(piece, "pipe", k) for k in range(1, 3 if in_halves else count)]
    came, one, two = lax.optimization_barrier((came, behind, behind))
    if in_halves:
        half = piece.shape[0] // 2
        third = [swap(came[1][:half], "pipe", 1), swap(came[0][half:], "pipe", 2)]
        came = came + [jnp.concatenate(third)]
    return came, one, two


def pick(tenant_of_block, slot_of_tenant, adapter_down, adapter_up, group_rows):
    data_count = lax.axis_size("dp")
    blocks_dev = tenant_of_block.shape[0] // data_count
    down_rows, ranks = adapter_down.shape[1:]
    used = blocks_dev * down_rows

    def kernel(tenant_ref, slot_ref, down_ref, up_ref, *rest):
        up_refs, (out_ref, rows, up_sem, down_sem, out_sem) = rest[:data_count], rest[data_count:]
        own_block = lax.axis_index(("pipe", "tensor")) * group_rows // BLOCK
        ups, downs, outs = [], [], []
        for k in range(data_count):
            data = wrap(lax.axis_index("dp") + k, data_count)
            slot = slot_ref[tenant_ref[data * blocks_dev + own_block]]
            ups.append(pltpu.make_async_copy(up_ref.at[slot], up_refs[k], up_sem.at[k]))
            ups[-1].start()
        for data in range(data_count):
            downs.append([])
            for block in range(blocks_dev):
                here = rows.at[data, pl.ds(block * down_rows, down_rows)]
                slot = slot_ref[tenant_ref[data * blocks_dev + block]]
                downs[data].append(
                    pltpu.make_async_copy(down_ref.at[slot], here, down_sem.at[data, block])
                )
                downs[data][-1].start()
            outs.append(pltpu.make_async_copy(rows.at[data], out_ref.at[data], out_sem.at[data]))
        for data in range(data_count):
            for copy in downs[data]:
                copy.wait()
            outs[data].start()
        for copy in ups + outs:
            copy.wait()

    up_shape = jax.ShapeDtypeStruct(adapter_up.shape[1:], adapter_up.dtype)
    out = call(
        kernel,
        "pick_rows",
        VMEM_MOST,
        out_shape=(up_shape,) * data_count
        + (pltpu.HBM((data_count, used, ranks), adapter_down.dtype),),
        in_specs=[SMEM, SMEM, HBM, HBM],
        out_specs=(VMEM,) * data_count + (HBM,),
        scratch_shapes=[
            pltpu.VMEM((data_count, used, ranks), adapter_down.dtype),
            pltpu.SemaphoreType.DMA((data_count,)),
            pltpu.SemaphoreType.DMA((data_count, blocks_dev)),
            pltpu.SemaphoreType.DMA((data_count,)),
        ],
    )(tenant_of_block, slot_of_tenant, adapter_down, adapter_up)
    return out[:data_count], out[data_count]


def base_product(at, tokens, weight, first, count):
    pipe_count, tensor_count, rows, depth = tokens.shape
    tile = 1024

    def kernel(at_ref, x_ref, w_ref, out_ref):
        x = x_ref[...].reshape(pipe_count * rows, depth)
        y = jnp.dot(x, w_ref[...], preferred_element_type=jnp.float32).astype(out_ref.dtype)
        for chip in range(pipe_count):
            out_ref[0, which_partner(chip, at_ref[1], pipe_count)] = y[chip * rows : (chip + 1) * rows]

    return call(
        kernel,
        "base_product",
        grid_spec=pltpu.PrefetchScalarGridSpec(
            num_scalar_prefetch=1,
            grid=(WIDTH // tile, count),
            in_specs=[
                pl.BlockSpec(
                    (pipe_count, 1, rows, depth),
                    lambda n, s, at: (0, partner(at[2], s + first, tensor_count), 0, 0),
                ),
                pl.BlockSpec((depth, tile), lambda n, s, at: (0, n)),
            ],
            out_specs=pl.BlockSpec((1, pipe_count, rows, tile), lambda n, s, at: (s, 0, 0, n)),
        ),
        out_shape=jax.ShapeDtypeStruct((count, pipe_count, rows, WIDTH), jnp.bfloat16),
    )(at, tokens, weight)


def low_product(at, tokens, down, pipe_count, tensor_count):
    tok_dev, depth = tokens.shape
    down_rows = depth // down.shape[0]
    rows = tok_dev // (pipe_count * tensor_count)

    def kernel(at_ref, x_ref, a_ref, out_ref):
        for block in range(tok_dev // BLOCK):
            a = a_ref[:, block * down_rows : (block + 1) * down_rows].reshape(depth, RANKS)
            x = x_ref[block * BLOCK : (block + 1) * BLOCK]
            y = jnp.dot(x, a, preferred_element_type=jnp.float32).astype(out_ref.dtype)
            for part in range(BLOCK // rows):
                chip, core = divmod(block * (BLOCK // rows) + part, tensor_count)
                core = which_partner(core, at_ref[2], tensor_count)
                out_ref[core, chip] = y[part * rows : (part + 1) * rows]

    return call(
        kernel,
        "low_product",
        in_specs=[SMEM, VMEM, VMEM],
        out_specs=VMEM,
        out_shape=jax.ShapeDtypeStruct((tensor_count, pipe_count, rows, RANKS), jnp.bfloat16),
    )(at, tokens, down)


def cotangent_product(at, cot_pieces, weight):
    tensor_count, pipe_count = len(cot_pieces), len(cot_pieces[0])
    rows = cot_pieces[0][0].shape[0]
    depth = weight.shape[0]
    tok_dev = tensor_count * pipe_count * rows
    tile = 256 if depth % 256 == 0 else depth
    order = [(s, k) for s in range(tensor_count) for k in range(pipe_count)]

    def kernel(at_ref, w_ref, *rest):
        cot_refs, (out_ref, cot, sems) = rest[: len(order)], rest[len(order) :]

        @pl.when(pl.program_id(0) == 0)
        def _():
            copies = []
            for i, (s, k) in enumerate(order):
                chip = came_from(at_ref[1], k, pipe_count)
                core = came_from(at_ref[2], s, tensor_count)
                first = pl.multiple_of((chip * tensor_count + core) * rows, rows)
                copies.append(
                    pltpu.make_async_copy(cot_refs[i], cot.at[pl.ds(first, rows)], sems.at[i])
                )
            for copy in copies:
                copy.start()
            for copy in copies:
                copy.wait()

        out_ref[...] = lax.dot_general(
            cot[...], w_ref[...], LAST_BOTH, preferred_element_type=jnp.float32
        )

    return call(
        kernel,
        "cotangent_product",
        grid=(depth // tile,),
        in_specs=[SMEM, pl.BlockSpec((tile, WIDTH), lambda n: (n, 0))] + [ANY] * len(order),
        out_specs=pl.BlockSpec((tok_dev, tile), lambda n: (0, n)),
        out_shape=jax.ShapeDtypeStruct((tok_dev, depth), jnp.float32),
        scratch_shapes=[
            pltpu.VMEM((tok_dev, WIDTH), jnp.bfloat16),
            pltpu.SemaphoreType.DMA((len(order),)),
        ],
    )(at, weight, *[cot_pieces[s][k] for s, k in order])


def input_gradient(at, base, grad_pieces, down):
    data_count, all_rows, _ = down.shape
    tensor_count = len(grad_pieces)
    pipe_count, rows, _ = grad_pieces[0].shape
    tok_dev, depth = base.shape
    down_rows = depth // data_count
    planes = next((n for n in range(1, data_count) if n * down_rows % 256 == 0), data_count)
    tile = planes * down_rows

    def kernel(at_ref, base_ref, a_ref, *rest):
        grad_refs, (out_ref, grad) = rest[:tensor_count], rest[tensor_count:]

        @pl.when(pl.program_id(0) == 0)
        def _():
            for s in range(tensor_count):
                core = came_from(at_ref[2], s, tensor_count)
                for k in range(pipe_count):
                    chip = came_from(at_ref[1], k, pipe_count)
                    first = pl.multiple_of((chip * tensor_count + core) * rows, rows)
                    grad[pl.ds(first, rows)] = grad_refs[s][k]

        for block in range(tok_dev // BLOCK):
            here = slice(block * BLOCK, (block + 1) * BLOCK)
            a = a_ref[:, block * down_rows : (block + 1) * down_rows].reshape(tile, RANKS)
            low = lax.dot_general(grad[here], a, LAST_BOTH, preferred_element_type=jnp.float32)
            out_ref[here] = (base_ref[here] + low).astype(out_ref.dtype)

    return call(
        kernel,
        "input_gradient",
        grid=(data_count // planes,),
        in_specs=[
            SMEM,
            pl.BlockSpec((tok_dev, tile), lambda n: (0, n)),
            pl.BlockSpec((planes, all_rows, RANKS), lambda n: (n, 0, 0)),
        ]
        + [VMEM] * tensor_count,
        out_specs=pl.BlockSpec((tok_dev, tile), lambda n: (0, n)),
        out_shape=jax.ShapeDtypeStruct((tok_dev, depth), jnp.bfloat16),
        scratch_shapes=[pltpu.VMEM((tok_dev, RANKS), jnp.bfloat16)],
    )(at, base, down, *grad_pieces)


def grad_down_pieces(at, x_features, grad_pieces):
    data_count, down_rows, tok_dev = x_features.shape
    tensor_count = len(grad_pieces)
    pipe_count, rows, _ = grad_pieces[0].shape
    blocks_dev = tok_dev // BLOCK

    def kernel(at_ref, x_ref, *rest):
        grad_refs, (out_ref, grad) = rest[:tensor_count], rest[tensor_count:]

        @pl.when(pl.program_id(0) == 0)
        def _():
            for s in range(tensor_count):
                core = came_from(at_ref[2], s, tensor_count)
                for k in range(pipe_count):
                    chip = came_from(at_ref[1], k, pipe_count)
                    first = pl.multiple_of((chip * tensor_count + core) * rows, rows)
                    grad[pl.ds(first, rows)] = grad_refs[s][k]

        for block in range(blocks_dev):
            here = slice(block * BLOCK, (block + 1) * BLOCK)
            out_ref[0, block] = jnp.dot(
                x_ref[0, :, here], grad[here], preferred_element_type=jnp.float32
            ).astype(out_ref.dtype)

    return call(
        kernel,
        "grad_down_pieces",
        grid=(data_count,),
        in_specs=[SMEM, pl.BlockSpec((1, down_rows, tok_dev), lambda d: (d, 0, 0))]
        + [VMEM] * tensor_count,
        out_specs=pl.BlockSpec((1, blocks_dev, down_rows, RANKS), lambda d: (d, 0, 0, 0)),
        out_shape=pltpu.HBM((data_count, blocks_dev, down_rows, RANKS), jnp.bfloat16),
        scratch_shapes=[pltpu.VMEM((tok_dev, RANKS), jnp.bfloat16)],
    )(at, x_features, *grad_pieces)


def grad_down(at, slot_of, slots, pieces):
    data_count, blocks_dev, down_rows, _ = pieces.shape
    parts = 2 if down_rows % 256 == 0 else 1
    part_rows = down_rows // parts

    def kernel(at_ref, piece_ref, out_ref, piece, total, piece_sem, out_sem):
        copies = [
            [
                pltpu.make_async_copy(
                    piece_ref.at[data, block], piece.at[data, block], piece_sem.at[data, block]
                )
                for block in range(blocks_dev)
            ]
            for data in range(data_count)
        ]
        for some in copies:
            for copy in some:
                copy.start()
        total[...] = jnp.zeros(total.shape, total.dtype)
        outs = []
        for part in range(parts):
            here = slice(part * part_rows, (part + 1) * part_rows)
            for data in range(data_count):
                for block in range(blocks_dev):
                    if part == 0:
                        copies[data][block].wait()
                    slot = slot_of(at_ref, data, block)
                    total[part, slot] += piece[data, block, here].astype(total.dtype)
            there = out_ref.at[:, pl.ds(part * part_rows, part_rows)]
            outs.append(pltpu.make_async_copy(total.at[part], there, out_sem.at[part]))
            outs[-1].start()
        for copy in outs:
            copy.wait()

    return call(
        kernel,
        "grad_down",
        VMEM_MOST,
        in_specs=[SMEM, HBM],
        out_specs=HBM,
        out_shape=pltpu.HBM((slots, down_rows, RANKS), jnp.float32),
        scratch_shapes=[
            pltpu.VMEM(pieces.shape, jnp.bfloat16),
            pltpu.VMEM((parts, slots, part_rows, RANKS), jnp.float32),
            pltpu.SemaphoreType.DMA((data_count, blocks_dev)),
            pltpu.SemaphoreType.DMA((parts,)),
        ],
    )(at, pieces)


def grad_up_pieces(at, low_pieces, cot_pieces, data_count, up_rows):
    tensor_count, pipe_count = len(cot_pieces), len(cot_pieces[0])
    group_count = tensor_count * pipe_count
    rows = cot_pieces[0][0].shape[0]
    cols = WIDTH // group_count
    tok_dev = group_count * rows
    blocks_dev = tok_dev // BLOCK
    group_half = group_count // 2
    order = [(s, k) for s in range(tensor_count) for k in range(pipe_count)]
    pieces = [cot_pieces[s][k] for s, k in order]
    in_kernel = cols % 128 == 0
    if not in_kernel:
        first_col = (at[1] * tensor_count + at[2]) * cols
        pieces = [lax.dynamic_slice_in_dim(piece, first_col, cols, 1) for piece in pieces]

    def kernel(at_ref, *rest):
        low_refs, rest = rest[:tensor_count], rest[tensor_count:]
        cot_refs, (out_ref, low, cot, sems) = rest[: len(order)], rest[len(order) :]
        my_group = at_ref[1] * tensor_count + at_ref[2]
        copies = []
        for i, (s, k) in enumerate(order):
            core = came_from(at_ref[2], s, tensor_count)
            chip = came_from(at_ref[1], k, pipe_count)
            first = pl.multiple_of((chip * tensor_count + core) * rows, rows)
            piece = cot_refs[i]
            if in_kernel:
                piece = piece.at[:, pl.ds(pl.multiple_of(my_group * cols, cols), cols)]
            copies.append(pltpu.make_async_copy(piece, cot.at[pl.ds(first, rows)], sems.at[i]))
        for copy in copies:
            copy.start()
        for s in range(tensor_count):
            core = came_from(at_ref[2], s, tensor_count)
            for k in range(pipe_count):
                first = pl.multiple_of((k * tensor_count + core) * rows, rows)
                low[pl.ds(first, rows)] = low_refs[s][k]
        for copy in copies:
            copy.wait()
        for block in range(blocks_dev):
            at = slice(block * BLOCK, (block + 1) * BLOCK)
            both = lax.dot_general(low[at], cot[at], FIRST_BOTH, preferred_element_type=jnp.float32)
            half = jnp.where(my_group < group_half, both[:ADAPTER_RANK], both[ADAPTER_RANK:])
            half = half.astype(out_ref.dtype)
            for data in range(data_count):
                k = wrap(data - at_ref[0], data_count)
                out_ref[k, block] = half[data * up_rows : (data + 1) * up_rows]

    return call(
        kernel,
        "grad_up_pieces",
        in_specs=[SMEM] + [VMEM] * tensor_count + [ANY] * len(order),
        out_specs=VMEM,
        out_shape=jax.ShapeDtypeStruct((data_count, blocks_dev, up_rows, cols), jnp.bfloat16),
        scratch_shapes=[
            pltpu.VMEM((tok_dev, RANKS), jnp.bfloat16),
            pltpu.VMEM((tok_dev, cols), jnp.bfloat16),
            pltpu.SemaphoreType.DMA((len(order),)),
        ],
    )(at, *low_pieces, *pieces)


def grad_up(at, slot_of, slots, pieces):
    data_count = len(pieces)
    blocks_dev, up_rows, cols = pieces[0].shape

    def kernel(at_ref, *rest):
        piece_refs, out_ref = rest[:data_count], rest[data_count]
        out_ref[...] = jnp.zeros(out_ref.shape, out_ref.dtype)
        for k in range(data_count):
            data = wrap(at_ref[0] - k, data_count)
            for block in range(blocks_dev):
                slot = slot_of(at_ref, data, block)
                out_ref[slot] += piece_refs[k][block].astype(out_ref.dtype)

    return call(
        kernel,
        "grad_up",
        in_specs=[SMEM] + [VMEM] * data_count,
        out_specs=VMEM,
        out_shape=jax.ShapeDtypeStruct((slots, up_rows, cols), jnp.float32),
    )(at, *pieces)


def own_rows(at, up, cotangent):
    data_count = len(up)
    rows = cotangent.shape[0]

    def kernel(at_ref, cot_ref, *rest):
        up_refs, (b_ref, grad_ref) = rest[:data_count], rest[data_count:]
        pieces = []
        for data in range(data_count):
            came = wrap(at_ref[0] - data, data_count)
            piece = up_refs[0][...]
            for k in range(1, data_count):
                piece = jnp.where(came == k, up_refs[k][...], piece)
            pieces.append(piece)
        b = jnp.concatenate(pieces, axis=0)
        b_ref[...] = b
        cot = cot_ref[...]
        grad_ref[...] = jnp.concatenate(
            [
                lax.dot_general(cot[:, half], b[:, half], LAST_BOTH, preferred_element_type=jnp.float32)
                for half in (slice(0, KEY_WIDTH), slice(KEY_WIDTH, WIDTH))
            ],
            axis=1,
        ).astype(grad_ref.dtype)

    return call(
        kernel,
        "own_rows",
        in_specs=[SMEM, VMEM] + [VMEM] * data_count,
        out_specs=(VMEM, VMEM),
        out_shape=(
            jax.ShapeDtypeStruct((ADAPTER_RANK, WIDTH), jnp.bfloat16),
            jax.ShapeDtypeStruct((rows, RANKS), jnp.bfloat16),
        ),
    )(at, cotangent, *up)


def keys_and_values(at, base_pieces, low_sum, b_own):
    rows = base_pieces[0].shape[0]
    count = len(base_pieces)

    def kernel(at_ref, low_ref, b_ref, *rest):
        base_refs, out_ref = rest[:count], rest[count]
        low = low_ref[at_ref[1]]
        for first, ranks in ((0, slice(0, ADAPTER_RANK)), (KEY_WIDTH, slice(ADAPTER_RANK, RANKS))):
            at = slice(first, first + KEY_WIDTH)
            y = jnp.dot(low[:, ranks], b_ref[:, at], preferred_element_type=jnp.float32)
            for base_ref in base_refs:
                y += base_ref[:, at].astype(jnp.float32)
            out_ref[:, at] = y.astype(out_ref.dtype)

    return call(
        kernel,
        "keys_and_values",
        in_specs=[SMEM, VMEM, VMEM] + [VMEM] * count,
        out_specs=VMEM,
        out_shape=jax.ShapeDtypeStruct((rows, WIDTH), jnp.bfloat16),
    )(at, low_sum, b_own, *base_pieces)


def body(
    tokens, key_value_weight, adapter_down, adapter_up, tenant_of_block, slot_of_tenant, cotangent
):
    data_count = lax.axis_size("dp")
    pipe_count = lax.axis_size("pipe")
    tensor_count = lax.axis_size("tensor")
    group_count = pipe_count * tensor_count
    at_data, at_pipe, at_tensor = (lax.axis_index(a) for a in ("dp", "pipe", "tensor"))
    my_group = at_pipe * tensor_count + at_tensor
    tok_dev, feature_count = tokens.shape
    blocks_dev = tok_dev // BLOCK
    rows = tok_dev // group_count
    down_rows = adapter_down.shape[1]
    up_rows = adapter_up.shape[1]
    slots = adapter_down.shape[0]
    blocks = tenant_of_block.shape[0]

    at = jnp.stack([at_data, at_pipe, at_tensor]).astype(jnp.int32)
    at = jnp.concatenate([at, tenant_of_block, slot_of_tenant])

    def slot_of(at_ref, data, block):
        return at_ref[3 + blocks + at_ref[3 + data * blocks_dev + block]]

    b_send, a_send = pick(tenant_of_block, slot_of_tenant, adapter_down, adapter_up, rows)
    b_came = [b_send[0]] + [shift(b_send[k], "dp", k) for k in range(1, data_count)]
    b_own, grad_rows = own_rows(at, b_came, cotangent)

    a_send, b_came = lax.optimization_barrier((a_send, b_came))
    a_recv = lax.all_to_all(a_send, "dp", 0, 0, tiled=True)

    behind, a_send = lax.optimization_barrier((tokens, a_send))
    cot_chips, base_tokens, x_tokens = gather_chips(cotangent, behind)
    cot_chips = [cotangent] + cot_chips

    tokens_by_group = base_tokens.reshape(pipe_count, tensor_count, rows, feature_count)
    base_send = base_product(at, tokens_by_group, key_value_weight, 1, tensor_count - 1)
    base_came = [swap(base_send[s - 1], "tensor", s) for s in range(1, tensor_count)]
    base_keep = base_product(at, tokens_by_group, key_value_weight, 0, 1)[0]
    base_chip = [
        sum([base_keep[k].astype(jnp.float32)] + [b[k].astype(jnp.float32) for b in base_came])
        for k in range(pipe_count)
    ]
    base_chip[1:] = [piece.astype(jnp.bfloat16) for piece in base_chip[1:]]
    base_chip_came = [swap(base_chip[k], "pipe", k) for k in range(1, pipe_count)]

    cot_pieces = [cot_chips] + [
        [swap(piece, "tensor", s) for piece in cot_chips] for s in range(1, tensor_count)
    ]
    input_base = cotangent_product(at, cot_pieces, key_value_weight)

    grad_chips = jnp.stack([grad_rows] + [swap(grad_rows, "pipe", k) for k in range(1, pipe_count)])
    grad_pieces = [grad_chips] + [swap(grad_chips, "tensor", s) for s in range(1, tensor_count)]
    x_features = x_tokens.T.reshape(data_count, down_rows, tok_dev)
    down_send = grad_down_pieces(at, x_features, grad_pieces)

    a_recv, down_send, input_base, base_chip_came[:2] = lax.optimization_barrier(
        (a_recv, down_send, input_base, base_chip_came[:2])
    )
    down_recv = lax.all_to_all(down_send, "dp", 0, 0, tiled=True)
    input_grad = input_gradient(at, input_base, grad_pieces, a_recv)

    low_down, base_chip_came = lax.optimization_barrier((a_recv, base_chip_came))
    low_part = low_product(at, tokens, low_down, pipe_count, tensor_count)
    low_core = sum(
        [low_part[0].astype(jnp.float32)]
        + [swap(low_part[s], "tensor", s).astype(jnp.float32) for s in range(1, tensor_count)]
    ).astype(jnp.bfloat16)
    low_came = [swap(low_core, "pipe", k) for k in range(1, pipe_count)]
    low_sum = sum([piece.astype(jnp.float32) for piece in [low_core] + low_came])
    low_sum = low_sum.astype(jnp.bfloat16)
    low_pieces = [low_sum] + [swap(low_sum, "tensor", s) for s in range(1, tensor_count)]
    key_value = keys_and_values(at, base_chip[:1] + base_chip_came, low_sum, b_own)

    up_pieces = grad_up_pieces(at, low_pieces, cot_pieces, data_count, up_rows)
    up_came = [up_pieces[0]] + [shift(up_pieces[k], "dp", k) for k in range(1, data_count)]
    grad_a = grad_down(at, slot_of, slots, down_recv)
    up_came, grad_a = lax.optimization_barrier((up_came, grad_a))
    grad_b = grad_up(at, slot_of, slots, up_came)
    return (key_value, input_grad, grad_a, grad_b)


def solution(mesh):
    atd = (
        P("dp", ("pipe", "tensor")),
        P(("pipe", "tensor"), None),
        P(None, ("pipe", "tensor", "dp"), None),
        P(None, "dp", None),
        P(),
        P(),
        P(("dp", "pipe", "tensor"), None),
    )
    return jax.shard_map(
        body,
        mesh=mesh,
        in_specs=atd,
        out_specs=(
            P(("dp", "pipe", "tensor"), None),
            P("dp", ("pipe", "tensor")),
            P(None, ("pipe", "tensor", "dp"), None),
            P(None, "dp", ("pipe", "tensor")),
        ),
        check_vma=False,
    )
```

```python
import jax
import jax.numpy as jnp
from jax import lax
from jax.experimental import pallas as pl
from jax.experimental.pallas import tpu as pltpu
from jax.sharding import PartitionSpec as P

KEY_WIDTH = 1024
ADAPTER_RANK = 64
BLOCK = 128
RANKS = 2 * ADAPTER_RANK
WIDTH = 2 * KEY_WIDTH
VMEM_LIMIT = 24 * 1024 * 1024
VMEM_MOST = 60 * 1024 * 1024
LAST_BOTH = (((1,), (1,)), ((), ()))
FIRST_BOTH = (((0,), (0,)), ((), ()))
SMEM = pl.BlockSpec(memory_space=pltpu.SMEM)
VMEM = pl.BlockSpec(memory_space=pltpu.VMEM)
HBM = pl.BlockSpec(memory_space=pltpu.HBM)
ANY = pl.BlockSpec(memory_space=pl.ANY)


def call(kernel, name, vmem=VMEM_LIMIT, **more):
    return pl.pallas_call(
        kernel,
        compiler_params=pltpu.CompilerParams(vmem_limit_bytes=vmem),
        cost_estimate=pl.CostEstimate(flops=1024, bytes_accessed=1024, transcendentals=0),
        name=name,
        **more,
    )


def wrap(index, count):
    return lax.rem(index + 2 * count, count)


def shift(piece, axis, k):
    count = lax.axis_size(axis)
    return lax.ppermute(piece, axis, [(i, (i + k) % count) for i in range(count)])


def paired(count):
    return count & (count - 1) == 0


def partner(index, k, count):
    return index ^ k if paired(count) else (index + k) % count


def came_from(index, k, count):
    return index ^ k if paired(count) else wrap(index - k, count)


def which_partner(other, index, count):
    return other ^ index if paired(count) else wrap(other - index, count)


def swap(piece, axis, k):
    count = lax.axis_size(axis)
    return lax.ppermute(piece, axis, [(i, partner(i, k, count)) for i in range(count)])


def gather_chips(piece, later, behind):
    count = lax.axis_size("pipe")
    in_halves = count == 4 and piece.shape[0] % 32 == 0
    came = [swap(piece if k == 1 else later, "pipe", k) for k in range(1, 3 if in_halves else count)]
    came, one, two = lax.optimization_barrier((came, behind, behind))
    if in_halves:
        half = piece.shape[0] // 2
        third = [swap(came[1][:half], "pipe", 1), swap(came[0][half:], "pipe", 2)]
        came = came + [jnp.concatenate(third)]
    return came, one, two


def pick(tenant_of_block, slot_of_tenant, adapter_down, adapter_up, group_rows):
    data_count = lax.axis_size("dp")
    blocks_dev = tenant_of_block.shape[0] // data_count
    down_rows, ranks = adapter_down.shape[1:]
    used = blocks_dev * down_rows

    def kernel(tenant_ref, slot_ref, down_ref, up_ref, *rest):
        up_refs, (out_ref, rows, up_sem, down_sem, out_sem) = rest[:data_count], rest[data_count:]
        own_block = lax.axis_index(("pipe", "tensor")) * group_rows // BLOCK
        ups, downs, outs = [], [], []
        for k in range(data_count):
            data = wrap(lax.axis_index("dp") + k, data_count)
            slot = slot_ref[tenant_ref[data * blocks_dev + own_block]]
            ups.append(pltpu.make_async_copy(up_ref.at[slot], up_refs[k], up_sem.at[k]))
            ups[-1].start()
        for data in range(data_count):
            downs.append([])
            for block in range(blocks_dev):
                here = rows.at[data, pl.ds(block * down_rows, down_rows)]
                slot = slot_ref[tenant_ref[data * blocks_dev + block]]
                downs[data].append(
                    pltpu.make_async_copy(down_ref.at[slot], here, down_sem.at[data, block])
                )
                downs[data][-1].start()
            outs.append(pltpu.make_async_copy(rows.at[data], out_ref.at[data], out_sem.at[data]))
        for data in range(data_count):
            for copy in downs[data]:
                copy.wait()
            outs[data].start()
        for copy in ups + outs:
            copy.wait()

    up_shape = jax.ShapeDtypeStruct(adapter_up.shape[1:], adapter_up.dtype)
    out = call(
        kernel,
        "pick_rows",
        VMEM_MOST,
        out_shape=(up_shape,) * data_count
        + (pltpu.HBM((data_count, used, ranks), adapter_down.dtype),),
        in_specs=[SMEM, SMEM, HBM, HBM],
        out_specs=(VMEM,) * data_count + (HBM,),
        scratch_shapes=[
            pltpu.VMEM((data_count, used, ranks), adapter_down.dtype),
            pltpu.SemaphoreType.DMA((data_count,)),
            pltpu.SemaphoreType.DMA((data_count, blocks_dev)),
            pltpu.SemaphoreType.DMA((data_count,)),
        ],
    )(tenant_of_block, slot_of_tenant, adapter_down, adapter_up)
    return out[:data_count], out[data_count]


def base_product(at, tokens, weight, first, count):
    pipe_count, tensor_count, rows, depth = tokens.shape
    tile = 1024

    def kernel(at_ref, x_ref, w_ref, out_ref):
        x = x_ref[...].reshape(pipe_count * rows, depth)
        y = jnp.dot(x, w_ref[...], preferred_element_type=jnp.float32).astype(out_ref.dtype)
        for chip in range(pipe_count):
            out_ref[0, which_partner(chip, at_ref[1], pipe_count)] = y[chip * rows : (chip + 1) * rows]

    return call(
        kernel,
        "base_product",
        VMEM_MOST,
        grid_spec=pltpu.PrefetchScalarGridSpec(
            num_scalar_prefetch=1,
            grid=(WIDTH // tile, count),
            in_specs=[
                pl.BlockSpec(
                    (pipe_count, 1, rows, depth),
                    lambda n, s, at: (0, partner(at[2], s + first, tensor_count), 0, 0),
                ),
                pl.BlockSpec((depth, tile), lambda n, s, at: (0, n)),
            ],
            out_specs=pl.BlockSpec((1, pipe_count, rows, tile), lambda n, s, at: (s, 0, 0, n)),
        ),
        out_shape=jax.ShapeDtypeStruct((count, pipe_count, rows, WIDTH), jnp.bfloat16),
    )(at, tokens, weight)


def low_product(at, tokens, down, pipe_count, tensor_count):
    tok_dev, depth = tokens.shape
    down_rows = depth // down.shape[0]
    rows = tok_dev // (pipe_count * tensor_count)

    def kernel(at_ref, x_ref, a_ref, out_ref):
        for block in range(tok_dev // BLOCK):
            a = a_ref[:, block * down_rows : (block + 1) * down_rows].reshape(depth, RANKS)
            x = x_ref[block * BLOCK : (block + 1) * BLOCK]
            y = jnp.dot(x, a, preferred_element_type=jnp.float32).astype(out_ref.dtype)
            for part in range(BLOCK // rows):
                chip, core = divmod(block * (BLOCK // rows) + part, tensor_count)
                core = which_partner(core, at_ref[2], tensor_count)
                out_ref[core, chip] = y[part * rows : (part + 1) * rows]

    return call(
        kernel,
        "low_product",
        in_specs=[SMEM, VMEM, VMEM],
        out_specs=VMEM,
        out_shape=jax.ShapeDtypeStruct((tensor_count, pipe_count, rows, RANKS), jnp.bfloat16),
    )(at, tokens, down)


def cotangent_product(at, cot_pieces, weight):
    tensor_count, pipe_count = len(cot_pieces), len(cot_pieces[0])
    rows = cot_pieces[0][0].shape[0]
    depth = weight.shape[0]
    tok_dev = tensor_count * pipe_count * rows
    tile = 256 if depth % 256 == 0 else depth
    order = [(s, k) for s in range(tensor_count) for k in range(pipe_count)]

    def kernel(at_ref, w_ref, *rest):
        cot_refs, (out_ref, cot, sems) = rest[: len(order)], rest[len(order) :]

        @pl.when(pl.program_id(0) == 0)
        def _():
            copies = []
            for i, (s, k) in enumerate(order):
                chip = came_from(at_ref[1], k, pipe_count)
                core = came_from(at_ref[2], s, tensor_count)
                first = pl.multiple_of((chip * tensor_count + core) * rows, rows)
                copies.append(
                    pltpu.make_async_copy(cot_refs[i], cot.at[pl.ds(first, rows)], sems.at[i])
                )
            for copy in copies:
                copy.start()
            for copy in copies:
                copy.wait()

        out_ref[...] = lax.dot_general(
            cot[...], w_ref[...], LAST_BOTH, preferred_element_type=jnp.float32
        )

    return call(
        kernel,
        "cotangent_product",
        VMEM_MOST,
        grid=(depth // tile,),
        in_specs=[SMEM, pl.BlockSpec((tile, WIDTH), lambda n: (n, 0))] + [ANY] * len(order),
        out_specs=pl.BlockSpec((tok_dev, tile), lambda n: (0, n)),
        out_shape=jax.ShapeDtypeStruct((tok_dev, depth), jnp.float32),
        scratch_shapes=[
            pltpu.VMEM((tok_dev, WIDTH), jnp.bfloat16),
            pltpu.SemaphoreType.DMA((len(order),)),
        ],
    )(at, weight, *[cot_pieces[s][k] for s, k in order])


def input_gradient(at, base, grad_pieces, down):
    data_count, all_rows, _ = down.shape
    tensor_count = len(grad_pieces)
    pipe_count, rows, _ = grad_pieces[0].shape
    tok_dev, depth = base.shape
    down_rows = depth // data_count
    planes = next((n for n in range(1, data_count) if n * down_rows % 256 == 0), data_count)
    tile = planes * down_rows

    def kernel(at_ref, base_ref, a_ref, *rest):
        grad_refs, (out_ref, grad) = rest[:tensor_count], rest[tensor_count:]

        @pl.when(pl.program_id(0) == 0)
        def _():
            for s in range(tensor_count):
                core = came_from(at_ref[2], s, tensor_count)
                for k in range(pipe_count):
                    chip = came_from(at_ref[1], k, pipe_count)
                    first = pl.multiple_of((chip * tensor_count + core) * rows, rows)
                    grad[pl.ds(first, rows)] = grad_refs[s][k]

        for block in range(tok_dev // BLOCK):
            here = slice(block * BLOCK, (block + 1) * BLOCK)
            a = a_ref[:, block * down_rows : (block + 1) * down_rows].reshape(tile, RANKS)
            low = lax.dot_general(grad[here], a, LAST_BOTH, preferred_element_type=jnp.float32)
            out_ref[here] = (base_ref[here] + low).astype(out_ref.dtype)

    return call(
        kernel,
        "input_gradient",
        grid=(data_count // planes,),
        in_specs=[
            SMEM,
            pl.BlockSpec((tok_dev, tile), lambda n: (0, n)),
            pl.BlockSpec((planes, all_rows, RANKS), lambda n: (n, 0, 0)),
        ]
        + [VMEM] * tensor_count,
        out_specs=pl.BlockSpec((tok_dev, tile), lambda n: (0, n)),
        out_shape=jax.ShapeDtypeStruct((tok_dev, depth), jnp.bfloat16),
        scratch_shapes=[pltpu.VMEM((tok_dev, RANKS), jnp.bfloat16)],
    )(at, base, down, *grad_pieces)


def grad_down_pieces(at, x_features, grad_pieces):
    data_count, down_rows, tok_dev = x_features.shape
    tensor_count = len(grad_pieces)
    pipe_count, rows, _ = grad_pieces[0].shape
    blocks_dev = tok_dev // BLOCK

    def kernel(at_ref, x_ref, *rest):
        grad_refs, (out_ref, grad) = rest[:tensor_count], rest[tensor_count:]

        @pl.when(pl.program_id(0) == 0)
        def _():
            for s in range(tensor_count):
                core = came_from(at_ref[2], s, tensor_count)
                for k in range(pipe_count):
                    chip = came_from(at_ref[1], k, pipe_count)
                    first = pl.multiple_of((chip * tensor_count + core) * rows, rows)
                    grad[pl.ds(first, rows)] = grad_refs[s][k]

        for block in range(blocks_dev):
            here = slice(block * BLOCK, (block + 1) * BLOCK)
            out_ref[0, block] = jnp.dot(
                x_ref[0, :, here], grad[here], preferred_element_type=jnp.float32
            ).astype(out_ref.dtype)

    return call(
        kernel,
        "grad_down_pieces",
        grid=(data_count,),
        in_specs=[SMEM, pl.BlockSpec((1, down_rows, tok_dev), lambda d: (d, 0, 0))]
        + [VMEM] * tensor_count,
        out_specs=pl.BlockSpec((1, blocks_dev, down_rows, RANKS), lambda d: (d, 0, 0, 0)),
        out_shape=pltpu.HBM((data_count, blocks_dev, down_rows, RANKS), jnp.bfloat16),
        scratch_shapes=[pltpu.VMEM((tok_dev, RANKS), jnp.bfloat16)],
    )(at, x_features, *grad_pieces)


def grad_down(at, slot_of, slots, pieces):
    data_count, blocks_dev, down_rows, _ = pieces.shape
    parts = 2 if down_rows % 256 == 0 else 1
    part_rows = down_rows // parts

    def kernel(at_ref, piece_ref, out_ref, piece, total, piece_sem, out_sem):
        copies = [
            [
                pltpu.make_async_copy(
                    piece_ref.at[data, block], piece.at[data, block], piece_sem.at[data, block]
                )
                for block in range(blocks_dev)
            ]
            for data in range(data_count)
        ]
        for some in copies:
            for copy in some:
                copy.start()
        total[...] = jnp.zeros(total.shape, total.dtype)
        outs = []
        for part in range(parts):
            here = slice(part * part_rows, (part + 1) * part_rows)
            for data in range(data_count):
                for block in range(blocks_dev):
                    if part == 0:
                        copies[data][block].wait()
                    slot = slot_of(at_ref, data, block)
                    total[part, slot] += piece[data, block, here].astype(total.dtype)
            there = out_ref.at[:, pl.ds(part * part_rows, part_rows)]
            outs.append(pltpu.make_async_copy(total.at[part], there, out_sem.at[part]))
            outs[-1].start()
        for copy in outs:
            copy.wait()

    return call(
        kernel,
        "grad_down",
        VMEM_MOST,
        in_specs=[SMEM, HBM],
        out_specs=HBM,
        out_shape=pltpu.HBM((slots, down_rows, RANKS), jnp.float32),
        scratch_shapes=[
            pltpu.VMEM(pieces.shape, jnp.bfloat16),
            pltpu.VMEM((parts, slots, part_rows, RANKS), jnp.float32),
            pltpu.SemaphoreType.DMA((data_count, blocks_dev)),
            pltpu.SemaphoreType.DMA((parts,)),
        ],
    )(at, pieces)


def grad_up_pieces(at, low_pieces, cot_pieces, data_count, up_rows):
    tensor_count, pipe_count = len(cot_pieces), len(cot_pieces[0])
    group_count = tensor_count * pipe_count
    rows = cot_pieces[0][0].shape[0]
    cols = WIDTH // group_count
    tok_dev = group_count * rows
    blocks_dev = tok_dev // BLOCK
    group_half = group_count // 2
    order = [(s, k) for s in range(tensor_count) for k in range(pipe_count)]
    pieces = [cot_pieces[s][k] for s, k in order]
    in_kernel = cols % 128 == 0
    if not in_kernel:
        first_col = (at[1] * tensor_count + at[2]) * cols
        pieces = [lax.dynamic_slice_in_dim(piece, first_col, cols, 1) for piece in pieces]

    def kernel(at_ref, *rest):
        low_refs, rest = rest[:tensor_count], rest[tensor_count:]
        cot_refs, (out_ref, low, cot, sems) = rest[: len(order)], rest[len(order) :]
        my_group = at_ref[1] * tensor_count + at_ref[2]
        copies = []
        for i, (s, k) in enumerate(order):
            core = came_from(at_ref[2], s, tensor_count)
            chip = came_from(at_ref[1], k, pipe_count)
            first = pl.multiple_of((chip * tensor_count + core) * rows, rows)
            piece = cot_refs[i]
            if in_kernel:
                piece = piece.at[:, pl.ds(pl.multiple_of(my_group * cols, cols), cols)]
            copies.append(pltpu.make_async_copy(piece, cot.at[pl.ds(first, rows)], sems.at[i]))
        for copy in copies:
            copy.start()
        for s in range(tensor_count):
            core = came_from(at_ref[2], s, tensor_count)
            for k in range(pipe_count):
                first = pl.multiple_of((k * tensor_count + core) * rows, rows)
                low[pl.ds(first, rows)] = low_refs[s][k]
        for copy in copies:
            copy.wait()
        for block in range(blocks_dev):
            at = slice(block * BLOCK, (block + 1) * BLOCK)
            both = lax.dot_general(low[at], cot[at], FIRST_BOTH, preferred_element_type=jnp.float32)
            half = jnp.where(my_group < group_half, both[:ADAPTER_RANK], both[ADAPTER_RANK:])
            half = half.astype(out_ref.dtype)
            for data in range(data_count):
                k = wrap(data - at_ref[0], data_count)
                out_ref[k, block] = half[data * up_rows : (data + 1) * up_rows]

    return call(
        kernel,
        "grad_up_pieces",
        in_specs=[SMEM] + [VMEM] * tensor_count + [ANY] * len(order),
        out_specs=VMEM,
        out_shape=jax.ShapeDtypeStruct((data_count, blocks_dev, up_rows, cols), jnp.bfloat16),
        scratch_shapes=[
            pltpu.VMEM((tok_dev, RANKS), jnp.bfloat16),
            pltpu.VMEM((tok_dev, cols), jnp.bfloat16),
            pltpu.SemaphoreType.DMA((len(order),)),
        ],
    )(at, *low_pieces, *pieces)


def grad_up(at, slot_of, slots, pieces):
    data_count = len(pieces)
    blocks_dev, up_rows, cols = pieces[0].shape

    def kernel(at_ref, *rest):
        piece_refs, out_ref = rest[:data_count], rest[data_count]
        out_ref[...] = jnp.zeros(out_ref.shape, out_ref.dtype)
        for k in range(data_count):
            data = wrap(at_ref[0] - k, data_count)
            for block in range(blocks_dev):
                slot = slot_of(at_ref, data, block)
                out_ref[slot] += piece_refs[k][block].astype(out_ref.dtype)

    return call(
        kernel,
        "grad_up",
        in_specs=[SMEM] + [VMEM] * data_count,
        out_specs=VMEM,
        out_shape=jax.ShapeDtypeStruct((slots, up_rows, cols), jnp.float32),
    )(at, *pieces)


def own_rows(at, up, cotangent):
    data_count = len(up)
    rows = cotangent.shape[0]

    def kernel(at_ref, cot_ref, *rest):
        up_refs, (b_ref, grad_ref) = rest[:data_count], rest[data_count:]
        pieces = []
        for data in range(data_count):
            came = wrap(at_ref[0] - data, data_count)
            piece = up_refs[0][...]
            for k in range(1, data_count):
                piece = jnp.where(came == k, up_refs[k][...], piece)
            pieces.append(piece)
        b = jnp.concatenate(pieces, axis=0)
        b_ref[...] = b
        cot = cot_ref[...]
        grad_ref[...] = jnp.concatenate(
            [
                lax.dot_general(cot[:, half], b[:, half], LAST_BOTH, preferred_element_type=jnp.float32)
                for half in (slice(0, KEY_WIDTH), slice(KEY_WIDTH, WIDTH))
            ],
            axis=1,
        ).astype(grad_ref.dtype)

    return call(
        kernel,
        "own_rows",
        in_specs=[SMEM, VMEM] + [VMEM] * data_count,
        out_specs=(VMEM, VMEM),
        out_shape=(
            jax.ShapeDtypeStruct((ADAPTER_RANK, WIDTH), jnp.bfloat16),
            jax.ShapeDtypeStruct((rows, RANKS), jnp.bfloat16),
        ),
    )(at, cotangent, *up)


def keys_and_values(at, base_pieces, low_sum, b_own):
    rows = base_pieces[0].shape[0]
    count = len(base_pieces)

    def kernel(at_ref, low_ref, b_ref, *rest):
        base_refs, out_ref = rest[:count], rest[count]
        low = low_ref[at_ref[1]]
        for first, ranks in ((0, slice(0, ADAPTER_RANK)), (KEY_WIDTH, slice(ADAPTER_RANK, RANKS))):
            at = slice(first, first + KEY_WIDTH)
            y = jnp.dot(low[:, ranks], b_ref[:, at], preferred_element_type=jnp.float32)
            for base_ref in base_refs:
                y += base_ref[:, at].astype(jnp.float32)
            out_ref[:, at] = y.astype(out_ref.dtype)

    return call(
        kernel,
        "keys_and_values",
        in_specs=[SMEM, VMEM, VMEM] + [VMEM] * count,
        out_specs=VMEM,
        out_shape=jax.ShapeDtypeStruct((rows, WIDTH), jnp.bfloat16),
    )(at, low_sum, b_own, *base_pieces)


def body(
    tokens, key_value_weight, adapter_down, adapter_up, tenant_of_block, slot_of_tenant, cotangent
):
    data_count = lax.axis_size("dp")
    pipe_count = lax.axis_size("pipe")
    tensor_count = lax.axis_size("tensor")
    group_count = pipe_count * tensor_count
    at_data, at_pipe, at_tensor = (lax.axis_index(a) for a in ("dp", "pipe", "tensor"))
    my_group = at_pipe * tensor_count + at_tensor
    tok_dev, feature_count = tokens.shape
    blocks_dev = tok_dev // BLOCK
    rows = tok_dev // group_count
    down_rows = adapter_down.shape[1]
    up_rows = adapter_up.shape[1]
    slots = adapter_down.shape[0]
    blocks = tenant_of_block.shape[0]

    at = jnp.stack([at_data, at_pipe, at_tensor]).astype(jnp.int32)
    at = jnp.concatenate([at, tenant_of_block, slot_of_tenant])

    def slot_of(at_ref, data, block):
        return at_ref[3 + blocks + at_ref[3 + data * blocks_dev + block]]

    b_send, a_send = pick(tenant_of_block, slot_of_tenant, adapter_down, adapter_up, rows)
    b_came = [b_send[0]] + [shift(b_send[k], "dp", k) for k in range(1, data_count)]
    b_own, grad_rows = own_rows(at, b_came, cotangent)

    a_send, b_came = lax.optimization_barrier((a_send, b_came))
    a_recv = lax.all_to_all(a_send, "dp", 0, 0, tiled=True)

    behind, cot_later, a_send = lax.optimization_barrier((tokens, cotangent, a_send))
    cot_chips, base_tokens, x_tokens = gather_chips(cotangent, cot_later, behind)
    cot_chips = [cotangent] + cot_chips

    tokens_by_group = base_tokens.reshape(pipe_count, tensor_count, rows, feature_count)
    base_send = base_product(at, tokens_by_group, key_value_weight, 1, tensor_count - 1)
    base_came = [swap(base_send[s - 1], "tensor", s) for s in range(1, tensor_count)]
    base_keep = base_product(at, tokens_by_group, key_value_weight, 0, 1)[0]
    base_chip = [
        sum([base_keep[k].astype(jnp.float32)] + [b[k].astype(jnp.float32) for b in base_came])
        for k in range(pipe_count)
    ]
    base_chip[1:] = [piece.astype(jnp.bfloat16) for piece in base_chip[1:]]
    base_chip_came = [swap(base_chip[k], "pipe", k) for k in range(1, pipe_count)]

    cot_pieces = [cot_chips] + [
        [swap(piece, "tensor", s) for piece in cot_chips] for s in range(1, tensor_count)
    ]
    input_base = cotangent_product(at, cot_pieces, key_value_weight)

    grad_chips = jnp.stack([grad_rows] + [swap(grad_rows, "pipe", k) for k in range(1, pipe_count)])
    grad_pieces = [grad_chips] + [swap(grad_chips, "tensor", s) for s in range(1, tensor_count)]
    x_features = x_tokens.T.reshape(data_count, down_rows, tok_dev)
    down_send = grad_down_pieces(at, x_features, grad_pieces)

    a_recv, down_send, base_chip_came[:2] = lax.optimization_barrier(
        (a_recv, down_send, base_chip_came[:2])
    )
    down_recv = lax.all_to_all(down_send, "dp", 0, 0, tiled=True)

    low_down, base_chip_came, input_base = lax.optimization_barrier(
        (a_recv, base_chip_came, input_base)
    )
    input_grad = input_gradient(at, input_base, grad_pieces, a_recv)
    low_part = low_product(at, tokens, low_down, pipe_count, tensor_count)
    low_core = sum(
        [low_part[0].astype(jnp.float32)]
        + [swap(low_part[s], "tensor", s).astype(jnp.float32) for s in range(1, tensor_count)]
    ).astype(jnp.bfloat16)
    low_came = [swap(low_core, "pipe", k) for k in range(1, pipe_count)]
    low_sum = sum([piece.astype(jnp.float32) for piece in [low_core] + low_came])
    low_sum = low_sum.astype(jnp.bfloat16)
    low_pieces = [low_sum] + [swap(low_sum, "tensor", s) for s in range(1, tensor_count)]
    key_value = keys_and_values(at, base_chip[:1] + base_chip_came, low_sum, b_own)

    up_pieces = grad_up_pieces(at, low_pieces, cot_pieces, data_count, up_rows)
    up_came = [up_pieces[0]] + [shift(up_pieces[k], "dp", k) for k in range(1, data_count)]
    grad_a = grad_down(at, slot_of, slots, down_recv)
    up_came, grad_a = lax.optimization_barrier((up_came, grad_a))
    grad_b = grad_up(at, slot_of, slots, up_came)
    return (key_value, input_grad, grad_a, grad_b)


def solution(mesh):
    atd = (
        P("dp", ("pipe", "tensor")),
        P(("pipe", "tensor"), None),
        P(None, ("pipe", "tensor", "dp"), None),
        P(None, "dp", None),
        P(),
        P(),
        P(("dp", "pipe", "tensor"), None),
    )
    return jax.shard_map(
        body,
        mesh=mesh,
        in_specs=atd,
        out_specs=(
            P(("dp", "pipe", "tensor"), None),
            P("dp", ("pipe", "tensor")),
            P(None, ("pipe", "tensor", "dp"), None),
            P(None, "dp", ("pipe", "tensor")),
        ),
        check_vma=False,
    )
```

```python
import jax
import jax.numpy as jnp
from jax import lax
from jax.experimental import pallas as pl
from jax.experimental.pallas import tpu as pltpu
from jax.sharding import PartitionSpec as P

KEY_WIDTH = 1024
ADAPTER_RANK = 64
BLOCK = 128
RANKS = 2 * ADAPTER_RANK
WIDTH = 2 * KEY_WIDTH
VMEM_LIMIT = 24 * 1024 * 1024
VMEM_MOST = 60 * 1024 * 1024
LAST_BOTH = (((1,), (1,)), ((), ()))
FIRST_BOTH = (((0,), (0,)), ((), ()))
SMEM = pl.BlockSpec(memory_space=pltpu.SMEM)
VMEM = pl.BlockSpec(memory_space=pltpu.VMEM)
HBM = pl.BlockSpec(memory_space=pltpu.HBM)
ANY = pl.BlockSpec(memory_space=pl.ANY)


def call(kernel, name, vmem=VMEM_LIMIT, **more):
    return pl.pallas_call(
        kernel,
        compiler_params=pltpu.CompilerParams(vmem_limit_bytes=vmem),
        cost_estimate=pl.CostEstimate(flops=1024, bytes_accessed=1024, transcendentals=0),
        name=name,
        **more,
    )


def wrap(index, count):
    return lax.rem(index + 2 * count, count)


def shift(piece, axis, k):
    count = lax.axis_size(axis)
    return lax.ppermute(piece, axis, [(i, (i + k) % count) for i in range(count)])


def paired(count):
    return count & (count - 1) == 0


def partner(index, k, count):
    return index ^ k if paired(count) else (index + k) % count


def came_from(index, k, count):
    return index ^ k if paired(count) else wrap(index - k, count)


def which_partner(other, index, count):
    return other ^ index if paired(count) else wrap(other - index, count)


def swap(piece, axis, k):
    count = lax.axis_size(axis)
    return lax.ppermute(piece, axis, [(i, partner(i, k, count)) for i in range(count)])


def gather_chips(piece, behind):
    count = lax.axis_size("pipe")
    in_halves = count == 4 and piece.shape[0] % 32 == 0
    came = [swap(piece, "pipe", k) for k in range(1, 3 if in_halves else count)]
    came, one, two = lax.optimization_barrier((came, behind, behind))
    if in_halves:
        half = piece.shape[0] // 2
        third = [swap(came[1][:half], "pipe", 1), swap(came[0][half:], "pipe", 2)]
        came = came + [jnp.concatenate(third)]
    return came, one, two


def pick(tenant_of_block, slot_of_tenant, adapter_down, adapter_up, group_rows):
    data_count = lax.axis_size("dp")
    blocks_dev = tenant_of_block.shape[0] // data_count
    down_rows, ranks = adapter_down.shape[1:]
    used = blocks_dev * down_rows

    def kernel(tenant_ref, slot_ref, down_ref, up_ref, *rest):
        up_refs, (out_ref, rows, up_sem, down_sem, out_sem) = rest[:data_count], rest[data_count:]
        own_block = lax.axis_index(("pipe", "tensor")) * group_rows // BLOCK
        ups, downs, outs = [], [], []
        for k in range(data_count):
            data = wrap(lax.axis_index("dp") + k, data_count)
            slot = slot_ref[tenant_ref[data * blocks_dev + own_block]]
            ups.append(pltpu.make_async_copy(up_ref.at[slot], up_refs[k], up_sem.at[k]))
            ups[-1].start()
        for data in range(data_count):
            downs.append([])
            for block in range(blocks_dev):
                here = rows.at[data, pl.ds(block * down_rows, down_rows)]
                slot = slot_ref[tenant_ref[data * blocks_dev + block]]
                downs[data].append(
                    pltpu.make_async_copy(down_ref.at[slot], here, down_sem.at[data, block])
                )
                downs[data][-1].start()
            outs.append(pltpu.make_async_copy(rows.at[data], out_ref.at[data], out_sem.at[data]))
        for data in range(data_count):
            for copy in downs[data]:
                copy.wait()
            outs[data].start()
        for copy in ups + outs:
            copy.wait()

    up_shape = jax.ShapeDtypeStruct(adapter_up.shape[1:], adapter_up.dtype)
    out = call(
        kernel,
        "pick_rows",
        VMEM_MOST,
        out_shape=(up_shape,) * data_count
        + (pltpu.HBM((data_count, used, ranks), adapter_down.dtype),),
        in_specs=[SMEM, SMEM, HBM, HBM],
        out_specs=(VMEM,) * data_count + (HBM,),
        scratch_shapes=[
            pltpu.VMEM((data_count, used, ranks), adapter_down.dtype),
            pltpu.SemaphoreType.DMA((data_count,)),
            pltpu.SemaphoreType.DMA((data_count, blocks_dev)),
            pltpu.SemaphoreType.DMA((data_count,)),
        ],
    )(tenant_of_block, slot_of_tenant, adapter_down, adapter_up)
    return out[:data_count], out[data_count]


def base_product(at, tokens, weight, first, count):
    pipe_count, tensor_count, rows, depth = tokens.shape
    tile = 1024

    def kernel(at_ref, x_ref, w_ref, out_ref):
        x = x_ref[...].reshape(pipe_count * rows, depth)
        y = jnp.dot(x, w_ref[...], preferred_element_type=jnp.float32).astype(out_ref.dtype)
        for chip in range(pipe_count):
            out_ref[0, which_partner(chip, at_ref[1], pipe_count)] = y[chip * rows : (chip + 1) * rows]

    return call(
        kernel,
        "base_product",
        grid_spec=pltpu.PrefetchScalarGridSpec(
            num_scalar_prefetch=1,
            grid=(WIDTH // tile, count),
            in_specs=[
                pl.BlockSpec(
                    (pipe_count, 1, rows, depth),
                    lambda n, s, at: (0, partner(at[2], s + first, tensor_count), 0, 0),
                ),
                pl.BlockSpec((depth, tile), lambda n, s, at: (0, n)),
            ],
            out_specs=pl.BlockSpec((1, pipe_count, rows, tile), lambda n, s, at: (s, 0, 0, n)),
        ),
        out_shape=jax.ShapeDtypeStruct((count, pipe_count, rows, WIDTH), jnp.bfloat16),
    )(at, tokens, weight)


def low_product(at, tokens, down, pipe_count, tensor_count):
    tok_dev, depth = tokens.shape
    down_rows = depth // down.shape[0]
    rows = tok_dev // (pipe_count * tensor_count)

    def kernel(at_ref, x_ref, a_ref, out_ref):
        for block in range(tok_dev // BLOCK):
            a = a_ref[:, block * down_rows : (block + 1) * down_rows].reshape(depth, RANKS)
            x = x_ref[block * BLOCK : (block + 1) * BLOCK]
            y = jnp.dot(x, a, preferred_element_type=jnp.float32).astype(out_ref.dtype)
            for part in range(BLOCK // rows):
                chip, core = divmod(block * (BLOCK // rows) + part, tensor_count)
                core = which_partner(core, at_ref[2], tensor_count)
                out_ref[core, chip] = y[part * rows : (part + 1) * rows]

    return call(
        kernel,
        "low_product",
        in_specs=[SMEM, VMEM, VMEM],
        out_specs=VMEM,
        out_shape=jax.ShapeDtypeStruct((tensor_count, pipe_count, rows, RANKS), jnp.bfloat16),
    )(at, tokens, down)


def cotangent_product(at, cot_pieces, weight):
    tensor_count, pipe_count = len(cot_pieces), len(cot_pieces[0])
    rows = cot_pieces[0][0].shape[0]
    depth = weight.shape[0]
    tok_dev = tensor_count * pipe_count * rows
    tile = 256 if depth % 256 == 0 else depth
    order = [(s, k) for s in range(tensor_count) for k in range(pipe_count)]

    def kernel(at_ref, w_ref, *rest):
        cot_refs, (out_ref, cot, sems) = rest[: len(order)], rest[len(order) :]

        @pl.when(pl.program_id(0) == 0)
        def _():
            copies = []
            for i, (s, k) in enumerate(order):
                chip = came_from(at_ref[1], k, pipe_count)
                core = came_from(at_ref[2], s, tensor_count)
                first = pl.multiple_of((chip * tensor_count + core) * rows, rows)
                copies.append(
                    pltpu.make_async_copy(cot_refs[i], cot.at[pl.ds(first, rows)], sems.at[i])
                )
            for copy in copies:
                copy.start()
            for copy in copies:
                copy.wait()

        out_ref[...] = lax.dot_general(
            cot[...], w_ref[...], LAST_BOTH, preferred_element_type=jnp.float32
        )

    return call(
        kernel,
        "cotangent_product",
        grid=(depth // tile,),
        in_specs=[SMEM, pl.BlockSpec((tile, WIDTH), lambda n: (n, 0))] + [ANY] * len(order),
        out_specs=pl.BlockSpec((tok_dev, tile), lambda n: (0, n)),
        out_shape=jax.ShapeDtypeStruct((tok_dev, depth), jnp.float32),
        scratch_shapes=[
            pltpu.VMEM((tok_dev, WIDTH), jnp.bfloat16),
            pltpu.SemaphoreType.DMA((len(order),)),
        ],
    )(at, weight, *[cot_pieces[s][k] for s, k in order])


def input_gradient(at, base, grad_pieces, down):
    data_count, all_rows, _ = down.shape
    tensor_count = len(grad_pieces)
    pipe_count, rows, _ = grad_pieces[0].shape
    tok_dev, depth = base.shape
    down_rows = depth // data_count
    planes = next((n for n in range(1, data_count) if n * down_rows % 256 == 0), data_count)
    tile = planes * down_rows

    def kernel(at_ref, base_ref, a_ref, *rest):
        grad_refs, (out_ref, grad) = rest[:tensor_count], rest[tensor_count:]

        @pl.when(pl.program_id(0) == 0)
        def _():
            for s in range(tensor_count):
                core = came_from(at_ref[2], s, tensor_count)
                for k in range(pipe_count):
                    chip = came_from(at_ref[1], k, pipe_count)
                    first = pl.multiple_of((chip * tensor_count + core) * rows, rows)
                    grad[pl.ds(first, rows)] = grad_refs[s][k]

        for block in range(tok_dev // BLOCK):
            here = slice(block * BLOCK, (block + 1) * BLOCK)
            a = a_ref[:, block * down_rows : (block + 1) * down_rows].reshape(tile, RANKS)
            low = lax.dot_general(grad[here], a, LAST_BOTH, preferred_element_type=jnp.float32)
            out_ref[here] = (base_ref[here] + low).astype(out_ref.dtype)

    return call(
        kernel,
        "input_gradient",
        grid=(data_count // planes,),
        in_specs=[
            SMEM,
            pl.BlockSpec((tok_dev, tile), lambda n: (0, n)),
            pl.BlockSpec((planes, all_rows, RANKS), lambda n: (n, 0, 0)),
        ]
        + [VMEM] * tensor_count,
        out_specs=pl.BlockSpec((tok_dev, tile), lambda n: (0, n)),
        out_shape=jax.ShapeDtypeStruct((tok_dev, depth), jnp.bfloat16),
        scratch_shapes=[pltpu.VMEM((tok_dev, RANKS), jnp.bfloat16)],
    )(at, base, down, *grad_pieces)


def grad_down_pieces(at, x_features, grad_pieces):
    data_count, down_rows, tok_dev = x_features.shape
    tensor_count = len(grad_pieces)
    pipe_count, rows, _ = grad_pieces[0].shape
    blocks_dev = tok_dev // BLOCK

    def kernel(at_ref, x_ref, *rest):
        grad_refs, (out_ref, grad) = rest[:tensor_count], rest[tensor_count:]

        @pl.when(pl.program_id(0) == 0)
        def _():
            for s in range(tensor_count):
                core = came_from(at_ref[2], s, tensor_count)
                for k in range(pipe_count):
                    chip = came_from(at_ref[1], k, pipe_count)
                    first = pl.multiple_of((chip * tensor_count + core) * rows, rows)
                    grad[pl.ds(first, rows)] = grad_refs[s][k]

        for block in range(blocks_dev):
            here = slice(block * BLOCK, (block + 1) * BLOCK)
            out_ref[0, block] = jnp.dot(
                x_ref[0, :, here], grad[here], preferred_element_type=jnp.float32
            ).astype(out_ref.dtype)

    return call(
        kernel,
        "grad_down_pieces",
        grid=(data_count,),
        in_specs=[SMEM, pl.BlockSpec((1, down_rows, tok_dev), lambda d: (d, 0, 0))]
        + [VMEM] * tensor_count,
        out_specs=pl.BlockSpec((1, blocks_dev, down_rows, RANKS), lambda d: (d, 0, 0, 0)),
        out_shape=pltpu.HBM((data_count, blocks_dev, down_rows, RANKS), jnp.bfloat16),
        scratch_shapes=[pltpu.VMEM((tok_dev, RANKS), jnp.bfloat16)],
    )(at, x_features, *grad_pieces)


def grad_down(at, slot_of, slots, pieces):
    data_count, blocks_dev, down_rows, _ = pieces.shape
    parts = 2 if down_rows % 256 == 0 else 1
    part_rows = down_rows // parts

    def kernel(at_ref, piece_ref, out_ref, piece, total, piece_sem, out_sem):
        copies = [
            [
                pltpu.make_async_copy(
                    piece_ref.at[data, block], piece.at[data, block], piece_sem.at[data, block]
                )
                for block in range(blocks_dev)
            ]
            for data in range(data_count)
        ]
        for some in copies:
            for copy in some:
                copy.start()
        total[...] = jnp.zeros(total.shape, total.dtype)
        outs = []
        for part in range(parts):
            here = slice(part * part_rows, (part + 1) * part_rows)
            for data in range(data_count):
                for block in range(blocks_dev):
                    if part == 0:
                        copies[data][block].wait()
                    slot = slot_of(at_ref, data, block)
                    total[part, slot] += piece[data, block, here].astype(total.dtype)
            there = out_ref.at[:, pl.ds(part * part_rows, part_rows)]
            outs.append(pltpu.make_async_copy(total.at[part], there, out_sem.at[part]))
            outs[-1].start()
        for copy in outs:
            copy.wait()

    return call(
        kernel,
        "grad_down",
        VMEM_MOST,
        in_specs=[SMEM, HBM],
        out_specs=HBM,
        out_shape=pltpu.HBM((slots, down_rows, RANKS), jnp.float32),
        scratch_shapes=[
            pltpu.VMEM(pieces.shape, jnp.bfloat16),
            pltpu.VMEM((parts, slots, part_rows, RANKS), jnp.float32),
            pltpu.SemaphoreType.DMA((data_count, blocks_dev)),
            pltpu.SemaphoreType.DMA((parts,)),
        ],
    )(at, pieces)


def grad_up_pieces(at, low_pieces, cot_pieces, data_count, up_rows):
    tensor_count, pipe_count = len(cot_pieces), len(cot_pieces[0])
    group_count = tensor_count * pipe_count
    rows = cot_pieces[0][0].shape[0]
    cols = WIDTH // group_count
    tok_dev = group_count * rows
    blocks_dev = tok_dev // BLOCK
    group_half = group_count // 2
    order = [(s, k) for s in range(tensor_count) for k in range(pipe_count)]
    pieces = [cot_pieces[s][k] for s, k in order]
    in_kernel = cols % 128 == 0
    if not in_kernel:
        first_col = (at[1] * tensor_count + at[2]) * cols
        pieces = [lax.dynamic_slice_in_dim(piece, first_col, cols, 1) for piece in pieces]

    def kernel(at_ref, *rest):
        low_refs, rest = rest[:tensor_count], rest[tensor_count:]
        cot_refs, (out_ref, low, cot, sems) = rest[: len(order)], rest[len(order) :]
        my_group = at_ref[1] * tensor_count + at_ref[2]
        copies = []
        for i, (s, k) in enumerate(order):
            core = came_from(at_ref[2], s, tensor_count)
            chip = came_from(at_ref[1], k, pipe_count)
            first = pl.multiple_of((chip * tensor_count + core) * rows, rows)
            piece = cot_refs[i]
            if in_kernel:
                piece = piece.at[:, pl.ds(pl.multiple_of(my_group * cols, cols), cols)]
            copies.append(pltpu.make_async_copy(piece, cot.at[pl.ds(first, rows)], sems.at[i]))
        for copy in copies:
            copy.start()
        for s in range(tensor_count):
            core = came_from(at_ref[2], s, tensor_count)
            for k in range(pipe_count):
                first = pl.multiple_of((k * tensor_count + core) * rows, rows)
                low[pl.ds(first, rows)] = low_refs[s][k]
        for copy in copies:
            copy.wait()
        for block in range(blocks_dev):
            at = slice(block * BLOCK, (block + 1) * BLOCK)
            both = lax.dot_general(low[at], cot[at], FIRST_BOTH, preferred_element_type=jnp.float32)
            half = jnp.where(my_group < group_half, both[:ADAPTER_RANK], both[ADAPTER_RANK:])
            half = half.astype(out_ref.dtype)
            for data in range(data_count):
                k = wrap(data - at_ref[0], data_count)
                out_ref[k, block] = half[data * up_rows : (data + 1) * up_rows]

    return call(
        kernel,
        "grad_up_pieces",
        in_specs=[SMEM] + [VMEM] * tensor_count + [ANY] * len(order),
        out_specs=VMEM,
        out_shape=jax.ShapeDtypeStruct((data_count, blocks_dev, up_rows, cols), jnp.bfloat16),
        scratch_shapes=[
            pltpu.VMEM((tok_dev, RANKS), jnp.bfloat16),
            pltpu.VMEM((tok_dev, cols), jnp.bfloat16),
            pltpu.SemaphoreType.DMA((len(order),)),
        ],
    )(at, *low_pieces, *pieces)


def grad_up(at, slot_of, slots, pieces):
    data_count = len(pieces)
    blocks_dev, up_rows, cols = pieces[0].shape

    def kernel(at_ref, *rest):
        piece_refs, out_ref = rest[:data_count], rest[data_count]
        out_ref[...] = jnp.zeros(out_ref.shape, out_ref.dtype)
        for k in range(data_count):
            data = wrap(at_ref[0] - k, data_count)
            for block in range(blocks_dev):
                slot = slot_of(at_ref, data, block)
                out_ref[slot] += piece_refs[k][block].astype(out_ref.dtype)

    return call(
        kernel,
        "grad_up",
        in_specs=[SMEM] + [VMEM] * data_count,
        out_specs=VMEM,
        out_shape=jax.ShapeDtypeStruct((slots, up_rows, cols), jnp.float32),
    )(at, *pieces)


def own_rows(at, up, cotangent):
    data_count = len(up)
    rows = cotangent.shape[0]

    def kernel(at_ref, cot_ref, *rest):
        up_refs, (b_ref, grad_ref) = rest[:data_count], rest[data_count:]
        pieces = []
        for data in range(data_count):
            came = wrap(at_ref[0] - data, data_count)
            piece = up_refs[0][...]
            for k in range(1, data_count):
                piece = jnp.where(came == k, up_refs[k][...], piece)
            pieces.append(piece)
        b = jnp.concatenate(pieces, axis=0)
        b_ref[...] = b
        cot = cot_ref[...]
        grad_ref[...] = jnp.concatenate(
            [
                lax.dot_general(cot[:, half], b[:, half], LAST_BOTH, preferred_element_type=jnp.float32)
                for half in (slice(0, KEY_WIDTH), slice(KEY_WIDTH, WIDTH))
            ],
            axis=1,
        ).astype(grad_ref.dtype)

    return call(
        kernel,
        "own_rows",
        in_specs=[SMEM, VMEM] + [VMEM] * data_count,
        out_specs=(VMEM, VMEM),
        out_shape=(
            jax.ShapeDtypeStruct((ADAPTER_RANK, WIDTH), jnp.bfloat16),
            jax.ShapeDtypeStruct((rows, RANKS), jnp.bfloat16),
        ),
    )(at, cotangent, *up)


def keys_and_values(at, base_pieces, low_sum, b_own):
    rows = base_pieces[0].shape[0]
    count = len(base_pieces)

    def kernel(at_ref, low_ref, b_ref, *rest):
        base_refs, out_ref = rest[:count], rest[count]
        low = low_ref[at_ref[1]]
        for first, ranks in ((0, slice(0, ADAPTER_RANK)), (KEY_WIDTH, slice(ADAPTER_RANK, RANKS))):
            at = slice(first, first + KEY_WIDTH)
            y = jnp.dot(low[:, ranks], b_ref[:, at], preferred_element_type=jnp.float32)
            for base_ref in base_refs:
                y += base_ref[:, at].astype(jnp.float32)
            out_ref[:, at] = y.astype(out_ref.dtype)

    return call(
        kernel,
        "keys_and_values",
        in_specs=[SMEM, VMEM, VMEM] + [VMEM] * count,
        out_specs=VMEM,
        out_shape=jax.ShapeDtypeStruct((rows, WIDTH), jnp.bfloat16),
    )(at, low_sum, b_own, *base_pieces)


def body(
    tokens, key_value_weight, adapter_down, adapter_up, tenant_of_block, slot_of_tenant, cotangent
):
    data_count = lax.axis_size("dp")
    pipe_count = lax.axis_size("pipe")
    tensor_count = lax.axis_size("tensor")
    group_count = pipe_count * tensor_count
    at_data, at_pipe, at_tensor = (lax.axis_index(a) for a in ("dp", "pipe", "tensor"))
    my_group = at_pipe * tensor_count + at_tensor
    tok_dev, feature_count = tokens.shape
    blocks_dev = tok_dev // BLOCK
    rows = tok_dev // group_count
    down_rows = adapter_down.shape[1]
    up_rows = adapter_up.shape[1]
    slots = adapter_down.shape[0]
    blocks = tenant_of_block.shape[0]

    at = jnp.stack([at_data, at_pipe, at_tensor]).astype(jnp.int32)
    at = jnp.concatenate([at, tenant_of_block, slot_of_tenant])

    def slot_of(at_ref, data, block):
        return at_ref[3 + blocks + at_ref[3 + data * blocks_dev + block]]

    b_send, a_send = pick(tenant_of_block, slot_of_tenant, adapter_down, adapter_up, rows)
    b_came = [b_send[0]] + [shift(b_send[k], "dp", k) for k in range(1, data_count)]
    b_own, grad_rows = own_rows(at, b_came, cotangent)

    a_send, grad_rows = lax.optimization_barrier((a_send, grad_rows))
    a_recv = lax.all_to_all(a_send, "dp", 0, 0, tiled=True)

    behind, a_send = lax.optimization_barrier((tokens, a_send))
    cot_chips, base_tokens, x_tokens = gather_chips(cotangent, behind)
    cot_chips = [cotangent] + cot_chips

    tokens_by_group = base_tokens.reshape(pipe_count, tensor_count, rows, feature_count)
    base_send = base_product(at, tokens_by_group, key_value_weight, 1, tensor_count - 1)
    base_came = [swap(base_send[s - 1], "tensor", s) for s in range(1, tensor_count)]
    base_keep = base_product(at, tokens_by_group, key_value_weight, 0, 1)[0]
    base_chip = [
        sum([base_keep[k].astype(jnp.float32)] + [b[k].astype(jnp.float32) for b in base_came])
        for k in range(pipe_count)
    ]
    base_chip[1:] = [piece.astype(jnp.bfloat16) for piece in base_chip[1:]]
    base_chip_came = [swap(base_chip[k], "pipe", k) for k in range(1, pipe_count)]

    cot_pieces = [cot_chips] + [
        [swap(piece, "tensor", s) for piece in cot_chips] for s in range(1, tensor_count)
    ]
    input_base = cotangent_product(at, cot_pieces, key_value_weight)

    grad_chips = jnp.stack([grad_rows] + [swap(grad_rows, "pipe", k) for k in range(1, pipe_count)])
    grad_pieces = [grad_chips] + [swap(grad_chips, "tensor", s) for s in range(1, tensor_count)]
    x_features = x_tokens.T.reshape(data_count, down_rows, tok_dev)
    down_send = grad_down_pieces(at, x_features, grad_pieces)

    a_recv, down_send, input_base, base_chip_came[:2] = lax.optimization_barrier(
        (a_recv, down_send, input_base, base_chip_came[:2])
    )
    down_recv = lax.all_to_all(down_send, "dp", 0, 0, tiled=True)
    input_grad = input_gradient(at, input_base, grad_pieces, a_recv)

    low_down, base_chip_came = lax.optimization_barrier((a_recv, base_chip_came))
    low_part = low_product(at, tokens, low_down, pipe_count, tensor_count)
    low_core = sum(
        [low_part[0].astype(jnp.float32)]
        + [swap(low_part[s], "tensor", s).astype(jnp.float32) for s in range(1, tensor_count)]
    ).astype(jnp.bfloat16)
    low_came = [swap(low_core, "pipe", k) for k in range(1, pipe_count)]
    low_sum = sum([piece.astype(jnp.float32) for piece in [low_core] + low_came])
    low_sum = low_sum.astype(jnp.bfloat16)
    low_pieces = [low_sum] + [swap(low_sum, "tensor", s) for s in range(1, tensor_count)]
    key_value = keys_and_values(at, base_chip[:1] + base_chip_came, low_sum, b_own)

    up_pieces = grad_up_pieces(at, low_pieces, cot_pieces, data_count, up_rows)
    up_came = [up_pieces[0]] + [shift(up_pieces[k], "dp", k) for k in range(1, data_count)]
    grad_a = grad_down(at, slot_of, slots, down_recv)
    up_came, grad_a = lax.optimization_barrier((up_came, grad_a))
    grad_b = grad_up(at, slot_of, slots, up_came)
    return (key_value, input_grad, grad_a, grad_b)


def solution(mesh):
    atd = (
        P("dp", ("pipe", "tensor")),
        P(("pipe", "tensor"), None),
        P(None, ("pipe", "tensor", "dp"), None),
        P(None, "dp", None),
        P(),
        P(),
        P(("dp", "pipe", "tensor"), None),
    )
    return jax.shard_map(
        body,
        mesh=mesh,
        in_specs=atd,
        out_specs=(
            P(("dp", "pipe", "tensor"), None),
            P("dp", ("pipe", "tensor")),
            P(None, ("pipe", "tensor", "dp"), None),
            P(None, "dp", ("pipe", "tensor")),
        ),
        check_vma=False,
    )
```

```python
import jax
import jax.numpy as jnp
from jax import lax
from jax.experimental import pallas as pl
from jax.experimental.pallas import tpu as pltpu
from jax.sharding import PartitionSpec as P

KEY_WIDTH = 1024
ADAPTER_RANK = 64
BLOCK = 128
RANKS = 2 * ADAPTER_RANK
WIDTH = 2 * KEY_WIDTH
VMEM_LIMIT = 24 * 1024 * 1024
VMEM_MOST = 60 * 1024 * 1024
LAST_BOTH = (((1,), (1,)), ((), ()))
FIRST_BOTH = (((0,), (0,)), ((), ()))
SMEM = pl.BlockSpec(memory_space=pltpu.SMEM)
VMEM = pl.BlockSpec(memory_space=pltpu.VMEM)
HBM = pl.BlockSpec(memory_space=pltpu.HBM)
ANY = pl.BlockSpec(memory_space=pl.ANY)


def call(kernel, name, vmem=VMEM_LIMIT, **more):
    return pl.pallas_call(
        kernel,
        compiler_params=pltpu.CompilerParams(vmem_limit_bytes=vmem),
        cost_estimate=pl.CostEstimate(flops=1024, bytes_accessed=1024, transcendentals=0),
        name=name,
        **more,
    )


def wrap(index, count):
    return lax.rem(index + 2 * count, count)


def shift(piece, axis, k):
    count = lax.axis_size(axis)
    return lax.ppermute(piece, axis, [(i, (i + k) % count) for i in range(count)])


def paired(count):
    return count & (count - 1) == 0


def partner(index, k, count):
    return index ^ k if paired(count) else (index + k) % count


def came_from(index, k, count):
    return index ^ k if paired(count) else wrap(index - k, count)


def which_partner(other, index, count):
    return other ^ index if paired(count) else wrap(other - index, count)


def swap(piece, axis, k):
    count = lax.axis_size(axis)
    return lax.ppermute(piece, axis, [(i, partner(i, k, count)) for i in range(count)])


def gather_chips(piece, behind):
    count = lax.axis_size("pipe")
    in_halves = count == 4 and piece.shape[0] % 32 == 0
    came = [swap(piece, "pipe", k) for k in range(1, 3 if in_halves else count)]
    came, one, two = lax.optimization_barrier((came, behind, behind))
    if in_halves:
        half = piece.shape[0] // 2
        third = [swap(came[1][:half], "pipe", 1), swap(came[0][half:], "pipe", 2)]
        came = came + [jnp.concatenate(third)]
    return came, one, two


def pick(tenant_of_block, slot_of_tenant, adapter_down, adapter_up, group_rows):
    data_count = lax.axis_size("dp")
    blocks_dev = tenant_of_block.shape[0] // data_count
    down_rows, ranks = adapter_down.shape[1:]
    used = blocks_dev * down_rows

    def kernel(tenant_ref, slot_ref, down_ref, up_ref, *rest):
        up_refs, (out_ref, rows, up_sem, down_sem, out_sem) = rest[:data_count], rest[data_count:]
        own_block = lax.axis_index(("pipe", "tensor")) * group_rows // BLOCK
        ups, downs, outs = [], [], []
        for k in range(data_count):
            data = wrap(lax.axis_index("dp") + k, data_count)
            slot = slot_ref[tenant_ref[data * blocks_dev + own_block]]
            ups.append(pltpu.make_async_copy(up_ref.at[slot], up_refs[k], up_sem.at[k]))
            ups[-1].start()
        for data in range(data_count):
            downs.append([])
            for block in range(blocks_dev):
                here = rows.at[data, pl.ds(block * down_rows, down_rows)]
                slot = slot_ref[tenant_ref[data * blocks_dev + block]]
                downs[data].append(
                    pltpu.make_async_copy(down_ref.at[slot], here, down_sem.at[data, block])
                )
                downs[data][-1].start()
            outs.append(pltpu.make_async_copy(rows.at[data], out_ref.at[data], out_sem.at[data]))
        for data in range(data_count):
            for copy in downs[data]:
                copy.wait()
            outs[data].start()
        for copy in ups + outs:
            copy.wait()

    up_shape = jax.ShapeDtypeStruct(adapter_up.shape[1:], adapter_up.dtype)
    out = call(
        kernel,
        "pick_rows",
        VMEM_MOST,
        out_shape=(up_shape,) * data_count
        + (pltpu.HBM((data_count, used, ranks), adapter_down.dtype),),
        in_specs=[SMEM, SMEM, HBM, HBM],
        out_specs=(VMEM,) * data_count + (HBM,),
        scratch_shapes=[
            pltpu.VMEM((data_count, used, ranks), adapter_down.dtype),
            pltpu.SemaphoreType.DMA((data_count,)),
            pltpu.SemaphoreType.DMA((data_count, blocks_dev)),
            pltpu.SemaphoreType.DMA((data_count,)),
        ],
    )(tenant_of_block, slot_of_tenant, adapter_down, adapter_up)
    return out[:data_count], out[data_count]


def base_product(at, tokens, weight, first, count, parts):
    pipe_count, tensor_count, rows, depth = tokens.shape
    tile = 1024
    chips = pipe_count // parts

    def kernel(at_ref, x_ref, w_ref, *out_refs):
        x = x_ref[...].reshape(pipe_count * rows, depth)
        y = jnp.dot(x, w_ref[...], preferred_element_type=jnp.float32).astype(out_refs[0].dtype)
        for chip in range(pipe_count):
            k = which_partner(chip, at_ref[1], pipe_count)
            for part, out_ref in enumerate(out_refs):

                @pl.when((k >= part * chips) & (k < (part + 1) * chips))
                def _():
                    out_ref[0, k - part * chips] = y[chip * rows : (chip + 1) * rows]

    out = call(
        kernel,
        "base_product",
        grid_spec=pltpu.PrefetchScalarGridSpec(
            num_scalar_prefetch=1,
            grid=(WIDTH // tile, count),
            in_specs=[
                pl.BlockSpec(
                    (pipe_count, 1, rows, depth),
                    lambda n, s, at: (0, partner(at[2], s + first, tensor_count), 0, 0),
                ),
                pl.BlockSpec((depth, tile), lambda n, s, at: (0, n)),
            ],
            out_specs=(pl.BlockSpec((1, chips, rows, tile), lambda n, s, at: (s, 0, 0, n)),) * parts,
        ),
        out_shape=(jax.ShapeDtypeStruct((count, chips, rows, WIDTH), jnp.bfloat16),) * parts,
    )(at, tokens, weight)
    return out


def low_product(at, tokens, down, pipe_count, tensor_count):
    tok_dev, depth = tokens.shape
    down_rows = depth // down.shape[0]
    rows = tok_dev // (pipe_count * tensor_count)

    def kernel(at_ref, x_ref, a_ref, out_ref):
        for block in range(tok_dev // BLOCK):
            a = a_ref[:, block * down_rows : (block + 1) * down_rows].reshape(depth, RANKS)
            x = x_ref[block * BLOCK : (block + 1) * BLOCK]
            y = jnp.dot(x, a, preferred_element_type=jnp.float32).astype(out_ref.dtype)
            for part in range(BLOCK // rows):
                chip, core = divmod(block * (BLOCK // rows) + part, tensor_count)
                core = which_partner(core, at_ref[2], tensor_count)
                out_ref[core, chip] = y[part * rows : (part + 1) * rows]

    return call(
        kernel,
        "low_product",
        in_specs=[SMEM, VMEM, VMEM],
        out_specs=VMEM,
        out_shape=jax.ShapeDtypeStruct((tensor_count, pipe_count, rows, RANKS), jnp.bfloat16),
    )(at, tokens, down)


def cotangent_product(at, cot_pieces, weight):
    tensor_count, pipe_count = len(cot_pieces), len(cot_pieces[0])
    rows = cot_pieces[0][0].shape[0]
    depth = weight.shape[0]
    tok_dev = tensor_count * pipe_count * rows
    tile = 256 if depth % 256 == 0 else depth
    order = [(s, k) for s in range(tensor_count) for k in range(pipe_count)]

    def kernel(at_ref, w_ref, *rest):
        cot_refs, (out_ref, cot, sems) = rest[: len(order)], rest[len(order) :]

        @pl.when(pl.program_id(0) == 0)
        def _():
            copies = []
            for i, (s, k) in enumerate(order):
                chip = came_from(at_ref[1], k, pipe_count)
                core = came_from(at_ref[2], s, tensor_count)
                first = pl.multiple_of((chip * tensor_count + core) * rows, rows)
                copies.append(
                    pltpu.make_async_copy(cot_refs[i], cot.at[pl.ds(first, rows)], sems.at[i])
                )
            for copy in copies:
                copy.start()
            for copy in copies:
                copy.wait()

        out_ref[...] = lax.dot_general(
            cot[...], w_ref[...], LAST_BOTH, preferred_element_type=jnp.float32
        )

    return call(
        kernel,
        "cotangent_product",
        grid=(depth // tile,),
        in_specs=[SMEM, pl.BlockSpec((tile, WIDTH), lambda n: (n, 0))] + [ANY] * len(order),
        out_specs=pl.BlockSpec((tok_dev, tile), lambda n: (0, n)),
        out_shape=jax.ShapeDtypeStruct((tok_dev, depth), jnp.float32),
        scratch_shapes=[
            pltpu.VMEM((tok_dev, WIDTH), jnp.bfloat16),
            pltpu.SemaphoreType.DMA((len(order),)),
        ],
    )(at, weight, *[cot_pieces[s][k] for s, k in order])


def input_gradient(at, base, grad_pieces, down):
    data_count, all_rows, _ = down.shape
    tensor_count = len(grad_pieces)
    pipe_count, rows, _ = grad_pieces[0].shape
    tok_dev, depth = base.shape
    down_rows = depth // data_count
    planes = next((n for n in range(1, data_count) if n * down_rows % 256 == 0), data_count)
    tile = planes * down_rows

    def kernel(at_ref, base_ref, a_ref, *rest):
        grad_refs, (out_ref, grad) = rest[:tensor_count], rest[tensor_count:]

        @pl.when(pl.program_id(0) == 0)
        def _():
            for s in range(tensor_count):
                core = came_from(at_ref[2], s, tensor_count)
                for k in range(pipe_count):
                    chip = came_from(at_ref[1], k, pipe_count)
                    first = pl.multiple_of((chip * tensor_count + core) * rows, rows)
                    grad[pl.ds(first, rows)] = grad_refs[s][k]

        for block in range(tok_dev // BLOCK):
            here = slice(block * BLOCK, (block + 1) * BLOCK)
            a = a_ref[:, block * down_rows : (block + 1) * down_rows].reshape(tile, RANKS)
            low = lax.dot_general(grad[here], a, LAST_BOTH, preferred_element_type=jnp.float32)
            out_ref[here] = (base_ref[here] + low).astype(out_ref.dtype)

    return call(
        kernel,
        "input_gradient",
        grid=(data_count // planes,),
        in_specs=[
            SMEM,
            pl.BlockSpec((tok_dev, tile), lambda n: (0, n)),
            pl.BlockSpec((planes, all_rows, RANKS), lambda n: (n, 0, 0)),
        ]
        + [VMEM] * tensor_count,
        out_specs=pl.BlockSpec((tok_dev, tile), lambda n: (0, n)),
        out_shape=jax.ShapeDtypeStruct((tok_dev, depth), jnp.bfloat16),
        scratch_shapes=[pltpu.VMEM((tok_dev, RANKS), jnp.bfloat16)],
    )(at, base, down, *grad_pieces)


def grad_down_pieces(at, x_features, grad_pieces):
    data_count, down_rows, tok_dev = x_features.shape
    tensor_count = len(grad_pieces)
    pipe_count, rows, _ = grad_pieces[0].shape
    blocks_dev = tok_dev // BLOCK

    def kernel(at_ref, x_ref, *rest):
        grad_refs, (out_ref, grad) = rest[:tensor_count], rest[tensor_count:]

        @pl.when(pl.program_id(0) == 0)
        def _():
            for s in range(tensor_count):
                core = came_from(at_ref[2], s, tensor_count)
                for k in range(pipe_count):
                    chip = came_from(at_ref[1], k, pipe_count)
                    first = pl.multiple_of((chip * tensor_count + core) * rows, rows)
                    grad[pl.ds(first, rows)] = grad_refs[s][k]

        for block in range(blocks_dev):
            here = slice(block * BLOCK, (block + 1) * BLOCK)
            out_ref[0, block] = jnp.dot(
                x_ref[0, :, here], grad[here], preferred_element_type=jnp.float32
            ).astype(out_ref.dtype)

    return call(
        kernel,
        "grad_down_pieces",
        grid=(data_count,),
        in_specs=[SMEM, pl.BlockSpec((1, down_rows, tok_dev), lambda d: (d, 0, 0))]
        + [VMEM] * tensor_count,
        out_specs=pl.BlockSpec((1, blocks_dev, down_rows, RANKS), lambda d: (d, 0, 0, 0)),
        out_shape=pltpu.HBM((data_count, blocks_dev, down_rows, RANKS), jnp.bfloat16),
        scratch_shapes=[pltpu.VMEM((tok_dev, RANKS), jnp.bfloat16)],
    )(at, x_features, *grad_pieces)


def grad_down(at, slot_of, slots, pieces):
    data_count, blocks_dev, down_rows, _ = pieces.shape
    parts = 2 if down_rows % 256 == 0 else 1
    part_rows = down_rows // parts

    def kernel(at_ref, piece_ref, out_ref, piece, total, piece_sem, out_sem):
        copies = [
            [
                pltpu.make_async_copy(
                    piece_ref.at[data, block], piece.at[data, block], piece_sem.at[data, block]
                )
                for block in range(blocks_dev)
            ]
            for data in range(data_count)
        ]
        for some in copies:
            for copy in some:
                copy.start()
        total[...] = jnp.zeros(total.shape, total.dtype)
        outs = []
        for part in range(parts):
            here = slice(part * part_rows, (part + 1) * part_rows)
            for data in range(data_count):
                for block in range(blocks_dev):
                    if part == 0:
                        copies[data][block].wait()
                    slot = slot_of(at_ref, data, block)
                    total[part, slot] += piece[data, block, here].astype(total.dtype)
            there = out_ref.at[:, pl.ds(part * part_rows, part_rows)]
            outs.append(pltpu.make_async_copy(total.at[part], there, out_sem.at[part]))
            outs[-1].start()
        for copy in outs:
            copy.wait()

    return call(
        kernel,
        "grad_down",
        VMEM_MOST,
        in_specs=[SMEM, HBM],
        out_specs=HBM,
        out_shape=pltpu.HBM((slots, down_rows, RANKS), jnp.float32),
        scratch_shapes=[
            pltpu.VMEM(pieces.shape, jnp.bfloat16),
            pltpu.VMEM((parts, slots, part_rows, RANKS), jnp.float32),
            pltpu.SemaphoreType.DMA((data_count, blocks_dev)),
            pltpu.SemaphoreType.DMA((parts,)),
        ],
    )(at, pieces)


def grad_up_pieces(at, low_pieces, cot_pieces, data_count, up_rows):
    tensor_count, pipe_count = len(cot_pieces), len(cot_pieces[0])
    group_count = tensor_count * pipe_count
    rows = cot_pieces[0][0].shape[0]
    cols = WIDTH // group_count
    tok_dev = group_count * rows
    blocks_dev = tok_dev // BLOCK
    group_half = group_count // 2
    order = [(s, k) for s in range(tensor_count) for k in range(pipe_count)]
    pieces = [cot_pieces[s][k] for s, k in order]
    in_kernel = cols % 128 == 0
    if not in_kernel:
        first_col = (at[1] * tensor_count + at[2]) * cols
        pieces = [lax.dynamic_slice_in_dim(piece, first_col, cols, 1) for piece in pieces]

    def kernel(at_ref, *rest):
        low_refs, rest = rest[:tensor_count], rest[tensor_count:]
        cot_refs, (out_ref, low, cot, sems) = rest[: len(order)], rest[len(order) :]
        my_group = at_ref[1] * tensor_count + at_ref[2]
        copies = []
        for i, (s, k) in enumerate(order):
            core = came_from(at_ref[2], s, tensor_count)
            chip = came_from(at_ref[1], k, pipe_count)
            first = pl.multiple_of((chip * tensor_count + core) * rows, rows)
            piece = cot_refs[i]
            if in_kernel:
                piece = piece.at[:, pl.ds(pl.multiple_of(my_group * cols, cols), cols)]
            copies.append(pltpu.make_async_copy(piece, cot.at[pl.ds(first, rows)], sems.at[i]))
        for copy in copies:
            copy.start()
        for s in range(tensor_count):
            core = came_from(at_ref[2], s, tensor_count)
            for k in range(pipe_count):
                first = pl.multiple_of((k * tensor_count + core) * rows, rows)
                low[pl.ds(first, rows)] = low_refs[s][k]
        for copy in copies:
            copy.wait()
        for block in range(blocks_dev):
            at = slice(block * BLOCK, (block + 1) * BLOCK)
            both = lax.dot_general(low[at], cot[at], FIRST_BOTH, preferred_element_type=jnp.float32)
            half = jnp.where(my_group < group_half, both[:ADAPTER_RANK], both[ADAPTER_RANK:])
            half = half.astype(out_ref.dtype)
            for data in range(data_count):
                k = wrap(data - at_ref[0], data_count)
                out_ref[k, block] = half[data * up_rows : (data + 1) * up_rows]

    return call(
        kernel,
        "grad_up_pieces",
        in_specs=[SMEM] + [VMEM] * tensor_count + [ANY] * len(order),
        out_specs=VMEM,
        out_shape=jax.ShapeDtypeStruct((data_count, blocks_dev, up_rows, cols), jnp.bfloat16),
        scratch_shapes=[
            pltpu.VMEM((tok_dev, RANKS), jnp.bfloat16),
            pltpu.VMEM((tok_dev, cols), jnp.bfloat16),
            pltpu.SemaphoreType.DMA((len(order),)),
        ],
    )(at, *low_pieces, *pieces)


def grad_up(at, slot_of, slots, pieces):
    data_count = len(pieces)
    blocks_dev, up_rows, cols = pieces[0].shape

    def kernel(at_ref, *rest):
        piece_refs, out_ref = rest[:data_count], rest[data_count]
        out_ref[...] = jnp.zeros(out_ref.shape, out_ref.dtype)
        for k in range(data_count):
            data = wrap(at_ref[0] - k, data_count)
            for block in range(blocks_dev):
                slot = slot_of(at_ref, data, block)
                out_ref[slot] += piece_refs[k][block].astype(out_ref.dtype)

    return call(
        kernel,
        "grad_up",
        in_specs=[SMEM] + [VMEM] * data_count,
        out_specs=VMEM,
        out_shape=jax.ShapeDtypeStruct((slots, up_rows, cols), jnp.float32),
    )(at, *pieces)


def own_rows(at, up, cotangent):
    data_count = len(up)
    rows = cotangent.shape[0]

    def kernel(at_ref, cot_ref, *rest):
        up_refs, (b_ref, grad_ref) = rest[:data_count], rest[data_count:]
        pieces = []
        for data in range(data_count):
            came = wrap(at_ref[0] - data, data_count)
            piece = up_refs[0][...]
            for k in range(1, data_count):
                piece = jnp.where(came == k, up_refs[k][...], piece)
            pieces.append(piece)
        b = jnp.concatenate(pieces, axis=0)
        b_ref[...] = b
        cot = cot_ref[...]
        grad_ref[...] = jnp.concatenate(
            [
                lax.dot_general(cot[:, half], b[:, half], LAST_BOTH, preferred_element_type=jnp.float32)
                for half in (slice(0, KEY_WIDTH), slice(KEY_WIDTH, WIDTH))
            ],
            axis=1,
        ).astype(grad_ref.dtype)

    return call(
        kernel,
        "own_rows",
        in_specs=[SMEM, VMEM] + [VMEM] * data_count,
        out_specs=(VMEM, VMEM),
        out_shape=(
            jax.ShapeDtypeStruct((ADAPTER_RANK, WIDTH), jnp.bfloat16),
            jax.ShapeDtypeStruct((rows, RANKS), jnp.bfloat16),
        ),
    )(at, cotangent, *up)


def keys_and_values(at, base_pieces, low_sum, b_own):
    rows = base_pieces[0].shape[0]
    count = len(base_pieces)

    def kernel(at_ref, low_ref, b_ref, *rest):
        base_refs, out_ref = rest[:count], rest[count]
        low = low_ref[at_ref[1]]
        for first, ranks in ((0, slice(0, ADAPTER_RANK)), (KEY_WIDTH, slice(ADAPTER_RANK, RANKS))):
            at = slice(first, first + KEY_WIDTH)
            y = jnp.dot(low[:, ranks], b_ref[:, at], preferred_element_type=jnp.float32)
            for base_ref in base_refs:
                y += base_ref[:, at].astype(jnp.float32)
            out_ref[:, at] = y.astype(out_ref.dtype)

    return call(
        kernel,
        "keys_and_values",
        in_specs=[SMEM, VMEM, VMEM] + [VMEM] * count,
        out_specs=VMEM,
        out_shape=jax.ShapeDtypeStruct((rows, WIDTH), jnp.bfloat16),
    )(at, low_sum, b_own, *base_pieces)


def body(
    tokens, key_value_weight, adapter_down, adapter_up, tenant_of_block, slot_of_tenant, cotangent
):
    data_count = lax.axis_size("dp")
    pipe_count = lax.axis_size("pipe")
    tensor_count = lax.axis_size("tensor")
    group_count = pipe_count * tensor_count
    at_data, at_pipe, at_tensor = (lax.axis_index(a) for a in ("dp", "pipe", "tensor"))
    my_group = at_pipe * tensor_count + at_tensor
    tok_dev, feature_count = tokens.shape
    blocks_dev = tok_dev // BLOCK
    rows = tok_dev // group_count
    down_rows = adapter_down.shape[1]
    up_rows = adapter_up.shape[1]
    slots = adapter_down.shape[0]
    blocks = tenant_of_block.shape[0]

    at = jnp.stack([at_data, at_pipe, at_tensor]).astype(jnp.int32)
    at = jnp.concatenate([at, tenant_of_block, slot_of_tenant])

    def slot_of(at_ref, data, block):
        return at_ref[3 + blocks + at_ref[3 + data * blocks_dev + block]]

    b_send, a_send = pick(tenant_of_block, slot_of_tenant, adapter_down, adapter_up, rows)
    b_came = [b_send[0]] + [shift(b_send[k], "dp", k) for k in range(1, data_count)]
    b_own, grad_rows = own_rows(at, b_came, cotangent)

    a_send, b_came = lax.optimization_barrier((a_send, b_came))
    a_recv = lax.all_to_all(a_send, "dp", 0, 0, tiled=True)

    behind, a_send = lax.optimization_barrier((tokens, a_send))
    cot_chips, base_tokens, x_tokens = gather_chips(cotangent, behind)
    cot_chips = [cotangent] + cot_chips

    tokens_by_group = base_tokens.reshape(pipe_count, tensor_count, rows, feature_count)
    parts = 2 if pipe_count % 2 == 0 else 1
    chips = pipe_count // parts
    base_send = base_product(at, tokens_by_group, key_value_weight, 1, tensor_count - 1, parts)
    base_came = [
        [swap(part[s - 1], "tensor", s) for part in base_send] for s in range(1, tensor_count)
    ]
    (base_keep,) = base_product(at, tokens_by_group, key_value_weight, 0, 1, 1)
    base_chip = [
        sum(
            [base_keep[0, k].astype(jnp.float32)]
            + [came[k // chips][k % chips].astype(jnp.float32) for came in base_came]
        )
        for k in range(pipe_count)
    ]
    base_chip[1:] = [piece.astype(jnp.bfloat16) for piece in base_chip[1:]]
    base_chip_came = [swap(base_chip[k], "pipe", k) for k in range(1, pipe_count)]

    cot_pieces = [cot_chips] + [
        [swap(piece, "tensor", s) for piece in cot_chips] for s in range(1, tensor_count)
    ]
    input_base = cotangent_product(at, cot_pieces, key_value_weight)

    grad_chips = jnp.stack([grad_rows] + [swap(grad_rows, "pipe", k) for k in range(1, pipe_count)])
    grad_pieces = [grad_chips] + [swap(grad_chips, "tensor", s) for s in range(1, tensor_count)]
    x_features = x_tokens.T.reshape(data_count, down_rows, tok_dev)
    down_send = grad_down_pieces(at, x_features, grad_pieces)

    a_recv, down_send, input_base, base_chip_came[:2] = lax.optimization_barrier(
        (a_recv, down_send, input_base, base_chip_came[:2])
    )
    down_recv = lax.all_to_all(down_send, "dp", 0, 0, tiled=True)
    input_grad = input_gradient(at, input_base, grad_pieces, a_recv)

    low_down, base_chip_came = lax.optimization_barrier((a_recv, base_chip_came))
    low_part = low_product(at, tokens, low_down, pipe_count, tensor_count)
    low_core = sum(
        [low_part[0].astype(jnp.float32)]
        + [swap(low_part[s], "tensor", s).astype(jnp.float32) for s in range(1, tensor_count)]
    ).astype(jnp.bfloat16)
    low_came = [swap(low_core, "pipe", k) for k in range(1, pipe_count)]
    low_sum = sum([piece.astype(jnp.float32) for piece in [low_core] + low_came])
    low_sum = low_sum.astype(jnp.bfloat16)
    low_pieces = [low_sum] + [swap(low_sum, "tensor", s) for s in range(1, tensor_count)]
    key_value = keys_and_values(at, base_chip[:1] + base_chip_came, low_sum, b_own)

    up_pieces = grad_up_pieces(at, low_pieces, cot_pieces, data_count, up_rows)
    up_came = [up_pieces[0]] + [shift(up_pieces[k], "dp", k) for k in range(1, data_count)]
    grad_a = grad_down(at, slot_of, slots, down_recv)
    up_came, grad_a = lax.optimization_barrier((up_came, grad_a))
    grad_b = grad_up(at, slot_of, slots, up_came)
    return (key_value, input_grad, grad_a, grad_b)


def solution(mesh):
    atd = (
        P("dp", ("pipe", "tensor")),
        P(("pipe", "tensor"), None),
        P(None, ("pipe", "tensor", "dp"), None),
        P(None, "dp", None),
        P(),
        P(),
        P(("dp", "pipe", "tensor"), None),
    )
    return jax.shard_map(
        body,
        mesh=mesh,
        in_specs=atd,
        out_specs=(
            P(("dp", "pipe", "tensor"), None),
            P("dp", ("pipe", "tensor")),
            P(None, ("pipe", "tensor", "dp"), None),
            P(None, "dp", ("pipe", "tensor")),
        ),
        check_vma=False,
    )
```

```python
import jax
import jax.numpy as jnp
from jax import lax
from jax.experimental import pallas as pl
from jax.experimental.pallas import tpu as pltpu
from jax.sharding import PartitionSpec as P

KEY_WIDTH = 1024
ADAPTER_RANK = 64
BLOCK = 128
RANKS = 2 * ADAPTER_RANK
WIDTH = 2 * KEY_WIDTH
VMEM_LIMIT = 24 * 1024 * 1024
VMEM_MOST = 60 * 1024 * 1024
LAST_BOTH = (((1,), (1,)), ((), ()))
FIRST_BOTH = (((0,), (0,)), ((), ()))
SMEM = pl.BlockSpec(memory_space=pltpu.SMEM)
VMEM = pl.BlockSpec(memory_space=pltpu.VMEM)
HBM = pl.BlockSpec(memory_space=pltpu.HBM)
ANY = pl.BlockSpec(memory_space=pl.ANY)


def call(kernel, name, vmem=VMEM_LIMIT, **more):
    return pl.pallas_call(
        kernel,
        compiler_params=pltpu.CompilerParams(vmem_limit_bytes=vmem),
        cost_estimate=pl.CostEstimate(flops=1024, bytes_accessed=1024, transcendentals=0),
        name=name,
        **more,
    )


def wrap(index, count):
    return lax.rem(index + 2 * count, count)


def shift(piece, axis, k):
    count = lax.axis_size(axis)
    return lax.ppermute(piece, axis, [(i, (i + k) % count) for i in range(count)])


def paired(count):
    return count & (count - 1) == 0


def partner(index, k, count):
    return index ^ k if paired(count) else (index + k) % count


def came_from(index, k, count):
    return index ^ k if paired(count) else wrap(index - k, count)


def which_partner(other, index, count):
    return other ^ index if paired(count) else wrap(other - index, count)


def swap(piece, axis, k):
    count = lax.axis_size(axis)
    return lax.ppermute(piece, axis, [(i, partner(i, k, count)) for i in range(count)])


def gather_chips(piece):
    count = lax.axis_size("pipe")
    if count != 4 or piece.shape[0] % 32:
        return [swap(piece, "pipe", k) for k in range(1, count)]
    first, second = swap(piece, "pipe", 1), swap(piece, "pipe", 2)
    half = piece.shape[0] // 2
    third = [swap(second[:half], "pipe", 1), swap(first[half:], "pipe", 2)]
    return [first, second, jnp.concatenate(third)]


def pick(tenant_of_block, slot_of_tenant, adapter_down, adapter_up, group_rows):
    data_count = lax.axis_size("dp")
    blocks_dev = tenant_of_block.shape[0] // data_count
    down_rows, ranks = adapter_down.shape[1:]
    used = blocks_dev * down_rows

    def kernel(tenant_ref, slot_ref, down_ref, up_ref, *rest):
        up_refs, (out_ref, rows, up_sem, down_sem, out_sem) = rest[:data_count], rest[data_count:]
        own_block = lax.axis_index(("pipe", "tensor")) * group_rows // BLOCK
        ups, downs, outs = [], [], []
        for k in range(data_count):
            data = wrap(lax.axis_index("dp") + k, data_count)
            slot = slot_ref[tenant_ref[data * blocks_dev + own_block]]
            ups.append(pltpu.make_async_copy(up_ref.at[slot], up_refs[k], up_sem.at[k]))
            ups[-1].start()
        for data in range(data_count):
            downs.append([])
            for block in range(blocks_dev):
                here = rows.at[data, pl.ds(block * down_rows, down_rows)]
                slot = slot_ref[tenant_ref[data * blocks_dev + block]]
                downs[data].append(
                    pltpu.make_async_copy(down_ref.at[slot], here, down_sem.at[data, block])
                )
                downs[data][-1].start()
            outs.append(pltpu.make_async_copy(rows.at[data], out_ref.at[data], out_sem.at[data]))
        for data in range(data_count):
            for copy in downs[data]:
                copy.wait()
            outs[data].start()
        for copy in ups + outs:
            copy.wait()

    up_shape = jax.ShapeDtypeStruct(adapter_up.shape[1:], adapter_up.dtype)
    out = call(
        kernel,
        "pick_rows",
        VMEM_MOST,
        out_shape=(up_shape,) * data_count
        + (pltpu.HBM((data_count, used, ranks), adapter_down.dtype),),
        in_specs=[SMEM, SMEM, HBM, HBM],
        out_specs=(VMEM,) * data_count + (HBM,),
        scratch_shapes=[
            pltpu.VMEM((data_count, used, ranks), adapter_down.dtype),
            pltpu.SemaphoreType.DMA((data_count,)),
            pltpu.SemaphoreType.DMA((data_count, blocks_dev)),
            pltpu.SemaphoreType.DMA((data_count,)),
        ],
    )(tenant_of_block, slot_of_tenant, adapter_down, adapter_up)
    return out[:data_count], out[data_count]


def base_product(at, tokens, weight, first, count, parts):
    pipe_count, tensor_count, rows, depth = tokens.shape
    tile = 1024
    chips = pipe_count // parts

    def kernel(at_ref, x_ref, w_ref, *out_refs):
        x = x_ref[...].reshape(pipe_count * rows, depth)
        y = jnp.dot(x, w_ref[...], preferred_element_type=jnp.float32).astype(out_refs[0].dtype)
        for chip in range(pipe_count):
            k = which_partner(chip, at_ref[1], pipe_count)
            for part, out_ref in enumerate(out_refs):

                @pl.when((k >= part * chips) & (k < (part + 1) * chips))
                def _():
                    out_ref[0, k - part * chips] = y[chip * rows : (chip + 1) * rows]

    out = call(
        kernel,
        "base_product",
        grid_spec=pltpu.PrefetchScalarGridSpec(
            num_scalar_prefetch=1,
            grid=(WIDTH // tile, count),
            in_specs=[
                pl.BlockSpec(
                    (pipe_count, 1, rows, depth),
                    lambda n, s, at: (0, partner(at[2], s + first, tensor_count), 0, 0),
                ),
                pl.BlockSpec((depth, tile), lambda n, s, at: (0, n)),
            ],
            out_specs=(pl.BlockSpec((1, chips, rows, tile), lambda n, s, at: (s, 0, 0, n)),) * parts,
        ),
        out_shape=(jax.ShapeDtypeStruct((count, chips, rows, WIDTH), jnp.bfloat16),) * parts,
    )(at, tokens, weight)
    return out


def low_product(at, tokens, down, pipe_count, tensor_count):
    tok_dev, depth = tokens.shape
    down_rows = depth // down.shape[0]
    rows = tok_dev // (pipe_count * tensor_count)

    def kernel(at_ref, x_ref, a_ref, out_ref):
        for block in range(tok_dev // BLOCK):
            a = a_ref[:, block * down_rows : (block + 1) * down_rows].reshape(depth, RANKS)
            x = x_ref[block * BLOCK : (block + 1) * BLOCK]
            y = jnp.dot(x, a, preferred_element_type=jnp.float32).astype(out_ref.dtype)
            for part in range(BLOCK // rows):
                chip, core = divmod(block * (BLOCK // rows) + part, tensor_count)
                core = which_partner(core, at_ref[2], tensor_count)
                out_ref[core, chip] = y[part * rows : (part + 1) * rows]

    return call(
        kernel,
        "low_product",
        in_specs=[SMEM, VMEM, VMEM],
        out_specs=VMEM,
        out_shape=jax.ShapeDtypeStruct((tensor_count, pipe_count, rows, RANKS), jnp.bfloat16),
    )(at, tokens, down)


def cotangent_product(at, cot_pieces, weight):
    tensor_count, pipe_count = len(cot_pieces), len(cot_pieces[0])
    rows = cot_pieces[0][0].shape[0]
    depth = weight.shape[0]
    tok_dev = tensor_count * pipe_count * rows
    tile = 256 if depth % 256 == 0 else depth
    order = [(s, k) for s in range(tensor_count) for k in range(pipe_count)]

    def kernel(at_ref, w_ref, *rest):
        cot_refs, (out_ref, cot, sems) = rest[: len(order)], rest[len(order) :]

        @pl.when(pl.program_id(0) == 0)
        def _():
            copies = []
            for i, (s, k) in enumerate(order):
                chip = came_from(at_ref[1], k, pipe_count)
                core = came_from(at_ref[2], s, tensor_count)
                first = pl.multiple_of((chip * tensor_count + core) * rows, rows)
                copies.append(
                    pltpu.make_async_copy(cot_refs[i], cot.at[pl.ds(first, rows)], sems.at[i])
                )
            for copy in copies:
                copy.start()
            for copy in copies:
                copy.wait()

        out_ref[...] = lax.dot_general(
            cot[...], w_ref[...], LAST_BOTH, preferred_element_type=jnp.float32
        )

    return call(
        kernel,
        "cotangent_product",
        grid=(depth // tile,),
        in_specs=[SMEM, pl.BlockSpec((tile, WIDTH), lambda n: (n, 0))] + [ANY] * len(order),
        out_specs=pl.BlockSpec((tok_dev, tile), lambda n: (0, n)),
        out_shape=jax.ShapeDtypeStruct((tok_dev, depth), jnp.float32),
        scratch_shapes=[
            pltpu.VMEM((tok_dev, WIDTH), jnp.bfloat16),
            pltpu.SemaphoreType.DMA((len(order),)),
        ],
    )(at, weight, *[cot_pieces[s][k] for s, k in order])


def input_gradient(at, base, grad_pieces, down):
    data_count, all_rows, _ = down.shape
    tensor_count = len(grad_pieces)
    pipe_count, rows, _ = grad_pieces[0].shape
    tok_dev, depth = base.shape
    down_rows = depth // data_count
    planes = next((n for n in range(1, data_count) if n * down_rows % 256 == 0), data_count)
    tile = planes * down_rows

    def kernel(at_ref, base_ref, a_ref, *rest):
        grad_refs, (out_ref, grad) = rest[:tensor_count], rest[tensor_count:]

        @pl.when(pl.program_id(0) == 0)
        def _():
            for s in range(tensor_count):
                core = came_from(at_ref[2], s, tensor_count)
                for k in range(pipe_count):
                    chip = came_from(at_ref[1], k, pipe_count)
                    first = pl.multiple_of((chip * tensor_count + core) * rows, rows)
                    grad[pl.ds(first, rows)] = grad_refs[s][k]

        for block in range(tok_dev // BLOCK):
            here = slice(block * BLOCK, (block + 1) * BLOCK)
            a = a_ref[:, block * down_rows : (block + 1) * down_rows].reshape(tile, RANKS)
            low = lax.dot_general(grad[here], a, LAST_BOTH, preferred_element_type=jnp.float32)
            out_ref[here] = (base_ref[here] + low).astype(out_ref.dtype)

    return call(
        kernel,
        "input_gradient",
        grid=(data_count // planes,),
        in_specs=[
            SMEM,
            pl.BlockSpec((tok_dev, tile), lambda n: (0, n)),
            pl.BlockSpec((planes, all_rows, RANKS), lambda n: (n, 0, 0)),
        ]
        + [VMEM] * tensor_count,
        out_specs=pl.BlockSpec((tok_dev, tile), lambda n: (0, n)),
        out_shape=jax.ShapeDtypeStruct((tok_dev, depth), jnp.bfloat16),
        scratch_shapes=[pltpu.VMEM((tok_dev, RANKS), jnp.bfloat16)],
    )(at, base, down, *grad_pieces)


def grad_down_pieces(at, x_features, grad_pieces):
    data_count, down_rows, tok_dev = x_features.shape
    tensor_count = len(grad_pieces)
    pipe_count, rows, _ = grad_pieces[0].shape
    blocks_dev = tok_dev // BLOCK

    def kernel(at_ref, x_ref, *rest):
        grad_refs, (out_ref, grad) = rest[:tensor_count], rest[tensor_count:]

        @pl.when(pl.program_id(0) == 0)
        def _():
            for s in range(tensor_count):
                core = came_from(at_ref[2], s, tensor_count)
                for k in range(pipe_count):
                    chip = came_from(at_ref[1], k, pipe_count)
                    first = pl.multiple_of((chip * tensor_count + core) * rows, rows)
                    grad[pl.ds(first, rows)] = grad_refs[s][k]

        for block in range(blocks_dev):
            here = slice(block * BLOCK, (block + 1) * BLOCK)
            out_ref[0, block] = jnp.dot(
                x_ref[0, :, here], grad[here], preferred_element_type=jnp.float32
            ).astype(out_ref.dtype)

    return call(
        kernel,
        "grad_down_pieces",
        grid=(data_count,),
        in_specs=[SMEM, pl.BlockSpec((1, down_rows, tok_dev), lambda d: (d, 0, 0))]
        + [VMEM] * tensor_count,
        out_specs=pl.BlockSpec((1, blocks_dev, down_rows, RANKS), lambda d: (d, 0, 0, 0)),
        out_shape=pltpu.HBM((data_count, blocks_dev, down_rows, RANKS), jnp.bfloat16),
        scratch_shapes=[pltpu.VMEM((tok_dev, RANKS), jnp.bfloat16)],
    )(at, x_features, *grad_pieces)


def grad_down(at, slot_of, slots, pieces):
    data_count, blocks_dev, down_rows, _ = pieces.shape
    parts = 2 if down_rows % 256 == 0 else 1
    part_rows = down_rows // parts

    def kernel(at_ref, piece_ref, out_ref, piece, total, piece_sem, out_sem):
        copies = [
            [
                pltpu.make_async_copy(
                    piece_ref.at[data, block], piece.at[data, block], piece_sem.at[data, block]
                )
                for block in range(blocks_dev)
            ]
            for data in range(data_count)
        ]
        for some in copies:
            for copy in some:
                copy.start()
        total[...] = jnp.zeros(total.shape, total.dtype)
        outs = []
        for part in range(parts):
            here = slice(part * part_rows, (part + 1) * part_rows)
            for data in range(data_count):
                for block in range(blocks_dev):
                    if part == 0:
                        copies[data][block].wait()
                    slot = slot_of(at_ref, data, block)
                    total[part, slot] += piece[data, block, here].astype(total.dtype)
            there = out_ref.at[:, pl.ds(part * part_rows, part_rows)]
            outs.append(pltpu.make_async_copy(total.at[part], there, out_sem.at[part]))
            outs[-1].start()
        for copy in outs:
            copy.wait()

    return call(
        kernel,
        "grad_down",
        VMEM_MOST,
        in_specs=[SMEM, HBM],
        out_specs=HBM,
        out_shape=pltpu.HBM((slots, down_rows, RANKS), jnp.float32),
        scratch_shapes=[
            pltpu.VMEM(pieces.shape, jnp.bfloat16),
            pltpu.VMEM((parts, slots, part_rows, RANKS), jnp.float32),
            pltpu.SemaphoreType.DMA((data_count, blocks_dev)),
            pltpu.SemaphoreType.DMA((parts,)),
        ],
    )(at, pieces)


def grad_up_pieces(at, low_pieces, cot_pieces, data_count, up_rows):
    tensor_count, pipe_count = len(cot_pieces), len(cot_pieces[0])
    group_count = tensor_count * pipe_count
    rows = cot_pieces[0][0].shape[0]
    cols = WIDTH // group_count
    tok_dev = group_count * rows
    blocks_dev = tok_dev // BLOCK
    group_half = group_count // 2
    order = [(s, k) for s in range(tensor_count) for k in range(pipe_count)]
    pieces = [cot_pieces[s][k] for s, k in order]
    in_kernel = cols % 128 == 0
    if not in_kernel:
        first_col = (at[1] * tensor_count + at[2]) * cols
        pieces = [lax.dynamic_slice_in_dim(piece, first_col, cols, 1) for piece in pieces]

    def kernel(at_ref, *rest):
        low_refs, rest = rest[:tensor_count], rest[tensor_count:]
        cot_refs, (out_ref, low, cot, sems) = rest[: len(order)], rest[len(order) :]
        my_group = at_ref[1] * tensor_count + at_ref[2]
        copies = []
        for i, (s, k) in enumerate(order):
            core = came_from(at_ref[2], s, tensor_count)
            chip = came_from(at_ref[1], k, pipe_count)
            first = pl.multiple_of((chip * tensor_count + core) * rows, rows)
            piece = cot_refs[i]
            if in_kernel:
                piece = piece.at[:, pl.ds(pl.multiple_of(my_group * cols, cols), cols)]
            copies.append(pltpu.make_async_copy(piece, cot.at[pl.ds(first, rows)], sems.at[i]))
        for copy in copies:
            copy.start()
        for s in range(tensor_count):
            core = came_from(at_ref[2], s, tensor_count)
            for k in range(pipe_count):
                first = pl.multiple_of((k * tensor_count + core) * rows, rows)
                low[pl.ds(first, rows)] = low_refs[s][k]
        for copy in copies:
            copy.wait()
        for block in range(blocks_dev):
            at = slice(block * BLOCK, (block + 1) * BLOCK)
            both = lax.dot_general(low[at], cot[at], FIRST_BOTH, preferred_element_type=jnp.float32)
            half = jnp.where(my_group < group_half, both[:ADAPTER_RANK], both[ADAPTER_RANK:])
            half = half.astype(out_ref.dtype)
            for data in range(data_count):
                k = wrap(data - at_ref[0], data_count)
                out_ref[k, block] = half[data * up_rows : (data + 1) * up_rows]

    return call(
        kernel,
        "grad_up_pieces",
        in_specs=[SMEM] + [VMEM] * tensor_count + [ANY] * len(order),
        out_specs=VMEM,
        out_shape=jax.ShapeDtypeStruct((data_count, blocks_dev, up_rows, cols), jnp.bfloat16),
        scratch_shapes=[
            pltpu.VMEM((tok_dev, RANKS), jnp.bfloat16),
            pltpu.VMEM((tok_dev, cols), jnp.bfloat16),
            pltpu.SemaphoreType.DMA((len(order),)),
        ],
    )(at, *low_pieces, *pieces)


def grad_up(at, slot_of, slots, pieces):
    data_count = len(pieces)
    blocks_dev, up_rows, cols = pieces[0].shape

    def kernel(at_ref, *rest):
        piece_refs, out_ref = rest[:data_count], rest[data_count]
        out_ref[...] = jnp.zeros(out_ref.shape, out_ref.dtype)
        for k in range(data_count):
            data = wrap(at_ref[0] - k, data_count)
            for block in range(blocks_dev):
                slot = slot_of(at_ref, data, block)
                out_ref[slot] += piece_refs[k][block].astype(out_ref.dtype)

    return call(
        kernel,
        "grad_up",
        in_specs=[SMEM] + [VMEM] * data_count,
        out_specs=VMEM,
        out_shape=jax.ShapeDtypeStruct((slots, up_rows, cols), jnp.float32),
    )(at, *pieces)


def own_rows(at, up, cotangent):
    data_count = len(up)
    rows = cotangent.shape[0]

    def kernel(at_ref, cot_ref, *rest):
        up_refs, (b_ref, grad_ref) = rest[:data_count], rest[data_count:]
        pieces = []
        for data in range(data_count):
            came = wrap(at_ref[0] - data, data_count)
            piece = up_refs[0][...]
            for k in range(1, data_count):
                piece = jnp.where(came == k, up_refs[k][...], piece)
            pieces.append(piece)
        b = jnp.concatenate(pieces, axis=0)
        b_ref[...] = b
        cot = cot_ref[...]
        grad_ref[...] = jnp.concatenate(
            [
                lax.dot_general(cot[:, half], b[:, half], LAST_BOTH, preferred_element_type=jnp.float32)
                for half in (slice(0, KEY_WIDTH), slice(KEY_WIDTH, WIDTH))
            ],
            axis=1,
        ).astype(grad_ref.dtype)

    return call(
        kernel,
        "own_rows",
        in_specs=[SMEM, VMEM] + [VMEM] * data_count,
        out_specs=(VMEM, VMEM),
        out_shape=(
            jax.ShapeDtypeStruct((ADAPTER_RANK, WIDTH), jnp.bfloat16),
            jax.ShapeDtypeStruct((rows, RANKS), jnp.bfloat16),
        ),
    )(at, cotangent, *up)


def keys_and_values(at, base_pieces, low_sum, b_own):
    rows = base_pieces[0].shape[0]
    count = len(base_pieces)

    def kernel(at_ref, low_ref, b_ref, *rest):
        base_refs, out_ref = rest[:count], rest[count]
        low = low_ref[at_ref[1]]
        for first, ranks in ((0, slice(0, ADAPTER_RANK)), (KEY_WIDTH, slice(ADAPTER_RANK, RANKS))):
            at = slice(first, first + KEY_WIDTH)
            y = jnp.dot(low[:, ranks], b_ref[:, at], preferred_element_type=jnp.float32)
            for base_ref in base_refs:
                y += base_ref[:, at].astype(jnp.float32)
            out_ref[:, at] = y.astype(out_ref.dtype)

    return call(
        kernel,
        "keys_and_values",
        in_specs=[SMEM, VMEM, VMEM] + [VMEM] * count,
        out_specs=VMEM,
        out_shape=jax.ShapeDtypeStruct((rows, WIDTH), jnp.bfloat16),
    )(at, low_sum, b_own, *base_pieces)


def body(
    tokens, key_value_weight, adapter_down, adapter_up, tenant_of_block, slot_of_tenant, cotangent
):
    data_count = lax.axis_size("dp")
    pipe_count = lax.axis_size("pipe")
    tensor_count = lax.axis_size("tensor")
    group_count = pipe_count * tensor_count
    at_data, at_pipe, at_tensor = (lax.axis_index(a) for a in ("dp", "pipe", "tensor"))
    my_group = at_pipe * tensor_count + at_tensor
    tok_dev, feature_count = tokens.shape
    blocks_dev = tok_dev // BLOCK
    rows = tok_dev // group_count
    down_rows = adapter_down.shape[1]
    up_rows = adapter_up.shape[1]
    slots = adapter_down.shape[0]
    blocks = tenant_of_block.shape[0]

    at = jnp.stack([at_data, at_pipe, at_tensor]).astype(jnp.int32)
    at = jnp.concatenate([at, tenant_of_block, slot_of_tenant])

    def slot_of(at_ref, data, block):
        return at_ref[3 + blocks + at_ref[3 + data * blocks_dev + block]]

    b_send, a_send = pick(tenant_of_block, slot_of_tenant, adapter_down, adapter_up, rows)
    b_came = [b_send[0]] + [shift(b_send[k], "dp", k) for k in range(1, data_count)]
    b_own, grad_rows = own_rows(at, b_came, cotangent)

    a_send, b_came = lax.optimization_barrier((a_send, b_came))
    a_recv = lax.all_to_all(a_send, "dp", 0, 0, tiled=True)

    cot_chips = [cotangent] + gather_chips(cotangent)

    base_tokens, a_send = lax.optimization_barrier((tokens, a_send))
    tokens_by_group = base_tokens.reshape(pipe_count, tensor_count, rows, feature_count)
    parts = 2 if pipe_count % 2 == 0 else 1
    chips = pipe_count // parts
    base_send = base_product(at, tokens_by_group, key_value_weight, 1, tensor_count - 1, parts)
    base_came = [
        [swap(part[s - 1], "tensor", s) for part in base_send] for s in range(1, tensor_count)
    ]
    (base_keep,) = base_product(at, tokens_by_group, key_value_weight, 0, 1, 1)
    base_chip = [
        sum(
            [base_keep[0, k].astype(jnp.float32)]
            + [came[k // chips][k % chips].astype(jnp.float32) for came in base_came]
        )
        for k in range(pipe_count)
    ]
    base_chip[1:] = [piece.astype(jnp.bfloat16) for piece in base_chip[1:]]
    base_chip_came = [swap(base_chip[k], "pipe", k) for k in range(1, pipe_count)]

    cot_pieces = [cot_chips] + [
        [swap(piece, "tensor", s) for piece in cot_chips] for s in range(1, tensor_count)
    ]

    grad_chips = jnp.stack([grad_rows] + [swap(grad_rows, "pipe", k) for k in range(1, pipe_count)])
    grad_pieces = [grad_chips] + [swap(grad_chips, "tensor", s) for s in range(1, tensor_count)]
    x_features = base_tokens.T.reshape(data_count, down_rows, tok_dev)
    down_send = grad_down_pieces(at, x_features, grad_pieces)

    a_recv, down_send, cot_pieces, base_chip_came[:2] = lax.optimization_barrier(
        (a_recv, down_send, cot_pieces, base_chip_came[:2])
    )
    down_recv = lax.all_to_all(down_send, "dp", 0, 0, tiled=True)

    input_base = cotangent_product(at, cot_pieces, key_value_weight)
    low_down, base_chip_came, input_base = lax.optimization_barrier(
        (a_recv, base_chip_came, input_base)
    )
    input_grad = input_gradient(at, input_base, grad_pieces, a_recv)
    low_part = low_product(at, tokens, low_down, pipe_count, tensor_count)
    low_core = sum(
        [low_part[0].astype(jnp.float32)]
        + [swap(low_part[s], "tensor", s).astype(jnp.float32) for s in range(1, tensor_count)]
    ).astype(jnp.bfloat16)
    low_came = [swap(low_core, "pipe", k) for k in range(1, pipe_count)]
    low_sum = sum([piece.astype(jnp.float32) for piece in [low_core] + low_came])
    low_sum = low_sum.astype(jnp.bfloat16)
    low_pieces = [low_sum] + [swap(low_sum, "tensor", s) for s in range(1, tensor_count)]
    key_value = keys_and_values(at, base_chip[:1] + base_chip_came, low_sum, b_own)

    up_pieces = grad_up_pieces(at, low_pieces, cot_pieces, data_count, up_rows)
    up_came = [up_pieces[0]] + [shift(up_pieces[k], "dp", k) for k in range(1, data_count)]
    grad_a = grad_down(at, slot_of, slots, down_recv)
    up_came, grad_a = lax.optimization_barrier((up_came, grad_a))
    grad_b = grad_up(at, slot_of, slots, up_came)
    return (key_value, input_grad, grad_a, grad_b)


def solution(mesh):
    atd = (
        P("dp", ("pipe", "tensor")),
        P(("pipe", "tensor"), None),
        P(None, ("pipe", "tensor", "dp"), None),
        P(None, "dp", None),
        P(),
        P(),
        P(("dp", "pipe", "tensor"), None),
    )
    return jax.shard_map(
        body,
        mesh=mesh,
        in_specs=atd,
        out_specs=(
            P(("dp", "pipe", "tensor"), None),
            P("dp", ("pipe", "tensor")),
            P(None, ("pipe", "tensor", "dp"), None),
            P(None, "dp", ("pipe", "tensor")),
        ),
        check_vma=False,
    )
```

```python
import jax
import jax.numpy as jnp
from jax import lax
from jax.experimental import pallas as pl
from jax.experimental.pallas import tpu as pltpu
from jax.sharding import PartitionSpec as P

KEY_WIDTH = 1024
ADAPTER_RANK = 64
BLOCK = 128
RANKS = 2 * ADAPTER_RANK
WIDTH = 2 * KEY_WIDTH
VMEM_LIMIT = 24 * 1024 * 1024
VMEM_MOST = 60 * 1024 * 1024
LAST_BOTH = (((1,), (1,)), ((), ()))
FIRST_BOTH = (((0,), (0,)), ((), ()))
SMEM = pl.BlockSpec(memory_space=pltpu.SMEM)
VMEM = pl.BlockSpec(memory_space=pltpu.VMEM)
HBM = pl.BlockSpec(memory_space=pltpu.HBM)
ANY = pl.BlockSpec(memory_space=pl.ANY)


def call(kernel, name, vmem=VMEM_LIMIT, **more):
    return pl.pallas_call(
        kernel,
        compiler_params=pltpu.CompilerParams(vmem_limit_bytes=vmem),
        cost_estimate=pl.CostEstimate(flops=1024, bytes_accessed=1024, transcendentals=0),
        name=name,
        **more,
    )


def wrap(index, count):
    return lax.rem(index + 2 * count, count)


def shift(piece, axis, k):
    count = lax.axis_size(axis)
    return lax.ppermute(piece, axis, [(i, (i + k) % count) for i in range(count)])


def paired(count):
    return count & (count - 1) == 0


def partner(index, k, count):
    return index ^ k if paired(count) else (index + k) % count


def came_from(index, k, count):
    return index ^ k if paired(count) else wrap(index - k, count)


def which_partner(other, index, count):
    return other ^ index if paired(count) else wrap(other - index, count)


def swap(piece, axis, k):
    count = lax.axis_size(axis)
    return lax.ppermute(piece, axis, [(i, partner(i, k, count)) for i in range(count)])


def gather_chips(piece):
    count = lax.axis_size("pipe")
    if count != 4 or piece.shape[0] % 32:
        return [swap(piece, "pipe", k) for k in range(1, count)]
    first, second = swap(piece, "pipe", 1), swap(piece, "pipe", 2)
    half = piece.shape[0] // 2
    third = [swap(second[:half], "pipe", 1), swap(first[half:], "pipe", 2)]
    return [first, second, jnp.concatenate(third)]


def pick(tenant_of_block, slot_of_tenant, adapter_down, adapter_up, group_rows):
    data_count = lax.axis_size("dp")
    blocks_dev = tenant_of_block.shape[0] // data_count
    down_rows, ranks = adapter_down.shape[1:]
    used = blocks_dev * down_rows

    def kernel(tenant_ref, slot_ref, down_ref, up_ref, *rest):
        up_refs, (out_ref, rows, up_sem, down_sem, out_sem) = rest[:data_count], rest[data_count:]
        own_block = lax.axis_index(("pipe", "tensor")) * group_rows // BLOCK
        ups, downs, outs = [], [], []
        for k in range(data_count):
            data = wrap(lax.axis_index("dp") + k, data_count)
            slot = slot_ref[tenant_ref[data * blocks_dev + own_block]]
            ups.append(pltpu.make_async_copy(up_ref.at[slot], up_refs[k], up_sem.at[k]))
            ups[-1].start()
        for data in range(data_count):
            downs.append([])
            for block in range(blocks_dev):
                here = rows.at[data, pl.ds(block * down_rows, down_rows)]
                slot = slot_ref[tenant_ref[data * blocks_dev + block]]
                downs[data].append(
                    pltpu.make_async_copy(down_ref.at[slot], here, down_sem.at[data, block])
                )
                downs[data][-1].start()
            outs.append(pltpu.make_async_copy(rows.at[data], out_ref.at[data], out_sem.at[data]))
        for data in range(data_count):
            for copy in downs[data]:
                copy.wait()
            outs[data].start()
        for copy in ups + outs:
            copy.wait()

    up_shape = jax.ShapeDtypeStruct(adapter_up.shape[1:], adapter_up.dtype)
    out = call(
        kernel,
        "pick_rows",
        VMEM_MOST,
        out_shape=(up_shape,) * data_count
        + (pltpu.HBM((data_count, used, ranks), adapter_down.dtype),),
        in_specs=[SMEM, SMEM, HBM, HBM],
        out_specs=(VMEM,) * data_count + (HBM,),
        scratch_shapes=[
            pltpu.VMEM((data_count, used, ranks), adapter_down.dtype),
            pltpu.SemaphoreType.DMA((data_count,)),
            pltpu.SemaphoreType.DMA((data_count, blocks_dev)),
            pltpu.SemaphoreType.DMA((data_count,)),
        ],
    )(tenant_of_block, slot_of_tenant, adapter_down, adapter_up)
    return out[:data_count], out[data_count]


def base_product(at, tokens, weight, first, count, parts):
    pipe_count, tensor_count, rows, depth = tokens.shape
    tile = 1024
    chips = pipe_count // parts

    def kernel(at_ref, x_ref, w_ref, *out_refs):
        x = x_ref[...].reshape(pipe_count * rows, depth)
        y = jnp.dot(x, w_ref[...], preferred_element_type=jnp.float32).astype(out_refs[0].dtype)
        for chip in range(pipe_count):
            k = which_partner(chip, at_ref[1], pipe_count)
            for part, out_ref in enumerate(out_refs):

                @pl.when((k >= part * chips) & (k < (part + 1) * chips))
                def _():
                    out_ref[0, k - part * chips] = y[chip * rows : (chip + 1) * rows]

    out = call(
        kernel,
        "base_product",
        grid_spec=pltpu.PrefetchScalarGridSpec(
            num_scalar_prefetch=1,
            grid=(WIDTH // tile, count),
            in_specs=[
                pl.BlockSpec(
                    (pipe_count, 1, rows, depth),
                    lambda n, s, at: (0, partner(at[2], s + first, tensor_count), 0, 0),
                ),
                pl.BlockSpec((depth, tile), lambda n, s, at: (0, n)),
            ],
            out_specs=(pl.BlockSpec((1, chips, rows, tile), lambda n, s, at: (s, 0, 0, n)),) * parts,
        ),
        out_shape=(jax.ShapeDtypeStruct((count, chips, rows, WIDTH), jnp.bfloat16),) * parts,
    )(at, tokens, weight)
    return out


def low_product(at, tokens, down, pipe_count, tensor_count):
    tok_dev, depth = tokens.shape
    down_rows = depth // down.shape[0]
    rows = tok_dev // (pipe_count * tensor_count)

    def kernel(at_ref, x_ref, a_ref, out_ref):
        for block in range(tok_dev // BLOCK):
            a = a_ref[:, block * down_rows : (block + 1) * down_rows].reshape(depth, RANKS)
            x = x_ref[block * BLOCK : (block + 1) * BLOCK]
            y = jnp.dot(x, a, preferred_element_type=jnp.float32).astype(out_ref.dtype)
            for part in range(BLOCK // rows):
                chip, core = divmod(block * (BLOCK // rows) + part, tensor_count)
                core = which_partner(core, at_ref[2], tensor_count)
                out_ref[core, chip] = y[part * rows : (part + 1) * rows]

    return call(
        kernel,
        "low_product",
        in_specs=[SMEM, VMEM, VMEM],
        out_specs=VMEM,
        out_shape=jax.ShapeDtypeStruct((tensor_count, pipe_count, rows, RANKS), jnp.bfloat16),
    )(at, tokens, down)


def cotangent_product(at, cot_pieces, weight):
    tensor_count, pipe_count = len(cot_pieces), len(cot_pieces[0])
    rows = cot_pieces[0][0].shape[0]
    depth = weight.shape[0]
    tok_dev = tensor_count * pipe_count * rows
    tile = 256 if depth % 256 == 0 else depth
    order = [(s, k) for s in range(tensor_count) for k in range(pipe_count)]

    def kernel(at_ref, w_ref, *rest):
        cot_refs, (out_ref, cot, sems) = rest[: len(order)], rest[len(order) :]

        @pl.when(pl.program_id(0) == 0)
        def _():
            copies = []
            for i, (s, k) in enumerate(order):
                chip = came_from(at_ref[1], k, pipe_count)
                core = came_from(at_ref[2], s, tensor_count)
                first = pl.multiple_of((chip * tensor_count + core) * rows, rows)
                copies.append(
                    pltpu.make_async_copy(cot_refs[i], cot.at[pl.ds(first, rows)], sems.at[i])
                )
            for copy in copies:
                copy.start()
            for copy in copies:
                copy.wait()

        out_ref[...] = lax.dot_general(
            cot[...], w_ref[...], LAST_BOTH, preferred_element_type=jnp.float32
        )

    return call(
        kernel,
        "cotangent_product",
        grid=(depth // tile,),
        in_specs=[SMEM, pl.BlockSpec((tile, WIDTH), lambda n: (n, 0))] + [ANY] * len(order),
        out_specs=pl.BlockSpec((tok_dev, tile), lambda n: (0, n)),
        out_shape=jax.ShapeDtypeStruct((tok_dev, depth), jnp.float32),
        scratch_shapes=[
            pltpu.VMEM((tok_dev, WIDTH), jnp.bfloat16),
            pltpu.SemaphoreType.DMA((len(order),)),
        ],
    )(at, weight, *[cot_pieces[s][k] for s, k in order])


def input_gradient(at, base, grad_pieces, down):
    data_count, all_rows, _ = down.shape
    tensor_count = len(grad_pieces)
    pipe_count, rows, _ = grad_pieces[0].shape
    tok_dev, depth = base.shape
    down_rows = depth // data_count
    planes = next((n for n in range(1, data_count) if n * down_rows % 256 == 0), data_count)
    tile = planes * down_rows

    def kernel(at_ref, base_ref, a_ref, *rest):
        grad_refs, (out_ref, grad) = rest[:tensor_count], rest[tensor_count:]

        @pl.when(pl.program_id(0) == 0)
        def _():
            for s in range(tensor_count):
                core = came_from(at_ref[2], s, tensor_count)
                for k in range(pipe_count):
                    chip = came_from(at_ref[1], k, pipe_count)
                    first = pl.multiple_of((chip * tensor_count + core) * rows, rows)
                    grad[pl.ds(first, rows)] = grad_refs[s][k]

        for block in range(tok_dev // BLOCK):
            here = slice(block * BLOCK, (block + 1) * BLOCK)
            a = a_ref[:, block * down_rows : (block + 1) * down_rows].reshape(tile, RANKS)
            low = lax.dot_general(grad[here], a, LAST_BOTH, preferred_element_type=jnp.float32)
            out_ref[here] = (base_ref[here] + low).astype(out_ref.dtype)

    return call(
        kernel,
        "input_gradient",
        grid=(data_count // planes,),
        in_specs=[
            SMEM,
            pl.BlockSpec((tok_dev, tile), lambda n: (0, n)),
            pl.BlockSpec((planes, all_rows, RANKS), lambda n: (n, 0, 0)),
        ]
        + [VMEM] * tensor_count,
        out_specs=pl.BlockSpec((tok_dev, tile), lambda n: (0, n)),
        out_shape=jax.ShapeDtypeStruct((tok_dev, depth), jnp.bfloat16),
        scratch_shapes=[pltpu.VMEM((tok_dev, RANKS), jnp.bfloat16)],
    )(at, base, down, *grad_pieces)


def grad_down_pieces(at, x_features, grad_pieces):
    data_count, down_rows, tok_dev = x_features.shape
    tensor_count = len(grad_pieces)
    pipe_count, rows, _ = grad_pieces[0].shape
    blocks_dev = tok_dev // BLOCK

    def kernel(at_ref, x_ref, *rest):
        grad_refs, (out_ref, grad) = rest[:tensor_count], rest[tensor_count:]

        @pl.when(pl.program_id(0) == 0)
        def _():
            for s in range(tensor_count):
                core = came_from(at_ref[2], s, tensor_count)
                for k in range(pipe_count):
                    chip = came_from(at_ref[1], k, pipe_count)
                    first = pl.multiple_of((chip * tensor_count + core) * rows, rows)
                    grad[pl.ds(first, rows)] = grad_refs[s][k]

        for block in range(blocks_dev):
            here = slice(block * BLOCK, (block + 1) * BLOCK)
            out_ref[0, block] = jnp.dot(
                x_ref[0, :, here], grad[here], preferred_element_type=jnp.float32
            ).astype(out_ref.dtype)

    return call(
        kernel,
        "grad_down_pieces",
        grid=(data_count,),
        in_specs=[SMEM, pl.BlockSpec((1, down_rows, tok_dev), lambda d: (d, 0, 0))]
        + [VMEM] * tensor_count,
        out_specs=pl.BlockSpec((1, blocks_dev, down_rows, RANKS), lambda d: (d, 0, 0, 0)),
        out_shape=pltpu.HBM((data_count, blocks_dev, down_rows, RANKS), jnp.bfloat16),
        scratch_shapes=[pltpu.VMEM((tok_dev, RANKS), jnp.bfloat16)],
    )(at, x_features, *grad_pieces)


def grad_down(at, slot_of, slots, pieces):
    data_count, blocks_dev, down_rows, _ = pieces.shape
    parts = 2 if down_rows % 256 == 0 else 1
    part_rows = down_rows // parts

    def kernel(at_ref, piece_ref, out_ref, piece, total, piece_sem, out_sem):
        copies = [
            [
                pltpu.make_async_copy(
                    piece_ref.at[data, block], piece.at[data, block], piece_sem.at[data, block]
                )
                for block in range(blocks_dev)
            ]
            for data in range(data_count)
        ]
        for some in copies:
            for copy in some:
                copy.start()
        total[...] = jnp.zeros(total.shape, total.dtype)
        outs = []
        for part in range(parts):
            here = slice(part * part_rows, (part + 1) * part_rows)
            for data in range(data_count):
                for block in range(blocks_dev):
                    if part == 0:
                        copies[data][block].wait()
                    slot = slot_of(at_ref, data, block)
                    total[part, slot] += piece[data, block, here].astype(total.dtype)
            there = out_ref.at[:, pl.ds(part * part_rows, part_rows)]
            outs.append(pltpu.make_async_copy(total.at[part], there, out_sem.at[part]))
            outs[-1].start()
        for copy in outs:
            copy.wait()

    return call(
        kernel,
        "grad_down",
        VMEM_MOST,
        in_specs=[SMEM, HBM],
        out_specs=HBM,
        out_shape=pltpu.HBM((slots, down_rows, RANKS), jnp.float32),
        scratch_shapes=[
            pltpu.VMEM(pieces.shape, jnp.bfloat16),
            pltpu.VMEM((parts, slots, part_rows, RANKS), jnp.float32),
            pltpu.SemaphoreType.DMA((data_count, blocks_dev)),
            pltpu.SemaphoreType.DMA((parts,)),
        ],
    )(at, pieces)


def grad_up_pieces(at, low_pieces, cot_pieces, data_count, up_rows):
    tensor_count, pipe_count = len(cot_pieces), len(cot_pieces[0])
    group_count = tensor_count * pipe_count
    rows = cot_pieces[0][0].shape[0]
    cols = WIDTH // group_count
    tok_dev = group_count * rows
    blocks_dev = tok_dev // BLOCK
    group_half = group_count // 2
    order = [(s, k) for s in range(tensor_count) for k in range(pipe_count)]
    pieces = [cot_pieces[s][k] for s, k in order]
    in_kernel = cols % 128 == 0
    if not in_kernel:
        first_col = (at[1] * tensor_count + at[2]) * cols
        pieces = [lax.dynamic_slice_in_dim(piece, first_col, cols, 1) for piece in pieces]

    def kernel(at_ref, *rest):
        low_refs, rest = rest[:tensor_count], rest[tensor_count:]
        cot_refs, (out_ref, low, cot, sems) = rest[: len(order)], rest[len(order) :]
        my_group = at_ref[1] * tensor_count + at_ref[2]
        copies = []
        for i, (s, k) in enumerate(order):
            core = came_from(at_ref[2], s, tensor_count)
            chip = came_from(at_ref[1], k, pipe_count)
            first = pl.multiple_of((chip * tensor_count + core) * rows, rows)
            piece = cot_refs[i]
            if in_kernel:
                piece = piece.at[:, pl.ds(pl.multiple_of(my_group * cols, cols), cols)]
            copies.append(pltpu.make_async_copy(piece, cot.at[pl.ds(first, rows)], sems.at[i]))
        for copy in copies:
            copy.start()
        for s in range(tensor_count):
            core = came_from(at_ref[2], s, tensor_count)
            for k in range(pipe_count):
                first = pl.multiple_of((k * tensor_count + core) * rows, rows)
                low[pl.ds(first, rows)] = low_refs[s][k]
        for copy in copies:
            copy.wait()
        for block in range(blocks_dev):
            at = slice(block * BLOCK, (block + 1) * BLOCK)
            both = lax.dot_general(low[at], cot[at], FIRST_BOTH, preferred_element_type=jnp.float32)
            half = jnp.where(my_group < group_half, both[:ADAPTER_RANK], both[ADAPTER_RANK:])
            half = half.astype(out_ref.dtype)
            for data in range(data_count):
                k = wrap(data - at_ref[0], data_count)
                out_ref[k, block] = half[data * up_rows : (data + 1) * up_rows]

    return call(
        kernel,
        "grad_up_pieces",
        in_specs=[SMEM] + [VMEM] * tensor_count + [ANY] * len(order),
        out_specs=VMEM,
        out_shape=jax.ShapeDtypeStruct((data_count, blocks_dev, up_rows, cols), jnp.bfloat16),
        scratch_shapes=[
            pltpu.VMEM((tok_dev, RANKS), jnp.bfloat16),
            pltpu.VMEM((tok_dev, cols), jnp.bfloat16),
            pltpu.SemaphoreType.DMA((len(order),)),
        ],
    )(at, *low_pieces, *pieces)


def grad_up(at, slot_of, slots, pieces):
    data_count = len(pieces)
    blocks_dev, up_rows, cols = pieces[0].shape

    def kernel(at_ref, *rest):
        piece_refs, out_ref = rest[:data_count], rest[data_count]
        out_ref[...] = jnp.zeros(out_ref.shape, out_ref.dtype)
        for k in range(data_count):
            data = wrap(at_ref[0] - k, data_count)
            for block in range(blocks_dev):
                slot = slot_of(at_ref, data, block)
                out_ref[slot] += piece_refs[k][block].astype(out_ref.dtype)

    return call(
        kernel,
        "grad_up",
        in_specs=[SMEM] + [VMEM] * data_count,
        out_specs=VMEM,
        out_shape=jax.ShapeDtypeStruct((slots, up_rows, cols), jnp.float32),
    )(at, *pieces)


def own_rows(at, up, cotangent):
    data_count = len(up)
    rows = cotangent.shape[0]

    def kernel(at_ref, cot_ref, *rest):
        up_refs, (b_ref, grad_ref) = rest[:data_count], rest[data_count:]
        pieces = []
        for data in range(data_count):
            came = wrap(at_ref[0] - data, data_count)
            piece = up_refs[0][...]
            for k in range(1, data_count):
                piece = jnp.where(came == k, up_refs[k][...], piece)
            pieces.append(piece)
        b = jnp.concatenate(pieces, axis=0)
        b_ref[...] = b
        cot = cot_ref[...]
        grad_ref[...] = jnp.concatenate(
            [
                lax.dot_general(cot[:, half], b[:, half], LAST_BOTH, preferred_element_type=jnp.float32)
                for half in (slice(0, KEY_WIDTH), slice(KEY_WIDTH, WIDTH))
            ],
            axis=1,
        ).astype(grad_ref.dtype)

    return call(
        kernel,
        "own_rows",
        in_specs=[SMEM, VMEM] + [VMEM] * data_count,
        out_specs=(VMEM, VMEM),
        out_shape=(
            jax.ShapeDtypeStruct((ADAPTER_RANK, WIDTH), jnp.bfloat16),
            jax.ShapeDtypeStruct((rows, RANKS), jnp.bfloat16),
        ),
    )(at, cotangent, *up)


def keys_and_values(at, base_pieces, low_sum, b_own):
    rows = base_pieces[0].shape[0]
    count = len(base_pieces)

    def kernel(at_ref, low_ref, b_ref, *rest):
        base_refs, out_ref = rest[:count], rest[count]
        low = low_ref[at_ref[1]]
        for first, ranks in ((0, slice(0, ADAPTER_RANK)), (KEY_WIDTH, slice(ADAPTER_RANK, RANKS))):
            at = slice(first, first + KEY_WIDTH)
            y = jnp.dot(low[:, ranks], b_ref[:, at], preferred_element_type=jnp.float32)
            for base_ref in base_refs:
                y += base_ref[:, at].astype(jnp.float32)
            out_ref[:, at] = y.astype(out_ref.dtype)

    return call(
        kernel,
        "keys_and_values",
        in_specs=[SMEM, VMEM, VMEM] + [VMEM] * count,
        out_specs=VMEM,
        out_shape=jax.ShapeDtypeStruct((rows, WIDTH), jnp.bfloat16),
    )(at, low_sum, b_own, *base_pieces)


def body(
    tokens, key_value_weight, adapter_down, adapter_up, tenant_of_block, slot_of_tenant, cotangent
):
    data_count = lax.axis_size("dp")
    pipe_count = lax.axis_size("pipe")
    tensor_count = lax.axis_size("tensor")
    group_count = pipe_count * tensor_count
    at_data, at_pipe, at_tensor = (lax.axis_index(a) for a in ("dp", "pipe", "tensor"))
    my_group = at_pipe * tensor_count + at_tensor
    tok_dev, feature_count = tokens.shape
    blocks_dev = tok_dev // BLOCK
    rows = tok_dev // group_count
    down_rows = adapter_down.shape[1]
    up_rows = adapter_up.shape[1]
    slots = adapter_down.shape[0]
    blocks = tenant_of_block.shape[0]

    at = jnp.stack([at_data, at_pipe, at_tensor]).astype(jnp.int32)
    at = jnp.concatenate([at, tenant_of_block, slot_of_tenant])

    def slot_of(at_ref, data, block):
        return at_ref[3 + blocks + at_ref[3 + data * blocks_dev + block]]

    b_send, a_send = pick(tenant_of_block, slot_of_tenant, adapter_down, adapter_up, rows)
    b_came = [b_send[0]] + [shift(b_send[k], "dp", k) for k in range(1, data_count)]
    b_own, grad_rows = own_rows(at, b_came, cotangent)

    a_send, b_came = lax.optimization_barrier((a_send, b_came))
    a_recv = lax.all_to_all(a_send, "dp", 0, 0, tiled=True)

    cot_chips = [cotangent] + gather_chips(cotangent)

    base_tokens, a_send = lax.optimization_barrier((tokens, a_send))
    tokens_by_group = base_tokens.reshape(pipe_count, tensor_count, rows, feature_count)
    parts = 2 if pipe_count % 2 == 0 else 1
    chips = pipe_count // parts
    base_send = base_product(at, tokens_by_group, key_value_weight, 1, tensor_count - 1, parts)
    base_came = [
        [swap(part[s - 1], "tensor", s) for part in base_send] for s in range(1, tensor_count)
    ]
    (base_keep,) = base_product(at, tokens_by_group, key_value_weight, 0, 1, 1)
    base_chip = [
        sum(
            [base_keep[0, k].astype(jnp.float32)]
            + [came[k // chips][k % chips].astype(jnp.float32) for came in base_came]
        )
        for k in range(pipe_count)
    ]
    base_chip[1:] = [piece.astype(jnp.bfloat16) for piece in base_chip[1:]]
    base_chip_came = [swap(base_chip[k], "pipe", k) for k in range(1, pipe_count)]

    cot_pieces = [cot_chips] + [
        [swap(piece, "tensor", s) for piece in cot_chips] for s in range(1, tensor_count)
    ]

    grad_chips = jnp.stack([grad_rows] + [swap(grad_rows, "pipe", k) for k in range(1, pipe_count)])
    grad_pieces = [grad_chips] + [swap(grad_chips, "tensor", s) for s in range(1, tensor_count)]
    x_features = base_tokens.T.reshape(data_count, down_rows, tok_dev)
    down_send = grad_down_pieces(at, x_features, grad_pieces)

    a_recv, down_send, cot_pieces, base_chip = lax.optimization_barrier(
        (a_recv, down_send, cot_pieces, base_chip)
    )
    down_recv = lax.all_to_all(down_send, "dp", 0, 0, tiled=True)

    input_base = cotangent_product(at, cot_pieces, key_value_weight)
    low_down, base_chip_came, input_base = lax.optimization_barrier(
        (a_recv, base_chip_came, input_base)
    )
    input_grad = input_gradient(at, input_base, grad_pieces, a_recv)
    low_part = low_product(at, tokens, low_down, pipe_count, tensor_count)
    low_core = sum(
        [low_part[0].astype(jnp.float32)]
        + [swap(low_part[s], "tensor", s).astype(jnp.float32) for s in range(1, tensor_count)]
    ).astype(jnp.bfloat16)
    low_came = [swap(low_core, "pipe", k) for k in range(1, pipe_count)]
    low_sum = sum([piece.astype(jnp.float32) for piece in [low_core] + low_came])
    low_sum = low_sum.astype(jnp.bfloat16)
    low_pieces = [low_sum] + [swap(low_sum, "tensor", s) for s in range(1, tensor_count)]
    key_value = keys_and_values(at, base_chip[:1] + base_chip_came, low_sum, b_own)

    up_pieces = grad_up_pieces(at, low_pieces, cot_pieces, data_count, up_rows)
    up_came = [up_pieces[0]] + [shift(up_pieces[k], "dp", k) for k in range(1, data_count)]
    grad_a = grad_down(at, slot_of, slots, down_recv)
    up_came, grad_a = lax.optimization_barrier((up_came, grad_a))
    grad_b = grad_up(at, slot_of, slots, up_came)
    return (key_value, input_grad, grad_a, grad_b)


def solution(mesh):
    atd = (
        P("dp", ("pipe", "tensor")),
        P(("pipe", "tensor"), None),
        P(None, ("pipe", "tensor", "dp"), None),
        P(None, "dp", None),
        P(),
        P(),
        P(("dp", "pipe", "tensor"), None),
    )
    return jax.shard_map(
        body,
        mesh=mesh,
        in_specs=atd,
        out_specs=(
            P(("dp", "pipe", "tensor"), None),
            P("dp", ("pipe", "tensor")),
            P(None, ("pipe", "tensor", "dp"), None),
            P(None, "dp", ("pipe", "tensor")),
        ),
        check_vma=False,
    )
```

```python
import jax
import jax.numpy as jnp
from jax import lax
from jax.experimental import pallas as pl
from jax.experimental.pallas import tpu as pltpu
from jax.sharding import PartitionSpec as P

KEY_WIDTH = 1024
ADAPTER_RANK = 64
BLOCK = 128
RANKS = 2 * ADAPTER_RANK
WIDTH = 2 * KEY_WIDTH
VMEM_LIMIT = 24 * 1024 * 1024
VMEM_MOST = 60 * 1024 * 1024
LAST_BOTH = (((1,), (1,)), ((), ()))
FIRST_BOTH = (((0,), (0,)), ((), ()))
SMEM = pl.BlockSpec(memory_space=pltpu.SMEM)
VMEM = pl.BlockSpec(memory_space=pltpu.VMEM)
HBM = pl.BlockSpec(memory_space=pltpu.HBM)
ANY = pl.BlockSpec(memory_space=pl.ANY)


def call(kernel, name, vmem=VMEM_LIMIT, **more):
    return pl.pallas_call(
        kernel,
        compiler_params=pltpu.CompilerParams(vmem_limit_bytes=vmem),
        cost_estimate=pl.CostEstimate(flops=1024, bytes_accessed=1024, transcendentals=0),
        name=name,
        **more,
    )


def wrap(index, count):
    return lax.rem(index + 2 * count, count)


def shift(piece, axis, k):
    count = lax.axis_size(axis)
    return lax.ppermute(piece, axis, [(i, (i + k) % count) for i in range(count)])


def paired(count):
    return count & (count - 1) == 0


def partner(index, k, count):
    return index ^ k if paired(count) else (index + k) % count


def came_from(index, k, count):
    return index ^ k if paired(count) else wrap(index - k, count)


def which_partner(other, index, count):
    return other ^ index if paired(count) else wrap(other - index, count)


def swap(piece, axis, k):
    count = lax.axis_size(axis)
    return lax.ppermute(piece, axis, [(i, partner(i, k, count)) for i in range(count)])


def gather_chips(piece):
    count = lax.axis_size("pipe")
    if count != 4 or piece.shape[0] % 32:
        return [swap(piece, "pipe", k) for k in range(1, count)]
    first, second = swap(piece, "pipe", 1), swap(piece, "pipe", 2)
    half = piece.shape[0] // 2
    third = [swap(second[:half], "pipe", 1), swap(first[half:], "pipe", 2)]
    return [first, second, jnp.concatenate(third)]


def up_rides(adapter_up):
    return adapter_up.shape[1] % 16 == 0


def pick(tenant_of_block, slot_of_tenant, adapter_down, adapter_up, blocks_dev, group_rows):
    data_count = tenant_of_block.shape[0] // blocks_dev
    down_rows, ranks = adapter_down.shape[1:]
    up_rows, width = adapter_up.shape[1:]
    first_up = blocks_dev * down_rows
    rides = up_rides(adapter_up)
    total = first_up + (up_rows * width // ranks if rides else 0)

    def kernel(
        tenant_ref, slot_ref, down_ref, up_ref, out_ref, rows, tiles, down_sem, up_sem, out_sem
    ):
        own_block = lax.axis_index(("pipe", "tensor")) * group_rows // BLOCK
        downs, ups, outs = [], [], []
        for data in range(data_count):
            downs.append([])
            for block in range(blocks_dev):
                here = rows.at[data, pl.ds(block * down_rows, down_rows)]
                slot = slot_ref[tenant_ref[data * blocks_dev + block]]
                downs[data].append(
                    pltpu.make_async_copy(down_ref.at[slot], here, down_sem.at[data, block])
                )
            if rides:
                slot = slot_ref[tenant_ref[data * blocks_dev + own_block]]
                ups.append(pltpu.make_async_copy(up_ref.at[slot], tiles.at[data], up_sem.at[data]))
            outs.append(pltpu.make_async_copy(rows.at[data], out_ref.at[data], out_sem.at[data]))
            for copy in downs[data] + ups[data:]:
                copy.start()
        for data in range(data_count):
            for copy in downs[data] + ups[data : data + 1]:
                copy.wait()
            for n in range(width // ranks if rides else 0):
                first = first_up + n * up_rows
                rows[data, first : first + up_rows] = tiles[data, :, n * ranks : (n + 1) * ranks]
            outs[data].start()
        for copy in outs:
            copy.wait()

    return call(
        kernel,
        "pick_rows",
        VMEM_MOST,
        out_shape=pltpu.HBM((data_count, total, ranks), adapter_down.dtype),
        in_specs=[SMEM, SMEM, HBM, HBM],
        out_specs=HBM,
        scratch_shapes=[
            pltpu.VMEM((data_count, total, ranks), adapter_down.dtype),
            pltpu.VMEM((data_count, up_rows, width), adapter_up.dtype),
            pltpu.SemaphoreType.DMA((data_count, blocks_dev)),
            pltpu.SemaphoreType.DMA((data_count,)),
            pltpu.SemaphoreType.DMA((data_count,)),
        ],
    )(tenant_of_block, slot_of_tenant, adapter_down, adapter_up)


def pick_up(at, slot_of, adapter_up, data_count):
    slots = jnp.stack([slot_of(at, data, at[3]) for data in range(data_count)])
    return jnp.take(adapter_up, slots, axis=0)


def base_product(at, tokens, weight, first, count, parts):
    pipe_count, tensor_count, rows, depth = tokens.shape
    tile = 1024
    chips = pipe_count // parts

    def kernel(at_ref, x_ref, w_ref, *out_refs):
        x = x_ref[...].reshape(pipe_count * rows, depth)
        y = jnp.dot(x, w_ref[...], preferred_element_type=jnp.float32).astype(out_refs[0].dtype)
        for chip in range(pipe_count):
            k = which_partner(chip, at_ref[1], pipe_count)
            for part, out_ref in enumerate(out_refs):

                @pl.when((k >= part * chips) & (k < (part + 1) * chips))
                def _():
                    out_ref[0, k - part * chips] = y[chip * rows : (chip + 1) * rows]

    out = call(
        kernel,
        "base_product",
        grid_spec=pltpu.PrefetchScalarGridSpec(
            num_scalar_prefetch=1,
            grid=(WIDTH // tile, count),
            in_specs=[
                pl.BlockSpec(
                    (pipe_count, 1, rows, depth),
                    lambda n, s, at: (0, partner(at[2], s + first, tensor_count), 0, 0),
                ),
                pl.BlockSpec((depth, tile), lambda n, s, at: (0, n)),
            ],
            out_specs=(pl.BlockSpec((1, chips, rows, tile), lambda n, s, at: (s, 0, 0, n)),) * parts,
        ),
        out_shape=(jax.ShapeDtypeStruct((count, chips, rows, WIDTH), jnp.bfloat16),) * parts,
    )(at, tokens, weight)
    return out


def low_product(at, tokens, down, pipe_count, tensor_count):
    tok_dev, depth = tokens.shape
    down_rows = depth // down.shape[0]
    rows = tok_dev // (pipe_count * tensor_count)

    def kernel(at_ref, x_ref, a_ref, out_ref):
        for block in range(tok_dev // BLOCK):
            a = a_ref[:, block * down_rows : (block + 1) * down_rows].reshape(depth, RANKS)
            x = x_ref[block * BLOCK : (block + 1) * BLOCK]
            y = jnp.dot(x, a, preferred_element_type=jnp.float32).astype(out_ref.dtype)
            for part in range(BLOCK // rows):
                chip, core = divmod(block * (BLOCK // rows) + part, tensor_count)
                core = which_partner(core, at_ref[2], tensor_count)
                out_ref[core, chip] = y[part * rows : (part + 1) * rows]

    return call(
        kernel,
        "low_product",
        in_specs=[SMEM, VMEM, VMEM],
        out_specs=VMEM,
        out_shape=jax.ShapeDtypeStruct((tensor_count, pipe_count, rows, RANKS), jnp.bfloat16),
    )(at, tokens, down)


def cotangent_product(at, cot_pieces, weight):
    tensor_count, pipe_count = len(cot_pieces), len(cot_pieces[0])
    rows = cot_pieces[0][0].shape[0]
    depth = weight.shape[0]
    tok_dev = tensor_count * pipe_count * rows
    tile = 256 if depth % 256 == 0 else depth
    order = [(s, k) for s in range(tensor_count) for k in range(pipe_count)]

    def kernel(at_ref, w_ref, *rest):
        cot_refs, (out_ref, cot, sems) = rest[: len(order)], rest[len(order) :]

        @pl.when(pl.program_id(0) == 0)
        def _():
            copies = []
            for i, (s, k) in enumerate(order):
                chip = came_from(at_ref[1], k, pipe_count)
                core = came_from(at_ref[2], s, tensor_count)
                first = pl.multiple_of((chip * tensor_count + core) * rows, rows)
                copies.append(
                    pltpu.make_async_copy(cot_refs[i], cot.at[pl.ds(first, rows)], sems.at[i])
                )
            for copy in copies:
                copy.start()
            for copy in copies:
                copy.wait()

        out_ref[...] = lax.dot_general(
            cot[...], w_ref[...], LAST_BOTH, preferred_element_type=jnp.float32
        )

    return call(
        kernel,
        "cotangent_product",
        grid=(depth // tile,),
        in_specs=[SMEM, pl.BlockSpec((tile, WIDTH), lambda n: (n, 0))] + [ANY] * len(order),
        out_specs=pl.BlockSpec((tok_dev, tile), lambda n: (0, n)),
        out_shape=jax.ShapeDtypeStruct((tok_dev, depth), jnp.float32),
        scratch_shapes=[
            pltpu.VMEM((tok_dev, WIDTH), jnp.bfloat16),
            pltpu.SemaphoreType.DMA((len(order),)),
        ],
    )(at, weight, *[cot_pieces[s][k] for s, k in order])


def input_gradient(at, base, grad_pieces, down):
    data_count, all_rows, _ = down.shape
    tensor_count = len(grad_pieces)
    pipe_count, _, rows, _ = grad_pieces[0].shape
    tok_dev, depth = base.shape
    down_rows = depth // data_count
    planes = next((n for n in range(1, data_count) if n * down_rows % 256 == 0), data_count)
    tile = planes * down_rows

    def kernel(at_ref, base_ref, a_ref, *rest):
        grad_refs, (out_ref, grad) = rest[:tensor_count], rest[tensor_count:]

        @pl.when(pl.program_id(0) == 0)
        def _():
            for s in range(tensor_count):
                core = came_from(at_ref[2], s, tensor_count)
                for k in range(pipe_count):
                    chip = came_from(at_ref[1], k, pipe_count)
                    first = pl.multiple_of((chip * tensor_count + core) * rows, rows)
                    grad[pl.ds(first, rows)] = grad_refs[s][k, 0]

        for block in range(tok_dev // BLOCK):
            here = slice(block * BLOCK, (block + 1) * BLOCK)
            a = a_ref[:, block * down_rows : (block + 1) * down_rows].reshape(tile, RANKS)
            low = lax.dot_general(grad[here], a, LAST_BOTH, preferred_element_type=jnp.float32)
            out_ref[here] = (base_ref[here] + low).astype(out_ref.dtype)

    grad_shape = (pipe_count, data_count, rows, RANKS)
    return call(
        kernel,
        "input_gradient",
        grid=(data_count // planes,),
        in_specs=[
            SMEM,
            pl.BlockSpec((tok_dev, tile), lambda n: (0, n)),
            pl.BlockSpec((planes, all_rows, RANKS), lambda n: (n, 0, 0)),
        ]
        + [pl.BlockSpec(grad_shape, lambda n: (0, 0, 0, 0))] * tensor_count,
        out_specs=pl.BlockSpec((tok_dev, tile), lambda n: (0, n)),
        out_shape=jax.ShapeDtypeStruct((tok_dev, depth), jnp.bfloat16),
        scratch_shapes=[pltpu.VMEM((tok_dev, RANKS), jnp.bfloat16)],
    )(at, base, down, *grad_pieces)


def grad_down(at, slot_of, slots, x_features, grad_pieces):
    data_count, down_rows, tok_dev = x_features.shape
    tensor_count = len(grad_pieces)
    pipe_count, _, rows, _ = grad_pieces[0].shape
    blocks_dev = tok_dev // BLOCK

    def kernel(at_ref, x_ref, *rest):
        grad_refs, (out_ref, grad, x, sems) = rest[:tensor_count], rest[tensor_count:]
        copies = [
            pltpu.make_async_copy(x_ref.at[data], x.at[data], sems.at[data])
            for data in range(data_count)
        ]
        for copy in copies:
            copy.start()
        for s in range(tensor_count):
            core = came_from(at_ref[2], s, tensor_count)
            for k in range(pipe_count):
                chip = came_from(at_ref[1], k, pipe_count)
                first = pl.multiple_of((chip * tensor_count + core) * rows, rows)
                for m in range(data_count):
                    data = wrap(at_ref[0] - m, data_count)
                    grad[data, pl.ds(first, rows)] = grad_refs[s][k, m]
        out_ref[...] = jnp.zeros(out_ref.shape, out_ref.dtype)
        for data in range(data_count):
            copies[data].wait()
            for block in range(blocks_dev):
                slot = slot_of(at_ref, data, block)
                here = slice(block * BLOCK, (block + 1) * BLOCK)
                out_ref[slot] += jnp.dot(
                    x[data, :, here], grad[data, here], preferred_element_type=jnp.float32
                )

    return call(
        kernel,
        "grad_down",
        VMEM_MOST,
        in_specs=[SMEM, HBM] + [VMEM] * tensor_count,
        out_specs=VMEM,
        out_shape=jax.ShapeDtypeStruct((slots, down_rows, RANKS), jnp.float32),
        scratch_shapes=[
            pltpu.VMEM((data_count, tok_dev, RANKS), jnp.bfloat16),
            pltpu.VMEM(x_features.shape, jnp.bfloat16),
            pltpu.SemaphoreType.DMA((data_count,)),
        ],
    )(at, x_features, *grad_pieces)


def grad_up_pieces(at, low_pieces, cot_pieces, data_count, up_rows):
    tensor_count, pipe_count = len(cot_pieces), len(cot_pieces[0])
    group_count = tensor_count * pipe_count
    rows = cot_pieces[0][0].shape[0]
    cols = WIDTH // group_count
    tok_dev = group_count * rows
    blocks_dev = tok_dev // BLOCK
    group_half = group_count // 2
    order = [(s, k) for s in range(tensor_count) for k in range(pipe_count)]
    pieces = [cot_pieces[s][k] for s, k in order]
    in_kernel = cols % 128 == 0
    if not in_kernel:
        first_col = (at[1] * tensor_count + at[2]) * cols
        pieces = [lax.dynamic_slice_in_dim(piece, first_col, cols, 1) for piece in pieces]

    def kernel(at_ref, *rest):
        low_refs, rest = rest[:tensor_count], rest[tensor_count:]
        cot_refs, (out_ref, low, cot, sems) = rest[: len(order)], rest[len(order) :]
        my_group = at_ref[1] * tensor_count + at_ref[2]
        copies = []
        for i, (s, k) in enumerate(order):
            core = came_from(at_ref[2], s, tensor_count)
            chip = came_from(at_ref[1], k, pipe_count)
            first = pl.multiple_of((chip * tensor_count + core) * rows, rows)
            piece = cot_refs[i]
            if in_kernel:
                piece = piece.at[:, pl.ds(pl.multiple_of(my_group * cols, cols), cols)]
            copies.append(pltpu.make_async_copy(piece, cot.at[pl.ds(first, rows)], sems.at[i]))
        for copy in copies:
            copy.start()
        for s in range(tensor_count):
            core = came_from(at_ref[2], s, tensor_count)
            for k in range(pipe_count):
                first = pl.multiple_of((k * tensor_count + core) * rows, rows)
                low[pl.ds(first, rows)] = low_refs[s][k]
        for copy in copies:
            copy.wait()
        for block in range(blocks_dev):
            at = slice(block * BLOCK, (block + 1) * BLOCK)
            both = lax.dot_general(low[at], cot[at], FIRST_BOTH, preferred_element_type=jnp.float32)
            half = jnp.where(my_group < group_half, both[:ADAPTER_RANK], both[ADAPTER_RANK:])
            half = half.astype(out_ref.dtype)
            for data in range(data_count):
                k = wrap(data - at_ref[0], data_count)
                out_ref[k, block] = half[data * up_rows : (data + 1) * up_rows]

    return call(
        kernel,
        "grad_up_pieces",
        in_specs=[SMEM] + [VMEM] * tensor_count + [ANY] * len(order),
        out_specs=VMEM,
        out_shape=jax.ShapeDtypeStruct((data_count, blocks_dev, up_rows, cols), jnp.bfloat16),
        scratch_shapes=[
            pltpu.VMEM((tok_dev, RANKS), jnp.bfloat16),
            pltpu.VMEM((tok_dev, cols), jnp.bfloat16),
            pltpu.SemaphoreType.DMA((len(order),)),
        ],
    )(at, *low_pieces, *pieces)


def grad_up(at, slot_of, slots, pieces):
    data_count = len(pieces)
    blocks_dev, up_rows, cols = pieces[0].shape

    def kernel(at_ref, *rest):
        piece_refs, out_ref = rest[:data_count], rest[data_count]
        out_ref[...] = jnp.zeros(out_ref.shape, out_ref.dtype)
        for k in range(data_count):
            data = wrap(at_ref[0] - k, data_count)
            for block in range(blocks_dev):
                slot = slot_of(at_ref, data, block)
                out_ref[slot] += piece_refs[k][block].astype(out_ref.dtype)

    return call(
        kernel,
        "grad_up",
        in_specs=[SMEM] + [VMEM] * data_count,
        out_specs=VMEM,
        out_shape=jax.ShapeDtypeStruct((slots, up_rows, cols), jnp.float32),
    )(at, *pieces)


def own_rows(came, up, cotangent, first_up):
    rows = cotangent.shape[0]
    data_count = came.shape[0]
    up_rows = ADAPTER_RANK // data_count

    def kernel(cot_ref, came_ref, b_ref, grad_ref, tiles, sem):
        if up is None:
            copy = pltpu.make_async_copy(came_ref.at[:, pl.ds(first_up, tiles.shape[1])], tiles, sem)
            copy.start()
            copy.wait()
            for data in range(data_count):
                for n in range(WIDTH // RANKS):
                    b_ref[
                        data * up_rows : (data + 1) * up_rows, n * RANKS : (n + 1) * RANKS
                    ] = tiles[data, n * up_rows : (n + 1) * up_rows]
        else:
            b_ref[...] = came_ref[...]
        cot, b = cot_ref[...], b_ref[...]
        grad_ref[...] = jnp.concatenate(
            [
                lax.dot_general(cot[:, half], b[:, half], LAST_BOTH, preferred_element_type=jnp.float32)
                for half in (slice(0, KEY_WIDTH), slice(KEY_WIDTH, WIDTH))
            ],
            axis=1,
        ).astype(grad_ref.dtype)

    tile_rows = up_rows * WIDTH // RANKS
    return call(
        kernel,
        "own_rows",
        in_specs=[VMEM, ANY if up is None else VMEM],
        out_specs=(VMEM, VMEM),
        out_shape=(
            jax.ShapeDtypeStruct((ADAPTER_RANK, WIDTH), jnp.bfloat16),
            jax.ShapeDtypeStruct((rows, RANKS), jnp.bfloat16),
        ),
        scratch_shapes=[
            pltpu.VMEM((data_count, tile_rows, RANKS), jnp.bfloat16),
            pltpu.SemaphoreType.DMA,
        ],
    )(cotangent, came if up is None else up)


def keys_and_values(at, base_pieces, low_sum, b_own):
    rows = base_pieces[0].shape[0]
    count = len(base_pieces)

    def kernel(at_ref, low_ref, b_ref, *rest):
        base_refs, out_ref = rest[:count], rest[count]
        low = low_ref[at_ref[1]]
        for first, ranks in ((0, slice(0, ADAPTER_RANK)), (KEY_WIDTH, slice(ADAPTER_RANK, RANKS))):
            at = slice(first, first + KEY_WIDTH)
            y = jnp.dot(low[:, ranks], b_ref[:, at], preferred_element_type=jnp.float32)
            for base_ref in base_refs:
                y += base_ref[:, at].astype(jnp.float32)
            out_ref[:, at] = y.astype(out_ref.dtype)

    return call(
        kernel,
        "keys_and_values",
        in_specs=[SMEM, VMEM, VMEM] + [VMEM] * count,
        out_specs=VMEM,
        out_shape=jax.ShapeDtypeStruct((rows, WIDTH), jnp.bfloat16),
    )(at, low_sum, b_own, *base_pieces)


def body(
    tokens, key_value_weight, adapter_down, adapter_up, tenant_of_block, slot_of_tenant, cotangent
):
    data_count = lax.axis_size("dp")
    pipe_count = lax.axis_size("pipe")
    tensor_count = lax.axis_size("tensor")
    group_count = pipe_count * tensor_count
    at_data, at_pipe, at_tensor = (lax.axis_index(a) for a in ("dp", "pipe", "tensor"))
    my_group = at_pipe * tensor_count + at_tensor
    tok_dev, feature_count = tokens.shape
    blocks_dev = tok_dev // BLOCK
    rows = tok_dev // group_count
    down_rows = adapter_down.shape[1]
    up_rows = adapter_up.shape[1]
    slots = adapter_down.shape[0]
    blocks = tenant_of_block.shape[0]

    own_block = my_group * rows // BLOCK
    at = jnp.stack([at_data, at_pipe, at_tensor, own_block]).astype(jnp.int32)
    at = jnp.concatenate([at, tenant_of_block, slot_of_tenant])

    def slot_of(at_ref, data, block):
        return at_ref[4 + blocks + at_ref[4 + data * blocks_dev + block]]

    a_send = pick(
        tenant_of_block, slot_of_tenant, adapter_down, adapter_up, blocks_dev, rows
    )
    a_recv = lax.all_to_all(a_send, "dp", 0, 0, tiled=True)
    up = None
    if not up_rides(adapter_up):
        up = lax.all_to_all(pick_up(at, slot_of, adapter_up, data_count), "dp", 0, 0, tiled=True)
        up = up.reshape(ADAPTER_RANK, WIDTH)

    cot_chips = [cotangent] + gather_chips(cotangent)

    base_tokens, a_send = lax.optimization_barrier((tokens, a_send))
    tokens_by_group = base_tokens.reshape(pipe_count, tensor_count, rows, feature_count)
    parts = 2 if pipe_count % 2 == 0 else 1
    chips = pipe_count // parts
    base_send = base_product(at, tokens_by_group, key_value_weight, 1, tensor_count - 1, parts)
    base_came = [
        [swap(part[s - 1], "tensor", s) for part in base_send] for s in range(1, tensor_count)
    ]
    (base_keep,) = base_product(at, tokens_by_group, key_value_weight, 0, 1, 1)
    base_chip = [
        sum(
            [base_keep[0, k].astype(jnp.float32)]
            + [came[k // chips][k % chips].astype(jnp.float32) for came in base_came]
        )
        for k in range(pipe_count)
    ]
    base_chip[1:] = [piece.astype(jnp.bfloat16) for piece in base_chip[1:]]
    base_chip_came = [swap(base_chip[k], "pipe", k) for k in range(1, pipe_count)]

    cot_pieces = [cot_chips] + [
        [swap(piece, "tensor", s) for piece in cot_chips] for s in range(1, tensor_count)
    ]
    input_base = cotangent_product(at, cot_pieces, key_value_weight)

    x_send = base_tokens.T.reshape(data_count, down_rows, tok_dev)

    a_recv, x_send, input_base, base_chip_came[:2] = lax.optimization_barrier(
        (a_recv, x_send, input_base, base_chip_came[:2])
    )
    b_own, grad_rows = own_rows(a_recv, up, cotangent, blocks_dev * down_rows)
    grad_data = [grad_rows] + [shift(grad_rows, "dp", k) for k in range(1, data_count)]
    x_send, grad_data = lax.optimization_barrier((x_send, grad_data))
    x_recv = lax.all_to_all(x_send, "dp", 0, 0, tiled=True)

    grad_all = jnp.stack(grad_data)
    grad_chips = jnp.stack([grad_all] + [swap(grad_all, "pipe", k) for k in range(1, pipe_count)])
    grad_pieces = [grad_chips] + [swap(grad_chips, "tensor", s) for s in range(1, tensor_count)]
    input_grad = input_gradient(at, input_base, grad_pieces, a_recv)

    low_down, base_chip_came, grad_data = lax.optimization_barrier(
        (a_recv, base_chip_came, grad_data)
    )
    low_part = low_product(at, tokens, low_down, pipe_count, tensor_count)
    low_core = sum(
        [low_part[0].astype(jnp.float32)]
        + [swap(low_part[s], "tensor", s).astype(jnp.float32) for s in range(1, tensor_count)]
    ).astype(jnp.bfloat16)
    low_came = [swap(low_core, "pipe", k) for k in range(1, pipe_count)]
    low_sum = sum([piece.astype(jnp.float32) for piece in [low_core] + low_came])
    low_sum = low_sum.astype(jnp.bfloat16)
    low_pieces = [low_sum] + [swap(low_sum, "tensor", s) for s in range(1, tensor_count)]
    key_value = keys_and_values(at, base_chip[:1] + base_chip_came, low_sum, b_own)

    up_pieces = grad_up_pieces(at, low_pieces, cot_pieces, data_count, up_rows)
    up_came = [up_pieces[0]] + [shift(up_pieces[k], "dp", k) for k in range(1, data_count)]
    grad_a = grad_down(at, slot_of, slots, x_recv, grad_pieces)
    up_came, grad_a = lax.optimization_barrier((up_came, grad_a))
    grad_b = grad_up(at, slot_of, slots, up_came)
    return (key_value, input_grad, grad_a, grad_b)


def solution(mesh):
    atd = (
        P("dp", ("pipe", "tensor")),
        P(("pipe", "tensor"), None),
        P(None, ("pipe", "tensor", "dp"), None),
        P(None, "dp", None),
        P(),
        P(),
        P(("dp", "pipe", "tensor"), None),
    )
    return jax.shard_map(
        body,
        mesh=mesh,
        in_specs=atd,
        out_specs=(
            P(("dp", "pipe", "tensor"), None),
            P("dp", ("pipe", "tensor")),
            P(None, ("pipe", "tensor", "dp"), None),
            P(None, "dp", ("pipe", "tensor")),
        ),
        check_vma=False,
    )
```

```python
import jax
import jax.numpy as jnp
from jax import lax
from jax.experimental import pallas as pl
from jax.experimental.pallas import tpu as pltpu
from jax.sharding import PartitionSpec as P

KEY_WIDTH = 1024
ADAPTER_RANK = 64
BLOCK = 128
RANKS = 2 * ADAPTER_RANK
WIDTH = 2 * KEY_WIDTH
VMEM_LIMIT = 24 * 1024 * 1024
VMEM_MOST = 60 * 1024 * 1024
LAST_BOTH = (((1,), (1,)), ((), ()))
FIRST_BOTH = (((0,), (0,)), ((), ()))
SMEM = pl.BlockSpec(memory_space=pltpu.SMEM)
VMEM = pl.BlockSpec(memory_space=pltpu.VMEM)
HBM = pl.BlockSpec(memory_space=pltpu.HBM)
ANY = pl.BlockSpec(memory_space=pl.ANY)


def call(kernel, name, vmem=VMEM_LIMIT, **more):
    return pl.pallas_call(
        kernel,
        compiler_params=pltpu.CompilerParams(vmem_limit_bytes=vmem),
        cost_estimate=pl.CostEstimate(flops=1024, bytes_accessed=1024, transcendentals=0),
        name=name,
        **more,
    )


def wrap(index, count):
    return lax.rem(index + 2 * count, count)


def shift(piece, axis, k):
    count = lax.axis_size(axis)
    return lax.ppermute(piece, axis, [(i, (i + k) % count) for i in range(count)])


def paired(count):
    return count & (count - 1) == 0


def partner(index, k, count):
    return index ^ k if paired(count) else (index + k) % count


def came_from(index, k, count):
    return index ^ k if paired(count) else wrap(index - k, count)


def which_partner(other, index, count):
    return other ^ index if paired(count) else wrap(other - index, count)


def swap(piece, axis, k):
    count = lax.axis_size(axis)
    return lax.ppermute(piece, axis, [(i, partner(i, k, count)) for i in range(count)])


def gather_chips(piece, behind):
    count = lax.axis_size("pipe")
    in_halves = count == 4 and piece.shape[0] % 32 == 0
    came = [swap(piece, "pipe", k) for k in range(1, 3 if in_halves else count)]
    came, one, two = lax.optimization_barrier((came, behind, behind))
    if in_halves:
        half = piece.shape[0] // 2
        third = [swap(came[1][:half], "pipe", 1), swap(came[0][half:], "pipe", 2)]
        came = came + [jnp.concatenate(third)]
    return came, one, two


def up_rides(adapter_up):
    return adapter_up.shape[1] % 16 == 0


def pick(tenant_of_block, slot_of_tenant, adapter_down, adapter_up, blocks_dev, group_rows):
    data_count = tenant_of_block.shape[0] // blocks_dev
    down_rows, ranks = adapter_down.shape[1:]
    up_rows, width = adapter_up.shape[1:]
    first_up = blocks_dev * down_rows
    rides = up_rides(adapter_up)
    total = first_up + (up_rows * width // ranks if rides else 0)

    def kernel(
        tenant_ref, slot_ref, down_ref, up_ref, out_ref, rows, tiles, down_sem, up_sem, out_sem
    ):
        own_block = lax.axis_index(("pipe", "tensor")) * group_rows // BLOCK
        downs, ups, outs = [], [], []
        for data in range(data_count):
            downs.append([])
            for block in range(blocks_dev):
                here = rows.at[data, pl.ds(block * down_rows, down_rows)]
                slot = slot_ref[tenant_ref[data * blocks_dev + block]]
                downs[data].append(
                    pltpu.make_async_copy(down_ref.at[slot], here, down_sem.at[data, block])
                )
            if rides:
                slot = slot_ref[tenant_ref[data * blocks_dev + own_block]]
                ups.append(pltpu.make_async_copy(up_ref.at[slot], tiles.at[data], up_sem.at[data]))
            outs.append(pltpu.make_async_copy(rows.at[data], out_ref.at[data], out_sem.at[data]))
            for copy in downs[data] + ups[data:]:
                copy.start()
        for data in range(data_count):
            for copy in downs[data] + ups[data : data + 1]:
                copy.wait()
            for n in range(width // ranks if rides else 0):
                first = first_up + n * up_rows
                rows[data, first : first + up_rows] = tiles[data, :, n * ranks : (n + 1) * ranks]
            outs[data].start()
        for copy in outs:
            copy.wait()

    return call(
        kernel,
        "pick_rows",
        VMEM_MOST,
        out_shape=pltpu.HBM((data_count, total, ranks), adapter_down.dtype),
        in_specs=[SMEM, SMEM, HBM, HBM],
        out_specs=HBM,
        scratch_shapes=[
            pltpu.VMEM((data_count, total, ranks), adapter_down.dtype),
            pltpu.VMEM((data_count, up_rows, width), adapter_up.dtype),
            pltpu.SemaphoreType.DMA((data_count, blocks_dev)),
            pltpu.SemaphoreType.DMA((data_count,)),
            pltpu.SemaphoreType.DMA((data_count,)),
        ],
    )(tenant_of_block, slot_of_tenant, adapter_down, adapter_up)


def pick_up(at, slot_of, adapter_up, data_count):
    slots = jnp.stack([slot_of(at, data, at[3]) for data in range(data_count)])
    return jnp.take(adapter_up, slots, axis=0)


def base_product(at, tokens, weight, first, count, parts):
    pipe_count, tensor_count, rows, depth = tokens.shape
    tile = 1024
    chips = pipe_count // parts

    def kernel(at_ref, x_ref, w_ref, *out_refs):
        x = x_ref[...].reshape(pipe_count * rows, depth)
        y = jnp.dot(x, w_ref[...], preferred_element_type=jnp.float32).astype(out_refs[0].dtype)
        for chip in range(pipe_count):
            k = which_partner(chip, at_ref[1], pipe_count)
            for part, out_ref in enumerate(out_refs):

                @pl.when((k >= part * chips) & (k < (part + 1) * chips))
                def _():
                    out_ref[0, k - part * chips] = y[chip * rows : (chip + 1) * rows]

    out = call(
        kernel,
        "base_product",
        grid_spec=pltpu.PrefetchScalarGridSpec(
            num_scalar_prefetch=1,
            grid=(WIDTH // tile, count),
            in_specs=[
                pl.BlockSpec(
                    (pipe_count, 1, rows, depth),
                    lambda n, s, at: (0, partner(at[2], s + first, tensor_count), 0, 0),
                ),
                pl.BlockSpec((depth, tile), lambda n, s, at: (0, n)),
            ],
            out_specs=(pl.BlockSpec((1, chips, rows, tile), lambda n, s, at: (s, 0, 0, n)),) * parts,
        ),
        out_shape=(jax.ShapeDtypeStruct((count, chips, rows, WIDTH), jnp.bfloat16),) * parts,
    )(at, tokens, weight)
    return out


def low_product(at, tokens, down, pipe_count, tensor_count):
    tok_dev, depth = tokens.shape
    down_rows = depth // down.shape[0]
    rows = tok_dev // (pipe_count * tensor_count)

    def kernel(at_ref, x_ref, a_ref, out_ref):
        for block in range(tok_dev // BLOCK):
            a = a_ref[:, block * down_rows : (block + 1) * down_rows].reshape(depth, RANKS)
            x = x_ref[block * BLOCK : (block + 1) * BLOCK]
            y = jnp.dot(x, a, preferred_element_type=jnp.float32).astype(out_ref.dtype)
            for part in range(BLOCK // rows):
                chip, core = divmod(block * (BLOCK // rows) + part, tensor_count)
                core = which_partner(core, at_ref[2], tensor_count)
                out_ref[core, chip] = y[part * rows : (part + 1) * rows]

    return call(
        kernel,
        "low_product",
        in_specs=[SMEM, VMEM, VMEM],
        out_specs=VMEM,
        out_shape=jax.ShapeDtypeStruct((tensor_count, pipe_count, rows, RANKS), jnp.bfloat16),
    )(at, tokens, down)


def cotangent_product(at, cot_pieces, weight):
    tensor_count, pipe_count = len(cot_pieces), len(cot_pieces[0])
    rows = cot_pieces[0][0].shape[0]
    depth = weight.shape[0]
    tok_dev = tensor_count * pipe_count * rows
    tile = 256 if depth % 256 == 0 else depth
    order = [(s, k) for s in range(tensor_count) for k in range(pipe_count)]

    def kernel(at_ref, w_ref, *rest):
        cot_refs, (out_ref, cot, sems) = rest[: len(order)], rest[len(order) :]

        @pl.when(pl.program_id(0) == 0)
        def _():
            copies = []
            for i, (s, k) in enumerate(order):
                chip = came_from(at_ref[1], k, pipe_count)
                core = came_from(at_ref[2], s, tensor_count)
                first = pl.multiple_of((chip * tensor_count + core) * rows, rows)
                copies.append(
                    pltpu.make_async_copy(cot_refs[i], cot.at[pl.ds(first, rows)], sems.at[i])
                )
            for copy in copies:
                copy.start()
            for copy in copies:
                copy.wait()

        out_ref[...] = lax.dot_general(
            cot[...], w_ref[...], LAST_BOTH, preferred_element_type=jnp.float32
        )

    return call(
        kernel,
        "cotangent_product",
        grid=(depth // tile,),
        in_specs=[SMEM, pl.BlockSpec((tile, WIDTH), lambda n: (n, 0))] + [ANY] * len(order),
        out_specs=pl.BlockSpec((tok_dev, tile), lambda n: (0, n)),
        out_shape=jax.ShapeDtypeStruct((tok_dev, depth), jnp.float32),
        scratch_shapes=[
            pltpu.VMEM((tok_dev, WIDTH), jnp.bfloat16),
            pltpu.SemaphoreType.DMA((len(order),)),
        ],
    )(at, weight, *[cot_pieces[s][k] for s, k in order])


def input_gradient(at, base, grad_pieces, down):
    data_count, all_rows, _ = down.shape
    tensor_count = len(grad_pieces)
    pipe_count, _, rows, _ = grad_pieces[0].shape
    tok_dev, depth = base.shape
    down_rows = depth // data_count
    planes = next((n for n in range(1, data_count) if n * down_rows % 256 == 0), data_count)
    tile = planes * down_rows

    def kernel(at_ref, base_ref, a_ref, *rest):
        grad_refs, (out_ref, grad) = rest[:tensor_count], rest[tensor_count:]

        @pl.when(pl.program_id(0) == 0)
        def _():
            for s in range(tensor_count):
                core = came_from(at_ref[2], s, tensor_count)
                for k in range(pipe_count):
                    chip = came_from(at_ref[1], k, pipe_count)
                    first = pl.multiple_of((chip * tensor_count + core) * rows, rows)
                    grad[pl.ds(first, rows)] = grad_refs[s][k, 0]

        for block in range(tok_dev // BLOCK):
            here = slice(block * BLOCK, (block + 1) * BLOCK)
            a = a_ref[:, block * down_rows : (block + 1) * down_rows].reshape(tile, RANKS)
            low = lax.dot_general(grad[here], a, LAST_BOTH, preferred_element_type=jnp.float32)
            out_ref[here] = (base_ref[here] + low).astype(out_ref.dtype)

    grad_shape = (pipe_count, data_count, rows, RANKS)
    return call(
        kernel,
        "input_gradient",
        grid=(data_count // planes,),
        in_specs=[
            SMEM,
            pl.BlockSpec((tok_dev, tile), lambda n: (0, n)),
            pl.BlockSpec((planes, all_rows, RANKS), lambda n: (n, 0, 0)),
        ]
        + [pl.BlockSpec(grad_shape, lambda n: (0, 0, 0, 0))] * tensor_count,
        out_specs=pl.BlockSpec((tok_dev, tile), lambda n: (0, n)),
        out_shape=jax.ShapeDtypeStruct((tok_dev, depth), jnp.bfloat16),
        scratch_shapes=[pltpu.VMEM((tok_dev, RANKS), jnp.bfloat16)],
    )(at, base, down, *grad_pieces)


def grad_down(at, slot_of, slots, x_features, grad_pieces):
    data_count, down_rows, tok_dev = x_features.shape
    tensor_count = len(grad_pieces)
    pipe_count, _, rows, _ = grad_pieces[0].shape
    blocks_dev = tok_dev // BLOCK

    def kernel(at_ref, x_ref, *rest):
        grad_refs, (out_ref, grad, x, sems) = rest[:tensor_count], rest[tensor_count:]
        copies = [
            pltpu.make_async_copy(x_ref.at[data], x.at[data], sems.at[data])
            for data in range(data_count)
        ]
        for copy in copies:
            copy.start()
        for s in range(tensor_count):
            core = came_from(at_ref[2], s, tensor_count)
            for k in range(pipe_count):
                chip = came_from(at_ref[1], k, pipe_count)
                first = pl.multiple_of((chip * tensor_count + core) * rows, rows)
                for m in range(data_count):
                    data = wrap(at_ref[0] - m, data_count)
                    grad[data, pl.ds(first, rows)] = grad_refs[s][k, m]
        out_ref[...] = jnp.zeros(out_ref.shape, out_ref.dtype)
        for data in range(data_count):
            copies[data].wait()
            for block in range(blocks_dev):
                slot = slot_of(at_ref, data, block)
                here = slice(block * BLOCK, (block + 1) * BLOCK)
                out_ref[slot] += jnp.dot(
                    x[data, :, here], grad[data, here], preferred_element_type=jnp.float32
                )

    return call(
        kernel,
        "grad_down",
        VMEM_MOST,
        in_specs=[SMEM, HBM] + [VMEM] * tensor_count,
        out_specs=VMEM,
        out_shape=jax.ShapeDtypeStruct((slots, down_rows, RANKS), jnp.float32),
        scratch_shapes=[
            pltpu.VMEM((data_count, tok_dev, RANKS), jnp.bfloat16),
            pltpu.VMEM(x_features.shape, jnp.bfloat16),
            pltpu.SemaphoreType.DMA((data_count,)),
        ],
    )(at, x_features, *grad_pieces)


def grad_up_pieces(at, low_pieces, cot_pieces, data_count, up_rows):
    tensor_count, pipe_count = len(cot_pieces), len(cot_pieces[0])
    group_count = tensor_count * pipe_count
    rows = cot_pieces[0][0].shape[0]
    cols = WIDTH // group_count
    tok_dev = group_count * rows
    blocks_dev = tok_dev // BLOCK
    group_half = group_count // 2
    order = [(s, k) for s in range(tensor_count) for k in range(pipe_count)]
    pieces = [cot_pieces[s][k] for s, k in order]
    in_kernel = cols % 128 == 0
    if not in_kernel:
        first_col = (at[1] * tensor_count + at[2]) * cols
        pieces = [lax.dynamic_slice_in_dim(piece, first_col, cols, 1) for piece in pieces]

    def kernel(at_ref, *rest):
        low_refs, rest = rest[:tensor_count], rest[tensor_count:]
        cot_refs, (out_ref, low, cot, sems) = rest[: len(order)], rest[len(order) :]
        my_group = at_ref[1] * tensor_count + at_ref[2]
        copies = []
        for i, (s, k) in enumerate(order):
            core = came_from(at_ref[2], s, tensor_count)
            chip = came_from(at_ref[1], k, pipe_count)
            first = pl.multiple_of((chip * tensor_count + core) * rows, rows)
            piece = cot_refs[i]
            if in_kernel:
                piece = piece.at[:, pl.ds(pl.multiple_of(my_group * cols, cols), cols)]
            copies.append(pltpu.make_async_copy(piece, cot.at[pl.ds(first, rows)], sems.at[i]))
        for copy in copies:
            copy.start()
        for s in range(tensor_count):
            core = came_from(at_ref[2], s, tensor_count)
            for k in range(pipe_count):
                first = pl.multiple_of((k * tensor_count + core) * rows, rows)
                low[pl.ds(first, rows)] = low_refs[s][k]
        for copy in copies:
            copy.wait()
        for block in range(blocks_dev):
            at = slice(block * BLOCK, (block + 1) * BLOCK)
            both = lax.dot_general(low[at], cot[at], FIRST_BOTH, preferred_element_type=jnp.float32)
            half = jnp.where(my_group < group_half, both[:ADAPTER_RANK], both[ADAPTER_RANK:])
            half = half.astype(out_ref.dtype)
            for data in range(data_count):
                k = wrap(data - at_ref[0], data_count)
                out_ref[k, block] = half[data * up_rows : (data + 1) * up_rows]

    return call(
        kernel,
        "grad_up_pieces",
        in_specs=[SMEM] + [VMEM] * tensor_count + [ANY] * len(order),
        out_specs=VMEM,
        out_shape=jax.ShapeDtypeStruct((data_count, blocks_dev, up_rows, cols), jnp.bfloat16),
        scratch_shapes=[
            pltpu.VMEM((tok_dev, RANKS), jnp.bfloat16),
            pltpu.VMEM((tok_dev, cols), jnp.bfloat16),
            pltpu.SemaphoreType.DMA((len(order),)),
        ],
    )(at, *low_pieces, *pieces)


def grad_up(at, slot_of, slots, pieces):
    data_count = len(pieces)
    blocks_dev, up_rows, cols = pieces[0].shape

    def kernel(at_ref, *rest):
        piece_refs, out_ref = rest[:data_count], rest[data_count]
        out_ref[...] = jnp.zeros(out_ref.shape, out_ref.dtype)
        for k in range(data_count):
            data = wrap(at_ref[0] - k, data_count)
            for block in range(blocks_dev):
                slot = slot_of(at_ref, data, block)
                out_ref[slot] += piece_refs[k][block].astype(out_ref.dtype)

    return call(
        kernel,
        "grad_up",
        in_specs=[SMEM] + [VMEM] * data_count,
        out_specs=VMEM,
        out_shape=jax.ShapeDtypeStruct((slots, up_rows, cols), jnp.float32),
    )(at, *pieces)


def own_rows(came, up, cotangent, first_up):
    rows = cotangent.shape[0]
    data_count = came.shape[0]
    up_rows = ADAPTER_RANK // data_count

    def kernel(cot_ref, came_ref, b_ref, grad_ref, tiles, sem):
        if up is None:
            copy = pltpu.make_async_copy(came_ref.at[:, pl.ds(first_up, tiles.shape[1])], tiles, sem)
            copy.start()
            copy.wait()
            for data in range(data_count):
                for n in range(WIDTH // RANKS):
                    b_ref[
                        data * up_rows : (data + 1) * up_rows, n * RANKS : (n + 1) * RANKS
                    ] = tiles[data, n * up_rows : (n + 1) * up_rows]
        else:
            b_ref[...] = came_ref[...]
        cot, b = cot_ref[...], b_ref[...]
        grad_ref[...] = jnp.concatenate(
            [
                lax.dot_general(cot[:, half], b[:, half], LAST_BOTH, preferred_element_type=jnp.float32)
                for half in (slice(0, KEY_WIDTH), slice(KEY_WIDTH, WIDTH))
            ],
            axis=1,
        ).astype(grad_ref.dtype)

    tile_rows = up_rows * WIDTH // RANKS
    return call(
        kernel,
        "own_rows",
        in_specs=[VMEM, ANY if up is None else VMEM],
        out_specs=(VMEM, VMEM),
        out_shape=(
            jax.ShapeDtypeStruct((ADAPTER_RANK, WIDTH), jnp.bfloat16),
            jax.ShapeDtypeStruct((rows, RANKS), jnp.bfloat16),
        ),
        scratch_shapes=[
            pltpu.VMEM((data_count, tile_rows, RANKS), jnp.bfloat16),
            pltpu.SemaphoreType.DMA,
        ],
    )(cotangent, came if up is None else up)


def keys_and_values(at, base_pieces, low_sum, b_own):
    rows = base_pieces[0].shape[0]
    count = len(base_pieces)

    def kernel(at_ref, low_ref, b_ref, *rest):
        base_refs, out_ref = rest[:count], rest[count]
        low = low_ref[at_ref[1]]
        for first, ranks in ((0, slice(0, ADAPTER_RANK)), (KEY_WIDTH, slice(ADAPTER_RANK, RANKS))):
            at = slice(first, first + KEY_WIDTH)
            y = jnp.dot(low[:, ranks], b_ref[:, at], preferred_element_type=jnp.float32)
            for base_ref in base_refs:
                y += base_ref[:, at].astype(jnp.float32)
            out_ref[:, at] = y.astype(out_ref.dtype)

    return call(
        kernel,
        "keys_and_values",
        in_specs=[SMEM, VMEM, VMEM] + [VMEM] * count,
        out_specs=VMEM,
        out_shape=jax.ShapeDtypeStruct((rows, WIDTH), jnp.bfloat16),
    )(at, low_sum, b_own, *base_pieces)


def body(
    tokens, key_value_weight, adapter_down, adapter_up, tenant_of_block, slot_of_tenant, cotangent
):
    data_count = lax.axis_size("dp")
    pipe_count = lax.axis_size("pipe")
    tensor_count = lax.axis_size("tensor")
    group_count = pipe_count * tensor_count
    at_data, at_pipe, at_tensor = (lax.axis_index(a) for a in ("dp", "pipe", "tensor"))
    my_group = at_pipe * tensor_count + at_tensor
    tok_dev, feature_count = tokens.shape
    blocks_dev = tok_dev // BLOCK
    rows = tok_dev // group_count
    down_rows = adapter_down.shape[1]
    up_rows = adapter_up.shape[1]
    slots = adapter_down.shape[0]
    blocks = tenant_of_block.shape[0]

    own_block = my_group * rows // BLOCK
    at = jnp.stack([at_data, at_pipe, at_tensor, own_block]).astype(jnp.int32)
    at = jnp.concatenate([at, tenant_of_block, slot_of_tenant])

    def slot_of(at_ref, data, block):
        return at_ref[4 + blocks + at_ref[4 + data * blocks_dev + block]]

    a_send = pick(
        tenant_of_block, slot_of_tenant, adapter_down, adapter_up, blocks_dev, rows
    )
    a_recv = lax.all_to_all(a_send, "dp", 0, 0, tiled=True)
    up = None
    if not up_rides(adapter_up):
        up = lax.all_to_all(pick_up(at, slot_of, adapter_up, data_count), "dp", 0, 0, tiled=True)
        up = up.reshape(ADAPTER_RANK, WIDTH)

    behind, a_send = lax.optimization_barrier((tokens, a_send))
    cot_chips, base_tokens, x_tokens = gather_chips(cotangent, behind)
    cot_chips = [cotangent] + cot_chips

    tokens_by_group = base_tokens.reshape(pipe_count, tensor_count, rows, feature_count)
    parts = 2 if pipe_count % 2 == 0 else 1
    chips = pipe_count // parts
    base_send = base_product(at, tokens_by_group, key_value_weight, 1, tensor_count - 1, parts)
    base_came = [
        [swap(part[s - 1], "tensor", s) for part in base_send] for s in range(1, tensor_count)
    ]
    (base_keep,) = base_product(at, tokens_by_group, key_value_weight, 0, 1, 1)
    base_chip = [
        sum(
            [base_keep[0, k].astype(jnp.float32)]
            + [came[k // chips][k % chips].astype(jnp.float32) for came in base_came]
        )
        for k in range(pipe_count)
    ]
    base_chip[1:] = [piece.astype(jnp.bfloat16) for piece in base_chip[1:]]
    base_chip_came = [swap(base_chip[k], "pipe", k) for k in range(1, pipe_count)]

    cot_pieces = [cot_chips] + [
        [swap(piece, "tensor", s) for piece in cot_chips] for s in range(1, tensor_count)
    ]
    input_base = cotangent_product(at, cot_pieces, key_value_weight)

    x_send = x_tokens.T.reshape(data_count, down_rows, tok_dev)

    a_recv, x_send, input_base, base_chip_came[:2] = lax.optimization_barrier(
        (a_recv, x_send, input_base, base_chip_came[:2])
    )
    b_own, grad_rows = own_rows(a_recv, up, cotangent, blocks_dev * down_rows)
    grad_data = [grad_rows] + [shift(grad_rows, "dp", k) for k in range(1, data_count)]
    x_send, grad_data = lax.optimization_barrier((x_send, grad_data))
    x_recv = lax.all_to_all(x_send, "dp", 0, 0, tiled=True)

    grad_all = jnp.stack(grad_data)
    grad_chips = jnp.stack([grad_all] + [swap(grad_all, "pipe", k) for k in range(1, pipe_count)])
    grad_pieces = [grad_chips] + [swap(grad_chips, "tensor", s) for s in range(1, tensor_count)]
    input_grad = input_gradient(at, input_base, grad_pieces, a_recv)

    low_down, base_chip_came, grad_data = lax.optimization_barrier(
        (a_recv, base_chip_came, grad_data)
    )
    low_part = low_product(at, tokens, low_down, pipe_count, tensor_count)
    low_core = sum(
        [low_part[0].astype(jnp.float32)]
        + [swap(low_part[s], "tensor", s).astype(jnp.float32) for s in range(1, tensor_count)]
    ).astype(jnp.bfloat16)
    low_came = [swap(low_core, "pipe", k) for k in range(1, pipe_count)]
    low_sum = sum([piece.astype(jnp.float32) for piece in [low_core] + low_came])
    low_sum = low_sum.astype(jnp.bfloat16)
    low_pieces = [low_sum] + [swap(low_sum, "tensor", s) for s in range(1, tensor_count)]
    key_value = keys_and_values(at, base_chip[:1] + base_chip_came, low_sum, b_own)

    up_pieces = grad_up_pieces(at, low_pieces, cot_pieces, data_count, up_rows)
    up_came = [up_pieces[0]] + [shift(up_pieces[k], "dp", k) for k in range(1, data_count)]
    grad_a = grad_down(at, slot_of, slots, x_recv, grad_pieces)
    up_came, grad_a = lax.optimization_barrier((up_came, grad_a))
    grad_b = grad_up(at, slot_of, slots, up_came)
    return (key_value, input_grad, grad_a, grad_b)


def solution(mesh):
    atd = (
        P("dp", ("pipe", "tensor")),
        P(("pipe", "tensor"), None),
        P(None, ("pipe", "tensor", "dp"), None),
        P(None, "dp", None),
        P(),
        P(),
        P(("dp", "pipe", "tensor"), None),
    )
    return jax.shard_map(
        body,
        mesh=mesh,
        in_specs=atd,
        out_specs=(
            P(("dp", "pipe", "tensor"), None),
            P("dp", ("pipe", "tensor")),
            P(None, ("pipe", "tensor", "dp"), None),
            P(None, "dp", ("pipe", "tensor")),
        ),
        check_vma=False,
    )
```
